32 devices in a mesh: groups: 2 (over y), rows: 4 (over z), tiles: 2 (over x), cols: 2 (over core).
Axes of the slice: x: 2, y: 2, z: 4, core: 2. Of those that a mesh axis runs over, the one named last changes fastest.
Arguments:
- embeddings: bfloat16 [16384, 768], P(('groups', 'rows'), 'cols'), parts along dimension 0
- start: float32 [16384, 64], P(('groups', 'rows'), 'cols'), parts along dimension 0, may hold values from -6 to 6
- pair_list: int32 [16, 2, 8], P(('groups', 'rows', 'tiles')), parts along dimension 0, may hold values from 0 to 63, as said below
- pair_count: int32 [16], P(('groups', 'rows', 'tiles')), parts along dimension 0, may hold values from 2 to 8, as said below
Outputs:
- vectors: float32 [16384, 64], P(('groups', 'rows'), 'cols'), parts along dimension 0
- degree: float32 [16384], P(('groups', 'rows')), parts along dimension 0
The draws below stay inside these ranges and needn't reach their ends.
There are 2 independent parts, one for each index of `groups`. The reference program is written for one: setup_inputs(seed, part) draws one part's arguments, and reference() takes and returns one part's arrays. A program takes and returns all parts, laid end to end along the dimension named above; each array names one. Nothing has to cross between parts.
Inputs may be any that keep to these rules, and one draw needn't show every extreme that they name: For list q let r = q // 2: every pair_list[q, 0, s] lies in r * 16 to (r + 1) * 16 - 1, and pair_list[q, 1, s] differs from pair_list[q, 0, s]. Among the live slots of list q, at most 2 have the same value of pair_list[q, 1, s] // 16; the list with 8 live slots has exactly 2 for every value. `pair_count`: some list has all 8 slots live.
All inputs are finite; a program needn't handle non-finite values.
Results may differ from the reference program's by a relative error of at most 0.0003.
Values may be sent and summed in bfloat16 or wider, within the bound.
No kernel may reach another device: no remote copies, remote signals or barrier semaphores. Data moves between devices by JAX's collectives and lax.ppermute only.
A program may use at most 128 MiB of HBM per device.

```python
import jax
import jax.numpy as jnp
from jax import lax

FEAT = 768
COLS = 64
BLOCK = 128
BLK_DEV = 16
CAP = 2
ITERS = 2
PAIR_SLOTS = 8
LISTS = 8
BLOCKS = 64
POINTS = 8192


def draw_embeddings(key, part):
    key = jax.random.fold_in(key, 3)
    values = jax.random.normal(key, (POINTS, FEAT), jnp.float32)
    return (values * FEAT ** (-0.5)).astype(jnp.bfloat16)


def draw_pair_list(key, part):
    key = jax.random.fold_in(key, 5)
    lanes = PAIR_SLOTS // CAP
    list_keys = jax.random.split(jax.random.fold_in(key, 1), LISTS)
    slot_owner = jnp.arange(PAIR_SLOTS, dtype=jnp.int32) % lanes
    owners = jax.vmap(lambda subkey: jax.random.permutation(subkey, slot_owner))(list_keys)
    home_rows = (jnp.arange(LISTS, dtype=jnp.int32) // (LISTS // lanes))[:, None]
    local_ids = jax.random.randint(jax.random.fold_in(key, 2), (LISTS, PAIR_SLOTS), 0, BLK_DEV, jnp.int32)
    other_ids = jax.random.randint(jax.random.fold_in(key, 3), (LISTS, PAIR_SLOTS), 0, BLK_DEV, jnp.int32)
    shifts = jax.random.randint(jax.random.fold_in(key, 4), (LISTS, PAIR_SLOTS), 1, BLK_DEV, jnp.int32)
    first_ids = home_rows * BLK_DEV + local_ids
    second_ids = jnp.where(owners == home_rows, home_rows * BLK_DEV + (local_ids + shifts) % BLK_DEV, owners * BLK_DEV + other_ids)
    return jnp.stack([first_ids, second_ids], axis=1).astype(jnp.int32)


def draw_pair_count(key, part):
    key = jax.random.fold_in(key, 7)
    counts = jax.random.randint(key, (LISTS,), PAIR_SLOTS // 4, PAIR_SLOTS + 1, jnp.int32)
    fullest = jax.random.randint(jax.random.fold_in(key, 1), (), 0, LISTS, jnp.int32)
    return jnp.where(jnp.arange(LISTS, dtype=jnp.int32) == fullest, PAIR_SLOTS, counts).astype(jnp.int32)


def block_levels(key, shape, cuts, least, high):
    loudness = 1.0
    for axis_at, parts in cuts:
        draws = jax.random.uniform(jax.random.fold_in(jax.random.fold_in(key, 6), axis_at), (parts,), jnp.float32, least / len(cuts), high / len(cuts))
        loudness = loudness * jnp.repeat(jnp.exp(draws), shape[axis_at] // parts).reshape((-1,) + (1,) * (len(shape) - 1 - axis_at))
    return loudness


def centred(key, dims, width, most, cuts=(), kind=jnp.bfloat16):
    array = jax.random.normal(key, dims, jnp.float32) * width
    if len(cuts) > 0:
        array = block_levels(key, dims, cuts, -0.22, 0.18) * array
    return jnp.clip(array, min=-most, max=most).astype(kind)


def setup_inputs(seed: int = 0, part: int = 0) -> dict:
    arg_keys = jax.random.split(jax.random.key(seed), 5)
    own_keys = jax.random.split(jax.random.fold_in(arg_keys[4], part), 5)
    embeddings = draw_embeddings(jax.random.fold_in(jax.random.fold_in(arg_keys[4], part), 71), part)
    start = centred(own_keys[1], (POINTS, COLS), 1.0, 6.0, ((0, 4), (1, 2)), jnp.float32)
    pair_list = draw_pair_list(jax.random.fold_in(jax.random.fold_in(arg_keys[4], part), 71), part)
    pair_count = draw_pair_count(jax.random.fold_in(jax.random.fold_in(arg_keys[4], part), 71), part)
    return {"embeddings": embeddings, "start": start, "pair_list": pair_list, "pair_count": pair_count}


kernel_gamma = 14.0

def upper_inverse(gram_matrix):
    lower = jnp.linalg.cholesky(gram_matrix)
    identity = jnp.eye(gram_matrix.shape[0], dtype=gram_matrix.dtype)
    inverse = lax.linalg.triangular_solve(lower, identity, left_side=True, lower=True)
    return inverse.T

def tile_of(left, right):
    inner_prod = jnp.dot(left.astype(jnp.float32), right.T.astype(jnp.float32), precision=lax.Precision.HIGHEST, preferred_element_type=jnp.float32)
    left_sq = lax.optimization_barrier(jnp.sum(left * left, axis=1))
    right_sq = lax.optimization_barrier(jnp.sum(right * right, axis=1))
    return jnp.exp(-kernel_gamma * (left_sq[:, None] + right_sq[None, :] - 2.0 * inner_prod - 2.0))

def apply_kernel(blocks, row_block, col_block, live_mask, values):
    block_size = blocks.shape[1]
    hollow = 1.0 - jnp.eye(block_size, dtype=jnp.float32)

    def diagonal_apply(block_pair):
        block_rows, block_values = block_pair
        return jnp.dot(tile_of(block_rows, block_rows) * hollow, block_values, precision=lax.Precision.HIGHEST)
    summed = lax.map(diagonal_apply, (blocks, values))

    def pair_step(running, pair_item):
        first_id, second_id, live_flag = pair_item
        kernel_tile = tile_of(blocks[first_id], blocks[second_id]) * live_flag
        running = running.at[first_id].add(jnp.dot(kernel_tile, values[second_id], precision=lax.Precision.HIGHEST))
        running = running.at[second_id].add(jnp.dot(kernel_tile.T, values[first_id], precision=lax.Precision.HIGHEST))
        return (running, None)
    summed, _ = lax.scan(pair_step, summed, (row_block, col_block, live_mask))
    return summed

def reference(embeddings, start, pair_list, pair_count):
    blocks = embeddings.astype(jnp.float32).reshape(BLOCKS, BLOCK, FEAT)
    row_block = pair_list[:, 0, :].reshape(-1).astype(jnp.int32)
    col_block = pair_list[:, 1, :].reshape(-1).astype(jnp.int32)
    live_mask = (jnp.arange(PAIR_SLOTS, dtype=jnp.int32)[None, :] < pair_count[:, None]).reshape(-1).astype(jnp.float32)
    all_ones = jnp.ones((BLOCKS, BLOCK, 1), jnp.float32)
    degree = apply_kernel(blocks, row_block, col_block, live_mask, all_ones).reshape(POINTS)
    inv_root = 1.0 / jnp.sqrt(degree)
    vectors = start
    for iteration in range(ITERS):
        inputs = (vectors * inv_root[:, None]).reshape(BLOCKS, BLOCK, COLS)
        mapped = apply_kernel(blocks, row_block, col_block, live_mask, inputs).reshape(POINTS, COLS) * inv_root[:, None]
        gram_matrix = jnp.dot(mapped.T, mapped, precision=lax.Precision.HIGHEST)
        inverse = upper_inverse(gram_matrix)
        vectors = jnp.dot(mapped, inverse, precision=lax.Precision.HIGHEST)
    return (vectors, degree)
```

```python
import functools

import jax
import jax.numpy as jnp
from jax import lax
from jax.experimental import pallas as pl
from jax.experimental.pallas import tpu as pltpu
from jax.sharding import PartitionSpec as P

BLOCK = 128
kernel_gamma = 14.0

VMEM = pl.BlockSpec(memory_space=pltpu.VMEM)
SMEM = pl.BlockSpec(memory_space=pltpu.SMEM)
F32 = jnp.float32
BF16 = jnp.bfloat16
HIGHEST = lax.Precision.HIGHEST
NT = (((1,), (1,)), ((), ()))


def call(body, outs, args, smem_in=(), smem_out=(), cycles=1000):
    single = not isinstance(outs, (list, tuple))
    shapes = [outs] if single else list(outs)
    result = pl.pallas_call(
        body,
        out_shape=shapes,
        in_specs=[SMEM if i in smem_in else VMEM for i in range(len(args))],
        out_specs=[SMEM if i in smem_out else VMEM for i in range(len(shapes))],
        compiler_params=pltpu.CompilerParams(vmem_limit_bytes=48 * 2**20),
    )(*args)
    return result[0] if single else result


def sds(shape, dtype):
    return jax.ShapeDtypeStruct(shape, dtype)


def at_block(index):
    return pl.ds(pl.multiple_of(index * BLOCK, BLOCK), BLOCK)


def eye_mask(size):
    return lax.broadcasted_iota(jnp.int32, (size, size), 0) == lax.broadcasted_iota(
        jnp.int32, (size, size), 1
    )


def halves(value):
    high = value.astype(BF16)
    low = (value - high.astype(F32)).astype(BF16)
    return high, low


def pack(tile):
    return jnp.concatenate(halves(tile), axis=0)


def product(packed, values):
    left = jnp.concatenate(halves(values), axis=0)
    both = jnp.dot(jnp.concatenate([left, left], axis=1), packed, preferred_element_type=F32)
    count = values.shape[0]
    return both[:count] + both[count:]


def gram(full):
    high = full.astype(BF16)
    rest = full - high.astype(F32)
    middle = rest.astype(BF16)
    low = (rest - middle.astype(F32)).astype(BF16)
    parts = jnp.concatenate([high, middle, low], axis=0)
    cross = lax.dot_general(parts, parts, NT, preferred_element_type=F32)
    n = full.shape[0]
    total = None
    for i, j in ((2, 2), (1, 2), (2, 1), (0, 2), (2, 0), (1, 1), (0, 1), (1, 0), (0, 0)):
        piece = cross[i * n : (i + 1) * n, j * n : (j + 1) * n]
        total = piece if total is None else total + piece
    return total


def lower_inverse(matrix):
    n = matrix.shape[0]
    rows = lax.broadcasted_iota(jnp.int32, (n, 1), 0)
    state = jnp.concatenate([matrix, eye_mask(n).astype(F32)], axis=1)
    for j in range(n - 1):
        pivot_row = state[j : j + 1, :]
        scaled = pivot_row / state[j : j + 1, j : j + 1]
        column = jnp.where(rows > j, state[:, j : j + 1], 0.0)
        state = state - column * scaled
    pivots = jnp.sum(jnp.where(eye_mask(n), state[:, :n], 0.0), axis=1, keepdims=True)
    return state[:, n:] / jnp.sqrt(pivots)


def both_columns(core, own, other):
    first = core == 0
    return jnp.concatenate(
        [jnp.where(first, own, other), jnp.where(first, other, own)], axis=0
    )


def plan_body(dims, me, *refs):
    row_count, capacity, slots, blocks_here, list_rows = dims
    lists = refs[: len(list_rows)]
    emb = refs[len(list_rows)]
    idx = refs[len(list_rows) + 1]
    sends = refs[len(list_rows) + 2 :]
    row = me[0]

    def clear(i, carry):
        for line in range(6):
            idx[line, i] = 0
        return carry

    lax.fori_loop(0, slots, clear, 0)

    def ranked(ref, line, want, write):
        count = ref[line, 2 * slots]

        def step(s, counts):
            near = ref[line, s]
            far = ref[line, slots + s]
            owner = far // blocks_here
            live = s < count
            return write(s, near, far, owner, live, counts)

        lax.fori_loop(0, slots, step, (0,) * want)

    def write_own(s, near, far, owner, live, counts):
        shift = lax.rem(owner - row + row_count, row_count)
        rank = functools.reduce(
            lambda total, k: total + jnp.where(shift == k, counts[k], 0), range(row_count), 0
        )

        @pl.when(live)
        def _():
            slot = shift * capacity + rank
            idx[0, slot] = near - row * blocks_here
            idx[1, slot] = far
            idx[2, slot] = 1
            idx[3, slot] = s

        return tuple(
            counts[k] + (live & (shift == k)).astype(jnp.int32) for k in range(row_count)
        )

    for k in range(row_count):
        if len(lists) == 1:
            line = lax.rem(row - k + row_count, row_count) * list_rows[0][1] + me[1]
            ref = lists[0]
        else:
            line = 0
            ref = lists[k]
        if k == 0:
            ranked(ref, line, row_count, write_own)

        def write_in(s, near, far, owner, live, counts, k=k):
            hit = live & (owner == row)

            @pl.when(hit)
            def _():
                slot = k * capacity + counts[0]
                idx[4, slot] = far - row * blocks_here
                idx[5, slot] = near

            return (counts[0] + hit.astype(jnp.int32),)

        ranked(ref, line, 1, write_in)
    for k in range(1, row_count):
        for j in range(capacity):
            sends[k - 1][j * BLOCK : (j + 1) * BLOCK, :] = emb[at_block(idx[4, k * capacity + j]), :]


def partial_distance(left, right):
    inner = lax.dot_general(left, right, NT, preferred_element_type=F32)
    left_sq = jnp.sum(jnp.square(left.astype(F32)), axis=1, keepdims=True)
    right_sq = jnp.sum(jnp.square(right.astype(F32)), axis=1, keepdims=True)
    right_row = jnp.sum(jnp.where(eye_mask(BLOCK), right_sq, 0.0), axis=0, keepdims=True)
    return left_sq + right_row - 2.0 * inner


def self_distance_body(own_blocks, tile_count, me, emb, out):
    for i in range(own_blocks):
        block = emb[at_block(i * tile_count + me[1]), :]
        out[i * BLOCK : (i + 1) * BLOCK, :] = partial_distance(block, block)


def pair_distance_body(row_count, capacity, idx, emb, *refs):
    out = refs[-1]
    for k in range(row_count):
        for j in range(capacity):
            slot = k * capacity + j
            left = emb[at_block(idx[0, slot]), :]
            if k == 0:
                right = emb[at_block(idx[4, j]), :]
            else:
                right = refs[k - 1][j * BLOCK : (j + 1) * BLOCK, :]
            out[slot * BLOCK : (slot + 1) * BLOCK, :] = partial_distance(left, right)


def self_tile_body(own_blocks, mine, other, packed, sums):
    for i in range(own_blocks):
        part = slice(i * BLOCK, (i + 1) * BLOCK)
        tile = jnp.exp(-kernel_gamma * (mine[part, :] + other[part, :] - 2.0))
        tile = jnp.where(eye_mask(BLOCK), 0.0, tile)
        packed[i] = pack(tile)
        sums[i : i + 1, :] = jnp.sum(tile, axis=0, keepdims=True)


def pair_tile_body(row_count, capacity, per_core, slots, me, idx, mine, other, self_sums, near_tiles, home_tiles, *refs):
    sends = refs[:-1]
    sums = refs[-1]
    core = me[2]
    sums[0 : 2 * slots, :] = jnp.zeros((2 * slots, BLOCK), F32)
    sums[2 * slots :, :] = self_sums[...]
    for k in range(row_count):
        for j in range(capacity):
            slot = k * capacity + j
            part = slice(slot * BLOCK, (slot + 1) * BLOCK)
            live = idx[2, slot] > 0
            tile = jnp.exp(-kernel_gamma * (mine[part, :] + other[part, :] - 2.0))
            tile = jnp.where(live, tile, 0.0)
            turned = tile.T
            near_tiles[slot] = pack(turned)

            @pl.when(live)
            def _():
                raw = idx[3, slot]
                sums[pl.ds(raw, 1), :] = jnp.sum(turned, axis=0, keepdims=True)
                sums[pl.ds(slots + raw, 1), :] = jnp.sum(tile, axis=0, keepdims=True)

            if k == 0:
                home_tiles[j] = pack(tile)
            else:

                @pl.when(core == j // per_core)
                def _():
                    sends[k - 1][j % per_core] = pack(tile)


def pick_columns(idx, row_count, capacity, source, sends):
    for k in range(1, row_count):
        back = row_count - k
        for j in range(capacity):
            sends[k - 1][:, j * BLOCK : (j + 1) * BLOCK] = source[:, at_block(idx[0, k * capacity + j])]
            place = capacity + j
            sends[k - 1][:, place * BLOCK : (place + 1) * BLOCK] = source[
                :, at_block(idx[4, back * capacity + j])
            ]


def pick_body(row_count, capacity, idx, source, *sends):
    pick_columns(idx, row_count, capacity, source, sends)


def apply_tiles(dims, me, idx, inverse, own, received, near_tiles, home_tiles, sent, shared, self_tiles, out):
    row_count, capacity, per_core, blocks_here, tile_count = dims
    row, tile_index, core = me[0], me[1], me[2]
    out[...] = jnp.zeros(out.shape, F32)

    def scaled(values, block):
        return values * inverse[pl.ds(block, 1), :]

    def add(block, packed, values):
        place = at_block(block)
        out[:, place] = out[:, place] + product(packed, values)

    for i in range(blocks_here // tile_count):
        block = i * tile_count + tile_index
        add(block, self_tiles[i], scaled(own[:, at_block(block)], row * blocks_here + block))
    for k in range(row_count):
        for j in range(capacity):
            slot = k * capacity + j
            if k == 0:
                values = own[:, at_block(idx[4, j])]
            else:
                values = received[row_count - k - 1][:, (capacity + j) * BLOCK : (capacity + j + 1) * BLOCK]
            add(idx[0, slot], near_tiles[slot], scaled(values, idx[1, slot]))
    for k in range(row_count):
        for j in range(capacity):
            if k == 0:
                slot = j
                values = own[:, at_block(idx[0, j])]
                packed = home_tiles[j]
            else:
                inner = j % per_core
                if j < per_core:
                    place = core * per_core + inner
                    packed = sent[k - 1][inner]
                else:
                    place = (1 - core) * per_core + inner
                    packed = shared[k - 1][inner]
                slot = k * capacity + place
                values = received[k - 1][:, at_block(place)]
            add(idx[4, slot], packed, scaled(values, idx[5, slot]))


def first_apply_body(dims, sum_count, me, idx, onehot, *refs):
    row_count = dims[0]
    sums = refs[:sum_count]
    refs = refs[sum_count:]
    others = row_count - 1
    own = refs[0]
    received = refs[1 : 1 + others]
    near_tiles, home_tiles = refs[1 + others : 3 + others]
    sent = refs[3 + others : 3 + 2 * others]
    shared = refs[3 + 2 * others : 3 + 3 * others]
    self_tiles, out, degree, inverse = refs[3 + 3 * others :]
    if sum_count == 1:

        def step(i, total):
            return total + jnp.dot(onehot[i], sums[0][i], precision=HIGHEST, preferred_element_type=F32)

        total = lax.fori_loop(0, sums[0].shape[0], step, jnp.zeros(degree.shape, F32))
    else:
        total = None
        for i in range(sum_count):
            piece = jnp.dot(onehot[i], sums[i][...], precision=HIGHEST, preferred_element_type=F32)
            total = piece if total is None else total + piece
    degree[...] = total
    inverse[...] = 1.0 / jnp.sqrt(total)
    apply_tiles(dims, me, idx, inverse, own, received, near_tiles, home_tiles, sent, shared, self_tiles, out)


def second_apply_body(dims, me, idx, inverse, *refs):
    others = dims[0] - 1
    own = refs[0]
    received = refs[1 : 1 + others]
    near_tiles, home_tiles = refs[1 + others : 3 + others]
    sent = refs[3 + others : 3 + 2 * others]
    shared = refs[3 + 2 * others : 3 + 3 * others]
    self_tiles, out = refs[3 + 3 * others :]
    apply_tiles(dims, me, idx, inverse, own, received, near_tiles, home_tiles, sent, shared, self_tiles, out)


def scale_rows(me, blocks_here, inverse, mine, other, out):
    for b in range(blocks_here):
        part = slice(b * BLOCK, (b + 1) * BLOCK)
        row = inverse[pl.ds(me[0] * blocks_here + b, 1), :]
        out[:, part] = (mine[:, part] + other[:, part]) * row


def mapped_body(row_count, capacity, blocks_here, me, idx, inverse, mine, other, out, *sends):
    scale_rows(me, blocks_here, inverse, mine, other, out)
    pick_columns(idx, row_count, capacity, out, sends)


def last_mapped_body(blocks_here, me, inverse, mine, other, out):
    scale_rows(me, blocks_here, inverse, mine, other, out)


def gram_body(me, own, other, out):
    out[...] = gram(both_columns(me[2], own[...], other[...]))


def factor_body(*refs):
    total = refs[0][...]
    for ref in refs[1:-1]:
        total = total + ref[...]
    refs[-1][...] = lower_inverse(total)


def second_gram_body(me, factor, own, other, mapped, out):
    full = both_columns(me[2], own[...], other[...])
    value = jnp.dot(factor[...], full, precision=HIGHEST, preferred_element_type=F32)
    mapped[...] = value
    out[...] = gram(value)


def final_body(me, mapped, *refs):
    out = refs[-1]
    total = refs[0][...]
    for ref in refs[1:-1]:
        total = total + ref[...]
    factor = lower_inverse(total)
    own_cols = out.shape[0]
    part = jnp.where(me[2] == 0, factor[:own_cols], factor[own_cols:])
    out[...] = jnp.dot(part, mapped[...], precision=HIGHEST, preferred_element_type=F32)


def shift_by(value, axes, size, shift):
    return lax.ppermute(value, axes, [(i, (i + shift) % size) for i in range(size)])


def gather_all(value, axes, size):
    if size > 8:
        return [lax.all_gather(value, axes)]
    return [value] + [shift_by(value, axes, size, k) for k in range(1, size)]


def local(embeddings, start, pair_list, pair_count):
    row_count = lax.axis_size("rows")
    tile_count = lax.axis_size("tiles")
    core_count = lax.axis_size("cols")
    row_index = lax.axis_index("rows")
    tile_index = lax.axis_index("tiles")
    col_index = lax.axis_index("cols")
    me = jnp.stack([row_index, tile_index, col_index]).astype(jnp.int32)
    rows_here, half_features = embeddings.shape
    blocks_here = rows_here // BLOCK
    slots = pair_list.shape[2]
    capacity = slots // row_count
    per_core = capacity // core_count
    own_blocks = blocks_here // tile_count
    own_cols = start.shape[1]
    team = row_count * tile_count
    block_count = row_count * blocks_here
    others = range(1, row_count)

    lists = jnp.concatenate([pair_list.reshape(1, 2 * slots), pair_count.reshape(1, 1)], axis=1)
    lists = gather_all(lists, ("rows", "tiles"), team)
    if len(lists) == 1:
        all_lists = lists[0].reshape(team, 2 * slots + 1)
        plan_lists = [all_lists]
        list_rows = ((team, tile_count),)
        origin = jnp.arange(team, dtype=jnp.int32)
    else:
        all_lists = jnp.concatenate(lists, axis=0)
        plan_lists = [lists[k * tile_count] for k in range(row_count)]
        list_rows = ((1, 0),) * row_count
        origin = (row_index * tile_count + tile_index - jnp.arange(team, dtype=jnp.int32)) % team

    planned = call(
        functools.partial(plan_body, (row_count, capacity, slots, blocks_here, list_rows)),
        [sds((6, slots), jnp.int32)] + [sds((capacity * BLOCK, half_features), BF16) for _ in others],
        [me, *plan_lists, embeddings],
        smem_in=range(1 + len(plan_lists)),
        smem_out=(0,),
    )
    idx, sends = planned[0], planned[1:]
    far = [shift_by(sends[k - 1], "rows", row_count, -k) for k in others]

    self_part = call(
        functools.partial(self_distance_body, own_blocks, tile_count),
        sds((own_blocks * BLOCK, BLOCK), F32),
        [me, embeddings],
        smem_in=(0,),
    )
    self_other = shift_by(self_part, "cols", core_count, 1)
    self_tiles, self_sums = call(
        functools.partial(self_tile_body, own_blocks),
        [sds((own_blocks, 2 * BLOCK, BLOCK), BF16), sds((own_blocks, BLOCK), F32)],
        [self_part, self_other],
    )

    pair_part = call(
        functools.partial(pair_distance_body, row_count, capacity),
        sds((slots * BLOCK, BLOCK), F32),
        [idx, embeddings, *far],
        smem_in=(0,),
    )
    pair_other = shift_by(pair_part, "cols", core_count, 1)

    values = start.T
    start_sends = call(
        functools.partial(pick_body, row_count, capacity),
        [sds((own_cols, 2 * capacity * BLOCK), F32) for _ in others],
        [idx, values],
        smem_in=(0,),
    )
    start_in = [shift_by(start_sends[k - 1], "rows", row_count, k) for k in others]

    tiles = call(
        functools.partial(pair_tile_body, row_count, capacity, per_core, slots),
        [sds((slots, 2 * BLOCK, BLOCK), BF16), sds((capacity, 2 * BLOCK, BLOCK), BF16)]
        + [sds((per_core, 2 * BLOCK, BLOCK), BF16) for _ in others]
        + [sds((2 * slots + own_blocks, BLOCK), F32)],
        [me, idx, pair_part, pair_other, self_sums],
        smem_in=(0, 1),
    )
    near_tiles, home_tiles, tile_sends, sums = tiles[0], tiles[1], tiles[2:-1], tiles[-1]
    all_sums = gather_all(sums, ("rows", "tiles"), team)
    sent = [shift_by(tile_sends[k - 1], "rows", row_count, k) for k in others]
    shared = [shift_by(tile, "cols", core_count, 1) for tile in sent]

    diagonal_ids = origin[:, None] // tile_count * blocks_here + (
        jnp.arange(own_blocks, dtype=jnp.int32)[None, :] * tile_count + origin[:, None] % tile_count
    )
    sum_ids = jnp.concatenate([all_lists[:, : 2 * slots], diagonal_ids], axis=1)
    onehot = (
        sum_ids[:, None, :] == jnp.arange(block_count, dtype=jnp.int32)[None, :, None]
    ).astype(F32)

    dims = (row_count, capacity, per_core, blocks_here, tile_count)
    tile_args = [near_tiles, home_tiles, *sent, *shared, self_tiles]
    block_shape = sds((own_cols, rows_here), F32)
    table = sds((block_count, BLOCK), F32)

    def team_sum(part):
        if tile_count == 2:
            return part, shift_by(part, "tiles", 2, 1)
        return lax.psum(part, "tiles"), jnp.zeros_like(part)

    part, degree, inverse = call(
        functools.partial(first_apply_body, dims, len(all_sums)),
        [block_shape, table, table],
        [me, idx, onehot, *all_sums, values, *start_in, *tile_args],
        smem_in=(0, 1),
    )
    mine, other = team_sum(part)
    first = call(
        functools.partial(mapped_body, row_count, capacity, blocks_here),
        [block_shape] + [sds((own_cols, 2 * capacity * BLOCK), F32) for _ in others],
        [me, idx, inverse, mine, other],
        smem_in=(0, 1),
    )
    mapped, sends = first[0], first[1:]
    received = [shift_by(sends[k - 1], "rows", row_count, k) for k in others]

    mapped_other = shift_by(mapped, "cols", core_count, 1)
    square = sds((2 * own_cols, 2 * own_cols), F32)
    first_gram = call(gram_body, square, [me, mapped, mapped_other], smem_in=(0,))
    grams = [first_gram] + [shift_by(first_gram, "rows", row_count, k) for k in others]
    factor = call(factor_body, square, grams)

    part = call(
        functools.partial(second_apply_body, dims),
        block_shape,
        [me, idx, inverse, mapped, *received, *tile_args],
        smem_in=(0, 1),
    )
    mine, other = team_sum(part)
    second = call(
        functools.partial(last_mapped_body, blocks_here),
        block_shape,
        [me, inverse, mine, other],
        smem_in=(0,),
    )
    second_other = shift_by(second, "cols", core_count, 1)
    full, second_gram = call(
        second_gram_body,
        [sds((2 * own_cols, rows_here), F32), square],
        [me, factor, second, second_other],
        smem_in=(0,),
    )
    grams = [second_gram] + [shift_by(second_gram, "rows", row_count, k) for k in others]
    vectors = call(final_body, block_shape, [me, full, *grams], smem_in=(0,))
    own_degree = lax.dynamic_slice_in_dim(degree, row_index * blocks_here, blocks_here, 0)
    return (vectors.T, own_degree.reshape(rows_here))


def solution(mesh):
    in_specs = (
        P(("groups", "rows"), "cols"),
        P(("groups", "rows"), "cols"),
        P(("groups", "rows", "tiles"), None, None),
        P(("groups", "rows", "tiles")),
    )
    out_specs = (P(("groups", "rows"), "cols"), P(("groups", "rows")))
    return jax.shard_map(local, mesh=mesh, in_specs=in_specs, out_specs=out_specs, check_vma=False)
```

```python
import functools

import jax
import jax.numpy as jnp
from jax import lax
from jax.experimental import pallas as pl
from jax.experimental.pallas import tpu as pltpu
from jax.sharding import PartitionSpec as P

BLOCK = 128
kernel_gamma = 14.0

VMEM = pl.BlockSpec(memory_space=pltpu.VMEM)
SMEM = pl.BlockSpec(memory_space=pltpu.SMEM)
ANY = pl.BlockSpec(memory_space=pl.ANY)
F32 = jnp.float32
BF16 = jnp.bfloat16
HIGHEST = lax.Precision.HIGHEST
NT = (((1,), (1,)), ((), ()))


def call(body, outs, args, smem_in=(), smem_out=(), any_in=()):
    single = not isinstance(outs, (list, tuple))
    shapes = [outs] if single else list(outs)
    result = pl.pallas_call(
        body,
        out_shape=shapes,
        in_specs=[
            SMEM if i in smem_in else ANY if i in any_in else VMEM for i in range(len(args))
        ],
        out_specs=[SMEM if i in smem_out else VMEM for i in range(len(shapes))],
        compiler_params=pltpu.CompilerParams(vmem_limit_bytes=48 * 2**20),
    )(*args)
    return result[0] if single else result


def sds(shape, dtype):
    return jax.ShapeDtypeStruct(shape, dtype)


def at_block(index):
    return pl.ds(pl.multiple_of(index * BLOCK, BLOCK), BLOCK)


def eye_mask(size):
    return lax.broadcasted_iota(jnp.int32, (size, size), 0) == lax.broadcasted_iota(
        jnp.int32, (size, size), 1
    )


def halves(value):
    high = value.astype(BF16)
    low = (value - high.astype(F32)).astype(BF16)
    return high, low


def pack(tile):
    return jnp.concatenate(halves(tile), axis=0)


def product(packed, values):
    left = jnp.concatenate(halves(values), axis=0)
    both = jnp.dot(jnp.concatenate([left, left], axis=1), packed, preferred_element_type=F32)
    count = values.shape[0]
    return both[:count] + both[count:]


def gram(full):
    high = full.astype(BF16)
    rest = full - high.astype(F32)
    middle = rest.astype(BF16)
    low = (rest - middle.astype(F32)).astype(BF16)
    parts = jnp.concatenate([high, middle, low], axis=0)
    cross = lax.dot_general(parts, parts, NT, preferred_element_type=F32)
    n = full.shape[0]
    total = None
    for i, j in ((2, 2), (1, 2), (2, 1), (0, 2), (2, 0), (1, 1), (0, 1), (1, 0), (0, 0)):
        piece = cross[i * n : (i + 1) * n, j * n : (j + 1) * n]
        total = piece if total is None else total + piece
    return total


def lower_inverse(matrix, step=4):
    n = matrix.shape[0]
    state = jnp.concatenate([matrix, eye_mask(n).astype(F32)], axis=1)
    done = []
    for j in range(0, n, step):
        top = j // 8 * 8
        if top > n - state.shape[0]:
            done.append(state[:8])
            state = state[8:]
        base = j - top
        rows = lax.broadcasted_iota(jnp.int32, state.shape, 0)
        columns = [jnp.broadcast_to(state[:, j + i : j + i + 1], state.shape) for i in range(step)]
        lines = [state[base + i : base + i + 1, :] for i in range(step)]
        pivot = [[columns[k][base + i : base + i + 1, :] for k in range(step)] for i in range(step)]
        for i in range(step):
            reciprocal = 1.0 / pivot[i][i]
            scaled = lines[i] * reciprocal
            ratio = [pivot[i][k] * reciprocal for k in range(step)]
            for k in range(i + 1, step):
                lines[k] = lines[k] - pivot[k][i] * scaled
                columns[k] = columns[k] - columns[i] * ratio[k]
                for m in range(i + 1, step):
                    pivot[k][m] = pivot[k][m] - pivot[k][i] * ratio[m]
            state = state - jnp.where(rows > base + i, columns[i], 0.0) * scaled
    state = jnp.concatenate([*done, state], axis=0)
    pivots = jnp.sum(jnp.where(eye_mask(n), state[:, :n], 0.0), axis=1, keepdims=True)
    return state[:, n:] / jnp.sqrt(pivots)


def both_columns(core, own, other):
    first = core == 0
    return jnp.concatenate(
        [jnp.where(first, own, other), jnp.where(first, other, own)], axis=0
    )


def plan_body(dims, me, lists, emb, idx, *sends):
    row_count, tile_count, capacity, slots, blocks_here = dims
    row = me[0]

    def clear(i, carry):
        for line in range(6):
            idx[line, i] = 0
        return carry

    lax.fori_loop(0, slots, clear, 0)

    def ranked(line, want, write):
        count = lists[line, 2 * slots]

        def step(s, counts):
            near = lists[line, s]
            far = lists[line, slots + s]
            return write(s, near, far, far // blocks_here, s < count, counts)

        lax.fori_loop(0, slots, step, (0,) * want)

    def write_own(s, near, far, owner, live, counts):
        shift = lax.rem(owner - row + row_count, row_count)
        rank = functools.reduce(
            lambda total, k: total + jnp.where(shift == k, counts[k], 0), range(row_count), 0
        )

        @pl.when(live)
        def _():
            slot = shift * capacity + rank
            idx[0, slot] = near - row * blocks_here
            idx[1, slot] = far
            idx[2, slot] = 1
            idx[3, slot] = s

        return tuple(
            counts[k] + (live & (shift == k)).astype(jnp.int32) for k in range(row_count)
        )

    for k in range(row_count):
        line = lax.rem(row - k + row_count, row_count) * tile_count + me[1]
        if k == 0:
            ranked(line, row_count, write_own)

        def write_in(s, near, far, owner, live, counts, k=k):
            hit = live & (owner == row)

            @pl.when(hit)
            def _():
                slot = k * capacity + counts[0]
                idx[4, slot] = far - row * blocks_here
                idx[5, slot] = near

            return (counts[0] + hit.astype(jnp.int32),)

        ranked(line, 1, write_in)
    for k in range(1, row_count):
        for j in range(capacity):
            sends[k - 1][j * BLOCK : (j + 1) * BLOCK, :] = emb[at_block(idx[4, k * capacity + j]), :]


def partial_distance(left, right):
    inner = lax.dot_general(left, right, NT, preferred_element_type=F32)
    left_sq = jnp.sum(jnp.square(left.astype(F32)), axis=1, keepdims=True)
    right_sq = jnp.sum(jnp.square(right.astype(F32)), axis=1, keepdims=True)
    right_row = jnp.sum(jnp.where(eye_mask(BLOCK), right_sq, 0.0), axis=0, keepdims=True)
    return left_sq + right_row - 2.0 * inner


def self_distance_body(own_blocks, tile_count, me, emb, out):
    for i in range(own_blocks):
        block = emb[at_block(i * tile_count + me[1]), :]
        out[i * BLOCK : (i + 1) * BLOCK, :] = partial_distance(block, block)


def pair_distance_body(row_count, capacity, idx, emb, *refs):
    out = refs[-1]
    for k in range(row_count):
        for j in range(capacity):
            slot = k * capacity + j
            left = emb[at_block(idx[0, slot]), :]
            if k == 0:
                right = emb[at_block(idx[4, j]), :]
            else:
                right = refs[k - 1][j * BLOCK : (j + 1) * BLOCK, :]
            out[slot * BLOCK : (slot + 1) * BLOCK, :] = partial_distance(left, right)


def self_tile_body(own_blocks, mine, other, packed, sums):
    for i in range(own_blocks):
        part = slice(i * BLOCK, (i + 1) * BLOCK)
        tile = jnp.exp(-kernel_gamma * (mine[part, :] + other[part, :] - 2.0))
        tile = jnp.where(eye_mask(BLOCK), 0.0, tile)
        packed[i] = pack(tile)
        sums[i : i + 1, :] = jnp.sum(tile, axis=0, keepdims=True)


def pair_tile_body(row_count, capacity, per_core, slots, me, idx, mine, other, self_sums, near_tiles, home_tiles, sends, sums):
    core = me[2]
    sums[0 : 2 * slots, :] = jnp.zeros((2 * slots, BLOCK), F32)
    sums[2 * slots :, :] = self_sums[...]
    for k in range(row_count):
        for j in range(capacity):
            slot = k * capacity + j
            part = slice(slot * BLOCK, (slot + 1) * BLOCK)
            live = idx[2, slot] > 0
            tile = jnp.exp(-kernel_gamma * (mine[part, :] + other[part, :] - 2.0))
            tile = jnp.where(live, tile, 0.0)
            turned = tile.T
            near_tiles[slot] = pack(turned)

            @pl.when(live)
            def _():
                raw = idx[3, slot]
                sums[pl.ds(raw, 1), :] = jnp.sum(turned, axis=0, keepdims=True)
                sums[pl.ds(slots + raw, 1), :] = jnp.sum(tile, axis=0, keepdims=True)

            if k == 0:
                home_tiles[j] = pack(tile)
            else:

                @pl.when(core == j // per_core)
                def _():
                    sends[lax.rem(me[0] + k, row_count), j % per_core] = pack(tile)


def pick_columns(me, idx, row_count, capacity, source, sends):
    for k in range(1, row_count):
        back = row_count - k
        there = lax.rem(me[0] + k, row_count)
        for j in range(capacity):
            sends[there, :, j * BLOCK : (j + 1) * BLOCK] = source[:, at_block(idx[0, k * capacity + j])]
            place = capacity + j
            sends[there, :, place * BLOCK : (place + 1) * BLOCK] = source[
                :, at_block(idx[4, back * capacity + j])
            ]


def pick_body(row_count, capacity, me, idx, source, *refs):
    pick_columns(me, idx, row_count, capacity, source, refs[-1])


def apply_tiles(dims, me, idx, inverse, own, received, near_tiles, home_tiles, sent, shared, self_tiles, out):
    row_count, capacity, per_core, blocks_here, tile_count = dims
    row, tile_index, core = me[0], me[1], me[2]
    out[...] = jnp.zeros(out.shape, F32)

    def scaled(values, block):
        return values * inverse[pl.ds(block, 1), :]

    def add(block, packed, values):
        place = at_block(block)
        out[:, place] = out[:, place] + product(packed, values)

    for i in range(blocks_here // tile_count):
        block = i * tile_count + tile_index
        add(block, self_tiles[i], scaled(own[:, at_block(block)], row * blocks_here + block))
    for k in range(row_count):
        owner = lax.rem(row + k, row_count)
        for j in range(capacity):
            slot = k * capacity + j
            if k == 0:
                values = own[:, at_block(idx[4, j])]
            else:
                values = received[owner, :, (capacity + j) * BLOCK : (capacity + j + 1) * BLOCK]
            add(idx[0, slot], near_tiles[slot], scaled(values, idx[1, slot]))
    for k in range(row_count):
        source = lax.rem(row - k + row_count, row_count)
        for j in range(capacity):
            if k == 0:
                slot = j
                values = own[:, at_block(idx[0, j])]
                packed = home_tiles[j]
            else:
                inner = j % per_core
                if j < per_core:
                    place = core * per_core + inner
                    packed = sent[source, inner]
                else:
                    place = (1 - core) * per_core + inner
                    packed = shared[source, inner]
                slot = k * capacity + place
                values = received[source, :, at_block(place)]
            add(idx[4, slot], packed, scaled(values, idx[5, slot]))


def first_apply_body(dims, me, idx, onehot, sums, *refs):
    inputs, (out, degree, inverse) = refs[:-3], refs[-3:]
    total = jnp.dot(onehot[...], sums[...], precision=HIGHEST, preferred_element_type=F32)
    degree[...] = total
    inverse[...] = 1.0 / jnp.sqrt(total)
    apply_tiles(dims, me, idx, inverse, *inputs, out)


def second_apply_body(dims, me, idx, inverse, gram_in, *refs):
    inputs, (out, gram_out) = refs[:-2], refs[-2:]
    apply_tiles(dims, me, idx, inverse, *inputs, out)
    gram_out[...] = gram_in[...]


def scale_rows(me, blocks_here, inverse, mine, other, out):
    for b in range(blocks_here):
        part = slice(b * BLOCK, (b + 1) * BLOCK)
        row = inverse[pl.ds(me[0] * blocks_here + b, 1), :]
        out[:, part] = (mine[:, part] + other[:, part]) * row


def mapped_body(row_count, capacity, blocks_here, me, idx, inverse, mine, other, out, sends):
    scale_rows(me, blocks_here, inverse, mine, other, out)
    pick_columns(me, idx, row_count, capacity, out, sends)


def last_mapped_body(blocks_here, me, inverse, mine, other, out):
    scale_rows(me, blocks_here, inverse, mine, other, out)


def gram_body(me, own, other, out):
    out[...] = gram(both_columns(me[2], own[...], other[...]))


def stacked_sum(stack):
    n = stack.shape[1]
    total = stack[:n, :]
    for i in range(1, stack.shape[0] // n):
        total = total + stack[i * n : (i + 1) * n, :]
    return total


def factor_body(after, grams, out):
    out[...] = lower_inverse(stacked_sum(grams))


def second_gram_body(me, factor, own, other, mapped, out):
    full = both_columns(me[2], own[...], other[...])
    value = jnp.dot(factor[...], full, precision=HIGHEST, preferred_element_type=F32)
    mapped[...] = value
    out[...] = gram(value)


def final_body(me, mapped, grams, out):
    factor = lower_inverse(stacked_sum(grams))
    own_cols = out.shape[0]
    part = jnp.where(me[2] == 0, factor[:own_cols], factor[own_cols:])
    out[...] = jnp.dot(part, mapped[...], precision=HIGHEST, preferred_element_type=F32)


def shift_by(value, axes, size, shift):
    return lax.ppermute(value, axes, [(i, (i + shift) % size) for i in range(size)])


def exchange(value):
    return lax.all_to_all(value, "rows", split_axis=0, concat_axis=0, tiled=True)


def gather(value, axes):
    return lax.all_gather(value, axes, axis=0, tiled=True)


def local(embeddings, start, pair_list, pair_count):
    row_count = lax.axis_size("rows")
    tile_count = lax.axis_size("tiles")
    core_count = lax.axis_size("cols")
    row_index = lax.axis_index("rows")
    tile_index = lax.axis_index("tiles")
    col_index = lax.axis_index("cols")
    me = jnp.stack([row_index, tile_index, col_index]).astype(jnp.int32)
    rows_here, half_features = embeddings.shape
    blocks_here = rows_here // BLOCK
    slots = pair_list.shape[2]
    capacity = slots // row_count
    per_core = capacity // core_count
    own_blocks = blocks_here // tile_count
    own_cols = start.shape[1]
    team = row_count * tile_count
    block_count = row_count * blocks_here
    others = range(1, row_count)

    lists = jnp.concatenate([pair_list.reshape(1, 2 * slots), pair_count.reshape(1, 1)], axis=1)
    lists = gather(lists, ("rows", "tiles"))
    planned = call(
        functools.partial(plan_body, (row_count, tile_count, capacity, slots, blocks_here)),
        [sds((6, slots), jnp.int32)] + [sds((capacity * BLOCK, half_features), BF16) for _ in others],
        [me, lists, embeddings],
        smem_in=(0, 1),
        smem_out=(0,),
    )
    idx, sends = planned[0], planned[1:]
    far = [shift_by(sends[k - 1], "rows", row_count, -k) for k in others]

    self_part = call(
        functools.partial(self_distance_body, own_blocks, tile_count),
        sds((own_blocks * BLOCK, BLOCK), F32),
        [me, embeddings],
        smem_in=(0,),
    )
    self_other = shift_by(self_part, "cols", core_count, 1)
    self_tiles, self_sums = call(
        functools.partial(self_tile_body, own_blocks),
        [sds((own_blocks, 2 * BLOCK, BLOCK), BF16), sds((own_blocks, BLOCK), F32)],
        [self_part, self_other],
    )
    values = start.T
    start_sends = call(
        functools.partial(pick_body, row_count, capacity),
        sds((row_count, own_cols, 2 * capacity * BLOCK), F32),
        [me, idx, values, *far[:-1]],
        smem_in=(0, 1),
        any_in=range(3, 2 + row_count),
    )
    start_in = exchange(start_sends)

    pair_part = call(
        functools.partial(pair_distance_body, row_count, capacity),
        sds((slots * BLOCK, BLOCK), F32),
        [idx, embeddings, *far],
        smem_in=(0,),
    )
    pair_other = shift_by(pair_part, "cols", core_count, 1)
    near_tiles, home_tiles, tile_sends, sums = call(
        functools.partial(pair_tile_body, row_count, capacity, per_core, slots),
        [
            sds((slots, 2 * BLOCK, BLOCK), BF16),
            sds((capacity, 2 * BLOCK, BLOCK), BF16),
            sds((row_count, per_core, 2 * BLOCK, BLOCK), BF16),
            sds((2 * slots + own_blocks, BLOCK), F32),
        ],
        [me, idx, pair_part, pair_other, self_sums],
        smem_in=(0, 1),
    )
    all_sums = gather(sums, ("rows", "tiles"))
    sent = exchange(tile_sends)
    shared = shift_by(sent, "cols", core_count, 1)

    team_ids = jnp.arange(team, dtype=jnp.int32)[:, None]
    diagonal_ids = team_ids // tile_count * blocks_here + (
        jnp.arange(own_blocks, dtype=jnp.int32)[None, :] * tile_count + team_ids % tile_count
    )
    sum_ids = jnp.concatenate([lists[:, : 2 * slots], diagonal_ids], axis=1).reshape(1, -1)
    onehot = (sum_ids == jnp.arange(block_count, dtype=jnp.int32)[:, None]).astype(F32)

    dims = (row_count, capacity, per_core, blocks_here, tile_count)
    tile_args = [near_tiles, home_tiles, sent, shared, self_tiles]
    block_shape = sds((own_cols, rows_here), F32)
    table = sds((block_count, BLOCK), F32)
    square = sds((2 * own_cols, 2 * own_cols), F32)

    def team_sum(part):
        if tile_count == 2:
            return part, shift_by(part, "tiles", 2, 1)
        return lax.psum(part, "tiles"), jnp.zeros_like(part)

    part, degree, inverse = call(
        functools.partial(first_apply_body, dims),
        [block_shape, table, table],
        [me, idx, onehot, all_sums, values, start_in, *tile_args],
        smem_in=(0, 1),
    )
    mine, other = team_sum(part)
    mapped, sends = call(
        functools.partial(mapped_body, row_count, capacity, blocks_here),
        [block_shape, sds((row_count, own_cols, 2 * capacity * BLOCK), F32)],
        [me, idx, inverse, mine, other],
        smem_in=(0, 1),
    )
    received = exchange(sends)

    mapped_other = shift_by(mapped, "cols", core_count, 1)
    first_gram = call(gram_body, square, [me, mapped, mapped_other], smem_in=(0,))
    part, first_gram = call(
        functools.partial(second_apply_body, dims),
        [block_shape, square],
        [me, idx, inverse, first_gram, mapped, received, *tile_args],
        smem_in=(0, 1),
    )
    mine, other = team_sum(part)
    first_grams = gather(first_gram, "rows")
    second = call(
        functools.partial(last_mapped_body, blocks_here),
        block_shape,
        [me, inverse, mine, other],
        smem_in=(0,),
    )
    second_other = shift_by(second, "cols", core_count, 1)
    factor = call(factor_body, square, [second, first_grams], any_in=(0,))
    full, second_gram = call(
        second_gram_body,
        [sds((2 * own_cols, rows_here), F32), square],
        [me, factor, second, second_other],
        smem_in=(0,),
    )
    second_grams = gather(second_gram, "rows")
    vectors = call(final_body, block_shape, [me, full, second_grams], smem_in=(0,))
    own_degree = lax.dynamic_slice_in_dim(degree, row_index * blocks_here, blocks_here, 0)
    return (vectors.T, own_degree.reshape(rows_here))


def solution(mesh):
    in_specs = (
        P(("groups", "rows"), "cols"),
        P(("groups", "rows"), "cols"),
        P(("groups", "rows", "tiles"), None, None),
        P(("groups", "rows", "tiles")),
    )
    out_specs = (P(("groups", "rows"), "cols"), P(("groups", "rows")))
    return jax.shard_map(local, mesh=mesh, in_specs=in_specs, out_specs=out_specs, check_vma=False)
```

```python
import functools

import jax
import jax.numpy as jnp
from jax import lax
from jax.experimental import pallas as pl
from jax.experimental.pallas import tpu as pltpu
from jax.sharding import PartitionSpec as P

BLOCK = 128
kernel_gamma = 14.0

VMEM = pl.BlockSpec(memory_space=pltpu.VMEM)
SMEM = pl.BlockSpec(memory_space=pltpu.SMEM)
ANY = pl.BlockSpec(memory_space=pl.ANY)
F32 = jnp.float32
BF16 = jnp.bfloat16
HIGHEST = lax.Precision.HIGHEST
NT = (((1,), (1,)), ((), ()))


def call(body, outs, args, smem_in=(), smem_out=(), any_in=()):
    single = not isinstance(outs, (list, tuple))
    shapes = [outs] if single else list(outs)
    result = pl.pallas_call(
        body,
        out_shape=shapes,
        in_specs=[
            SMEM if i in smem_in else ANY if i in any_in else VMEM for i in range(len(args))
        ],
        out_specs=[SMEM if i in smem_out else VMEM for i in range(len(shapes))],
        compiler_params=pltpu.CompilerParams(vmem_limit_bytes=48 * 2**20),
    )(*args)
    return result[0] if single else result


def sds(shape, dtype):
    return jax.ShapeDtypeStruct(shape, dtype)


def at_block(index):
    return pl.ds(pl.multiple_of(index * BLOCK, BLOCK), BLOCK)


def eye_mask(size):
    return lax.broadcasted_iota(jnp.int32, (size, size), 0) == lax.broadcasted_iota(
        jnp.int32, (size, size), 1
    )


def halves(value):
    high = value.astype(BF16)
    low = (value - high.astype(F32)).astype(BF16)
    return high, low


def pack(tile):
    return jnp.concatenate(halves(tile), axis=0)


def product(packed, values):
    left = jnp.concatenate(halves(values), axis=0)
    both = jnp.dot(jnp.concatenate([left, left], axis=1), packed, preferred_element_type=F32)
    count = values.shape[0]
    return both[:count] + both[count:]


def gram(full):
    high = full.astype(BF16)
    rest = full - high.astype(F32)
    middle = rest.astype(BF16)
    low = (rest - middle.astype(F32)).astype(BF16)
    parts = jnp.concatenate([high, middle, low], axis=0)
    cross = lax.dot_general(parts, parts, NT, preferred_element_type=F32)
    n = full.shape[0]
    total = None
    for i, j in ((2, 2), (1, 2), (2, 1), (0, 2), (2, 0), (1, 1), (0, 1), (1, 0), (0, 0)):
        piece = cross[i * n : (i + 1) * n, j * n : (j + 1) * n]
        total = piece if total is None else total + piece
    return total


def lower_inverse(matrix, step=4):
    n = matrix.shape[0]
    state = jnp.concatenate([matrix, eye_mask(n).astype(F32)], axis=1)
    done = []
    for j in range(0, n, step):
        top = j // 8 * 8
        if top > n - state.shape[0]:
            done.append(state[:8])
            state = state[8:]
        base = j - top
        rows = lax.broadcasted_iota(jnp.int32, state.shape, 0)
        columns = [jnp.broadcast_to(state[:, j + i : j + i + 1], state.shape) for i in range(step)]
        lines = [state[base + i : base + i + 1, :] for i in range(step)]
        pivot = [[columns[k][base + i : base + i + 1, :] for k in range(step)] for i in range(step)]
        for i in range(step):
            reciprocal = 1.0 / pivot[i][i]
            scaled = lines[i] * reciprocal
            ratio = [pivot[i][k] * reciprocal for k in range(step)]
            for k in range(i + 1, step):
                lines[k] = lines[k] - pivot[k][i] * scaled
                columns[k] = columns[k] - columns[i] * ratio[k]
                for m in range(i + 1, step):
                    pivot[k][m] = pivot[k][m] - pivot[k][i] * ratio[m]
            state = state - jnp.where(rows > base + i, columns[i], 0.0) * scaled
    state = jnp.concatenate([*done, state], axis=0)
    pivots = jnp.sum(jnp.where(eye_mask(n), state[:, :n], 0.0), axis=1, keepdims=True)
    return state[:, n:] / jnp.sqrt(pivots)


def both_columns(core, own, other):
    first = core == 0
    return jnp.concatenate(
        [jnp.where(first, own, other), jnp.where(first, other, own)], axis=0
    )


def plan_body(dims, me, *refs):
    row_count, capacity, slots, blocks_here = dims
    lists, (emb, after, idx), sends = refs[:row_count], refs[row_count : row_count + 3], refs[row_count + 3 :]
    row = me[0]

    def clear(i, carry):
        for line in range(6):
            idx[line, i] = 0
        return carry

    lax.fori_loop(0, slots, clear, 0)

    def ranked(listed, want, write):
        count = listed[0, 2 * slots]

        def step(s, counts):
            near = listed[0, s]
            far = listed[0, slots + s]
            return write(s, near, far, far // blocks_here, s < count, counts)

        lax.fori_loop(0, slots, step, (0,) * want)

    def write_own(s, near, far, owner, live, counts):
        shift = lax.rem(owner - row + row_count, row_count)
        rank = functools.reduce(
            lambda total, k: total + jnp.where(shift == k, counts[k], 0), range(row_count), 0
        )

        @pl.when(live)
        def _():
            slot = shift * capacity + rank
            idx[0, slot] = near - row * blocks_here
            idx[1, slot] = far
            idx[2, slot] = 1
            idx[3, slot] = s

        return tuple(
            counts[k] + (live & (shift == k)).astype(jnp.int32) for k in range(row_count)
        )

    for k in range(row_count):
        if k == 0:
            ranked(lists[k], row_count, write_own)

        def write_in(s, near, far, owner, live, counts, k=k):
            hit = live & (owner == row)

            @pl.when(hit)
            def _():
                slot = k * capacity + counts[0]
                idx[4, slot] = far - row * blocks_here
                idx[5, slot] = near

            return (counts[0] + hit.astype(jnp.int32),)

        ranked(lists[k], 1, write_in)
    for k in range(1, row_count):
        for j in range(capacity):
            sends[k - 1][j * BLOCK : (j + 1) * BLOCK, :] = emb[at_block(idx[4, k * capacity + j]), :]


def partial_distance(left, right):
    inner = lax.dot_general(left, right, NT, preferred_element_type=F32)
    left_sq = jnp.sum(jnp.square(left.astype(F32)), axis=1, keepdims=True)
    right_sq = jnp.sum(jnp.square(right.astype(F32)), axis=1, keepdims=True)
    right_row = jnp.sum(jnp.where(eye_mask(BLOCK), right_sq, 0.0), axis=0, keepdims=True)
    return left_sq + right_row - 2.0 * inner


def self_distance_body(own_blocks, tile_count, me, emb, out):
    for i in range(own_blocks):
        block = emb[at_block(i * tile_count + me[1]), :]
        out[i * BLOCK : (i + 1) * BLOCK, :] = partial_distance(block, block)


def pair_distance_body(row_count, capacity, idx, emb, *refs):
    out = refs[-1]
    for k in range(row_count):
        for j in range(capacity):
            slot = k * capacity + j
            left = emb[at_block(idx[0, slot]), :]
            if k == 0:
                right = emb[at_block(idx[4, j]), :]
            else:
                right = refs[k - 1][j * BLOCK : (j + 1) * BLOCK, :]
            out[slot * BLOCK : (slot + 1) * BLOCK, :] = partial_distance(left, right)


def self_tile_body(own_blocks, mine, other, packed, sums):
    for i in range(own_blocks):
        part = slice(i * BLOCK, (i + 1) * BLOCK)
        tile = jnp.exp(-kernel_gamma * (mine[part, :] + other[part, :] - 2.0))
        tile = jnp.where(eye_mask(BLOCK), 0.0, tile)
        packed[i] = pack(tile)
        sums[i : i + 1, :] = jnp.sum(tile, axis=0, keepdims=True)


def pair_tile_body(row_count, capacity, per_core, slots, me, idx, mine, other, self_sums, ids, after, near_tiles, home_tiles, sends, copies, sums):
    core = me[2]
    own_blocks = self_sums.shape[0]
    sums[...] = jnp.zeros(sums.shape, F32)
    sums[2 * slots : 2 * slots + own_blocks, :] = self_sums[...]
    sums[2 * slots + own_blocks : 2 * slots + own_blocks + 1, :] = ids[...]
    for k in range(row_count):
        for j in range(capacity):
            slot = k * capacity + j
            part = slice(slot * BLOCK, (slot + 1) * BLOCK)
            live = idx[2, slot] > 0
            tile = jnp.exp(-kernel_gamma * (mine[part, :] + other[part, :] - 2.0))
            tile = jnp.where(live, tile, 0.0)
            turned = tile.T
            near_tiles[slot] = pack(turned)

            @pl.when(live)
            def _():
                raw = idx[3, slot]
                sums[pl.ds(raw, 1), :] = jnp.sum(turned, axis=0, keepdims=True)
                sums[pl.ds(slots + raw, 1), :] = jnp.sum(tile, axis=0, keepdims=True)

            if k == 0:
                home_tiles[j] = pack(tile)
            else:

                @pl.when(core == j // per_core)
                def _():
                    sends[lax.rem(me[0] + k, row_count), j % per_core] = pack(tile)

    for i in range(copies.shape[0]):
        copies[i] = sums[...]


def pick_columns(me, idx, row_count, capacity, source, sends):
    for k in range(1, row_count):
        back = row_count - k
        there = lax.rem(me[0] + k, row_count)
        for j in range(capacity):
            sends[there, :, j * BLOCK : (j + 1) * BLOCK] = source[:, at_block(idx[0, k * capacity + j])]
            place = capacity + j
            sends[there, :, place * BLOCK : (place + 1) * BLOCK] = source[
                :, at_block(idx[4, back * capacity + j])
            ]


def pick_body(row_count, capacity, me, idx, source, *refs):
    pick_columns(me, idx, row_count, capacity, source, refs[-1])


def apply_tiles(dims, me, idx, inverse, own, received, near_tiles, home_tiles, sent, shared, self_tiles, out):
    row_count, capacity, per_core, blocks_here, tile_count = dims
    row, tile_index, core = me[0], me[1], me[2]
    out[...] = jnp.zeros(out.shape, F32)

    def scaled(values, block):
        return values * inverse[pl.ds(block, 1), :]

    def add(block, packed, values):
        place = at_block(block)
        out[:, place] = out[:, place] + product(packed, values)

    for i in range(blocks_here // tile_count):
        block = i * tile_count + tile_index
        add(block, self_tiles[i], scaled(own[:, at_block(block)], row * blocks_here + block))
    for k in range(row_count):
        owner = lax.rem(row + k, row_count)
        for j in range(capacity):
            slot = k * capacity + j
            if k == 0:
                values = own[:, at_block(idx[4, j])]
            else:
                values = received[owner, :, (capacity + j) * BLOCK : (capacity + j + 1) * BLOCK]
            add(idx[0, slot], near_tiles[slot], scaled(values, idx[1, slot]))
    for k in range(row_count):
        source = lax.rem(row - k + row_count, row_count)
        for j in range(capacity):
            if k == 0:
                slot = j
                values = own[:, at_block(idx[0, j])]
                packed = home_tiles[j]
            else:
                inner = j % per_core
                if j < per_core:
                    place = core * per_core + inner
                    packed = sent[source, inner]
                else:
                    place = (1 - core) * per_core + inner
                    packed = shared[source, inner]
                slot = k * capacity + place
                values = received[source, :, at_block(place)]
            add(idx[4, slot], packed, scaled(values, idx[5, slot]))


def first_apply_body(dims, id_row, me, idx, sums, *refs):
    inputs, (out, degree, inverse) = refs[:-3], refs[-3:]
    team, rows = sums.shape[0], sums.shape[1]
    blocks = lax.broadcasted_iota(jnp.int32, (degree.shape[0], rows), 0).astype(F32)

    def part(i):
        chosen = sums[i]
        onehot = (blocks == chosen[id_row : id_row + 1, :rows]).astype(F32)
        return jnp.dot(onehot, chosen, precision=HIGHEST, preferred_element_type=F32)

    if team <= 8:
        total = functools.reduce(lambda total, i: total + part(i), range(1, team), part(0))
    else:
        total = lax.fori_loop(1, team, lambda i, total: total + part(i), part(0))
    degree[...] = total
    inverse[...] = 1.0 / jnp.sqrt(total)
    apply_tiles(dims, me, idx, inverse, *inputs, out)


def copy_square(square, out):
    half = square.shape[0] // 2
    folded = jnp.concatenate([square[:half], square[half:]], axis=1)
    for i in range(out.shape[0]):
        out[i] = folded


def second_apply_body(dims, me, idx, inverse, gram_in, *refs):
    inputs, (out, grams) = refs[:-2], refs[-2:]
    apply_tiles(dims, me, idx, inverse, *inputs, out)
    copy_square(gram_in[...], grams)


def scale_rows(me, blocks_here, inverse, mine, other, out):
    for b in range(blocks_here):
        part = slice(b * BLOCK, (b + 1) * BLOCK)
        row = inverse[pl.ds(me[0] * blocks_here + b, 1), :]
        out[:, part] = (mine[:, part] + other[:, part]) * row


def mapped_body(row_count, capacity, blocks_here, me, idx, inverse, mine, other, out, sends):
    scale_rows(me, blocks_here, inverse, mine, other, out)
    pick_columns(me, idx, row_count, capacity, out, sends)


def last_mapped_body(blocks_here, me, inverse, mine, other, after, out):
    scale_rows(me, blocks_here, inverse, mine, other, out)


def gram_body(me, own, other, out):
    out[...] = gram(both_columns(me[2], own[...], other[...]))


def stacked_sum(stack):
    total = functools.reduce(lambda total, i: total + stack[i], range(1, stack.shape[0]), stack[0])
    width = total.shape[1] // 2
    return jnp.concatenate([total[:, :width], total[:, width:]], axis=0)


def factor_body(after, grams, out):
    out[...] = lower_inverse(stacked_sum(grams))


def second_gram_body(me, factor, own, other, mapped, out):
    full = both_columns(me[2], own[...], other[...])
    value = jnp.dot(factor[...], full, precision=HIGHEST, preferred_element_type=F32)
    mapped[...] = value
    square = gram(value)
    copy_square(square, out)


def final_body(me, mapped, grams, out):
    factor = lower_inverse(stacked_sum(grams))
    own_cols = out.shape[0]
    part = jnp.where(me[2] == 0, factor[:own_cols], factor[own_cols:])
    out[...] = jnp.dot(part, mapped[...], precision=HIGHEST, preferred_element_type=F32)


def shift_by(value, axes, size, shift):
    return lax.ppermute(value, axes, [(i, (i + shift) % size) for i in range(size)])


def exchange(value, axes="rows"):
    return lax.all_to_all(value, axes, split_axis=0, concat_axis=0, tiled=True)


def local(embeddings, start, pair_list, pair_count):
    row_count = lax.axis_size("rows")
    tile_count = lax.axis_size("tiles")
    core_count = lax.axis_size("cols")
    row_index = lax.axis_index("rows")
    tile_index = lax.axis_index("tiles")
    col_index = lax.axis_index("cols")
    me = jnp.stack([row_index, tile_index, col_index]).astype(jnp.int32)
    rows_here, half_features = embeddings.shape
    blocks_here = rows_here // BLOCK
    slots = pair_list.shape[2]
    capacity = slots // row_count
    per_core = capacity // core_count
    own_blocks = blocks_here // tile_count
    own_cols = start.shape[1]
    team = row_count * tile_count
    block_count = row_count * blocks_here
    others = range(1, row_count)

    own_list = jnp.concatenate([pair_list.reshape(1, 2 * slots), pair_count.reshape(1, 1)], axis=1)
    lists = [own_list] + [shift_by(own_list, "rows", row_count, k) for k in others]
    self_part = call(
        functools.partial(self_distance_body, own_blocks, tile_count),
        sds((own_blocks * BLOCK, BLOCK), F32),
        [me, embeddings],
        smem_in=(0,),
    )
    planned = call(
        functools.partial(plan_body, (row_count, capacity, slots, blocks_here)),
        [sds((6, slots), jnp.int32)] + [sds((capacity * BLOCK, half_features), BF16) for _ in others],
        [me, *lists, embeddings, self_part],
        smem_in=range(1 + row_count),
        any_in=(row_count + 2,),
        smem_out=(0,),
    )
    idx, sends = planned[0], planned[1:]
    far = [shift_by(sends[k - 1], "rows", row_count, -k) for k in others]

    self_other = shift_by(self_part, "cols", core_count, 1)
    self_tiles, self_sums = call(
        functools.partial(self_tile_body, own_blocks),
        [sds((own_blocks, 2 * BLOCK, BLOCK), BF16), sds((own_blocks, BLOCK), F32)],
        [self_part, self_other],
    )
    pair_part = call(
        functools.partial(pair_distance_body, row_count, capacity),
        sds((slots * BLOCK, BLOCK), F32),
        [idx, embeddings, *far],
        smem_in=(0,),
    )
    pair_other = shift_by(pair_part, "cols", core_count, 1)
    values = start.T
    start_sends = call(
        functools.partial(pick_body, row_count, capacity),
        sds((row_count, own_cols, 2 * capacity * BLOCK), F32),
        [me, idx, values, pair_part],
        smem_in=(0, 1),
        any_in=(3,),
    )
    start_in = exchange(start_sends)

    id_row = 2 * slots + own_blocks
    sum_rows = -(-(id_row + 1) // 8) * 8
    diagonal_ids = row_index * blocks_here + (
        jnp.arange(own_blocks, dtype=jnp.int32)[None, :] * tile_count + tile_index
    )
    ids = jnp.concatenate([own_list[:, : 2 * slots], diagonal_ids], axis=1).astype(F32)
    ids = jnp.pad(ids, ((0, 0), (0, BLOCK - id_row)), constant_values=-1.0)
    near_tiles, home_tiles, tile_sends, sums, _ = call(
        functools.partial(pair_tile_body, row_count, capacity, per_core, slots),
        [
            sds((slots, 2 * BLOCK, BLOCK), BF16),
            sds((capacity, 2 * BLOCK, BLOCK), BF16),
            sds((row_count, per_core, 2 * BLOCK, BLOCK), BF16),
            sds((team, sum_rows, BLOCK), F32),
            sds((sum_rows, BLOCK), F32),
        ],
        [me, idx, pair_part, pair_other, self_sums, ids, start_sends],
        smem_in=(0, 1),
        any_in=(6,),
    )
    all_sums = exchange(sums, ("rows", "tiles"))
    sent = exchange(tile_sends)
    shared = shift_by(sent, "cols", core_count, 1)

    dims = (row_count, capacity, per_core, blocks_here, tile_count)
    tile_args = [near_tiles, home_tiles, sent, shared, self_tiles]
    block_shape = sds((own_cols, rows_here), F32)
    table = sds((block_count, BLOCK), F32)
    square = sds((2 * own_cols, 2 * own_cols), F32)
    squares = sds((row_count, own_cols, 4 * own_cols), F32)

    def team_sum(part):
        if tile_count == 2:
            return part, shift_by(part, "tiles", 2, 1)
        return lax.psum(part, "tiles"), jnp.zeros_like(part)

    part, degree, inverse = call(
        functools.partial(first_apply_body, dims, id_row),
        [block_shape, table, table],
        [me, idx, all_sums, values, start_in, *tile_args],
        smem_in=(0, 1),
    )
    mine, other = team_sum(part)
    mapped, sends = call(
        functools.partial(mapped_body, row_count, capacity, blocks_here),
        [block_shape, sds((row_count, own_cols, 2 * capacity * BLOCK), F32)],
        [me, idx, inverse, mine, other],
        smem_in=(0, 1),
    )
    received = exchange(sends)

    mapped_other = shift_by(mapped, "cols", core_count, 1)
    first_gram = call(gram_body, square, [me, mapped, mapped_other], smem_in=(0,))
    part, first_grams = call(
        functools.partial(second_apply_body, dims),
        [block_shape, squares],
        [me, idx, inverse, first_gram, mapped, received, *tile_args],
        smem_in=(0, 1),
    )
    mine, other = team_sum(part)
    first_grams = exchange(first_grams)
    second = call(
        functools.partial(last_mapped_body, blocks_here),
        block_shape,
        [me, inverse, mine, other, first_grams],
        smem_in=(0,),
        any_in=(4,),
    )
    second_other = shift_by(second, "cols", core_count, 1)
    factor = call(factor_body, square, [second, first_grams], any_in=(0,))
    full, second_grams = call(
        second_gram_body,
        [sds((2 * own_cols, rows_here), F32), squares],
        [me, factor, second, second_other],
        smem_in=(0,),
    )
    second_grams = exchange(second_grams)
    vectors = call(final_body, block_shape, [me, full, second_grams], smem_in=(0,))
    own_degree = lax.dynamic_slice_in_dim(degree, row_index * blocks_here, blocks_here, 0)
    return (vectors.T, own_degree.reshape(rows_here))


def solution(mesh):
    in_specs = (
        P(("groups", "rows"), "cols"),
        P(("groups", "rows"), "cols"),
        P(("groups", "rows", "tiles"), None, None),
        P(("groups", "rows", "tiles")),
    )
    out_specs = (P(("groups", "rows"), "cols"), P(("groups", "rows")))
    return jax.shard_map(local, mesh=mesh, in_specs=in_specs, out_specs=out_specs, check_vma=False)
```

```python
import functools

import jax
import jax.numpy as jnp
from jax import lax
from jax.experimental import pallas as pl
from jax.experimental.pallas import tpu as pltpu
from jax.sharding import PartitionSpec as P

BLOCK = 128
kernel_gamma = 14.0

VMEM = pl.BlockSpec(memory_space=pltpu.VMEM)
SMEM = pl.BlockSpec(memory_space=pltpu.SMEM)
ANY = pl.BlockSpec(memory_space=pl.ANY)
F32 = jnp.float32
BF16 = jnp.bfloat16
HIGHEST = lax.Precision.HIGHEST
NT = (((1,), (1,)), ((), ()))


def call(body, outs, args, smem_in=(), smem_out=(), any_in=()):
    single = not isinstance(outs, (list, tuple))
    shapes = [outs] if single else list(outs)
    result = pl.pallas_call(
        body,
        out_shape=shapes,
        in_specs=[
            SMEM if i in smem_in else ANY if i in any_in else VMEM for i in range(len(args))
        ],
        out_specs=[SMEM if i in smem_out else VMEM for i in range(len(shapes))],
        compiler_params=pltpu.CompilerParams(vmem_limit_bytes=48 * 2**20),
    )(*args)
    return result[0] if single else result


def sds(shape, dtype):
    return jax.ShapeDtypeStruct(shape, dtype)


def at_block(index):
    return pl.ds(pl.multiple_of(index * BLOCK, BLOCK), BLOCK)


def eye_mask(size):
    return lax.broadcasted_iota(jnp.int32, (size, size), 0) == lax.broadcasted_iota(
        jnp.int32, (size, size), 1
    )


def halves(value):
    high = value.astype(BF16)
    low = (value - high.astype(F32)).astype(BF16)
    return high, low


def pack(tile):
    return jnp.concatenate(halves(tile), axis=0)


def product(packed, values):
    left = jnp.concatenate(halves(values), axis=0)
    both = jnp.dot(jnp.concatenate([left, left], axis=1), packed, preferred_element_type=F32)
    count = values.shape[0]
    return both[:count] + both[count:]


def thirds(value):
    high = value.astype(BF16)
    rest = value - high.astype(F32)
    middle = rest.astype(BF16)
    low = (rest - middle.astype(F32)).astype(BF16)
    return jnp.concatenate([high, middle, low], axis=0)


def gram(parts):
    cross = lax.dot_general(parts, parts, NT, preferred_element_type=F32)
    n = parts.shape[0] // 3
    total = None
    for i, j in ((2, 2), (1, 2), (2, 1), (0, 2), (2, 0), (1, 1), (0, 1), (1, 0), (0, 0)):
        piece = cross[i * n : (i + 1) * n, j * n : (j + 1) * n]
        total = piece if total is None else total + piece
    return total


def times(left, parts):
    left = thirds(left)
    m = left.shape[0] // 3
    product3 = jnp.dot(
        jnp.concatenate([left, left, left], axis=1), parts, preferred_element_type=F32
    )
    return (product3[2 * m :] + product3[m : 2 * m]) + product3[:m]


def lower_inverse(matrix, step=4):
    n = matrix.shape[0]
    state = jnp.concatenate([matrix, eye_mask(n).astype(F32)], axis=1)
    done = []
    for j in range(0, n, step):
        top = j // 8 * 8
        if top > n - state.shape[0]:
            done.append(state[:8])
            state = state[8:]
        base = j - top
        rows = lax.broadcasted_iota(jnp.int32, state.shape, 0)
        columns = [jnp.broadcast_to(state[:, j + i : j + i + 1], state.shape) for i in range(step)]
        lines = [state[base + i : base + i + 1, :] for i in range(step)]
        pivot = [[columns[k][base + i : base + i + 1, :] for k in range(step)] for i in range(step)]
        for i in range(step):
            reciprocal = 1.0 / pivot[i][i]
            scaled = lines[i] * reciprocal
            ratio = [pivot[i][k] * reciprocal for k in range(step)]
            for k in range(i + 1, step):
                lines[k] = lines[k] - pivot[k][i] * scaled
                columns[k] = columns[k] - columns[i] * ratio[k]
                for m in range(i + 1, step):
                    pivot[k][m] = pivot[k][m] - pivot[k][i] * ratio[m]
            state = state - jnp.where(rows > base + i, columns[i], 0.0) * scaled
    state = jnp.concatenate([*done, state], axis=0)
    pivots = jnp.sum(jnp.where(eye_mask(n), state[:, :n], 0.0), axis=1, keepdims=True)
    return state[:, n:] / jnp.sqrt(pivots)


def both_columns(core, own, other):
    first = core == 0
    return jnp.concatenate(
        [jnp.where(first, own, other), jnp.where(first, other, own)], axis=0
    )


def plan_body(dims, me, *refs):
    row_count, capacity, slots, blocks_here = dims
    lists, (emb, after, idx), sends = refs[:row_count], refs[row_count : row_count + 3], refs[row_count + 3 :]
    row = me[0]

    def clear(i, carry):
        for line in range(6):
            idx[line, i] = 0
        return carry

    lax.fori_loop(0, slots, clear, 0)

    def ranked(listed, want, write):
        count = listed[0, 2 * slots]

        def step(s, counts):
            near = listed[0, s]
            far = listed[0, slots + s]
            return write(s, near, far, far // blocks_here, s < count, counts)

        lax.fori_loop(0, slots, step, (0,) * want)

    def write_own(s, near, far, owner, live, counts):
        shift = lax.rem(owner - row + row_count, row_count)
        rank = functools.reduce(
            lambda total, k: total + jnp.where(shift == k, counts[k], 0), range(row_count), 0
        )

        @pl.when(live)
        def _():
            slot = shift * capacity + rank
            idx[0, slot] = near - row * blocks_here
            idx[1, slot] = far
            idx[2, slot] = 1
            idx[3, slot] = s

        return tuple(
            counts[k] + (live & (shift == k)).astype(jnp.int32) for k in range(row_count)
        )

    for k in range(row_count):
        if k == 0:
            ranked(lists[k], row_count, write_own)

        def write_in(s, near, far, owner, live, counts, k=k):
            hit = live & (owner == row)

            @pl.when(hit)
            def _():
                slot = k * capacity + counts[0]
                idx[4, slot] = far - row * blocks_here
                idx[5, slot] = near

            return (counts[0] + hit.astype(jnp.int32),)

        ranked(lists[k], 1, write_in)
    for k in range(1, row_count):
        for j in range(capacity):
            sends[k - 1][j * BLOCK : (j + 1) * BLOCK, :] = emb[at_block(idx[4, k * capacity + j]), :]


def partial_distance(left, right):
    inner = lax.dot_general(left, right, NT, preferred_element_type=F32)
    left_sq = jnp.sum(jnp.square(left.astype(F32)), axis=1, keepdims=True)
    right_sq = jnp.sum(jnp.square(right.astype(F32)), axis=1, keepdims=True)
    right_row = jnp.sum(jnp.where(eye_mask(BLOCK), right_sq, 0.0), axis=0, keepdims=True)
    return left_sq + right_row - 2.0 * inner


def self_distance_body(own_blocks, tile_count, me, emb, out):
    for i in range(own_blocks):
        block = emb[at_block(i * tile_count + me[1]), :]
        out[i * BLOCK : (i + 1) * BLOCK, :] = partial_distance(block, block)


def pair_distance_body(shifts, capacity, idx, emb, *refs):
    far, out = refs[:-1], refs[-1]
    if shifts[0] == 0:
        far = (None, *far)
    for place, k in enumerate(shifts):
        for j in range(capacity):
            left = emb[at_block(idx[0, k * capacity + j]), :]
            if k == 0:
                right = emb[at_block(idx[4, j]), :]
            else:
                right = far[place][j * BLOCK : (j + 1) * BLOCK, :]
            slot = place * capacity + j
            out[slot * BLOCK : (slot + 1) * BLOCK, :] = partial_distance(left, right)


def self_tile_body(own_blocks, mine, other, packed, sums):
    for i in range(own_blocks):
        part = slice(i * BLOCK, (i + 1) * BLOCK)
        tile = jnp.exp(-kernel_gamma * (mine[part, :] + other[part, :] - 2.0))
        tile = jnp.where(eye_mask(BLOCK), 0.0, tile)
        packed[i] = pack(tile)
        sums[i : i + 1, :] = jnp.sum(tile, axis=0, keepdims=True)


def pair_tile_body(row_count, capacity, per_core, tile_count, blocks_here, me, idx, mine, other, last_mine, last_other, self_sums, *refs):
    near_tiles, home_tiles = refs[-2 - row_count : -row_count]
    sends = refs[-row_count : -1]
    table = refs[-1]
    row, tile_index, core = me[0], me[1], me[2]
    first_slots = mine.shape[0] // BLOCK
    table[...] = jnp.zeros(table.shape, F32)
    for i in range(self_sums.shape[0]):
        table[pl.ds(row * blocks_here + i * tile_count + tile_index, 1), :] = self_sums[i : i + 1, :]

    def add(block, line):
        place = pl.ds(block, 1)
        table[place, :] = table[place, :] + line

    for k in range(row_count):
        for j in range(capacity):
            slot = k * capacity + j
            if slot < first_slots:
                part = slice(slot * BLOCK, (slot + 1) * BLOCK)
                distance = mine[part, :] + other[part, :]
            else:
                part = slice((slot - first_slots) * BLOCK, (slot - first_slots + 1) * BLOCK)
                distance = last_mine[part, :] + last_other[part, :]
            tile = jnp.exp(-kernel_gamma * (distance - 2.0))
            tile = jnp.where(idx[2, slot] > 0, tile, 0.0)
            turned = tile.T
            near_tiles[slot] = pack(turned)
            add(row * blocks_here + idx[0, slot], jnp.sum(turned, axis=0, keepdims=True))
            add(idx[1, slot], jnp.sum(tile, axis=0, keepdims=True))
            if k == 0:
                home_tiles[j] = pack(tile)
            else:

                @pl.when(core == j // per_core)
                def _():
                    sends[k - 1][j % per_core] = pack(tile)


def pick_columns(idx, row_count, capacity, source, sends):
    for k in range(1, row_count):
        back = row_count - k
        for j in range(capacity):
            sends[k - 1][:, j * BLOCK : (j + 1) * BLOCK] = source[:, at_block(idx[0, k * capacity + j])]
            place = capacity + j
            sends[k - 1][:, place * BLOCK : (place + 1) * BLOCK] = source[
                :, at_block(idx[4, back * capacity + j])
            ]


def pick_body(row_count, capacity, idx, source, after, *sends):
    pick_columns(idx, row_count, capacity, source, sends)


def apply_tiles(dims, me, idx, inverse, own, received, near_tiles, home_tiles, sent, shared, self_tiles, out):
    row_count, capacity, per_core, blocks_here, tile_count = dims
    row, tile_index, core = me[0], me[1], me[2]
    out[...] = jnp.zeros(out.shape, F32)

    def scaled(values, block):
        return values * inverse[pl.ds(block, 1), :]

    def add(block, packed, values):
        place = at_block(block)
        out[:, place] = out[:, place] + product(packed, values)

    for i in range(blocks_here // tile_count):
        block = i * tile_count + tile_index
        add(block, self_tiles[i], scaled(own[:, at_block(block)], row * blocks_here + block))
    for k in range(row_count):
        for j in range(capacity):
            slot = k * capacity + j
            if k == 0:
                values = own[:, at_block(idx[4, j])]
            else:
                values = received[row_count - k - 1][:, (capacity + j) * BLOCK : (capacity + j + 1) * BLOCK]
            add(idx[0, slot], near_tiles[slot], scaled(values, idx[1, slot]))
    for k in range(row_count):
        for j in range(capacity):
            if k == 0:
                slot = j
                values = own[:, at_block(idx[0, j])]
                packed = home_tiles[j]
            else:
                inner = j % per_core
                if j < per_core:
                    place = core * per_core + inner
                    packed = sent[k - 1][inner]
                else:
                    place = (1 - core) * per_core + inner
                    packed = shared[k - 1][inner]
                slot = k * capacity + place
                values = received[k - 1][:, at_block(place)]
            add(idx[4, slot], packed, scaled(values, idx[5, slot]))


def split_inputs(row_count, refs):
    others = row_count - 1
    received = refs[1 : 1 + others]
    near_tiles, home_tiles = refs[1 + others : 3 + others]
    sent = refs[3 + others : 3 + 2 * others]
    shared = refs[3 + 2 * others : 3 + 3 * others]
    return (refs[0], received, near_tiles, home_tiles, sent, shared, refs[-1])


def first_apply_body(dims, me, idx, mine, other, *refs):
    inputs, (out, degree, inverse) = refs[:-3], refs[-3:]
    total = mine[...] + other[...]
    degree[...] = total
    inverse[...] = 1.0 / jnp.sqrt(total)
    apply_tiles(dims, me, idx, inverse, *split_inputs(dims[0], inputs), out)


def second_apply_body(dims, me, idx, inverse, *refs):
    apply_tiles(dims, me, idx, inverse, *split_inputs(dims[0], refs[:-1]), refs[-1])


def scale_rows(me, blocks_here, inverse, mine, other, out):
    for b in range(blocks_here):
        part = slice(b * BLOCK, (b + 1) * BLOCK)
        row = inverse[pl.ds(me[0] * blocks_here + b, 1), :]
        out[:, part] = (mine[:, part] + other[:, part]) * row


def mapped_body(row_count, capacity, blocks_here, me, idx, inverse, mine, other, out, *sends):
    scale_rows(me, blocks_here, inverse, mine, other, out)
    pick_columns(idx, row_count, capacity, out, sends)


def last_mapped_body(blocks_here, me, inverse, mine, other, after, out):
    scale_rows(me, blocks_here, inverse, mine, other, out)


def folded(square):
    half = square.shape[0] // 2
    return jnp.concatenate([square[:half], square[half:]], axis=1)


def unfolded(mine, other):
    total = mine[...] + other[...]
    width = total.shape[1] // 2
    return jnp.concatenate([total[:, :width], total[:, width:]], axis=0)


def gram_body(me, own, other, out):
    out[...] = folded(gram(thirds(both_columns(me[2], own[...], other[...]))))


def factor_body(after, mine, other, out):
    out[...] = lower_inverse(unfolded(mine, other))


def second_gram_body(me, factor, own, other, mapped, out):
    full = both_columns(me[2], own[...], other[...])
    parts = thirds(times(factor[...], thirds(full)))
    mapped[...] = parts
    out[...] = folded(gram(parts))


def final_body(me, mapped, mine, other, out):
    factor = lower_inverse(unfolded(mine, other))
    own_cols = out.shape[0]
    part = jnp.where(me[2] == 0, factor[:own_cols], factor[own_cols:])
    out[...] = times(part, mapped[...])


def shift_by(value, axes, size, shift):
    return lax.ppermute(value, axes, [(i, (i + shift) % size) for i in range(size)])


def pair_sum(value, axes):
    terms = None
    steps = [(name, 1 << bit) for name in axes for bit in range((lax.axis_size(name) - 1).bit_length())]
    for name, flip in steps:
        if terms is not None:
            value = terms[0] + terms[1]
        size = lax.axis_size(name)
        terms = (value, lax.ppermute(value, name, [(i, i ^ flip) for i in range(size)]))
    return terms


def local(embeddings, start, pair_list, pair_count):
    row_count = lax.axis_size("rows")
    tile_count = lax.axis_size("tiles")
    core_count = lax.axis_size("cols")
    row_index = lax.axis_index("rows")
    tile_index = lax.axis_index("tiles")
    col_index = lax.axis_index("cols")
    me = jnp.stack([row_index, tile_index, col_index]).astype(jnp.int32)
    rows_here, half_features = embeddings.shape
    blocks_here = rows_here // BLOCK
    slots = pair_list.shape[2]
    capacity = slots // row_count
    per_core = capacity // core_count
    own_blocks = blocks_here // tile_count
    own_cols = start.shape[1]
    block_count = row_count * blocks_here
    others = range(1, row_count)

    own_list = jnp.concatenate([pair_list.reshape(1, 2 * slots), pair_count.reshape(1, 1)], axis=1)
    lists = [own_list] + [shift_by(own_list, "rows", row_count, k) for k in others]
    self_part = call(
        functools.partial(self_distance_body, own_blocks, tile_count),
        sds((own_blocks * BLOCK, BLOCK), F32),
        [me, embeddings],
        smem_in=(0,),
    )
    planned = call(
        functools.partial(plan_body, (row_count, capacity, slots, blocks_here)),
        [sds((6, slots), jnp.int32)] + [sds((capacity * BLOCK, half_features), BF16) for _ in others],
        [me, *lists, embeddings, self_part],
        smem_in=range(1 + row_count),
        any_in=(row_count + 2,),
        smem_out=(0,),
    )
    idx, sends = planned[0], planned[1:]
    far = [shift_by(sends[k - 1], "rows", row_count, -k) for k in others]

    self_other = shift_by(self_part, "cols", core_count, 1)
    self_tiles, self_sums = call(
        functools.partial(self_tile_body, own_blocks),
        [sds((own_blocks, 2 * BLOCK, BLOCK), BF16), sds((own_blocks, BLOCK), F32)],
        [self_part, self_other],
    )
    values = start.T
    start_sends = call(
        functools.partial(pick_body, row_count, capacity),
        [sds((own_cols, 2 * capacity * BLOCK), F32) for _ in others],
        [idx, values, far[0]],
        smem_in=(0,),
        any_in=(2,),
    )
    start_in = [shift_by(start_sends[k - 1], "rows", row_count, k) for k in others]

    first_part = call(
        functools.partial(pair_distance_body, range(row_count - 1), capacity),
        sds(((slots - capacity) * BLOCK, BLOCK), F32),
        [idx, embeddings, *far[:-1]],
        smem_in=(0,),
    )
    first_other = shift_by(first_part, "cols", core_count, 1)
    last_part = call(
        functools.partial(pair_distance_body, (row_count - 1,), capacity),
        sds((capacity * BLOCK, BLOCK), F32),
        [idx, embeddings, far[-1]],
        smem_in=(0,),
    )
    last_other = shift_by(last_part, "cols", core_count, 1)
    table = sds((block_count, BLOCK), F32)
    tiles = call(
        functools.partial(pair_tile_body, row_count, capacity, per_core, tile_count, blocks_here),
        [sds((slots, 2 * BLOCK, BLOCK), BF16), sds((capacity, 2 * BLOCK, BLOCK), BF16)]
        + [sds((per_core, 2 * BLOCK, BLOCK), BF16) for _ in others]
        + [table],
        [me, idx, first_part, first_other, last_part, last_other, self_sums, *start_in],
        smem_in=(0, 1),
        any_in=range(7, 6 + row_count),
    )
    near_tiles, home_tiles, tile_sends = tiles[0], tiles[1], tiles[2:-1]
    degree_terms = pair_sum(tiles[-1], ("tiles", "rows"))
    sent = [shift_by(tile_sends[k - 1], "rows", row_count, k) for k in others]
    shared = [shift_by(tile, "cols", core_count, 1) for tile in sent]

    dims = (row_count, capacity, per_core, blocks_here, tile_count)
    tile_args = [near_tiles, home_tiles, *sent, *shared, self_tiles]
    block_shape = sds((own_cols, rows_here), F32)
    square = sds((2 * own_cols, 2 * own_cols), F32)
    folded_square = sds((own_cols, 4 * own_cols), F32)

    part, degree, inverse = call(
        functools.partial(first_apply_body, dims),
        [block_shape, table, table],
        [me, idx, *degree_terms, values, *start_in, *tile_args],
        smem_in=(0, 1),
    )
    mine, other = pair_sum(part, ("tiles",))
    first = call(
        functools.partial(mapped_body, row_count, capacity, blocks_here),
        [block_shape] + [sds((own_cols, 2 * capacity * BLOCK), F32) for _ in others],
        [me, idx, inverse, mine, other],
        smem_in=(0, 1),
    )
    mapped, sends = first[0], first[1:]
    received = [shift_by(sends[k - 1], "rows", row_count, k) for k in others]

    mapped_other = shift_by(mapped, "cols", core_count, 1)
    first_gram = call(gram_body, folded_square, [me, mapped, mapped_other], smem_in=(0,))
    gram_terms = pair_sum(first_gram, ("rows",))
    part = call(
        functools.partial(second_apply_body, dims),
        block_shape,
        [me, idx, inverse, mapped, *received, *tile_args],
        smem_in=(0, 1),
    )
    mine, other = pair_sum(part, ("tiles",))
    second = call(
        functools.partial(last_mapped_body, blocks_here),
        block_shape,
        [me, inverse, mine, other, gram_terms[0]],
        smem_in=(0,),
        any_in=(4,),
    )
    second_other = shift_by(second, "cols", core_count, 1)
    factor = call(factor_body, square, [second, *gram_terms], any_in=(0,))
    full, second_gram = call(
        second_gram_body,
        [sds((6 * own_cols, rows_here), BF16), folded_square],
        [me, factor, second, second_other],
        smem_in=(0,),
    )
    vectors = call(
        final_body, block_shape, [me, full, *pair_sum(second_gram, ("rows",))], smem_in=(0,)
    )
    own_degree = lax.dynamic_slice_in_dim(degree, row_index * blocks_here, blocks_here, 0)
    return (vectors.T, own_degree.reshape(rows_here))


def solution(mesh):
    in_specs = (
        P(("groups", "rows"), "cols"),
        P(("groups", "rows"), "cols"),
        P(("groups", "rows", "tiles"), None, None),
        P(("groups", "rows", "tiles")),
    )
    out_specs = (P(("groups", "rows"), "cols"), P(("groups", "rows")))
    return jax.shard_map(local, mesh=mesh, in_specs=in_specs, out_specs=out_specs, check_vma=False)
```

```python
import functools

import jax
import jax.numpy as jnp
from jax import lax
from jax.experimental import pallas as pl
from jax.experimental.pallas import tpu as pltpu
from jax.sharding import PartitionSpec as P

BLOCK = 128
kernel_gamma = 14.0

VMEM = pl.BlockSpec(memory_space=pltpu.VMEM)
SMEM = pl.BlockSpec(memory_space=pltpu.SMEM)
ANY = pl.BlockSpec(memory_space=pl.ANY)
HBM = pl.BlockSpec(memory_space=pltpu.HBM)
F32 = jnp.float32
BF16 = jnp.bfloat16
HIGHEST = lax.Precision.HIGHEST
NT = (((1,), (1,)), ((), ()))


def call(body, outs, args, smem_in=(), smem_out=(), any_in=(), hbm_in=(), scratch=()):
    single = not isinstance(outs, (list, tuple))
    shapes = [outs] if single else list(outs)
    result = pl.pallas_call(
        body,
        out_shape=shapes,
        in_specs=[
            SMEM if i in smem_in else ANY if i in any_in else HBM if i in hbm_in else VMEM
            for i in range(len(args))
        ],
        out_specs=[SMEM if i in smem_out else VMEM for i in range(len(shapes))],
        scratch_shapes=list(scratch),
        compiler_params=pltpu.CompilerParams(vmem_limit_bytes=48 * 2**20),
    )(*args)
    return result[0] if single else result


def sds(shape, dtype):
    return jax.ShapeDtypeStruct(shape, dtype)


def at_block(index):
    return pl.ds(pl.multiple_of(index * BLOCK, BLOCK), BLOCK)


def eye_mask(size):
    return lax.broadcasted_iota(jnp.int32, (size, size), 0) == lax.broadcasted_iota(
        jnp.int32, (size, size), 1
    )


def halves(value):
    high = value.astype(BF16)
    low = (value - high.astype(F32)).astype(BF16)
    return high, low


def pack(tile):
    return jnp.concatenate(halves(tile), axis=0)


def product(packed, values):
    left = jnp.concatenate(halves(values), axis=0)
    both = jnp.dot(jnp.concatenate([left, left], axis=1), packed, preferred_element_type=F32)
    count = values.shape[0]
    return both[:count] + both[count:]


def thirds(value):
    high = value.astype(BF16)
    rest = value - high.astype(F32)
    middle = rest.astype(BF16)
    low = (rest - middle.astype(F32)).astype(BF16)
    return jnp.concatenate([high, middle, low], axis=0)


def gram(parts):
    cross = lax.dot_general(parts, parts, NT, preferred_element_type=F32)
    n = parts.shape[0] // 3
    total = None
    for i, j in ((2, 2), (1, 2), (2, 1), (0, 2), (2, 0), (1, 1), (0, 1), (1, 0), (0, 0)):
        piece = cross[i * n : (i + 1) * n, j * n : (j + 1) * n]
        total = piece if total is None else total + piece
    return total


def times(left, parts):
    left = thirds(left)
    m = left.shape[0] // 3
    product3 = jnp.dot(
        jnp.concatenate([left, left, left], axis=1), parts, preferred_element_type=F32
    )
    return (product3[2 * m :] + product3[m : 2 * m]) + product3[:m]


def lower_inverse(matrix, step=4):
    n = matrix.shape[0]
    state = jnp.concatenate([matrix, eye_mask(n).astype(F32)], axis=1)
    done = []
    for j in range(0, n, step):
        top = j // 8 * 8
        if top > n - state.shape[0]:
            done.append(state[:8])
            state = state[8:]
        base = j - top
        rows = lax.broadcasted_iota(jnp.int32, state.shape, 0)
        columns = [jnp.broadcast_to(state[:, j + i : j + i + 1], state.shape) for i in range(step)]
        lines = [state[base + i : base + i + 1, :] for i in range(step)]
        pivot = [[columns[k][base + i : base + i + 1, :] for k in range(step)] for i in range(step)]
        for i in range(step):
            reciprocal = 1.0 / pivot[i][i]
            scaled = lines[i] * reciprocal
            ratio = [pivot[i][k] * reciprocal for k in range(step)]
            for k in range(i + 1, step):
                lines[k] = lines[k] - pivot[k][i] * scaled
                columns[k] = columns[k] - columns[i] * ratio[k]
                for m in range(i + 1, step):
                    pivot[k][m] = pivot[k][m] - pivot[k][i] * ratio[m]
            state = state - jnp.where(rows > base + i, columns[i], 0.0) * scaled
    state = jnp.concatenate([*done, state], axis=0)
    pivots = jnp.sum(jnp.where(eye_mask(n), state[:, :n], 0.0), axis=1, keepdims=True)
    return state[:, n:] / jnp.sqrt(pivots)


def both_columns(core, own, other):
    first = core == 0
    return jnp.concatenate(
        [jnp.where(first, own, other), jnp.where(first, other, own)], axis=0
    )


def plan_body(dims, me, *refs):
    row_count, capacity, slots, blocks_here = dims
    lists, (emb_hbm, idx) = refs[:row_count], refs[row_count : row_count + 2]
    sends, (emb, done) = refs[row_count + 2 : -2], refs[-2:]
    row = me[0]
    copy = pltpu.make_async_copy(emb_hbm, emb, done)
    copy.start()

    def clear(i, carry):
        for line in range(6):
            idx[line, i] = 0
        return carry

    lax.fori_loop(0, slots, clear, 0)

    def ranked(listed, want, write):
        count = listed[2, 0]

        def step(s, counts):
            near = listed[0, s]
            far = listed[1, s]
            return write(s, near, far, far // blocks_here, s < count, counts)

        lax.fori_loop(0, slots, step, (0,) * want)

    def write_own(s, near, far, owner, live, counts):
        shift = lax.rem(owner - row + row_count, row_count)
        rank = functools.reduce(
            lambda total, k: total + jnp.where(shift == k, counts[k], 0), range(row_count), 0
        )

        @pl.when(live)
        def _():
            slot = shift * capacity + rank
            idx[0, slot] = near - row * blocks_here
            idx[1, slot] = far
            idx[2, slot] = 1
            idx[3, slot] = s

        return tuple(
            counts[k] + (live & (shift == k)).astype(jnp.int32) for k in range(row_count)
        )

    for k in range(row_count):
        if k == 0:
            ranked(lists[k], row_count, write_own)

        def write_in(s, near, far, owner, live, counts, k=k):
            hit = live & (owner == row)

            @pl.when(hit)
            def _():
                slot = k * capacity + counts[0]
                idx[4, slot] = far - row * blocks_here
                idx[5, slot] = near

            return (counts[0] + hit.astype(jnp.int32),)

        ranked(lists[k], 1, write_in)
    copy.wait()
    for k in range(1, row_count):
        for j in range(capacity):
            sends[k - 1][j * BLOCK : (j + 1) * BLOCK, :] = emb[at_block(idx[4, k * capacity + j]), :]


def partial_distance(left, right):
    inner = lax.dot_general(left, right, NT, preferred_element_type=F32)
    left_sq = jnp.sum(jnp.square(left.astype(F32)), axis=1, keepdims=True)
    right_sq = jnp.sum(jnp.square(right.astype(F32)), axis=1, keepdims=True)
    right_row = jnp.sum(jnp.where(eye_mask(BLOCK), right_sq, 0.0), axis=0, keepdims=True)
    return left_sq + right_row - 2.0 * inner


def self_distance_body(own_blocks, tile_count, me, emb, out):
    for i in range(own_blocks):
        block = emb[at_block(i * tile_count + me[1]), :]
        out[i * BLOCK : (i + 1) * BLOCK, :] = partial_distance(block, block)


def pair_distance_body(row_count, capacity, idx, emb, *refs):
    out = refs[-1]
    for k in range(row_count):
        for j in range(capacity):
            slot = k * capacity + j
            left = emb[at_block(idx[0, slot]), :]
            if k == 0:
                right = emb[at_block(idx[4, j]), :]
            else:
                right = refs[k - 1][j * BLOCK : (j + 1) * BLOCK, :]
            out[slot * BLOCK : (slot + 1) * BLOCK, :] = partial_distance(left, right)


def self_tile_body(own_blocks, mine, other, packed, sums):
    for i in range(own_blocks):
        part = slice(i * BLOCK, (i + 1) * BLOCK)
        tile = jnp.exp(-kernel_gamma * (mine[part, :] + other[part, :] - 2.0))
        tile = jnp.where(eye_mask(BLOCK), 0.0, tile)
        packed[i] = pack(tile)
        sums[i : i + 1, :] = jnp.sum(tile, axis=0, keepdims=True)


def pair_tile_body(dims, me, idx, mine, other, self_sums, values, near_tiles, home_tiles, table, *sends):
    row_count, capacity, per_core, blocks_here, tile_count = dims
    row, tile_index, core = me[0], me[1], me[2]
    table[...] = jnp.zeros(table.shape, F32)
    for i in range(self_sums.shape[0]):
        table[pl.ds(row * blocks_here + i * tile_count + tile_index, 1), :] = self_sums[i : i + 1, :]

    def add(block, line):
        place = pl.ds(block, 1)
        table[place, :] = table[place, :] + line

    for k in range(row_count):
        for j in range(capacity):
            slot = k * capacity + j
            part = slice(slot * BLOCK, (slot + 1) * BLOCK)
            tile = jnp.exp(-kernel_gamma * (mine[part, :] + other[part, :] - 2.0))
            tile = jnp.where(idx[2, slot] > 0, tile, 0.0)
            turned = tile.T
            near_tiles[slot] = pack(turned)
            add(row * blocks_here + idx[0, slot], jnp.sum(turned, axis=0, keepdims=True))
            add(idx[1, slot], jnp.sum(tile, axis=0, keepdims=True))
            if k == 0:
                home_tiles[j] = pack(tile)
            else:

                @pl.when(core == j // per_core)
                def _():
                    inner = j % per_core
                    sends[k - 1][inner * BLOCK : (inner + 1) * BLOCK, :] = tile

    pick_columns(idx, row_count, capacity, values, sends, per_core * BLOCK)


def pick_columns(idx, row_count, capacity, source, sends, base):
    count = source.shape[0]
    for k in range(1, row_count):
        back = row_count - k
        blocks = [idx[0, k * capacity + j] for j in range(capacity)]
        blocks += [idx[4, back * capacity + j] for j in range(capacity)]
        for place, block in enumerate(blocks):
            rows = slice(base + place * count, base + (place + 1) * count)
            sends[k - 1][rows, :] = source[:, at_block(block)]


def apply_tiles(dims, me, idx, inverse, own, received, base, near_tiles, home_tiles, sent, shared, self_tiles, out):
    row_count, capacity, per_core, blocks_here, tile_count = dims
    row, tile_index, core = me[0], me[1], me[2]
    count = out.shape[0]
    out[...] = jnp.zeros(out.shape, F32)

    def scaled(values, block):
        return values * inverse[pl.ds(block, 1), :]

    def add(block, packed, values):
        place = at_block(block)
        out[:, place] = out[:, place] + product(packed, values)

    def arrived(k, place):
        return received[k - 1][pl.ds(pl.multiple_of(base + place * count, 8), count), :]

    for i in range(blocks_here // tile_count):
        block = i * tile_count + tile_index
        add(block, self_tiles[i], scaled(own[:, at_block(block)], row * blocks_here + block))
    for k in range(row_count):
        for j in range(capacity):
            slot = k * capacity + j
            if k == 0:
                values = own[:, at_block(idx[4, j])]
            else:
                values = arrived(row_count - k, capacity + j)
            add(idx[0, slot], near_tiles[slot], scaled(values, idx[1, slot]))
    for k in range(row_count):
        for j in range(capacity):
            if k == 0:
                slot = j
                values = own[:, at_block(idx[0, j])]
                packed = home_tiles[j]
            else:
                inner = j % per_core
                part = slice(inner * BLOCK, (inner + 1) * BLOCK)
                if j < per_core:
                    place = core * per_core + inner
                    packed = pack(sent[k - 1][part, :])
                else:
                    place = (1 - core) * per_core + inner
                    packed = pack(shared[k - 1][part, :])
                slot = k * capacity + place
                values = arrived(k, place)
            add(idx[4, slot], packed, scaled(values, idx[5, slot]))


def first_apply_body(dims, me, idx, *refs):
    row_count, per_core = dims[0], dims[2]
    terms, refs = refs[:row_count], refs[row_count:]
    own, near_tiles, home_tiles, self_tiles = refs[:4]
    sent, shared = refs[4 : 3 + row_count], refs[3 + row_count : 2 + 2 * row_count]
    out, degree, inverse = refs[-3:]
    total = functools.reduce(lambda total, term: total + term[...], terms[1:], terms[0][...])
    degree[...] = total
    inverse[...] = 1.0 / jnp.sqrt(total)
    apply_tiles(
        dims, me, idx, inverse, own, sent, per_core * BLOCK, near_tiles, home_tiles, sent, shared, self_tiles, out
    )


def second_apply_body(dims, me, idx, inverse, after, *refs):
    row_count = dims[0]
    own, near_tiles, home_tiles, self_tiles = refs[:4]
    sent, shared = refs[4 : 3 + row_count], refs[3 + row_count : 2 + 2 * row_count]
    received, out = refs[2 + 2 * row_count : -1], refs[-1]
    apply_tiles(dims, me, idx, inverse, own, received, 0, near_tiles, home_tiles, sent, shared, self_tiles, out)


def scale_rows(me, blocks_here, inverse, mine, other, out):
    for b in range(blocks_here):
        part = slice(b * BLOCK, (b + 1) * BLOCK)
        row = inverse[pl.ds(me[0] * blocks_here + b, 1), :]
        out[:, part] = (mine[:, part] + other[:, part]) * row


def mapped_body(row_count, capacity, blocks_here, me, idx, inverse, mine, other, out, *sends):
    scale_rows(me, blocks_here, inverse, mine, other, out)
    pick_columns(idx, row_count, capacity, out, sends, 0)


def last_mapped_body(blocks_here, me, inverse, mine, other, *refs):
    scale_rows(me, blocks_here, inverse, mine, other, refs[-1])


def folded(square):
    half = square.shape[0] // 2
    return jnp.concatenate([square[:half], square[half:]], axis=1)


def unfolded(terms):
    total = functools.reduce(lambda total, term: total + term[...], terms[1:], terms[0][...])
    width = total.shape[1] // 2
    return jnp.concatenate([total[:, :width], total[:, width:]], axis=0)


def gram_body(me, own, other, out):
    out[...] = folded(gram(thirds(both_columns(me[2], own[...], other[...]))))


def factor_body(after, *refs):
    refs[-1][...] = lower_inverse(unfolded(refs[:-1]))


def second_gram_body(me, factor, own, other, mapped, out):
    full = both_columns(me[2], own[...], other[...])
    parts = thirds(times(factor[...], thirds(full)))
    mapped[...] = parts
    out[...] = folded(gram(parts))


def final_body(me, mapped, *refs):
    out = refs[-1]
    factor = lower_inverse(unfolded(refs[:-1]))
    own_cols = out.shape[0]
    part = jnp.where(me[2] == 0, factor[:own_cols], factor[own_cols:])
    out[...] = times(part, mapped[...])


def shift_by(value, axes, size, shift):
    return lax.ppermute(value, axes, [(i, (i + shift) % size) for i in range(size)])


def row_terms(value, row_count):
    return [value] + [shift_by(value, "rows", row_count, k) for k in range(1, row_count)]


def pair_sum(value, axes):
    terms = None
    steps = [(name, 1 << bit) for name in axes for bit in range((lax.axis_size(name) - 1).bit_length())]
    for name, flip in steps:
        if terms is not None:
            value = terms[0] + terms[1]
        size = lax.axis_size(name)
        terms = (value, lax.ppermute(value, name, [(i, i ^ flip) for i in range(size)]))
    return terms


def local(embeddings, start, pair_list, pair_count):
    row_count = lax.axis_size("rows")
    tile_count = lax.axis_size("tiles")
    core_count = lax.axis_size("cols")
    row_index = lax.axis_index("rows")
    tile_index = lax.axis_index("tiles")
    col_index = lax.axis_index("cols")
    me = jnp.stack([row_index, tile_index, col_index]).astype(jnp.int32)
    rows_here, half_features = embeddings.shape
    blocks_here = rows_here // BLOCK
    slots = pair_list.shape[2]
    capacity = slots // row_count
    per_core = capacity // core_count
    own_blocks = blocks_here // tile_count
    own_cols = start.shape[1]
    block_count = row_count * blocks_here
    others = range(1, row_count)

    own_list = jnp.concatenate(
        [pair_list[0], jnp.broadcast_to(pair_count[:, None], (1, slots))], axis=0
    )
    lists = row_terms(own_list, row_count)
    planned = call(
        functools.partial(plan_body, (row_count, capacity, slots, blocks_here)),
        [sds((6, slots), jnp.int32)] + [sds((capacity * BLOCK, half_features), BF16) for _ in others],
        [me, *lists, embeddings],
        smem_in=range(1 + row_count),
        hbm_in=(row_count + 1,),
        smem_out=(0,),
        scratch=[pltpu.VMEM(embeddings.shape, BF16), pltpu.SemaphoreType.DMA],
    )
    idx, sends = planned[0], planned[1:]
    far = [shift_by(sends[k - 1], "rows", row_count, -k) for k in others]

    self_part = call(
        functools.partial(self_distance_body, own_blocks, tile_count),
        sds((own_blocks * BLOCK, BLOCK), F32),
        [me, embeddings],
        smem_in=(0,),
    )
    self_other = shift_by(self_part, "cols", core_count, 1)
    self_tiles, self_sums = call(
        functools.partial(self_tile_body, own_blocks),
        [sds((own_blocks, 2 * BLOCK, BLOCK), BF16), sds((own_blocks, BLOCK), F32)],
        [self_part, self_other],
    )
    pair_part = call(
        functools.partial(pair_distance_body, row_count, capacity),
        sds((slots * BLOCK, BLOCK), F32),
        [idx, embeddings, *far],
        smem_in=(0,),
    )
    pair_other = shift_by(pair_part, "cols", core_count, 1)

    values = start.T
    dims = (row_count, capacity, per_core, blocks_here, tile_count)
    table = sds((block_count, BLOCK), F32)
    picked = 2 * capacity * own_cols
    tiles = call(
        functools.partial(pair_tile_body, dims),
        [sds((slots, 2 * BLOCK, BLOCK), BF16), sds((capacity, 2 * BLOCK, BLOCK), BF16), table]
        + [sds((per_core * BLOCK + picked, BLOCK), F32) for _ in others],
        [me, idx, pair_part, pair_other, self_sums, values],
        smem_in=(0, 1),
    )
    near_tiles, home_tiles, degrees, sends = tiles[0], tiles[1], tiles[2], tiles[3:]
    mine, other = pair_sum(degrees, ("tiles",))
    degree_terms = row_terms(mine + other, row_count)
    sent = [shift_by(sends[k - 1], "rows", row_count, k) for k in others]
    shared = [shift_by(message, "cols", core_count, 1) for message in sent]

    tile_args = [near_tiles, home_tiles, self_tiles, *sent, *shared]
    block_shape = sds((own_cols, rows_here), F32)
    square = sds((2 * own_cols, 2 * own_cols), F32)
    folded_square = sds((own_cols, 4 * own_cols), F32)

    part, degree, inverse = call(
        functools.partial(first_apply_body, dims),
        [block_shape, table, table],
        [me, idx, *degree_terms, values, *tile_args],
        smem_in=(0, 1),
    )
    mine, other = pair_sum(part, ("tiles",))
    first = call(
        functools.partial(mapped_body, row_count, capacity, blocks_here),
        [block_shape] + [sds((picked, BLOCK), F32) for _ in others],
        [me, idx, inverse, mine, other],
        smem_in=(0, 1),
    )
    mapped, sends = first[0], first[1:]
    received = [shift_by(sends[k - 1], "rows", row_count, k) for k in others]

    mapped_other = shift_by(mapped, "cols", core_count, 1)
    first_gram = call(gram_body, folded_square, [me, mapped, mapped_other], smem_in=(0,))
    gram_terms = row_terms(first_gram, row_count)
    part = call(
        functools.partial(second_apply_body, dims),
        block_shape,
        [me, idx, inverse, first_gram, mapped, *tile_args, *received],
        smem_in=(0, 1),
        any_in=(3,),
    )
    mine, other = pair_sum(part, ("tiles",))
    second = call(
        functools.partial(last_mapped_body, blocks_here),
        block_shape,
        [me, inverse, mine, other, *gram_terms[1:]],
        smem_in=(0,),
        any_in=range(4, 3 + row_count),
    )
    second_other = shift_by(second, "cols", core_count, 1)
    factor = call(factor_body, square, [second, *gram_terms], any_in=(0,))
    full, second_gram = call(
        second_gram_body,
        [sds((6 * own_cols, rows_here), BF16), folded_square],
        [me, factor, second, second_other],
        smem_in=(0,),
    )
    vectors = call(
        final_body, block_shape, [me, full, *row_terms(second_gram, row_count)], smem_in=(0,)
    )
    own_degree = lax.dynamic_slice_in_dim(degree, row_index * blocks_here, blocks_here, 0)
    return (vectors.T, own_degree.reshape(rows_here))


def solution(mesh):
    in_specs = (
        P(("groups", "rows"), "cols"),
        P(("groups", "rows"), "cols"),
        P(("groups", "rows", "tiles"), None, None),
        P(("groups", "rows", "tiles")),
    )
    out_specs = (P(("groups", "rows"), "cols"), P(("groups", "rows")))
    return jax.shard_map(local, mesh=mesh, in_specs=in_specs, out_specs=out_specs, check_vma=False)
```

```python
import functools

import jax
import jax.numpy as jnp
from jax import lax
from jax.experimental import pallas as pl
from jax.experimental.pallas import tpu as pltpu
from jax.sharding import PartitionSpec as P

BLOCK = 128
kernel_gamma = 14.0

VMEM = pl.BlockSpec(memory_space=pltpu.VMEM)
SMEM = pl.BlockSpec(memory_space=pltpu.SMEM)
ANY = pl.BlockSpec(memory_space=pl.ANY)
F32 = jnp.float32
BF16 = jnp.bfloat16
HIGHEST = lax.Precision.HIGHEST
NT = (((1,), (1,)), ((), ()))


def call(body, outs, args, smem_in=(), smem_out=(), any_in=()):
    single = not isinstance(outs, (list, tuple))
    shapes = [outs] if single else list(outs)
    result = pl.pallas_call(
        body,
        out_shape=shapes,
        in_specs=[
            SMEM if i in smem_in else ANY if i in any_in else VMEM for i in range(len(args))
        ],
        out_specs=[SMEM if i in smem_out else VMEM for i in range(len(shapes))],
        compiler_params=pltpu.CompilerParams(vmem_limit_bytes=48 * 2**20),
    )(*args)
    return result[0] if single else result


def sds(shape, dtype):
    return jax.ShapeDtypeStruct(shape, dtype)


def at_block(index):
    return pl.ds(pl.multiple_of(index * BLOCK, BLOCK), BLOCK)


def eye_mask(size):
    return lax.broadcasted_iota(jnp.int32, (size, size), 0) == lax.broadcasted_iota(
        jnp.int32, (size, size), 1
    )


def halves(value):
    high = value.astype(BF16)
    low = (value - high.astype(F32)).astype(BF16)
    return high, low


def pack(tile):
    return jnp.concatenate(halves(tile), axis=0)


def product(packed, values):
    left = jnp.concatenate(halves(values), axis=0)
    both = jnp.dot(jnp.concatenate([left, left], axis=1), packed, preferred_element_type=F32)
    count = values.shape[0]
    return both[:count] + both[count:]


def thirds(value):
    high = value.astype(BF16)
    rest = value - high.astype(F32)
    middle = rest.astype(BF16)
    low = (rest - middle.astype(F32)).astype(BF16)
    return jnp.concatenate([high, middle, low], axis=0)


def gram(parts):
    cross = lax.dot_general(parts, parts, NT, preferred_element_type=F32)
    n = parts.shape[0] // 3
    total = None
    for i, j in ((2, 2), (1, 2), (2, 1), (0, 2), (2, 0), (1, 1), (0, 1), (1, 0), (0, 0)):
        piece = cross[i * n : (i + 1) * n, j * n : (j + 1) * n]
        total = piece if total is None else total + piece
    return total


def times(left, parts):
    left = thirds(left)
    m = left.shape[0] // 3
    product3 = jnp.dot(
        jnp.concatenate([left, left, left], axis=1), parts, preferred_element_type=F32
    )
    return (product3[2 * m :] + product3[m : 2 * m]) + product3[:m]


def lower_inverse(matrix, step=4):
    n = matrix.shape[0]
    state = jnp.concatenate([matrix, eye_mask(n).astype(F32)], axis=1)
    done = []
    for j in range(0, n, step):
        top = j // 8 * 8
        if top > n - state.shape[0]:
            done.append(state[:8])
            state = state[8:]
        base = j - top
        rows = lax.broadcasted_iota(jnp.int32, state.shape, 0)
        columns = [jnp.broadcast_to(state[:, j + i : j + i + 1], state.shape) for i in range(step)]
        lines = [state[base + i : base + i + 1, :] for i in range(step)]
        pivot = [[columns[k][base + i : base + i + 1, :] for k in range(step)] for i in range(step)]
        for i in range(step):
            reciprocal = 1.0 / pivot[i][i]
            scaled = lines[i] * reciprocal
            ratio = [pivot[i][k] * reciprocal for k in range(step)]
            for k in range(i + 1, step):
                lines[k] = lines[k] - pivot[k][i] * scaled
                columns[k] = columns[k] - columns[i] * ratio[k]
                for m in range(i + 1, step):
                    pivot[k][m] = pivot[k][m] - pivot[k][i] * ratio[m]
            state = state - jnp.where(rows > base + i, columns[i], 0.0) * scaled
    state = jnp.concatenate([*done, state], axis=0)
    pivots = jnp.sum(jnp.where(eye_mask(n), state[:, :n], 0.0), axis=1, keepdims=True)
    return state[:, n:] / jnp.sqrt(pivots)


def both_columns(core, own, other):
    first = core == 0
    return jnp.concatenate(
        [jnp.where(first, own, other), jnp.where(first, other, own)], axis=0
    )


def plan_body(dims, me, *refs):
    row_count, capacity, slots, blocks_here = dims
    lists, (emb, after, idx) = refs[:row_count], refs[row_count : row_count + 3]
    sends = refs[row_count + 3 :]
    row = me[0]

    def clear(i, carry):
        for line in range(6):
            idx[line, i] = 0
        return carry

    lax.fori_loop(0, slots, clear, 0)

    def ranked(listed, want, write):
        count = listed[2, 0]

        def step(s, counts):
            near = listed[0, s]
            far = listed[1, s]
            return write(s, near, far, far // blocks_here, s < count, counts)

        lax.fori_loop(0, slots, step, (0,) * want)

    def write_own(s, near, far, owner, live, counts):
        shift = lax.rem(owner - row + row_count, row_count)
        rank = functools.reduce(
            lambda total, k: total + jnp.where(shift == k, counts[k], 0), range(row_count), 0
        )

        @pl.when(live)
        def _():
            slot = shift * capacity + rank
            idx[0, slot] = near - row * blocks_here
            idx[1, slot] = far
            idx[2, slot] = 1
            idx[3, slot] = s

        return tuple(
            counts[k] + (live & (shift == k)).astype(jnp.int32) for k in range(row_count)
        )

    for k in range(row_count):
        if k == 0:
            ranked(lists[k], row_count, write_own)

        def write_in(s, near, far, owner, live, counts, k=k):
            hit = live & (owner == row)

            @pl.when(hit)
            def _():
                slot = k * capacity + counts[0]
                idx[4, slot] = far - row * blocks_here
                idx[5, slot] = near

            return (counts[0] + hit.astype(jnp.int32),)

        ranked(lists[k], 1, write_in)
    for k in range(1, row_count):
        for j in range(capacity):
            sends[k - 1][j * BLOCK : (j + 1) * BLOCK, :] = emb[at_block(idx[4, k * capacity + j]), :]


def partial_distance(left, right):
    inner = lax.dot_general(left, right, NT, preferred_element_type=F32)
    left_sq = jnp.sum(jnp.square(left.astype(F32)), axis=1, keepdims=True)
    right_sq = jnp.sum(jnp.square(right.astype(F32)), axis=1, keepdims=True)
    right_row = jnp.sum(jnp.where(eye_mask(BLOCK), right_sq, 0.0), axis=0, keepdims=True)
    return left_sq + right_row - 2.0 * inner


def self_distance_body(own_blocks, tile_count, me, emb, out):
    for i in range(own_blocks):
        block = emb[at_block(i * tile_count + me[1]), :]
        out[i * BLOCK : (i + 1) * BLOCK, :] = partial_distance(block, block)


def pair_distance_body(row_count, capacity, idx, emb, *refs):
    out = refs[-1]
    for k in range(row_count):
        for j in range(capacity):
            slot = k * capacity + j
            left = emb[at_block(idx[0, slot]), :]
            if k == 0:
                right = emb[at_block(idx[4, j]), :]
            else:
                right = refs[k - 1][j * BLOCK : (j + 1) * BLOCK, :]
            out[slot * BLOCK : (slot + 1) * BLOCK, :] = partial_distance(left, right)


def self_tile_body(own_blocks, mine, other, packed, sums):
    for i in range(own_blocks):
        part = slice(i * BLOCK, (i + 1) * BLOCK)
        tile = jnp.exp(-kernel_gamma * (mine[part, :] + other[part, :] - 2.0))
        tile = jnp.where(eye_mask(BLOCK), 0.0, tile)
        packed[i] = pack(tile)
        sums[i : i + 1, :] = jnp.sum(tile, axis=0, keepdims=True)


def pair_tile_body(dims, me, idx, mine, other, self_sums, values, near_tiles, home_tiles, table, *sends):
    row_count, capacity, per_core, blocks_here, tile_count = dims
    row, tile_index, core = me[0], me[1], me[2]
    table[...] = jnp.zeros(table.shape, F32)
    for i in range(self_sums.shape[0]):
        table[pl.ds(row * blocks_here + i * tile_count + tile_index, 1), :] = self_sums[i : i + 1, :]

    def add(block, line):
        place = pl.ds(block, 1)
        table[place, :] = table[place, :] + line

    for k in range(row_count):
        for j in range(capacity):
            slot = k * capacity + j
            part = slice(slot * BLOCK, (slot + 1) * BLOCK)
            tile = jnp.exp(-kernel_gamma * (mine[part, :] + other[part, :] - 2.0))
            tile = jnp.where(idx[2, slot] > 0, tile, 0.0)
            turned = tile.T
            near_tiles[slot] = pack(turned)
            add(row * blocks_here + idx[0, slot], jnp.sum(turned, axis=0, keepdims=True))
            add(idx[1, slot], jnp.sum(tile, axis=0, keepdims=True))
            if k == 0:
                home_tiles[j] = pack(tile)
            else:

                @pl.when(core == j // per_core)
                def _():
                    inner = j % per_core
                    sends[k - 1][inner * BLOCK : (inner + 1) * BLOCK, :] = tile

    pick_columns(idx, row_count, capacity, values, sends, per_core * BLOCK)


def split_body(row_count, per_core, *refs):
    others = row_count - 1
    messages, outs = refs[:others], refs[-others:]
    for message, out in zip(messages, outs):
        for inner in range(per_core):
            out[inner] = pack(message[inner * BLOCK : (inner + 1) * BLOCK, :])


def pick_columns(idx, row_count, capacity, source, sends, base):
    count = source.shape[0]
    for k in range(1, row_count):
        back = row_count - k
        blocks = [idx[0, k * capacity + j] for j in range(capacity)]
        blocks += [idx[4, back * capacity + j] for j in range(capacity)]
        for place, block in enumerate(blocks):
            rows = slice(base + place * count, base + (place + 1) * count)
            sends[k - 1][rows, :] = source[:, at_block(block)]


def apply_tiles(dims, me, idx, inverse, own, received, base, near_tiles, home_tiles, sent, shared, self_tiles, out):
    row_count, capacity, per_core, blocks_here, tile_count = dims
    row, tile_index, core = me[0], me[1], me[2]
    count = out.shape[0]
    out[...] = jnp.zeros(out.shape, F32)

    def scaled(values, block):
        return values * inverse[pl.ds(block, 1), :]

    def add(block, packed, values):
        place = at_block(block)
        out[:, place] = out[:, place] + product(packed, values)

    def arrived(k, place):
        return received[k - 1][pl.ds(pl.multiple_of(base + place * count, 8), count), :]

    for i in range(blocks_here // tile_count):
        block = i * tile_count + tile_index
        add(block, self_tiles[i], scaled(own[:, at_block(block)], row * blocks_here + block))
    for k in range(row_count):
        for j in range(capacity):
            slot = k * capacity + j
            if k == 0:
                values = own[:, at_block(idx[4, j])]
            else:
                values = arrived(row_count - k, capacity + j)
            add(idx[0, slot], near_tiles[slot], scaled(values, idx[1, slot]))
    for k in range(row_count):
        for j in range(capacity):
            if k == 0:
                slot = j
                values = own[:, at_block(idx[0, j])]
                packed = home_tiles[j]
            else:
                inner = j % per_core
                if j < per_core:
                    place = core * per_core + inner
                    packed = sent[k - 1][inner]
                else:
                    place = (1 - core) * per_core + inner
                    packed = shared[k - 1][inner]
                slot = k * capacity + place
                values = arrived(k, place)
            add(idx[4, slot], packed, scaled(values, idx[5, slot]))


def first_apply_body(dims, me, idx, *refs):
    row_count, per_core = dims[0], dims[2]
    terms, refs = refs[:row_count], refs[row_count:]
    own, near_tiles, home_tiles, self_tiles = refs[:4]
    sent, shared = refs[4 : 3 + row_count], refs[3 + row_count : 2 + 2 * row_count]
    messages = refs[2 + 2 * row_count : -3]
    out, degree, inverse = refs[-3:]
    total = functools.reduce(lambda total, term: total + term[...], terms[1:], terms[0][...])
    degree[...] = total
    inverse[...] = 1.0 / jnp.sqrt(total)
    apply_tiles(
        dims, me, idx, inverse, own, messages, per_core * BLOCK, near_tiles, home_tiles, sent, shared, self_tiles, out
    )


def second_apply_body(dims, me, idx, inverse, after, *refs):
    row_count = dims[0]
    own, near_tiles, home_tiles, self_tiles = refs[:4]
    sent, shared = refs[4 : 3 + row_count], refs[3 + row_count : 2 + 2 * row_count]
    received, out = refs[2 + 2 * row_count : -1], refs[-1]
    apply_tiles(dims, me, idx, inverse, own, received, 0, near_tiles, home_tiles, sent, shared, self_tiles, out)


def scale_rows(me, blocks_here, inverse, mine, other, out):
    for b in range(blocks_here):
        part = slice(b * BLOCK, (b + 1) * BLOCK)
        row = inverse[pl.ds(me[0] * blocks_here + b, 1), :]
        out[:, part] = (mine[:, part] + other[:, part]) * row


def mapped_body(row_count, capacity, blocks_here, me, idx, inverse, mine, other, out, *sends):
    scale_rows(me, blocks_here, inverse, mine, other, out)
    pick_columns(idx, row_count, capacity, out, sends, 0)


def last_mapped_body(blocks_here, me, inverse, mine, other, *refs):
    scale_rows(me, blocks_here, inverse, mine, other, refs[-1])


def folded(square):
    half = square.shape[0] // 2
    return jnp.concatenate([square[:half], square[half:]], axis=1)


def unfolded(terms):
    total = functools.reduce(lambda total, term: total + term[...], terms[1:], terms[0][...])
    width = total.shape[1] // 2
    return jnp.concatenate([total[:, :width], total[:, width:]], axis=0)


def gram_body(me, own, other, out):
    out[...] = folded(gram(thirds(both_columns(me[2], own[...], other[...]))))


def factor_body(after, *refs):
    refs[-1][...] = lower_inverse(unfolded(refs[:-1]))


def second_gram_body(me, factor, own, other, mapped, out):
    full = both_columns(me[2], own[...], other[...])
    parts = thirds(times(factor[...], thirds(full)))
    mapped[...] = parts
    out[...] = folded(gram(parts))


def final_body(me, mapped, *refs):
    out = refs[-1]
    factor = lower_inverse(unfolded(refs[:-1]))
    own_cols = out.shape[0]
    part = jnp.where(me[2] == 0, factor[:own_cols], factor[own_cols:])
    out[...] = times(part, mapped[...])


def shift_by(value, axes, size, shift):
    return lax.ppermute(value, axes, [(i, (i + shift) % size) for i in range(size)])


def row_terms(value, row_count):
    return [value] + [shift_by(value, "rows", row_count, k) for k in range(1, row_count)]


def pair_step(value, name, flip):
    return lax.ppermute(value, name, [(i, i ^ flip) for i in range(lax.axis_size(name))])


def pair_sum(value, axes):
    terms = None
    steps = [(name, 1 << bit) for name in axes for bit in range((lax.axis_size(name) - 1).bit_length())]
    for name, flip in steps:
        if terms is not None:
            value = terms[0] + terms[1]
        terms = (value, pair_step(value, name, flip))
    return terms


def local(embeddings, start, pair_list, pair_count):
    row_count = lax.axis_size("rows")
    tile_count = lax.axis_size("tiles")
    core_count = lax.axis_size("cols")
    row_index = lax.axis_index("rows")
    tile_index = lax.axis_index("tiles")
    col_index = lax.axis_index("cols")
    me = jnp.stack([row_index, tile_index, col_index]).astype(jnp.int32)
    rows_here, half_features = embeddings.shape
    blocks_here = rows_here // BLOCK
    slots = pair_list.shape[2]
    capacity = slots // row_count
    per_core = capacity // core_count
    own_blocks = blocks_here // tile_count
    own_cols = start.shape[1]
    block_count = row_count * blocks_here
    others = range(1, row_count)

    own_list = jnp.concatenate(
        [pair_list[0], jnp.broadcast_to(pair_count[:, None], (1, slots))], axis=0
    )
    lists = row_terms(own_list, row_count)
    self_part = call(
        functools.partial(self_distance_body, own_blocks, tile_count),
        sds((own_blocks * BLOCK, BLOCK), F32),
        [me, embeddings],
        smem_in=(0,),
    )
    planned = call(
        functools.partial(plan_body, (row_count, capacity, slots, blocks_here)),
        [sds((6, slots), jnp.int32)] + [sds((capacity * BLOCK, half_features), BF16) for _ in others],
        [me, *lists, embeddings, self_part],
        smem_in=range(1 + row_count),
        any_in=(row_count + 2,),
        smem_out=(0,),
    )
    idx, sends = planned[0], planned[1:]
    far = [shift_by(sends[k - 1], "rows", row_count, -k) for k in others]

    self_other = shift_by(self_part, "cols", core_count, 1)
    self_tiles, self_sums = call(
        functools.partial(self_tile_body, own_blocks),
        [sds((own_blocks, 2 * BLOCK, BLOCK), BF16), sds((own_blocks, BLOCK), F32)],
        [self_part, self_other],
    )
    pair_part = call(
        functools.partial(pair_distance_body, row_count, capacity),
        sds((slots * BLOCK, BLOCK), F32),
        [idx, embeddings, *far],
        smem_in=(0,),
    )
    pair_other = shift_by(pair_part, "cols", core_count, 1)

    values = start.T
    dims = (row_count, capacity, per_core, blocks_here, tile_count)
    table = sds((block_count, BLOCK), F32)
    picked = 2 * capacity * own_cols
    tiles = call(
        functools.partial(pair_tile_body, dims),
        [sds((slots, 2 * BLOCK, BLOCK), BF16), sds((capacity, 2 * BLOCK, BLOCK), BF16), table]
        + [sds((per_core * BLOCK + picked, BLOCK), F32) for _ in others],
        [me, idx, pair_part, pair_other, self_sums, values],
        smem_in=(0, 1),
    )
    near_tiles, home_tiles, degrees, sends = tiles[0], tiles[1], tiles[2], tiles[3:]
    mine, other = pair_sum(degrees, ("tiles",))
    degree_terms = row_terms(mine + other, row_count)
    messages = [shift_by(sends[k - 1], "rows", row_count, k) for k in others]
    sent = call(
        functools.partial(split_body, row_count, per_core),
        [sds((per_core, 2 * BLOCK, BLOCK), BF16) for _ in others],
        [*messages, *degree_terms],
        any_in=range(row_count - 1, 2 * row_count - 1),
    )
    shared = [shift_by(tile, "cols", core_count, 1) for tile in sent]

    tile_args = [near_tiles, home_tiles, self_tiles, *sent, *shared]
    block_shape = sds((own_cols, rows_here), F32)
    square = sds((2 * own_cols, 2 * own_cols), F32)
    folded_square = sds((own_cols, 4 * own_cols), F32)

    part, degree, inverse = call(
        functools.partial(first_apply_body, dims),
        [block_shape, table, table],
        [me, idx, *degree_terms, values, *tile_args, *messages],
        smem_in=(0, 1),
    )
    mine, other = pair_sum(part, ("tiles",))
    first = call(
        functools.partial(mapped_body, row_count, capacity, blocks_here),
        [block_shape] + [sds((picked, BLOCK), F32) for _ in others],
        [me, idx, inverse, mine, other],
        smem_in=(0, 1),
    )
    mapped, sends = first[0], first[1:]
    received = [shift_by(sends[k - 1], "rows", row_count, k) for k in others]

    mapped_other = shift_by(mapped, "cols", core_count, 1)
    first_gram = call(gram_body, folded_square, [me, mapped, mapped_other], smem_in=(0,))
    steps = (row_count - 1).bit_length()
    for bit in range(steps - 1):
        first_gram = first_gram + pair_step(first_gram, "rows", 1 << bit)
    part = call(
        functools.partial(second_apply_body, dims),
        block_shape,
        [me, idx, inverse, first_gram, mapped, *tile_args, *received],
        smem_in=(0, 1),
        any_in=(3,),
    )
    gram_terms = (first_gram, pair_step(first_gram, "rows", 1 << (steps - 1)))
    mine, other = pair_sum(part, ("tiles",))
    second = call(
        functools.partial(last_mapped_body, blocks_here),
        block_shape,
        [me, inverse, mine, other, gram_terms[1]],
        smem_in=(0,),
        any_in=(4,),
    )
    second_other = shift_by(second, "cols", core_count, 1)
    factor = call(factor_body, square, [second, *gram_terms], any_in=(0,))
    full, second_gram = call(
        second_gram_body,
        [sds((6 * own_cols, rows_here), BF16), folded_square],
        [me, factor, second, second_other],
        smem_in=(0,),
    )
    vectors = call(
        final_body, block_shape, [me, full, *row_terms(second_gram, row_count)], smem_in=(0,)
    )
    own_degree = lax.dynamic_slice_in_dim(degree, row_index * blocks_here, blocks_here, 0)
    return (vectors.T, own_degree.reshape(rows_here))


def solution(mesh):
    in_specs = (
        P(("groups", "rows"), "cols"),
        P(("groups", "rows"), "cols"),
        P(("groups", "rows", "tiles"), None, None),
        P(("groups", "rows", "tiles")),
    )
    out_specs = (P(("groups", "rows"), "cols"), P(("groups", "rows")))
    return jax.shard_map(local, mesh=mesh, in_specs=in_specs, out_specs=out_specs, check_vma=False)
```

```python
import functools

import jax
import jax.numpy as jnp
from jax import lax
from jax.experimental import pallas as pl
from jax.experimental.pallas import tpu as pltpu
from jax.sharding import PartitionSpec as P

BLOCK = 128
kernel_gamma = 14.0

VMEM = pl.BlockSpec(memory_space=pltpu.VMEM)
SMEM = pl.BlockSpec(memory_space=pltpu.SMEM)
ANY = pl.BlockSpec(memory_space=pl.ANY)
F32 = jnp.float32
BF16 = jnp.bfloat16
HIGHEST = lax.Precision.HIGHEST
NT = (((1,), (1,)), ((), ()))


def call(body, outs, args, smem_in=(), smem_out=(), any_in=()):
    single = not isinstance(outs, (list, tuple))
    shapes = [outs] if single else list(outs)
    result = pl.pallas_call(
        body,
        out_shape=shapes,
        in_specs=[
            SMEM if i in smem_in else ANY if i in any_in else VMEM for i in range(len(args))
        ],
        out_specs=[SMEM if i in smem_out else VMEM for i in range(len(shapes))],
        compiler_params=pltpu.CompilerParams(vmem_limit_bytes=48 * 2**20),
    )(*args)
    return result[0] if single else result


def sds(shape, dtype):
    return jax.ShapeDtypeStruct(shape, dtype)


def at_block(index):
    return pl.ds(pl.multiple_of(index * BLOCK, BLOCK), BLOCK)


def eye_mask(size):
    return lax.broadcasted_iota(jnp.int32, (size, size), 0) == lax.broadcasted_iota(
        jnp.int32, (size, size), 1
    )


def halves(value):
    high = value.astype(BF16)
    low = (value - high.astype(F32)).astype(BF16)
    return high, low


def pack(tile):
    return jnp.concatenate(halves(tile), axis=0)


def product(packed, values):
    left = jnp.concatenate(halves(values), axis=0)
    both = jnp.dot(jnp.concatenate([left, left], axis=1), packed, preferred_element_type=F32)
    count = values.shape[0]
    return both[:count] + both[count:]


def thirds(value):
    high = value.astype(BF16)
    rest = value - high.astype(F32)
    middle = rest.astype(BF16)
    low = (rest - middle.astype(F32)).astype(BF16)
    return jnp.concatenate([high, middle, low], axis=0)


def gram(parts):
    cross = lax.dot_general(parts, parts, NT, preferred_element_type=F32)
    n = parts.shape[0] // 3
    total = None
    for i, j in ((2, 2), (1, 2), (2, 1), (0, 2), (2, 0), (1, 1), (0, 1), (1, 0), (0, 0)):
        piece = cross[i * n : (i + 1) * n, j * n : (j + 1) * n]
        total = piece if total is None else total + piece
    return total


def times(left, parts):
    left = thirds(left)
    m = left.shape[0] // 3
    product3 = jnp.dot(
        jnp.concatenate([left, left, left], axis=1), parts, preferred_element_type=F32
    )
    return (product3[2 * m :] + product3[m : 2 * m]) + product3[:m]


def lower_inverse(matrix, step=8):
    n = matrix.shape[0]
    state = jnp.concatenate([matrix, eye_mask(n).astype(F32)], axis=1)
    done = []
    for j in range(0, n, step):
        top = j // 8 * 8
        if top > n - state.shape[0]:
            done.append(state[:8])
            state = state[8:]
        base = j - top
        rows = lax.broadcasted_iota(jnp.int32, state.shape, 0)
        columns = [jnp.broadcast_to(state[:, j + i : j + i + 1], state.shape) for i in range(step)]
        lines = [state[base + i : base + i + 1, :] for i in range(step)]
        pivot = [[columns[k][base + i : base + i + 1, :] for k in range(step)] for i in range(step)]
        for i in range(step):
            reciprocal = 1.0 / pivot[i][i]
            scaled = lines[i] * reciprocal
            ratio = [pivot[i][k] * reciprocal for k in range(step)]
            for k in range(i + 1, step):
                lines[k] = lines[k] - pivot[k][i] * scaled
                columns[k] = columns[k] - columns[i] * ratio[k]
                for m in range(i + 1, step):
                    pivot[k][m] = pivot[k][m] - pivot[k][i] * ratio[m]
            state = state - jnp.where(rows > base + i, columns[i], 0.0) * scaled
    state = jnp.concatenate([*done, state], axis=0)
    pivots = jnp.sum(jnp.where(eye_mask(n), state[:, :n], 0.0), axis=1, keepdims=True)
    return state[:, n:] / jnp.sqrt(pivots)


def both_columns(core, own, other):
    first = core == 0
    return jnp.concatenate(
        [jnp.where(first, own, other), jnp.where(first, other, own)], axis=0
    )


def plan_body(dims, me, *refs):
    row_count, capacity, slots, blocks_here = dims
    lists, (emb, after, idx) = refs[:row_count], refs[row_count : row_count + 3]
    sends = refs[row_count + 3 :]
    row = me[0]

    def clear(i, carry):
        for line in range(6):
            idx[line, i] = 0
        return carry

    lax.fori_loop(0, slots, clear, 0)

    def ranked(listed, want, write):
        count = listed[2, 0]

        def step(s, counts):
            near = listed[0, s]
            far = listed[1, s]
            return write(s, near, far, far // blocks_here, s < count, counts)

        lax.fori_loop(0, slots, step, (0,) * want)

    def write_own(s, near, far, owner, live, counts):
        shift = lax.rem(owner - row + row_count, row_count)
        rank = functools.reduce(
            lambda total, k: total + jnp.where(shift == k, counts[k], 0), range(row_count), 0
        )

        @pl.when(live)
        def _():
            slot = shift * capacity + rank
            idx[0, slot] = near - row * blocks_here
            idx[1, slot] = far
            idx[2, slot] = 1
            idx[3, slot] = s

        return tuple(
            counts[k] + (live & (shift == k)).astype(jnp.int32) for k in range(row_count)
        )

    for k in range(row_count):
        if k == 0:
            ranked(lists[k], row_count, write_own)

        def write_in(s, near, far, owner, live, counts, k=k):
            hit = live & (owner == row)

            @pl.when(hit)
            def _():
                slot = k * capacity + counts[0]
                idx[4, slot] = far - row * blocks_here
                idx[5, slot] = near

            return (counts[0] + hit.astype(jnp.int32),)

        ranked(lists[k], 1, write_in)
    for k in range(1, row_count):
        for j in range(capacity):
            sends[k - 1][j * BLOCK : (j + 1) * BLOCK, :] = emb[at_block(idx[4, k * capacity + j]), :]


def partial_distance(left, right):
    inner = lax.dot_general(left, right, NT, preferred_element_type=F32)
    left_sq = jnp.sum(jnp.square(left.astype(F32)), axis=1, keepdims=True)
    right_sq = jnp.sum(jnp.square(right.astype(F32)), axis=1, keepdims=True)
    right_row = jnp.sum(jnp.where(eye_mask(BLOCK), right_sq, 0.0), axis=0, keepdims=True)
    return left_sq + right_row - 2.0 * inner


def self_distance_body(own_blocks, tile_count, me, emb, out):
    for i in range(own_blocks):
        block = emb[at_block(i * tile_count + me[1]), :]
        out[i * BLOCK : (i + 1) * BLOCK, :] = partial_distance(block, block)


def pair_distance_body(row_count, capacity, idx, emb, *refs):
    out = refs[-1]
    for k in range(row_count):
        for j in range(capacity):
            slot = k * capacity + j
            left = emb[at_block(idx[0, slot]), :]
            if k == 0:
                right = emb[at_block(idx[4, j]), :]
            else:
                right = refs[k - 1][j * BLOCK : (j + 1) * BLOCK, :]
            out[slot * BLOCK : (slot + 1) * BLOCK, :] = partial_distance(left, right)


def self_tile_body(own_blocks, mine, other, packed, sums):
    for i in range(own_blocks):
        part = slice(i * BLOCK, (i + 1) * BLOCK)
        tile = jnp.exp(-kernel_gamma * (mine[part, :] + other[part, :] - 2.0))
        tile = jnp.where(eye_mask(BLOCK), 0.0, tile)
        packed[i] = pack(tile)
        sums[i : i + 1, :] = jnp.sum(tile, axis=0, keepdims=True)


def pair_tile_body(dims, me, idx, mine, other, self_sums, values, near_tiles, home_tiles, table, *sends):
    row_count, capacity, per_core, blocks_here, tile_count = dims
    row, tile_index, core = me[0], me[1], me[2]
    table[...] = jnp.zeros(table.shape, F32)
    for i in range(self_sums.shape[0]):
        table[pl.ds(row * blocks_here + i * tile_count + tile_index, 1), :] = self_sums[i : i + 1, :]

    def add(block, line):
        place = pl.ds(block, 1)
        table[place, :] = table[place, :] + line

    for k in range(row_count):
        for j in range(capacity):
            slot = k * capacity + j
            part = slice(slot * BLOCK, (slot + 1) * BLOCK)
            tile = jnp.exp(-kernel_gamma * (mine[part, :] + other[part, :] - 2.0))
            tile = jnp.where(idx[2, slot] > 0, tile, 0.0)
            turned = tile.T
            near_tiles[slot] = pack(turned)
            add(row * blocks_here + idx[0, slot], jnp.sum(turned, axis=0, keepdims=True))
            add(idx[1, slot], jnp.sum(tile, axis=0, keepdims=True))
            if k == 0:
                home_tiles[j] = pack(tile)
            else:

                @pl.when(core == j // per_core)
                def _():
                    inner = j % per_core
                    sends[k - 1][inner * BLOCK : (inner + 1) * BLOCK, :] = tile

    pick_columns(idx, row_count, capacity, values, sends, per_core * BLOCK)


def split_body(row_count, per_core, *refs):
    others = row_count - 1
    messages, outs = refs[:others], refs[-others:]
    for message, out in zip(messages, outs):
        for inner in range(per_core):
            out[inner] = pack(message[inner * BLOCK : (inner + 1) * BLOCK, :])


def pick_columns(idx, row_count, capacity, source, sends, base):
    count = source.shape[0]
    for k in range(1, row_count):
        back = row_count - k
        blocks = [idx[0, k * capacity + j] for j in range(capacity)]
        blocks += [idx[4, back * capacity + j] for j in range(capacity)]
        for place, block in enumerate(blocks):
            rows = slice(base + place * count, base + (place + 1) * count)
            sends[k - 1][rows, :] = source[:, at_block(block)]


def apply_tiles(dims, me, idx, inverse, own, received, base, near_tiles, home_tiles, sent, shared, self_tiles, out):
    row_count, capacity, per_core, blocks_here, tile_count = dims
    row, tile_index, core = me[0], me[1], me[2]
    count = out.shape[0]
    out[...] = jnp.zeros(out.shape, F32)

    def scaled(values, block):
        return values * inverse[pl.ds(block, 1), :]

    def add(block, packed, values):
        place = at_block(block)
        out[:, place] = out[:, place] + product(packed, values)

    def arrived(k, place):
        return received[k - 1][pl.ds(pl.multiple_of(base + place * count, 8), count), :]

    for i in range(blocks_here // tile_count):
        block = i * tile_count + tile_index
        add(block, self_tiles[i], scaled(own[:, at_block(block)], row * blocks_here + block))
    for k in range(row_count):
        for j in range(capacity):
            slot = k * capacity + j
            if k == 0:
                values = own[:, at_block(idx[4, j])]
            else:
                values = arrived(row_count - k, capacity + j)
            add(idx[0, slot], near_tiles[slot], scaled(values, idx[1, slot]))
    for k in range(row_count):
        for j in range(capacity):
            if k == 0:
                slot = j
                values = own[:, at_block(idx[0, j])]
                packed = home_tiles[j]
            else:
                inner = j % per_core
                if j < per_core:
                    place = core * per_core + inner
                    packed = sent[k - 1][inner]
                else:
                    place = (1 - core) * per_core + inner
                    packed = shared[k - 1][inner]
                slot = k * capacity + place
                values = arrived(k, place)
            add(idx[4, slot], packed, scaled(values, idx[5, slot]))


def first_apply_body(dims, me, idx, *refs):
    row_count, per_core = dims[0], dims[2]
    terms, refs = refs[:2], refs[2:]
    own, near_tiles, home_tiles, self_tiles = refs[:4]
    sent, shared = refs[4 : 3 + row_count], refs[3 + row_count : 2 + 2 * row_count]
    messages = refs[2 + 2 * row_count : -3]
    out, degree, inverse = refs[-3:]
    total = terms[0][...] + terms[1][...]
    degree[...] = total
    inverse[...] = 1.0 / jnp.sqrt(total)
    apply_tiles(
        dims, me, idx, inverse, own, messages, per_core * BLOCK, near_tiles, home_tiles, sent, shared, self_tiles, out
    )


def second_apply_body(dims, me, idx, inverse, after, *refs):
    row_count = dims[0]
    own, near_tiles, home_tiles, self_tiles = refs[:4]
    sent, shared = refs[4 : 3 + row_count], refs[3 + row_count : 2 + 2 * row_count]
    received, out = refs[2 + 2 * row_count : -1], refs[-1]
    apply_tiles(dims, me, idx, inverse, own, received, 0, near_tiles, home_tiles, sent, shared, self_tiles, out)


def scale_rows(me, blocks_here, inverse, mine, other, out):
    for b in range(blocks_here):
        part = slice(b * BLOCK, (b + 1) * BLOCK)
        row = inverse[pl.ds(me[0] * blocks_here + b, 1), :]
        out[:, part] = (mine[:, part] + other[:, part]) * row


def mapped_body(row_count, capacity, blocks_here, me, idx, inverse, mine, other, out, *sends):
    scale_rows(me, blocks_here, inverse, mine, other, out)
    pick_columns(idx, row_count, capacity, out, sends, 0)


def last_mapped_body(blocks_here, me, inverse, mine, other, *refs):
    scale_rows(me, blocks_here, inverse, mine, other, refs[-1])


def folded(square):
    half = square.shape[0] // 2
    return jnp.concatenate([square[:half], square[half:]], axis=1)


def unfolded(terms):
    total = functools.reduce(lambda total, term: total + term[...], terms[1:], terms[0][...])
    width = total.shape[1] // 2
    return jnp.concatenate([total[:, :width], total[:, width:]], axis=0)


def gram_body(me, own, other, out):
    out[...] = folded(gram(thirds(both_columns(me[2], own[...], other[...]))))


def factor_body(after, *refs):
    refs[-1][...] = lower_inverse(unfolded(refs[:-1]))


def second_gram_body(me, factor, own, other, mapped, out):
    full = both_columns(me[2], own[...], other[...])
    parts = thirds(times(factor[...], thirds(full)))
    mapped[...] = parts[: mapped.shape[0]]
    out[...] = folded(gram(parts))


def final_body(me, mapped, *refs):
    out = refs[-1]
    factor = lower_inverse(unfolded(refs[:-1]))
    own_cols = out.shape[0]
    part = jnp.where(me[2] == 0, factor[:own_cols], factor[own_cols:])
    left = jnp.concatenate(halves(part), axis=0)
    both = jnp.dot(
        jnp.concatenate([left, left], axis=1), mapped[...], preferred_element_type=F32
    )
    out[...] = both[own_cols:] + both[:own_cols]


def shift_by(value, axes, size, shift):
    return lax.ppermute(value, axes, [(i, (i + shift) % size) for i in range(size)])


def row_terms(value, row_count):
    return [value] + [shift_by(value, "rows", row_count, k) for k in range(1, row_count)]


def pair_step(value, name, flip):
    return lax.ppermute(value, name, [(i, i ^ flip) for i in range(lax.axis_size(name))])


def pair_sum(value, axes):
    terms = None
    steps = [(name, 1 << bit) for name in axes for bit in range((lax.axis_size(name) - 1).bit_length())]
    for name, flip in steps:
        if terms is not None:
            value = terms[0] + terms[1]
        terms = (value, pair_step(value, name, flip))
    return terms


def local(embeddings, start, pair_list, pair_count):
    row_count = lax.axis_size("rows")
    tile_count = lax.axis_size("tiles")
    core_count = lax.axis_size("cols")
    row_index = lax.axis_index("rows")
    tile_index = lax.axis_index("tiles")
    col_index = lax.axis_index("cols")
    me = jnp.stack([row_index, tile_index, col_index]).astype(jnp.int32)
    rows_here, half_features = embeddings.shape
    blocks_here = rows_here // BLOCK
    slots = pair_list.shape[2]
    capacity = slots // row_count
    per_core = capacity // core_count
    own_blocks = blocks_here // tile_count
    own_cols = start.shape[1]
    block_count = row_count * blocks_here
    others = range(1, row_count)

    own_list = jnp.concatenate(
        [pair_list[0], jnp.broadcast_to(pair_count[:, None], (1, slots))], axis=0
    )
    lists = row_terms(own_list, row_count)
    self_part = call(
        functools.partial(self_distance_body, own_blocks, tile_count),
        sds((own_blocks * BLOCK, BLOCK), F32),
        [me, embeddings],
        smem_in=(0,),
    )
    planned = call(
        functools.partial(plan_body, (row_count, capacity, slots, blocks_here)),
        [sds((6, slots), jnp.int32)] + [sds((capacity * BLOCK, half_features), BF16) for _ in others],
        [me, *lists, embeddings, self_part],
        smem_in=range(1 + row_count),
        any_in=(row_count + 2,),
        smem_out=(0,),
    )
    idx, sends = planned[0], planned[1:]
    far = [shift_by(sends[k - 1], "rows", row_count, -k) for k in others]

    self_other = shift_by(self_part, "cols", core_count, 1)
    self_tiles, self_sums = call(
        functools.partial(self_tile_body, own_blocks),
        [sds((own_blocks, 2 * BLOCK, BLOCK), BF16), sds((own_blocks, BLOCK), F32)],
        [self_part, self_other],
    )
    pair_part = call(
        functools.partial(pair_distance_body, row_count, capacity),
        sds((slots * BLOCK, BLOCK), F32),
        [idx, embeddings, *far],
        smem_in=(0,),
    )
    pair_other = shift_by(pair_part, "cols", core_count, 1)

    values = start.T
    dims = (row_count, capacity, per_core, blocks_here, tile_count)
    table = sds((block_count, BLOCK), F32)
    picked = 2 * capacity * own_cols
    tiles = call(
        functools.partial(pair_tile_body, dims),
        [sds((slots, 2 * BLOCK, BLOCK), BF16), sds((capacity, 2 * BLOCK, BLOCK), BF16), table]
        + [sds((per_core * BLOCK + picked, BLOCK), F32) for _ in others],
        [me, idx, pair_part, pair_other, self_sums, values],
        smem_in=(0, 1),
    )
    near_tiles, home_tiles, degrees, sends = tiles[0], tiles[1], tiles[2], tiles[3:]
    degrees = functools.reduce(jnp.add, row_terms(degrees, row_count))
    degree_terms = pair_sum(degrees, ("tiles",))
    messages = [shift_by(sends[k - 1], "rows", row_count, k) for k in others]
    sent = call(
        functools.partial(split_body, row_count, per_core),
        [sds((per_core, 2 * BLOCK, BLOCK), BF16) for _ in others],
        [*messages, *degree_terms],
        any_in=(row_count - 1, row_count),
    )
    shared = [shift_by(tile, "cols", core_count, 1) for tile in sent]

    tile_args = [near_tiles, home_tiles, self_tiles, *sent, *shared]
    block_shape = sds((own_cols, rows_here), F32)
    square = sds((2 * own_cols, 2 * own_cols), F32)
    folded_square = sds((own_cols, 4 * own_cols), F32)

    part, degree, inverse = call(
        functools.partial(first_apply_body, dims),
        [block_shape, table, table],
        [me, idx, *degree_terms, values, *tile_args, *messages],
        smem_in=(0, 1),
    )
    mine, other = pair_sum(part, ("tiles",))
    first = call(
        functools.partial(mapped_body, row_count, capacity, blocks_here),
        [block_shape] + [sds((picked, BLOCK), F32) for _ in others],
        [me, idx, inverse, mine, other],
        smem_in=(0, 1),
    )
    mapped, sends = first[0], first[1:]
    received = [shift_by(sends[k - 1], "rows", row_count, k) for k in others]

    mapped_other = shift_by(mapped, "cols", core_count, 1)
    first_gram = call(gram_body, folded_square, [me, mapped, mapped_other], smem_in=(0,))
    steps = (row_count - 1).bit_length()
    for bit in range(steps - 1):
        first_gram = first_gram + pair_step(first_gram, "rows", 1 << bit)
    part = call(
        functools.partial(second_apply_body, dims),
        block_shape,
        [me, idx, inverse, first_gram, mapped, *tile_args, *received],
        smem_in=(0, 1),
        any_in=(3,),
    )
    gram_terms = (first_gram, pair_step(first_gram, "rows", 1 << (steps - 1)))
    mine, other = pair_sum(part, ("tiles",))
    second = call(
        functools.partial(last_mapped_body, blocks_here),
        block_shape,
        [me, inverse, mine, other, gram_terms[1]],
        smem_in=(0,),
        any_in=(4,),
    )
    second_other = shift_by(second, "cols", core_count, 1)
    factor = call(factor_body, square, [second, *gram_terms], any_in=(0,))
    full, second_gram = call(
        second_gram_body,
        [sds((4 * own_cols, rows_here), BF16), folded_square],
        [me, factor, second, second_other],
        smem_in=(0,),
    )
    vectors = call(
        final_body, block_shape, [me, full, *row_terms(second_gram, row_count)], smem_in=(0,)
    )
    own_degree = lax.dynamic_slice_in_dim(degree, row_index * blocks_here, blocks_here, 0)
    return (vectors.T, own_degree.reshape(rows_here))


def solution(mesh):
    in_specs = (
        P(("groups", "rows"), "cols"),
        P(("groups", "rows"), "cols"),
        P(("groups", "rows", "tiles"), None, None),
        P(("groups", "rows", "tiles")),
    )
    out_specs = (P(("groups", "rows"), "cols"), P(("groups", "rows")))
    return jax.shard_map(local, mesh=mesh, in_specs=in_specs, out_specs=out_specs, check_vma=False)
```

```python
import functools

import jax
import jax.numpy as jnp
from jax import lax
from jax.experimental import pallas as pl
from jax.experimental.pallas import tpu as pltpu
from jax.sharding import PartitionSpec as P

BLOCK = 128
kernel_gamma = 14.0
CODE_TOP = 32767.0
CODE_ROWS = 16

VMEM = pl.BlockSpec(memory_space=pltpu.VMEM)
SMEM = pl.BlockSpec(memory_space=pltpu.SMEM)
ANY = pl.BlockSpec(memory_space=pl.ANY)
F32 = jnp.float32
BF16 = jnp.bfloat16
HIGHEST = lax.Precision.HIGHEST
NT = (((1,), (1,)), ((), ()))


def call(body, outs, args, smem_in=(), smem_out=(), any_in=(), scratch=()):
    single = not isinstance(outs, (list, tuple))
    shapes = [outs] if single else list(outs)
    result = pl.pallas_call(
        body,
        out_shape=shapes,
        in_specs=[
            SMEM if i in smem_in else ANY if i in any_in else VMEM for i in range(len(args))
        ],
        out_specs=[SMEM if i in smem_out else VMEM for i in range(len(shapes))],
        scratch_shapes=list(scratch),
        compiler_params=pltpu.CompilerParams(vmem_limit_bytes=48 * 2**20),
    )(*args)
    return result[0] if single else result


def sds(shape, dtype):
    return jax.ShapeDtypeStruct(shape, dtype)


def at_block(index):
    return pl.ds(pl.multiple_of(index * BLOCK, BLOCK), BLOCK)


def eye_mask(size):
    return lax.broadcasted_iota(jnp.int32, (size, size), 0) == lax.broadcasted_iota(
        jnp.int32, (size, size), 1
    )


def halves(value):
    high = value.astype(BF16)
    low = (value - high.astype(F32)).astype(BF16)
    return high, low


def pack(tile):
    return jnp.concatenate(halves(tile), axis=0)


def encode(values):
    most = jnp.max(jnp.abs(values), axis=0, keepdims=True)
    power = jnp.floor(jnp.log2(jnp.maximum(most, 1e-30))) + 1.0
    steps = jnp.floor(values * (CODE_TOP * jnp.exp2(-power)) + 0.5)
    steps = jnp.minimum(jnp.maximum(steps, -CODE_TOP), CODE_TOP)
    return steps.astype(jnp.int32).astype(jnp.int16), power


def decode(steps, power):
    return steps.astype(jnp.int32).astype(F32) * (jnp.exp2(power) * (1.0 / CODE_TOP))


def as_rows(powers, count):
    rows = jnp.concatenate([*powers, jnp.zeros((count - len(powers), BLOCK), F32)], axis=0)
    return rows.astype(jnp.int32).astype(jnp.int16)


def power_rows(rows):
    return rows.astype(jnp.int32).astype(F32)


def row_at(rows, place):
    if isinstance(place, int):
        return rows[place : place + 1, :]
    line = rows[:1, :]
    for i in range(1, rows.shape[0]):
        line = jnp.where(place == i, rows[i : i + 1, :], line)
    return line


def product(packed, values):
    left = jnp.concatenate(halves(values), axis=0)
    both = jnp.dot(jnp.concatenate([left, left], axis=1), packed, preferred_element_type=F32)
    count = values.shape[0]
    return both[:count] + both[count:]


def thirds(value):
    high = value.astype(BF16)
    rest = value - high.astype(F32)
    middle = rest.astype(BF16)
    low = (rest - middle.astype(F32)).astype(BF16)
    return jnp.concatenate([high, middle, low], axis=0)


def gram(parts):
    cross = lax.dot_general(parts, parts, NT, preferred_element_type=F32)
    n = parts.shape[0] // 3
    total = None
    for i, j in ((2, 2), (1, 2), (2, 1), (0, 2), (2, 0), (1, 1), (0, 1), (1, 0), (0, 0)):
        piece = cross[i * n : (i + 1) * n, j * n : (j + 1) * n]
        total = piece if total is None else total + piece
    return total


def times(left, parts):
    left = thirds(left)
    m = left.shape[0] // 3
    product3 = jnp.dot(
        jnp.concatenate([left, left, left], axis=1), parts, preferred_element_type=F32
    )
    return (product3[2 * m :] + product3[m : 2 * m]) + product3[:m]


def lower_inverse(matrix, step=8):
    n = matrix.shape[0]
    state = jnp.concatenate([matrix, eye_mask(n).astype(F32)], axis=1)
    done = []
    for j in range(0, n, step):
        top = j // 8 * 8
        if top > n - state.shape[0]:
            done.append(state[:8])
            state = state[8:]
        base = j - top
        rows = lax.broadcasted_iota(jnp.int32, state.shape, 0)
        columns = [jnp.broadcast_to(state[:, j + i : j + i + 1], state.shape) for i in range(step)]
        lines = [state[base + i : base + i + 1, :] for i in range(step)]
        pivot = [[columns[k][base + i : base + i + 1, :] for k in range(step)] for i in range(step)]
        for i in range(step):
            reciprocal = 1.0 / pivot[i][i]
            scaled = lines[i] * reciprocal
            ratio = [pivot[i][k] * reciprocal for k in range(step)]
            for k in range(i + 1, step):
                lines[k] = lines[k] - pivot[k][i] * scaled
                columns[k] = columns[k] - columns[i] * ratio[k]
                for m in range(i + 1, step):
                    pivot[k][m] = pivot[k][m] - pivot[k][i] * ratio[m]
            state = state - jnp.where(rows > base + i, columns[i], 0.0) * scaled
    state = jnp.concatenate([*done, state], axis=0)
    pivots = jnp.sum(jnp.where(eye_mask(n), state[:, :n], 0.0), axis=1, keepdims=True)
    return state[:, n:] / jnp.sqrt(pivots)


def both_columns(core, own, other):
    first = core == 0
    return jnp.concatenate(
        [jnp.where(first, own, other), jnp.where(first, other, own)], axis=0
    )


def plan_body(dims, me, *refs):
    row_count, capacity, slots, blocks_here = dims
    lists, (emb, after, idx) = refs[:row_count], refs[row_count : row_count + 3]
    sends = refs[row_count + 3 :]
    row = me[0]

    def clear(i, carry):
        for line in range(6):
            idx[line, i] = 0
        return carry

    lax.fori_loop(0, slots, clear, 0)

    def ranked(listed, want, write):
        count = listed[2, 0]

        def step(s, counts):
            near = listed[0, s]
            far = listed[1, s]
            return write(s, near, far, far // blocks_here, s < count, counts)

        lax.fori_loop(0, slots, step, (0,) * want)

    def write_own(s, near, far, owner, live, counts):
        shift = lax.rem(owner - row + row_count, row_count)
        rank = functools.reduce(
            lambda total, k: total + jnp.where(shift == k, counts[k], 0), range(row_count), 0
        )

        @pl.when(live)
        def _():
            slot = shift * capacity + rank
            idx[0, slot] = near - row * blocks_here
            idx[1, slot] = far
            idx[2, slot] = 1
            idx[3, slot] = s

        return tuple(
            counts[k] + (live & (shift == k)).astype(jnp.int32) for k in range(row_count)
        )

    for k in range(row_count):
        if k == 0:
            ranked(lists[k], row_count, write_own)

        def write_in(s, near, far, owner, live, counts, k=k):
            hit = live & (owner == row)

            @pl.when(hit)
            def _():
                slot = k * capacity + counts[0]
                idx[4, slot] = far - row * blocks_here
                idx[5, slot] = near

            return (counts[0] + hit.astype(jnp.int32),)

        ranked(lists[k], 1, write_in)
    for k in range(1, row_count):
        for j in range(capacity):
            sends[k - 1][j * BLOCK : (j + 1) * BLOCK, :] = emb[at_block(idx[4, k * capacity + j]), :]


def partial_distance(left, right):
    inner = lax.dot_general(left, right, NT, preferred_element_type=F32)
    left_sq = jnp.sum(jnp.square(left.astype(F32)), axis=1, keepdims=True)
    right_sq = jnp.sum(jnp.square(right.astype(F32)), axis=1, keepdims=True)
    right_row = jnp.sum(jnp.where(eye_mask(BLOCK), right_sq, 0.0), axis=0, keepdims=True)
    return left_sq + right_row - 2.0 * inner


def self_distance_body(own_blocks, tile_count, me, emb, out):
    for i in range(own_blocks):
        block = emb[at_block(i * tile_count + me[1]), :]
        out[i * BLOCK : (i + 1) * BLOCK, :] = partial_distance(block, block)


def pair_distance_body(row_count, capacity, idx, emb, *refs):
    out = refs[-1]
    for k in range(row_count):
        for j in range(capacity):
            slot = k * capacity + j
            left = emb[at_block(idx[0, slot]), :]
            if k == 0:
                right = emb[at_block(idx[4, j]), :]
            else:
                right = refs[k - 1][j * BLOCK : (j + 1) * BLOCK, :]
            out[slot * BLOCK : (slot + 1) * BLOCK, :] = partial_distance(left, right)


def self_tile_body(own_blocks, mine, other, packed, sums):
    for i in range(own_blocks):
        part = slice(i * BLOCK, (i + 1) * BLOCK)
        tile = jnp.exp(-kernel_gamma * (mine[part, :] + other[part, :] - 2.0))
        tile = jnp.where(eye_mask(BLOCK), 0.0, tile)
        packed[i] = pack(tile)
        sums[i : i + 1, :] = jnp.sum(tile, axis=0, keepdims=True)


def pair_tile_body(dims, me, idx, mine, other, self_sums, values, near_tiles, home_tiles, table, *refs):
    sends, (codes, powers) = refs[:-2], refs[-2:]
    row_count, capacity, per_core, blocks_here, tile_count = dims
    row, tile_index, core = me[0], me[1], me[2]
    table[...] = jnp.zeros(table.shape, F32)
    for i in range(self_sums.shape[0]):
        table[pl.ds(row * blocks_here + i * tile_count + tile_index, 1), :] = self_sums[i : i + 1, :]

    def add(block, line):
        place = pl.ds(block, 1)
        table[place, :] = table[place, :] + line

    encode_blocks(values, codes, powers)
    for k in range(row_count):
        tiles = []
        for j in range(capacity):
            slot = k * capacity + j
            part = slice(slot * BLOCK, (slot + 1) * BLOCK)
            tile = jnp.exp(-kernel_gamma * (mine[part, :] + other[part, :] - 2.0))
            tile = jnp.where(idx[2, slot] > 0, tile, 0.0)
            turned = tile.T
            near_tiles[slot] = pack(turned)
            add(row * blocks_here + idx[0, slot], jnp.sum(turned, axis=0, keepdims=True))
            add(idx[1, slot], jnp.sum(tile, axis=0, keepdims=True))
            if k == 0:
                home_tiles[j] = pack(tile)
            tiles.append(tile)
        if k > 0:
            lines = []
            for inner in range(per_core):
                tile = jnp.where(core == 0, tiles[inner], tiles[per_core + inner])
                steps, power = encode(tile)
                sends[k - 1][inner * BLOCK : (inner + 1) * BLOCK, :] = steps
                lines.append(power)
            pick_columns(idx, k, row_count, capacity, codes, powers, sends[k - 1], per_core * BLOCK, lines)


def encode_blocks(values, codes, powers):
    for b in range(powers.shape[0]):
        part = slice(b * BLOCK, (b + 1) * BLOCK)
        steps, power = encode(values[:, part])
        codes[:, part] = steps
        powers[b : b + 1, :] = power


def split_body(row_count, per_core, *refs):
    others = row_count - 1
    messages, outs = refs[:others], refs[-others:]
    for message, out in zip(messages, outs):
        powers = power_rows(message[message.shape[0] - CODE_ROWS :, :])
        for inner in range(per_core):
            steps = message[inner * BLOCK : (inner + 1) * BLOCK, :]
            out[inner] = pack(decode(steps, powers[inner : inner + 1, :]))


def pick_columns(idx, k, row_count, capacity, codes, powers, send, base, lines):
    count = codes.shape[0]
    back = row_count - k
    blocks = [idx[0, k * capacity + j] for j in range(capacity)]
    blocks += [idx[4, back * capacity + j] for j in range(capacity)]
    for place, block in enumerate(blocks):
        send[base + place * count : base + (place + 1) * count, :] = codes[:, at_block(block)]
        lines.append(powers[pl.ds(block, 1), :])
    send[base + len(blocks) * count :, :] = as_rows(lines, CODE_ROWS)


def apply_tiles(dims, me, idx, inverse, own, received, base, near_tiles, home_tiles, sent, shared, self_tiles, out):
    row_count, capacity, per_core, blocks_here, tile_count = dims
    row, tile_index, core = me[0], me[1], me[2]
    count = out.shape[0]
    out[...] = jnp.zeros(out.shape, F32)

    def scaled(values, block):
        return values * inverse[pl.ds(block, 1), :]

    def add(block, packed, values):
        place = at_block(block)
        out[:, place] = out[:, place] + product(packed, values)

    lines = [power_rows(message[message.shape[0] - CODE_ROWS :, :]) for message in received]
    first_line = base // BLOCK

    def arrived(k, place):
        steps = received[k - 1][pl.ds(pl.multiple_of(base + place * count, CODE_ROWS), count), :]
        rows = lines[k - 1][first_line : first_line + 2 * capacity, :]
        return decode(steps, row_at(rows, place))

    for i in range(blocks_here // tile_count):
        block = i * tile_count + tile_index
        add(block, self_tiles[i], scaled(own[:, at_block(block)], row * blocks_here + block))
    for k in range(row_count):
        for j in range(capacity):
            slot = k * capacity + j
            if k == 0:
                values = own[:, at_block(idx[4, j])]
            else:
                values = arrived(row_count - k, capacity + j)
            add(idx[0, slot], near_tiles[slot], scaled(values, idx[1, slot]))
    for k in range(row_count):
        for j in range(capacity):
            if k == 0:
                slot = j
                values = own[:, at_block(idx[0, j])]
                packed = home_tiles[j]
            else:
                inner = j % per_core
                if j < per_core:
                    place = core * per_core + inner
                    packed = sent[k - 1][inner]
                else:
                    place = (1 - core) * per_core + inner
                    packed = shared[k - 1][inner]
                slot = k * capacity + place
                values = arrived(k, place)
            add(idx[4, slot], packed, scaled(values, idx[5, slot]))


def first_apply_body(dims, coded, me, idx, *refs):
    row_count, per_core = dims[0], dims[2]
    terms, refs = refs[:2], refs[2:]
    own, near_tiles, home_tiles, self_tiles = refs[:4]
    sent, shared = refs[4 : 3 + row_count], refs[3 + row_count : 2 + 2 * row_count]
    messages = refs[2 + 2 * row_count : -4]
    out, degree, inverse, total_out = refs[-4:]
    total = terms[0][...] + terms[1][...]
    degree[...] = total
    inverse[...] = 1.0 / jnp.sqrt(total)
    apply_tiles(
        dims, me, idx, inverse, own, messages, per_core * BLOCK, near_tiles, home_tiles, sent, shared, self_tiles, total_out
    )
    if not coded:
        out[...] = total_out[...]
        return
    lines = []
    blocks_here = dims[3]
    for b in range(blocks_here):
        part = slice(b * BLOCK, (b + 1) * BLOCK)
        steps, power = encode(total_out[:, part])
        out[:, part] = steps
        lines.append(power)
    out[:, blocks_here * BLOCK :] = as_rows(lines, out.shape[0])


def second_apply_body(dims, me, idx, inverse, after, *refs):
    row_count = dims[0]
    own, near_tiles, home_tiles, self_tiles = refs[:4]
    sent, shared = refs[4 : 3 + row_count], refs[3 + row_count : 2 + 2 * row_count]
    received, out = refs[2 + 2 * row_count : -1], refs[-1]
    apply_tiles(dims, me, idx, inverse, own, received, 0, near_tiles, home_tiles, sent, shared, self_tiles, out)


def mapped_body(dims, coded, me, idx, inverse, mine, other, out, *refs):
    row_count, capacity, per_core, blocks_here, tile_count = dims
    sends, (codes, powers) = refs[:-2], refs[-2:]
    if coded:
        tail = blocks_here * BLOCK
        my_powers, other_powers = power_rows(mine[:, tail:]), power_rows(other[:, tail:])
    for b in range(blocks_here):
        part = slice(b * BLOCK, (b + 1) * BLOCK)
        row = inverse[pl.ds(me[0] * blocks_here + b, 1), :]
        if coded:
            line = slice(b, b + 1)
            value = decode(mine[:, part], my_powers[line]) + decode(other[:, part], other_powers[line])
        else:
            value = mine[:, part] + other[:, part]
        out[:, part] = value * row
    encode_blocks(out, codes, powers)
    for k in range(1, row_count):
        pick_columns(idx, k, row_count, capacity, codes, powers, sends[k - 1], 0, [])


def last_mapped_body(blocks_here, me, inverse, mine, other, after, out):
    for b in range(blocks_here):
        part = slice(b * BLOCK, (b + 1) * BLOCK)
        row = inverse[pl.ds(me[0] * blocks_here + b, 1), :]
        out[:, part] = (mine[:, part] + other[:, part]) * row


def folded(square):
    half = square.shape[0] // 2
    return jnp.concatenate([square[:half], square[half:]], axis=1)


def unfolded(terms):
    total = functools.reduce(lambda total, term: total + term[...], terms[1:], terms[0][...])
    width = total.shape[1] // 2
    return jnp.concatenate([total[:, :width], total[:, width:]], axis=0)


def gram_body(me, own, other, out):
    out[...] = folded(gram(thirds(both_columns(me[2], own[...], other[...]))))


def factor_body(after, *refs):
    refs[-1][...] = lower_inverse(unfolded(refs[:-1]))


def second_gram_body(me, factor, own, other, mapped, out):
    full = both_columns(me[2], own[...], other[...])
    parts = thirds(times(factor[...], thirds(full)))
    mapped[...] = parts[: mapped.shape[0]]
    out[...] = folded(gram(parts))


def final_body(me, mapped, *refs):
    out = refs[-1]
    factor = lower_inverse(unfolded(refs[:-1]))
    own_cols = out.shape[0]
    part = jnp.where(me[2] == 0, factor[:own_cols], factor[own_cols:])
    left = jnp.concatenate(halves(part), axis=0)
    both = jnp.dot(
        jnp.concatenate([left, left], axis=1), mapped[...], preferred_element_type=F32
    )
    out[...] = both[own_cols:] + both[:own_cols]


def shift_by(value, axes, size, shift):
    return lax.ppermute(value, axes, [(i, (i + shift) % size) for i in range(size)])


def row_terms(value, row_count):
    return [value] + [shift_by(value, "rows", row_count, k) for k in range(1, row_count)]


def pair_step(value, name, flip):
    return lax.ppermute(value, name, [(i, i ^ flip) for i in range(lax.axis_size(name))])


def pair_sum(value, axes):
    terms = None
    steps = [(name, 1 << bit) for name in axes for bit in range((lax.axis_size(name) - 1).bit_length())]
    for name, flip in steps:
        if terms is not None:
            value = terms[0] + terms[1]
        terms = (value, pair_step(value, name, flip))
    return terms


def local(embeddings, start, pair_list, pair_count):
    row_count = lax.axis_size("rows")
    tile_count = lax.axis_size("tiles")
    core_count = lax.axis_size("cols")
    row_index = lax.axis_index("rows")
    tile_index = lax.axis_index("tiles")
    col_index = lax.axis_index("cols")
    me = jnp.stack([row_index, tile_index, col_index]).astype(jnp.int32)
    rows_here, half_features = embeddings.shape
    blocks_here = rows_here // BLOCK
    slots = pair_list.shape[2]
    capacity = slots // row_count
    per_core = capacity // core_count
    own_blocks = blocks_here // tile_count
    own_cols = start.shape[1]
    block_count = row_count * blocks_here
    others = range(1, row_count)

    own_list = jnp.concatenate(
        [pair_list[0], jnp.broadcast_to(pair_count[:, None], (1, slots))], axis=0
    )
    lists = row_terms(own_list, row_count)
    self_part = call(
        functools.partial(self_distance_body, own_blocks, tile_count),
        sds((own_blocks * BLOCK, BLOCK), F32),
        [me, embeddings],
        smem_in=(0,),
    )
    planned = call(
        functools.partial(plan_body, (row_count, capacity, slots, blocks_here)),
        [sds((6, slots), jnp.int32)] + [sds((capacity * BLOCK, half_features), BF16) for _ in others],
        [me, *lists, embeddings, self_part],
        smem_in=range(1 + row_count),
        any_in=(row_count + 2,),
        smem_out=(0,),
    )
    idx, sends = planned[0], planned[1:]
    far = [shift_by(sends[k - 1], "rows", row_count, -k) for k in others]

    self_other = shift_by(self_part, "cols", core_count, 1)
    self_tiles, self_sums = call(
        functools.partial(self_tile_body, own_blocks),
        [sds((own_blocks, 2 * BLOCK, BLOCK), BF16), sds((own_blocks, BLOCK), F32)],
        [self_part, self_other],
    )
    pair_part = call(
        functools.partial(pair_distance_body, row_count, capacity),
        sds((slots * BLOCK, BLOCK), F32),
        [idx, embeddings, *far],
        smem_in=(0,),
    )
    pair_other = shift_by(pair_part, "cols", core_count, 1)

    values = start.T
    dims = (row_count, capacity, per_core, blocks_here, tile_count)
    table = sds((block_count, BLOCK), F32)
    picked = 2 * capacity * own_cols
    code_scratch = [pltpu.VMEM((own_cols, rows_here), jnp.int16), pltpu.VMEM((blocks_here, BLOCK), F32)]
    coded = tile_count == 2
    tiles = call(
        functools.partial(pair_tile_body, dims),
        [sds((slots, 2 * BLOCK, BLOCK), BF16), sds((capacity, 2 * BLOCK, BLOCK), BF16), table]
        + [sds((per_core * BLOCK + picked + CODE_ROWS, BLOCK), jnp.int16) for _ in others],
        [me, idx, pair_part, pair_other, self_sums, values],
        smem_in=(0, 1),
        scratch=code_scratch,
    )
    near_tiles, home_tiles, degrees, sends = tiles[0], tiles[1], tiles[2], tiles[3:]
    degrees = functools.reduce(jnp.add, row_terms(degrees, row_count))
    degree_terms = pair_sum(degrees, ("tiles",))
    messages = [shift_by(sends[k - 1], "rows", row_count, k) for k in others]
    sent = call(
        functools.partial(split_body, row_count, per_core),
        [sds((per_core, 2 * BLOCK, BLOCK), BF16) for _ in others],
        [*messages, *degree_terms],
        any_in=(row_count - 1, row_count),
    )
    shared = [shift_by(tile, "cols", core_count, 1) for tile in sent]

    tile_args = [near_tiles, home_tiles, self_tiles, *sent, *shared]
    block_shape = sds((own_cols, rows_here), F32)
    square = sds((2 * own_cols, 2 * own_cols), F32)
    folded_square = sds((own_cols, 4 * own_cols), F32)

    part, degree, inverse = call(
        functools.partial(first_apply_body, dims, coded),
        [sds((own_cols, rows_here + BLOCK), jnp.int16) if coded else block_shape, table, table],
        [me, idx, *degree_terms, values, *tile_args, *messages],
        smem_in=(0, 1),
        scratch=[pltpu.VMEM((own_cols, rows_here), F32)],
    )
    mine, other = pair_sum(part, ("tiles",))
    first = call(
        functools.partial(mapped_body, dims, coded),
        [block_shape] + [sds((picked + CODE_ROWS, BLOCK), jnp.int16) for _ in others],
        [me, idx, inverse, mine, other],
        smem_in=(0, 1),
        scratch=code_scratch,
    )
    mapped, sends = first[0], first[1:]
    received = [shift_by(sends[k - 1], "rows", row_count, k) for k in others]

    mapped_other = shift_by(mapped, "cols", core_count, 1)
    first_gram = call(gram_body, folded_square, [me, mapped, mapped_other], smem_in=(0,))
    steps = (row_count - 1).bit_length()
    for bit in range(steps - 1):
        first_gram = first_gram + pair_step(first_gram, "rows", 1 << bit)
    part = call(
        functools.partial(second_apply_body, dims),
        block_shape,
        [me, idx, inverse, first_gram, mapped, *tile_args, *received],
        smem_in=(0, 1),
        any_in=(3,),
    )
    gram_terms = (first_gram, pair_step(first_gram, "rows", 1 << (steps - 1)))
    mine, other = pair_sum(part, ("tiles",))
    second = call(
        functools.partial(last_mapped_body, blocks_here),
        block_shape,
        [me, inverse, mine, other, gram_terms[1]],
        smem_in=(0,),
        any_in=(4,),
    )
    second_other = shift_by(second, "cols", core_count, 1)
    factor = call(factor_body, square, [second, *gram_terms], any_in=(0,))
    full, second_gram = call(
        second_gram_body,
        [sds((4 * own_cols, rows_here), BF16), folded_square],
        [me, factor, second, second_other],
        smem_in=(0,),
    )
    vectors = call(
        final_body, block_shape, [me, full, *row_terms(second_gram, row_count)], smem_in=(0,)
    )
    own_degree = lax.dynamic_slice_in_dim(degree, row_index * blocks_here, blocks_here, 0)
    return (vectors.T, own_degree.reshape(rows_here))


def solution(mesh):
    in_specs = (
        P(("groups", "rows"), "cols"),
        P(("groups", "rows"), "cols"),
        P(("groups", "rows", "tiles"), None, None),
        P(("groups", "rows", "tiles")),
    )
    out_specs = (P(("groups", "rows"), "cols"), P(("groups", "rows")))
    return jax.shard_map(local, mesh=mesh, in_specs=in_specs, out_specs=out_specs, check_vma=False)
```

```python
import functools

import jax
import jax.numpy as jnp
from jax import lax
from jax.experimental import pallas as pl
from jax.experimental.pallas import tpu as pltpu
from jax.sharding import PartitionSpec as P

BLOCK = 128
kernel_gamma = 14.0
CODE_TOP = 32767.0
PART_TOP = 16384.0
CODE_ROWS = 16

VMEM = pl.BlockSpec(memory_space=pltpu.VMEM)
SMEM = pl.BlockSpec(memory_space=pltpu.SMEM)
ANY = pl.BlockSpec(memory_space=pl.ANY)
F32 = jnp.float32
BF16 = jnp.bfloat16
HIGHEST = lax.Precision.HIGHEST
NT = (((1,), (1,)), ((), ()))


def call(body, outs, args, smem_in=(), smem_out=(), any_in=(), scratch=(), cost=0):
    single = not isinstance(outs, (list, tuple))
    shapes = [outs] if single else list(outs)
    result = pl.pallas_call(
        body,
        out_shape=shapes,
        in_specs=[
            SMEM if i in smem_in else ANY if i in any_in else VMEM for i in range(len(args))
        ],
        out_specs=[SMEM if i in smem_out else VMEM for i in range(len(shapes))],
        scratch_shapes=list(scratch),
        cost_estimate=pl.CostEstimate(
            flops=cost * 10**9, bytes_accessed=cost * 10**6, transcendentals=0
        )
        if cost
        else None,
        compiler_params=pltpu.CompilerParams(vmem_limit_bytes=48 * 2**20),
    )(*args)
    return result[0] if single else result


def sds(shape, dtype):
    return jax.ShapeDtypeStruct(shape, dtype)


def at_block(index):
    return pl.ds(pl.multiple_of(index * BLOCK, BLOCK), BLOCK)


def eye_mask(size):
    return lax.broadcasted_iota(jnp.int32, (size, size), 0) == lax.broadcasted_iota(
        jnp.int32, (size, size), 1
    )


def halves(value):
    high = value.astype(BF16)
    low = (value - high.astype(F32)).astype(BF16)
    return high, low


def pack(tile):
    return jnp.concatenate(halves(tile), axis=0)


def scale_of(power, part):
    return jnp.exp2(power) * (part * (1.0 / PART_TOP))


def encode(values):
    most = jnp.maximum(jnp.max(jnp.abs(values), axis=0, keepdims=True), 1e-30)
    power = jnp.floor(jnp.log2(most)) + 1.0
    part = jnp.floor(most * jnp.exp2(-power) * PART_TOP) + 1.0
    steps = jnp.floor(values * (CODE_TOP / scale_of(power, part)) + 0.5)
    steps = jnp.minimum(jnp.maximum(steps, -CODE_TOP), CODE_TOP)
    return steps.astype(jnp.int32).astype(jnp.int16), power, part


def decode(steps, scale):
    return steps.astype(jnp.int32).astype(F32) * (scale * (1.0 / CODE_TOP))


def as_rows(powers, parts, count):
    fill = jnp.zeros((count // 2 - len(powers), BLOCK), F32)
    fill = [fill] if fill.shape[0] else []
    rows = jnp.concatenate([*powers, *fill, *parts, *fill], axis=0)
    return rows.astype(jnp.int32).astype(jnp.int16)


def scale_rows(rows):
    rows = rows.astype(jnp.int32).astype(F32)
    half = rows.shape[0] // 2
    return scale_of(rows[:half], rows[half:])


def row_at(rows, place):
    if isinstance(place, int):
        return rows[place : place + 1, :]
    line = rows[:1, :]
    for i in range(1, rows.shape[0]):
        line = jnp.where(place == i, rows[i : i + 1, :], line)
    return line


def product(packed, values):
    left = jnp.concatenate(halves(values), axis=0)
    both = jnp.dot(jnp.concatenate([left, left], axis=1), packed, preferred_element_type=F32)
    count = values.shape[0]
    return both[:count] + both[count:]


def thirds(value):
    high = value.astype(BF16)
    rest = value - high.astype(F32)
    middle = rest.astype(BF16)
    low = (rest - middle.astype(F32)).astype(BF16)
    return jnp.concatenate([high, middle, low], axis=0)


def gram(parts):
    cross = lax.dot_general(parts, parts, NT, preferred_element_type=F32)
    n = parts.shape[0] // 3
    total = None
    for i, j in ((2, 2), (1, 2), (2, 1), (0, 2), (2, 0), (1, 1), (0, 1), (1, 0), (0, 0)):
        piece = cross[i * n : (i + 1) * n, j * n : (j + 1) * n]
        total = piece if total is None else total + piece
    return total


def times(left, parts):
    left = thirds(left)
    m = left.shape[0] // 3
    product3 = jnp.dot(
        jnp.concatenate([left, left, left], axis=1), parts, preferred_element_type=F32
    )
    return (product3[2 * m :] + product3[m : 2 * m]) + product3[:m]


def lower_inverse(matrix, step=8):
    n = matrix.shape[0]
    state = jnp.concatenate([matrix, eye_mask(n).astype(F32)], axis=1)
    done = []
    for j in range(0, n, step):
        top = j // 8 * 8
        if top > n - state.shape[0]:
            done.append(state[:8])
            state = state[8:]
        base = j - top
        rows = lax.broadcasted_iota(jnp.int32, state.shape, 0)
        columns = [jnp.broadcast_to(state[:, j + i : j + i + 1], state.shape) for i in range(step)]
        lines = [state[base + i : base + i + 1, :] for i in range(step)]
        pivot = [[columns[k][base + i : base + i + 1, :] for k in range(step)] for i in range(step)]
        for i in range(step):
            reciprocal = 1.0 / pivot[i][i]
            scaled = lines[i] * reciprocal
            ratio = [pivot[i][k] * reciprocal for k in range(step)]
            for k in range(i + 1, step):
                lines[k] = lines[k] - pivot[k][i] * scaled
                columns[k] = columns[k] - columns[i] * ratio[k]
                for m in range(i + 1, step):
                    pivot[k][m] = pivot[k][m] - pivot[k][i] * ratio[m]
            state = state - jnp.where(rows > base + i, columns[i], 0.0) * scaled
    state = jnp.concatenate([*done, state], axis=0)
    pivots = jnp.sum(jnp.where(eye_mask(n), state[:, :n], 0.0), axis=1, keepdims=True)
    return state[:, n:] / jnp.sqrt(pivots)


def both_columns(core, own, other):
    first = core == 0
    return jnp.concatenate(
        [jnp.where(first, own, other), jnp.where(first, other, own)], axis=0
    )


def plan_body(dims, me, *refs):
    row_count, capacity, slots, blocks_here = dims
    lists, (emb, after, idx) = refs[:row_count], refs[row_count : row_count + 3]
    sends = refs[row_count + 3 :]
    row = me[0]

    for i in range(slots):
        for line in (0, 1, 2, 4, 5):
            idx[line, i] = 0

    def ranked(listed, want, write):
        count = listed[2, 0]

        def step(s, counts):
            near = listed[0, s]
            far = listed[1, s]
            return write(s, near, far, far // blocks_here, s < count, counts)

        if slots <= 8:
            counts = (0,) * want
            for s in range(slots):
                counts = step(s, counts)
        else:
            lax.fori_loop(0, slots, step, (0,) * want)

    def write_own(s, near, far, owner, live, counts):
        shift = lax.rem(owner - row + row_count, row_count)
        rank = functools.reduce(
            lambda total, k: total + jnp.where(shift == k, counts[k], 0), range(row_count), 0
        )

        @pl.when(live)
        def _():
            slot = shift * capacity + rank
            idx[0, slot] = near - row * blocks_here
            idx[1, slot] = far
            idx[2, slot] = 1

        return tuple(
            counts[k] + (live & (shift == k)).astype(jnp.int32) for k in range(row_count)
        )

    for k in range(row_count):
        if k == 0:
            ranked(lists[k], row_count, write_own)

        def write_in(s, near, far, owner, live, counts, k=k):
            hit = live & (owner == row)

            @pl.when(hit)
            def _():
                slot = k * capacity + counts[0]
                idx[4, slot] = far - row * blocks_here
                idx[5, slot] = near

            return (counts[0] + hit.astype(jnp.int32),)

        ranked(lists[k], 1, write_in)
    for k in range(1, row_count):
        for j in range(capacity):
            sends[k - 1][j * BLOCK : (j + 1) * BLOCK, :] = emb[at_block(idx[4, k * capacity + j]), :]


def partial_distance(left, right):
    inner = lax.dot_general(left, right, NT, preferred_element_type=F32)
    left_sq = jnp.sum(jnp.square(left.astype(F32)), axis=1, keepdims=True)
    right_sq = jnp.sum(jnp.square(right.astype(F32)), axis=1, keepdims=True)
    right_row = jnp.sum(jnp.where(eye_mask(BLOCK), right_sq, 0.0), axis=0, keepdims=True)
    return left_sq + right_row - 2.0 * inner


def self_distance_body(own_blocks, tile_count, me, emb, out):
    for i in range(own_blocks):
        block = emb[at_block(i * tile_count + me[1]), :]
        out[i * BLOCK : (i + 1) * BLOCK, :] = partial_distance(block, block)


def pair_distance_body(row_count, capacity, idx, emb, *refs):
    out = refs[-1]
    for k in range(row_count):
        for j in range(capacity):
            slot = k * capacity + j
            left = emb[at_block(idx[0, slot]), :]
            if k == 0:
                right = emb[at_block(idx[4, j]), :]
            else:
                right = refs[k - 1][j * BLOCK : (j + 1) * BLOCK, :]
            out[slot * BLOCK : (slot + 1) * BLOCK, :] = partial_distance(left, right)


def self_tile_body(own_blocks, mine, other, packed, sums):
    for i in range(own_blocks):
        part = slice(i * BLOCK, (i + 1) * BLOCK)
        tile = jnp.exp(-kernel_gamma * (mine[part, :] + other[part, :] - 2.0))
        tile = jnp.where(eye_mask(BLOCK), 0.0, tile)
        packed[i] = pack(tile)
        sums[i : i + 1, :] = jnp.sum(tile, axis=0, keepdims=True)


def pair_tile_body(dims, me, idx, mine, other, self_sums, near_tiles, home_tiles, table, *chosen):
    row_count, capacity, per_core, blocks_here, tile_count = dims
    row, tile_index, core = me[0], me[1], me[2]
    table[...] = jnp.zeros(table.shape, F32)
    for i in range(self_sums.shape[0]):
        table[pl.ds(row * blocks_here + i * tile_count + tile_index, 1), :] = self_sums[i : i + 1, :]

    def add(block, line):
        place = pl.ds(block, 1)
        table[place, :] = table[place, :] + line

    for k in range(row_count):
        tiles = []
        for j in range(capacity):
            slot = k * capacity + j
            part = slice(slot * BLOCK, (slot + 1) * BLOCK)
            tile = jnp.exp(-kernel_gamma * (mine[part, :] + other[part, :] - 2.0))
            tile = jnp.where(idx[2, slot] > 0, tile, 0.0)
            turned = tile.T
            near_tiles[slot] = pack(turned)
            add(row * blocks_here + idx[0, slot], jnp.sum(turned, axis=0, keepdims=True))
            add(idx[1, slot], jnp.sum(tile, axis=0, keepdims=True))
            if k == 0:
                home_tiles[j] = pack(tile)
            tiles.append(tile)
        if k > 0:
            for inner in range(per_core):
                part = slice(inner * BLOCK, (inner + 1) * BLOCK)
                chosen[k - 1][part, :] = jnp.where(core == 0, tiles[inner], tiles[per_core + inner])


def encode_blocks(values, codes, powers, parts):
    for b in range(powers.shape[0]):
        at = slice(b * BLOCK, (b + 1) * BLOCK)
        steps, power, part = encode(values[:, at])
        codes[:, at] = steps
        powers[b : b + 1, :] = power
        parts[b : b + 1, :] = part


def start_body(values, codes, powers, parts):
    encode_blocks(values, codes, powers, parts)


def message_body(dims, idx, codes, powers, parts, *refs):
    row_count, capacity, per_core, blocks_here, tile_count = dims
    chosen, sends = refs[: row_count - 1], refs[row_count - 1 :]
    for k in range(1, row_count):
        lines = ([], [])
        for inner in range(per_core):
            at = slice(inner * BLOCK, (inner + 1) * BLOCK)
            steps, power, part = encode(chosen[k - 1][at, :])
            sends[k - 1][at, :] = steps
            lines[0].append(power)
            lines[1].append(part)
        pick_columns(idx, k, row_count, capacity, codes, powers, parts, sends[k - 1], per_core * BLOCK, lines)


def split_body(row_count, per_core, *refs):
    others = row_count - 1
    messages, outs = refs[:others], refs[-others:]
    for message, out in zip(messages, outs):
        scales = scale_rows(message[message.shape[0] - CODE_ROWS :, :])
        for inner in range(per_core):
            steps = message[inner * BLOCK : (inner + 1) * BLOCK, :]
            out[inner] = pack(decode(steps, scales[inner : inner + 1, :]))


def pick_columns(idx, k, row_count, capacity, codes, powers, parts, send, base, lines):
    count = codes.shape[0]
    back = row_count - k
    blocks = [idx[0, k * capacity + j] for j in range(capacity)]
    blocks += [idx[4, back * capacity + j] for j in range(capacity)]
    for place, block in enumerate(blocks):
        send[base + place * count : base + (place + 1) * count, :] = codes[:, at_block(block)]
        lines[0].append(powers[pl.ds(block, 1), :])
        lines[1].append(parts[pl.ds(block, 1), :])
    send[base + len(blocks) * count :, :] = as_rows(*lines, CODE_ROWS)


def apply_tiles(dims, me, idx, inverse, own, received, base, near_tiles, home_tiles, sent, shared, self_tiles, out):
    row_count, capacity, per_core, blocks_here, tile_count = dims
    row, tile_index, core = me[0], me[1], me[2]
    count = out.shape[0]
    out[...] = jnp.zeros(out.shape, F32)

    def scaled(values, block):
        return values * inverse[pl.ds(block, 1), :]

    def add(block, packed, values):
        place = at_block(block)
        out[:, place] = out[:, place] + product(packed, values)

    lines = [scale_rows(message[message.shape[0] - CODE_ROWS :, :]) for message in received]
    first_line = base // BLOCK

    def arrived(k, place):
        steps = received[k - 1][pl.ds(pl.multiple_of(base + place * count, CODE_ROWS), count), :]
        rows = lines[k - 1][first_line : first_line + 2 * capacity, :]
        return decode(steps, row_at(rows, place))

    for i in range(blocks_here // tile_count):
        block = i * tile_count + tile_index
        add(block, self_tiles[i], scaled(own[:, at_block(block)], row * blocks_here + block))
    for k in range(row_count):
        for j in range(capacity):
            slot = k * capacity + j
            if k == 0:
                values = own[:, at_block(idx[4, j])]
            else:
                values = arrived(row_count - k, capacity + j)
            add(idx[0, slot], near_tiles[slot], scaled(values, idx[1, slot]))
    for k in range(row_count):
        for j in range(capacity):
            if k == 0:
                slot = j
                values = own[:, at_block(idx[0, j])]
                packed = home_tiles[j]
            else:
                inner = j % per_core
                if j < per_core:
                    place = core * per_core + inner
                    packed = sent[k - 1][inner]
                else:
                    place = (1 - core) * per_core + inner
                    packed = shared[k - 1][inner]
                slot = k * capacity + place
                values = arrived(k, place)
            add(idx[4, slot], packed, scaled(values, idx[5, slot]))


def first_apply_body(dims, coded, me, idx, *refs):
    row_count, per_core = dims[0], dims[2]
    terms, refs = refs[:row_count], refs[row_count:]
    own, near_tiles, home_tiles, self_tiles = refs[:4]
    sent, shared = refs[4 : 3 + row_count], refs[3 + row_count : 2 + 2 * row_count]
    messages = refs[2 + 2 * row_count : -4]
    out, degree, inverse, total_out = refs[-4:]
    total = functools.reduce(lambda total, term: total + term[...], terms[1:], terms[0][...])
    degree[...] = total
    inverse[...] = 1.0 / jnp.sqrt(total)
    apply_tiles(
        dims, me, idx, inverse, own, messages, per_core * BLOCK, near_tiles, home_tiles, sent, shared, self_tiles, total_out
    )
    if not coded:
        out[...] = total_out[...]
        return
    lines = ([], [])
    blocks_here = dims[3]
    for b in range(blocks_here):
        at = slice(b * BLOCK, (b + 1) * BLOCK)
        steps, power, part = encode(total_out[:, at])
        out[:, at] = steps
        lines[0].append(power)
        lines[1].append(part)
    out[:, blocks_here * BLOCK :] = as_rows(*lines, out.shape[0])


def second_apply_body(dims, me, idx, inverse, after, *refs):
    row_count = dims[0]
    own, near_tiles, home_tiles, self_tiles = refs[:4]
    sent, shared = refs[4 : 3 + row_count], refs[3 + row_count : 2 + 2 * row_count]
    received, out = refs[2 + 2 * row_count : -1], refs[-1]
    apply_tiles(dims, me, idx, inverse, own, received, 0, near_tiles, home_tiles, sent, shared, self_tiles, out)


def mapped_body(dims, coded, me, idx, inverse, mine, other, out, *refs):
    row_count, capacity, per_core, blocks_here, tile_count = dims
    sends, (codes, powers, parts) = refs[:-3], refs[-3:]
    if coded:
        tail = blocks_here * BLOCK
        my_scales, other_scales = scale_rows(mine[:, tail:]), scale_rows(other[:, tail:])
    for b in range(blocks_here):
        part = slice(b * BLOCK, (b + 1) * BLOCK)
        row = inverse[pl.ds(me[0] * blocks_here + b, 1), :]
        if coded:
            line = slice(b, b + 1)
            value = decode(mine[:, part], my_scales[line]) + decode(other[:, part], other_scales[line])
        else:
            value = mine[:, part] + other[:, part]
        out[:, part] = value * row
    encode_blocks(out, codes, powers, parts)
    for k in range(1, row_count):
        pick_columns(idx, k, row_count, capacity, codes, powers, parts, sends[k - 1], 0, ([], []))


def last_mapped_body(blocks_here, me, inverse, mine, other, after, out):
    for b in range(blocks_here):
        part = slice(b * BLOCK, (b + 1) * BLOCK)
        row = inverse[pl.ds(me[0] * blocks_here + b, 1), :]
        out[:, part] = (mine[:, part] + other[:, part]) * row


def folded(square):
    half = square.shape[0] // 2
    return jnp.concatenate([square[:half], square[half:]], axis=1)


def unfolded(terms):
    total = functools.reduce(lambda total, term: total + term[...], terms[1:], terms[0][...])
    width = total.shape[1] // 2
    return jnp.concatenate([total[:, :width], total[:, width:]], axis=0)


def gram_body(me, own, other, out):
    out[...] = folded(gram(thirds(both_columns(me[2], own[...], other[...]))))


def factor_body(after, *refs):
    refs[-1][...] = lower_inverse(unfolded(refs[:-1]))


def second_gram_body(me, factor, own, other, mapped, out):
    full = both_columns(me[2], own[...], other[...])
    parts = thirds(times(factor[...], thirds(full)))
    mapped[...] = parts[: mapped.shape[0]]
    out[...] = folded(gram(parts))


def final_body(me, mapped, *refs):
    out = refs[-1]
    factor = lower_inverse(unfolded(refs[:-1]))
    own_cols = out.shape[0]
    part = jnp.where(me[2] == 0, factor[:own_cols], factor[own_cols:])
    left = jnp.concatenate(halves(part), axis=0)
    both = jnp.dot(
        jnp.concatenate([left, left], axis=1), mapped[...], preferred_element_type=F32
    )
    out[...] = both[own_cols:] + both[:own_cols]


def shift_by(value, axes, size, shift):
    return lax.ppermute(value, axes, [(i, (i + shift) % size) for i in range(size)])


def row_terms(value, row_count):
    return [value] + [shift_by(value, "rows", row_count, k) for k in range(1, row_count)]


def pair_step(value, name, flip):
    return lax.ppermute(value, name, [(i, i ^ flip) for i in range(lax.axis_size(name))])


def pair_sum(value, axes):
    terms = None
    steps = [(name, 1 << bit) for name in axes for bit in range((lax.axis_size(name) - 1).bit_length())]
    for name, flip in steps:
        if terms is not None:
            value = terms[0] + terms[1]
        terms = (value, pair_step(value, name, flip))
    return terms


def local(embeddings, start, pair_list, pair_count):
    row_count = lax.axis_size("rows")
    tile_count = lax.axis_size("tiles")
    core_count = lax.axis_size("cols")
    row_index = lax.axis_index("rows")
    tile_index = lax.axis_index("tiles")
    col_index = lax.axis_index("cols")
    me = jnp.stack([row_index, tile_index, col_index]).astype(jnp.int32)
    rows_here, half_features = embeddings.shape
    blocks_here = rows_here // BLOCK
    slots = pair_list.shape[2]
    capacity = slots // row_count
    per_core = capacity // core_count
    own_blocks = blocks_here // tile_count
    own_cols = start.shape[1]
    block_count = row_count * blocks_here
    others = range(1, row_count)

    own_list = jnp.concatenate(
        [pair_list[0], jnp.broadcast_to(pair_count[:, None], (1, slots))], axis=0
    )
    lists = row_terms(own_list, row_count)
    self_part = call(
        functools.partial(self_distance_body, own_blocks, tile_count),
        sds((own_blocks * BLOCK, BLOCK), F32),
        [me, embeddings],
        smem_in=(0,),
    )
    planned = call(
        functools.partial(plan_body, (row_count, capacity, slots, blocks_here)),
        [sds((6, slots), jnp.int32)] + [sds((capacity * BLOCK, half_features), BF16) for _ in others],
        [me, *lists, embeddings, self_part],
        smem_in=range(1 + row_count),
        any_in=(row_count + 2,),
        smem_out=(0,),
    )
    idx, sends = planned[0], planned[1:]
    far = [shift_by(sends[k - 1], "rows", row_count, -k) for k in others]

    self_other = shift_by(self_part, "cols", core_count, 1)
    self_tiles, self_sums = call(
        functools.partial(self_tile_body, own_blocks),
        [sds((own_blocks, 2 * BLOCK, BLOCK), BF16), sds((own_blocks, BLOCK), F32)],
        [self_part, self_other],
    )
    values = start.T
    code_shapes = [((own_cols, rows_here), jnp.int16), ((blocks_here, BLOCK), F32), ((blocks_here, BLOCK), F32)]
    start_codes = call(start_body, [sds(*shape) for shape in code_shapes], [values])
    code_scratch = [pltpu.VMEM(*shape) for shape in code_shapes]
    coded = tile_count == 2
    pair_part = call(
        functools.partial(pair_distance_body, row_count, capacity),
        sds((slots * BLOCK, BLOCK), F32),
        [idx, embeddings, *far],
        smem_in=(0,),
    )
    pair_other = shift_by(pair_part, "cols", core_count, 1)

    dims = (row_count, capacity, per_core, blocks_here, tile_count)
    table = sds((block_count, BLOCK), F32)
    picked = 2 * capacity * own_cols
    tiles = call(
        functools.partial(pair_tile_body, dims),
        [sds((slots, 2 * BLOCK, BLOCK), BF16), sds((capacity, 2 * BLOCK, BLOCK), BF16), table]
        + [sds((per_core * BLOCK, BLOCK), F32) for _ in others],
        [me, idx, pair_part, pair_other, self_sums],
        smem_in=(0, 1),
    )
    near_tiles, home_tiles, degrees, chosen = tiles[0], tiles[1], tiles[2], tiles[3:]
    mine, other = pair_sum(degrees, ("tiles",))
    degree_terms = row_terms(mine + other, row_count)
    sends = call(
        functools.partial(message_body, dims),
        [sds((per_core * BLOCK + picked + CODE_ROWS, BLOCK), jnp.int16) for _ in others],
        [idx, *start_codes, *chosen],
        smem_in=(0,),
        cost=3,
    )
    messages = [shift_by(sends[k - 1], "rows", row_count, k) for k in others]
    sent = call(
        functools.partial(split_body, row_count, per_core),
        [sds((per_core, 2 * BLOCK, BLOCK), BF16) for _ in others],
        [*messages, *degree_terms],
        any_in=range(row_count - 1, 2 * row_count - 1),
    )
    shared = [shift_by(tile, "cols", core_count, 1) for tile in sent]

    tile_args = [near_tiles, home_tiles, self_tiles, *sent, *shared]
    block_shape = sds((own_cols, rows_here), F32)
    square = sds((2 * own_cols, 2 * own_cols), F32)
    folded_square = sds((own_cols, 4 * own_cols), F32)

    part, degree, inverse = call(
        functools.partial(first_apply_body, dims, coded),
        [sds((own_cols, rows_here + BLOCK), jnp.int16) if coded else block_shape, table, table],
        [me, idx, *degree_terms, values, *tile_args, *messages],
        smem_in=(0, 1),
        scratch=[pltpu.VMEM((own_cols, rows_here), F32)],
    )
    mine, other = pair_sum(part, ("tiles",))
    first = call(
        functools.partial(mapped_body, dims, coded),
        [block_shape] + [sds((picked + CODE_ROWS, BLOCK), jnp.int16) for _ in others],
        [me, idx, inverse, mine, other],
        smem_in=(0, 1),
        scratch=code_scratch,
    )
    mapped, sends = first[0], first[1:]
    received = [shift_by(sends[k - 1], "rows", row_count, k) for k in others]

    mapped_other = shift_by(mapped, "cols", core_count, 1)
    first_gram = call(gram_body, folded_square, [me, mapped, mapped_other], smem_in=(0,))
    part = call(
        functools.partial(second_apply_body, dims),
        block_shape,
        [me, idx, inverse, first_gram, mapped, *tile_args, *received],
        smem_in=(0, 1),
        any_in=(3,),
    )
    gram_terms = pair_sum(first_gram, ("rows",))
    mine, other = pair_sum(part, ("tiles",))
    second = call(
        functools.partial(last_mapped_body, blocks_here),
        block_shape,
        [me, inverse, mine, other, gram_terms[1]],
        smem_in=(0,),
        any_in=(4,),
    )
    second_other = shift_by(second, "cols", core_count, 1)
    factor = call(factor_body, square, [second, *gram_terms], any_in=(0,))
    full, second_gram = call(
        second_gram_body,
        [sds((4 * own_cols, rows_here), BF16), folded_square],
        [me, factor, second, second_other],
        smem_in=(0,),
    )
    vectors = call(
        final_body, block_shape, [me, full, *row_terms(second_gram, row_count)], smem_in=(0,)
    )
    own_degree = lax.dynamic_slice_in_dim(degree, row_index * blocks_here, blocks_here, 0)
    return (vectors.T, own_degree.reshape(rows_here))


def solution(mesh):
    in_specs = (
        P(("groups", "rows"), "cols"),
        P(("groups", "rows"), "cols"),
        P(("groups", "rows", "tiles"), None, None),
        P(("groups", "rows", "tiles")),
    )
    out_specs = (P(("groups", "rows"), "cols"), P(("groups", "rows")))
    return jax.shard_map(local, mesh=mesh, in_specs=in_specs, out_specs=out_specs, check_vma=False)
```

```python
import functools

import jax
import jax.numpy as jnp
from jax import lax
from jax.experimental import pallas as pl
from jax.experimental.pallas import tpu as pltpu
from jax.sharding import PartitionSpec as P

BLOCK = 128
kernel_gamma = 14.0
CODE_TOP = 32767.0
PART_TOP = 16384.0
CODE_ROWS = 16

VMEM = pl.BlockSpec(memory_space=pltpu.VMEM)
SMEM = pl.BlockSpec(memory_space=pltpu.SMEM)
ANY = pl.BlockSpec(memory_space=pl.ANY)
F32 = jnp.float32
BF16 = jnp.bfloat16
HIGHEST = lax.Precision.HIGHEST
NT = (((1,), (1,)), ((), ()))


def call(body, outs, args, smem_in=(), smem_out=(), any_in=(), scratch=()):
    single = not isinstance(outs, (list, tuple))
    shapes = [outs] if single else list(outs)
    result = pl.pallas_call(
        body,
        out_shape=shapes,
        in_specs=[
            SMEM if i in smem_in else ANY if i in any_in else VMEM for i in range(len(args))
        ],
        out_specs=[SMEM if i in smem_out else VMEM for i in range(len(shapes))],
        scratch_shapes=list(scratch),
        compiler_params=pltpu.CompilerParams(vmem_limit_bytes=48 * 2**20),
    )(*args)
    return result[0] if single else result


def sds(shape, dtype):
    return jax.ShapeDtypeStruct(shape, dtype)


def at_block(index):
    return pl.ds(pl.multiple_of(index * BLOCK, BLOCK), BLOCK)


def eye_mask(size):
    return lax.broadcasted_iota(jnp.int32, (size, size), 0) == lax.broadcasted_iota(
        jnp.int32, (size, size), 1
    )


def halves(value):
    high = value.astype(BF16)
    low = (value - high.astype(F32)).astype(BF16)
    return high, low


def pack(tile):
    return jnp.concatenate(halves(tile), axis=0)


def scale_of(power, part):
    return jnp.exp2(power) * (part * (1.0 / PART_TOP))


def encode(values):
    most = jnp.maximum(jnp.max(jnp.abs(values), axis=0, keepdims=True), 1e-30)
    power = jnp.floor(jnp.log2(most)) + 1.0
    part = jnp.floor(most * jnp.exp2(-power) * PART_TOP) + 1.0
    steps = jnp.floor(values * (CODE_TOP / scale_of(power, part)) + 0.5)
    steps = jnp.minimum(jnp.maximum(steps, -CODE_TOP), CODE_TOP)
    return steps.astype(jnp.int32).astype(jnp.int16), power, part


def decode(steps, scale):
    return steps.astype(jnp.int32).astype(F32) * (scale * (1.0 / CODE_TOP))


def as_rows(powers, parts, count):
    fill = jnp.zeros((count // 2 - len(powers), BLOCK), F32)
    fill = [fill] if fill.shape[0] else []
    rows = jnp.concatenate([*powers, *fill, *parts, *fill], axis=0)
    return rows.astype(jnp.int32).astype(jnp.int16)


def scale_rows(rows):
    rows = rows.astype(jnp.int32).astype(F32)
    half = rows.shape[0] // 2
    return scale_of(rows[:half], rows[half:])


def row_at(rows, place):
    if isinstance(place, int):
        return rows[place : place + 1, :]
    line = rows[:1, :]
    for i in range(1, rows.shape[0]):
        line = jnp.where(place == i, rows[i : i + 1, :], line)
    return line


def product(packed, values):
    left = jnp.concatenate(halves(values), axis=0)
    both = jnp.dot(jnp.concatenate([left, left], axis=1), packed, preferred_element_type=F32)
    count = values.shape[0]
    return both[:count] + both[count:]


def thirds(value):
    high = value.astype(BF16)
    rest = value - high.astype(F32)
    middle = rest.astype(BF16)
    low = (rest - middle.astype(F32)).astype(BF16)
    return jnp.concatenate([high, middle, low], axis=0)


def gram(parts):
    cross = lax.dot_general(parts, parts, NT, preferred_element_type=F32)
    n = parts.shape[0] // 3
    total = None
    for i, j in ((2, 2), (1, 2), (2, 1), (0, 2), (2, 0), (1, 1), (0, 1), (1, 0), (0, 0)):
        piece = cross[i * n : (i + 1) * n, j * n : (j + 1) * n]
        total = piece if total is None else total + piece
    return total


def times(left, parts):
    left = thirds(left)
    m = left.shape[0] // 3
    product3 = jnp.dot(
        jnp.concatenate([left, left, left], axis=1), parts, preferred_element_type=F32
    )
    return (product3[2 * m :] + product3[m : 2 * m]) + product3[:m]


def lower_inverse(matrix, step=8):
    n = matrix.shape[0]
    state = jnp.concatenate([matrix, eye_mask(n).astype(F32)], axis=1)
    done = []
    for j in range(0, n, step):
        top = j // 8 * 8
        if top > n - state.shape[0]:
            done.append(state[:8])
            state = state[8:]
        base = j - top
        rows = lax.broadcasted_iota(jnp.int32, state.shape, 0)
        columns = [jnp.broadcast_to(state[:, j + i : j + i + 1], state.shape) for i in range(step)]
        lines = [state[base + i : base + i + 1, :] for i in range(step)]
        pivot = [[columns[k][base + i : base + i + 1, :] for k in range(step)] for i in range(step)]
        for i in range(step):
            reciprocal = 1.0 / pivot[i][i]
            scaled = lines[i] * reciprocal
            ratio = [pivot[i][k] * reciprocal for k in range(step)]
            for k in range(i + 1, step):
                lines[k] = lines[k] - pivot[k][i] * scaled
                columns[k] = columns[k] - columns[i] * ratio[k]
                for m in range(i + 1, step):
                    pivot[k][m] = pivot[k][m] - pivot[k][i] * ratio[m]
            state = state - jnp.where(rows > base + i, columns[i], 0.0) * scaled
    state = jnp.concatenate([*done, state], axis=0)
    pivots = jnp.sum(jnp.where(eye_mask(n), state[:, :n], 0.0), axis=1, keepdims=True)
    return state[:, n:] / jnp.sqrt(pivots)


def both_columns(core, own, other):
    first = core == 0
    return jnp.concatenate(
        [jnp.where(first, own, other), jnp.where(first, other, own)], axis=0
    )


def plan_body(dims, me, *refs):
    row_count, capacity, slots, blocks_here = dims
    lists, (emb, after, idx) = refs[:row_count], refs[row_count : row_count + 3]
    sends = refs[row_count + 3 :]
    row = me[0]

    for i in range(slots):
        for line in (0, 1, 2, 4, 5):
            idx[line, i] = 0

    def ranked(listed, want, write):
        count = listed[2, 0]

        def step(s, counts):
            near = listed[0, s]
            far = listed[1, s]
            return write(s, near, far, far // blocks_here, s < count, counts)

        if slots <= 8:
            counts = (0,) * want
            for s in range(slots):
                counts = step(s, counts)
        else:
            lax.fori_loop(0, slots, step, (0,) * want)

    def write_own(s, near, far, owner, live, counts):
        shift = lax.rem(owner - row + row_count, row_count)
        rank = functools.reduce(
            lambda total, k: total + jnp.where(shift == k, counts[k], 0), range(row_count), 0
        )

        @pl.when(live)
        def _():
            slot = shift * capacity + rank
            idx[0, slot] = near - row * blocks_here
            idx[1, slot] = far
            idx[2, slot] = 1

        return tuple(
            counts[k] + (live & (shift == k)).astype(jnp.int32) for k in range(row_count)
        )

    for k in range(row_count):
        if k == 0:
            ranked(lists[k], row_count, write_own)

        def write_in(s, near, far, owner, live, counts, k=k):
            hit = live & (owner == row)

            @pl.when(hit)
            def _():
                slot = k * capacity + counts[0]
                idx[4, slot] = far - row * blocks_here
                idx[5, slot] = near

            return (counts[0] + hit.astype(jnp.int32),)

        ranked(lists[k], 1, write_in)
    for k in range(1, row_count):
        for j in range(capacity):
            sends[k - 1][j * BLOCK : (j + 1) * BLOCK, :] = emb[at_block(idx[4, k * capacity + j]), :]


def partial_distance(left, right):
    inner = lax.dot_general(left, right, NT, preferred_element_type=F32)
    left_sq = jnp.sum(jnp.square(left.astype(F32)), axis=1, keepdims=True)
    right_sq = jnp.sum(jnp.square(right.astype(F32)), axis=1, keepdims=True)
    right_row = jnp.sum(jnp.where(eye_mask(BLOCK), right_sq, 0.0), axis=0, keepdims=True)
    return left_sq + right_row - 2.0 * inner


def self_distance_body(own_blocks, tile_count, me, emb, out):
    for i in range(own_blocks):
        block = emb[at_block(i * tile_count + me[1]), :]
        out[i * BLOCK : (i + 1) * BLOCK, :] = partial_distance(block, block)


def pair_distance_body(row_count, capacity, idx, emb, *refs):
    out = refs[-1]
    for k in range(row_count):
        for j in range(capacity):
            slot = k * capacity + j
            left = emb[at_block(idx[0, slot]), :]
            if k == 0:
                right = emb[at_block(idx[4, j]), :]
            else:
                right = refs[k - 1][j * BLOCK : (j + 1) * BLOCK, :]
            out[slot * BLOCK : (slot + 1) * BLOCK, :] = partial_distance(left, right)


def self_tile_body(own_blocks, mine, other, packed, sums):
    for i in range(own_blocks):
        part = slice(i * BLOCK, (i + 1) * BLOCK)
        tile = jnp.exp(-kernel_gamma * (mine[part, :] + other[part, :] - 2.0))
        tile = jnp.where(eye_mask(BLOCK), 0.0, tile)
        packed[i] = pack(tile)
        sums[i : i + 1, :] = jnp.sum(tile, axis=0, keepdims=True)


def pair_tile_body(dims, me, idx, mine, other, self_sums, codes, powers, parts, near_tiles, home_tiles, table, *sends):
    row_count, capacity, per_core, blocks_here, tile_count = dims
    row, tile_index, core = me[0], me[1], me[2]
    table[...] = jnp.zeros(table.shape, F32)
    for i in range(self_sums.shape[0]):
        table[pl.ds(row * blocks_here + i * tile_count + tile_index, 1), :] = self_sums[i : i + 1, :]

    def add(block, line):
        place = pl.ds(block, 1)
        table[place, :] = table[place, :] + line

    for k in range(row_count):
        tiles = []
        for j in range(capacity):
            slot = k * capacity + j
            part = slice(slot * BLOCK, (slot + 1) * BLOCK)
            tile = jnp.exp(-kernel_gamma * (mine[part, :] + other[part, :] - 2.0))
            tile = jnp.where(idx[2, slot] > 0, tile, 0.0)
            turned = tile.T
            near_tiles[slot] = pack(turned)
            add(row * blocks_here + idx[0, slot], jnp.sum(turned, axis=0, keepdims=True))
            add(idx[1, slot], jnp.sum(tile, axis=0, keepdims=True))
            if k == 0:
                home_tiles[j] = pack(tile)
            tiles.append(tile)
        if k > 0:
            lines = ([], [])
            for inner in range(per_core):
                at = slice(inner * BLOCK, (inner + 1) * BLOCK)
                steps, power, part = encode(jnp.where(core == 0, tiles[inner], tiles[per_core + inner]))
                sends[k - 1][at, :] = steps
                lines[0].append(power)
                lines[1].append(part)
            pick_columns(idx, k, row_count, capacity, codes, powers, parts, sends[k - 1], per_core * BLOCK, lines)


def encode_blocks(values, codes, powers, parts):
    for b in range(powers.shape[0]):
        at = slice(b * BLOCK, (b + 1) * BLOCK)
        steps, power, part = encode(values[:, at])
        codes[:, at] = steps
        powers[b : b + 1, :] = power
        parts[b : b + 1, :] = part


def start_body(values, codes, powers, parts):
    encode_blocks(values, codes, powers, parts)


def split_body(row_count, per_core, *refs):
    others = row_count - 1
    messages, outs = refs[:others], refs[-others:]
    for message, out in zip(messages, outs):
        scales = scale_rows(message[message.shape[0] - CODE_ROWS :, :])
        for inner in range(per_core):
            steps = message[inner * BLOCK : (inner + 1) * BLOCK, :]
            out[inner] = pack(decode(steps, scales[inner : inner + 1, :]))


def pick_columns(idx, k, row_count, capacity, codes, powers, parts, send, base, lines):
    count = codes.shape[0]
    back = row_count - k
    blocks = [idx[0, k * capacity + j] for j in range(capacity)]
    blocks += [idx[4, back * capacity + j] for j in range(capacity)]
    for place, block in enumerate(blocks):
        send[base + place * count : base + (place + 1) * count, :] = codes[:, at_block(block)]
        lines[0].append(powers[pl.ds(block, 1), :])
        lines[1].append(parts[pl.ds(block, 1), :])
    send[base + len(blocks) * count :, :] = as_rows(*lines, CODE_ROWS)


def apply_tiles(dims, me, idx, inverse, own, received, base, near_tiles, home_tiles, sent, shared, self_tiles, out):
    row_count, capacity, per_core, blocks_here, tile_count = dims
    row, tile_index, core = me[0], me[1], me[2]
    count = out.shape[0]
    out[...] = jnp.zeros(out.shape, F32)

    def scaled(values, block):
        return values * inverse[pl.ds(block, 1), :]

    def add(block, packed, values):
        place = at_block(block)
        out[:, place] = out[:, place] + product(packed, values)

    lines = [scale_rows(message[message.shape[0] - CODE_ROWS :, :]) for message in received]
    first_line = base // BLOCK

    def arrived(k, place):
        steps = received[k - 1][pl.ds(pl.multiple_of(base + place * count, CODE_ROWS), count), :]
        rows = lines[k - 1][first_line : first_line + 2 * capacity, :]
        return decode(steps, row_at(rows, place))

    for i in range(blocks_here // tile_count):
        block = i * tile_count + tile_index
        add(block, self_tiles[i], scaled(own[:, at_block(block)], row * blocks_here + block))
    for k in range(row_count):
        for j in range(capacity):
            slot = k * capacity + j
            if k == 0:
                values = own[:, at_block(idx[4, j])]
            else:
                values = arrived(row_count - k, capacity + j)
            add(idx[0, slot], near_tiles[slot], scaled(values, idx[1, slot]))
    for k in range(row_count):
        for j in range(capacity):
            if k == 0:
                slot = j
                values = own[:, at_block(idx[0, j])]
                packed = home_tiles[j]
            else:
                inner = j % per_core
                if j < per_core:
                    place = core * per_core + inner
                    packed = sent[k - 1][inner]
                else:
                    place = (1 - core) * per_core + inner
                    packed = shared[k - 1][inner]
                slot = k * capacity + place
                values = arrived(k, place)
            add(idx[4, slot], packed, scaled(values, idx[5, slot]))


def first_apply_body(dims, coded, me, idx, *refs):
    row_count, per_core = dims[0], dims[2]
    terms, refs = refs[:2], refs[2:]
    own, near_tiles, home_tiles, self_tiles = refs[:4]
    sent, shared = refs[4 : 3 + row_count], refs[3 + row_count : 2 + 2 * row_count]
    messages = refs[2 + 2 * row_count : -4]
    out, degree, inverse, total_out = refs[-4:]
    total = terms[0][...] + terms[1][...]
    degree[...] = total
    inverse[...] = 1.0 / jnp.sqrt(total)
    apply_tiles(
        dims, me, idx, inverse, own, messages, per_core * BLOCK, near_tiles, home_tiles, sent, shared, self_tiles, total_out
    )
    put_sum(coded, total_out, out)


def put_sum(coded, total, out):
    if not coded:
        out[...] = total[...]
        return
    lines = ([], [])
    blocks_here = total.shape[1] // BLOCK
    for b in range(blocks_here):
        at = slice(b * BLOCK, (b + 1) * BLOCK)
        steps, power, part = encode(total[:, at])
        out[:, at] = steps
        lines[0].append(power)
        lines[1].append(part)
    out[:, blocks_here * BLOCK :] = as_rows(*lines, out.shape[0])


def take_sum(coded, me, blocks_here, inverse, mine, other, out):
    if coded:
        tail = blocks_here * BLOCK
        my_scales, other_scales = scale_rows(mine[:, tail:]), scale_rows(other[:, tail:])
    for b in range(blocks_here):
        at = slice(b * BLOCK, (b + 1) * BLOCK)
        row = inverse[pl.ds(me[0] * blocks_here + b, 1), :]
        if coded:
            line = slice(b, b + 1)
            value = decode(mine[:, at], my_scales[line]) + decode(other[:, at], other_scales[line])
        else:
            value = mine[:, at] + other[:, at]
        out[:, at] = value * row


def second_apply_body(dims, coded, me, idx, inverse, after, *refs):
    row_count = dims[0]
    own, near_tiles, home_tiles, self_tiles = refs[:4]
    sent, shared = refs[4 : 3 + row_count], refs[3 + row_count : 2 + 2 * row_count]
    received, (out, total_out) = refs[2 + 2 * row_count : -2], refs[-2:]
    apply_tiles(
        dims, me, idx, inverse, own, received, 0, near_tiles, home_tiles, sent, shared, self_tiles, total_out
    )
    put_sum(coded, total_out, out)


def mapped_body(dims, coded, me, idx, inverse, mine, other, out, *refs):
    row_count, capacity, per_core, blocks_here, tile_count = dims
    sends, (codes, powers, parts) = refs[:-3], refs[-3:]
    take_sum(coded, me, blocks_here, inverse, mine, other, out)
    encode_blocks(out, codes, powers, parts)
    for k in range(1, row_count):
        pick_columns(idx, k, row_count, capacity, codes, powers, parts, sends[k - 1], 0, ([], []))


def last_mapped_body(blocks_here, coded, me, inverse, mine, other, after, out):
    take_sum(coded, me, blocks_here, inverse, mine, other, out)


def folded(square):
    half = square.shape[0] // 2
    return jnp.concatenate([square[:half], square[half:]], axis=1)


def unfolded(terms):
    total = functools.reduce(lambda total, term: total + term[...], terms[1:], terms[0][...])
    width = total.shape[1] // 2
    return jnp.concatenate([total[:, :width], total[:, width:]], axis=0)


def gram_body(me, own, other, out):
    out[...] = folded(gram(thirds(both_columns(me[2], own[...], other[...]))))


def factor_body(after, *refs):
    refs[-1][...] = lower_inverse(unfolded(refs[:-1]))


def second_gram_body(me, factor, own, other, mapped, out):
    full = both_columns(me[2], own[...], other[...])
    parts = thirds(times(factor[...], thirds(full)))
    mapped[...] = parts[: mapped.shape[0]]
    out[...] = folded(gram(parts))


def final_body(me, mapped, *refs):
    out = refs[-1]
    factor = lower_inverse(unfolded(refs[:-1]))
    own_cols = out.shape[0]
    part = jnp.where(me[2] == 0, factor[:own_cols], factor[own_cols:])
    left = jnp.concatenate(halves(part), axis=0)
    both = jnp.dot(
        jnp.concatenate([left, left], axis=1), mapped[...], preferred_element_type=F32
    )
    out[...] = both[own_cols:] + both[:own_cols]


def shift_by(value, axes, size, shift):
    return lax.ppermute(value, axes, [(i, (i + shift) % size) for i in range(size)])


def row_terms(value, row_count):
    return [value] + [shift_by(value, "rows", row_count, k) for k in range(1, row_count)]


def pair_step(value, name, flip):
    return lax.ppermute(value, name, [(i, i ^ flip) for i in range(lax.axis_size(name))])


def pair_sum(value, axes):
    terms = None
    steps = [(name, 1 << bit) for name in axes for bit in range((lax.axis_size(name) - 1).bit_length())]
    for name, flip in steps:
        if terms is not None:
            value = terms[0] + terms[1]
        terms = (value, pair_step(value, name, flip))
    return terms


def local(embeddings, start, pair_list, pair_count):
    row_count = lax.axis_size("rows")
    tile_count = lax.axis_size("tiles")
    core_count = lax.axis_size("cols")
    row_index = lax.axis_index("rows")
    tile_index = lax.axis_index("tiles")
    col_index = lax.axis_index("cols")
    me = jnp.stack([row_index, tile_index, col_index]).astype(jnp.int32)
    rows_here, half_features = embeddings.shape
    blocks_here = rows_here // BLOCK
    slots = pair_list.shape[2]
    capacity = slots // row_count
    per_core = capacity // core_count
    own_blocks = blocks_here // tile_count
    own_cols = start.shape[1]
    block_count = row_count * blocks_here
    others = range(1, row_count)

    own_list = jnp.concatenate(
        [pair_list[0], jnp.broadcast_to(pair_count[:, None], (1, slots))], axis=0
    )
    lists = row_terms(own_list, row_count)
    self_part = call(
        functools.partial(self_distance_body, own_blocks, tile_count),
        sds((own_blocks * BLOCK, BLOCK), F32),
        [me, embeddings],
        smem_in=(0,),
    )
    planned = call(
        functools.partial(plan_body, (row_count, capacity, slots, blocks_here)),
        [sds((6, slots), jnp.int32)] + [sds((capacity * BLOCK, half_features), BF16) for _ in others],
        [me, *lists, embeddings, self_part],
        smem_in=range(1 + row_count),
        any_in=(row_count + 2,),
        smem_out=(0,),
    )
    idx, sends = planned[0], planned[1:]
    far = [shift_by(sends[k - 1], "rows", row_count, -k) for k in others]

    self_other = shift_by(self_part, "cols", core_count, 1)
    self_tiles, self_sums = call(
        functools.partial(self_tile_body, own_blocks),
        [sds((own_blocks, 2 * BLOCK, BLOCK), BF16), sds((own_blocks, BLOCK), F32)],
        [self_part, self_other],
    )
    values = start.T
    code_shapes = [((own_cols, rows_here), jnp.int16), ((blocks_here, BLOCK), F32), ((blocks_here, BLOCK), F32)]
    start_codes = call(start_body, [sds(*shape) for shape in code_shapes], [values])
    code_scratch = [pltpu.VMEM(*shape) for shape in code_shapes]
    coded = tile_count == 2
    pair_part = call(
        functools.partial(pair_distance_body, row_count, capacity),
        sds((slots * BLOCK, BLOCK), F32),
        [idx, embeddings, *far],
        smem_in=(0,),
    )
    pair_other = shift_by(pair_part, "cols", core_count, 1)

    dims = (row_count, capacity, per_core, blocks_here, tile_count)
    table = sds((block_count, BLOCK), F32)
    picked = 2 * capacity * own_cols
    tiles = call(
        functools.partial(pair_tile_body, dims),
        [sds((slots, 2 * BLOCK, BLOCK), BF16), sds((capacity, 2 * BLOCK, BLOCK), BF16), table]
        + [sds((per_core * BLOCK + picked + CODE_ROWS, BLOCK), jnp.int16) for _ in others],
        [me, idx, pair_part, pair_other, self_sums, *start_codes],
        smem_in=(0, 1),
    )
    near_tiles, home_tiles, degrees, sends = tiles[0], tiles[1], tiles[2], tiles[3:]
    degrees = functools.reduce(jnp.add, row_terms(degrees, row_count))
    degree_terms = pair_sum(degrees, ("tiles",))
    messages = [shift_by(sends[k - 1], "rows", row_count, k) for k in others]
    sent = call(
        functools.partial(split_body, row_count, per_core),
        [sds((per_core, 2 * BLOCK, BLOCK), BF16) for _ in others],
        [*messages, degree_terms[1]],
        any_in=(row_count - 1,),
    )
    shared = [shift_by(tile, "cols", core_count, 1) for tile in sent]

    tile_args = [near_tiles, home_tiles, self_tiles, *sent, *shared]
    block_shape = sds((own_cols, rows_here), F32)
    sum_shape = sds((own_cols, rows_here + BLOCK), jnp.int16) if coded else block_shape
    square = sds((2 * own_cols, 2 * own_cols), F32)
    folded_square = sds((own_cols, 4 * own_cols), F32)

    part, degree, inverse = call(
        functools.partial(first_apply_body, dims, coded),
        [sum_shape, table, table],
        [me, idx, *degree_terms, values, *tile_args, *messages],
        smem_in=(0, 1),
        scratch=[pltpu.VMEM((own_cols, rows_here), F32)],
    )
    mine, other = pair_sum(part, ("tiles",))
    first = call(
        functools.partial(mapped_body, dims, coded),
        [block_shape] + [sds((picked + CODE_ROWS, BLOCK), jnp.int16) for _ in others],
        [me, idx, inverse, mine, other],
        smem_in=(0, 1),
        scratch=code_scratch,
    )
    mapped, sends = first[0], first[1:]
    received = [shift_by(sends[k - 1], "rows", row_count, k) for k in others]

    mapped_other = shift_by(mapped, "cols", core_count, 1)
    first_gram = call(gram_body, folded_square, [me, mapped, mapped_other], smem_in=(0,))
    steps = (row_count - 1).bit_length()
    for bit in range(steps - 1):
        first_gram = first_gram + pair_step(first_gram, "rows", 1 << bit)
    part = call(
        functools.partial(second_apply_body, dims, coded),
        sum_shape,
        [me, idx, inverse, first_gram, mapped, *tile_args, *received],
        smem_in=(0, 1),
        any_in=(3,),
        scratch=[pltpu.VMEM((own_cols, rows_here), F32)],
    )
    gram_terms = (first_gram, pair_step(first_gram, "rows", 1 << (steps - 1)))
    mine, other = pair_sum(part, ("tiles",))
    second = call(
        functools.partial(last_mapped_body, blocks_here, coded),
        block_shape,
        [me, inverse, mine, other, gram_terms[1]],
        smem_in=(0,),
        any_in=(4,),
    )
    second_other = shift_by(second, "cols", core_count, 1)
    factor = call(factor_body, square, [second, *gram_terms], any_in=(0,))
    full, second_gram = call(
        second_gram_body,
        [sds((4 * own_cols, rows_here), BF16), folded_square],
        [me, factor, second, second_other],
        smem_in=(0,),
    )
    vectors = call(
        final_body, block_shape, [me, full, *row_terms(second_gram, row_count)], smem_in=(0,)
    )
    own_degree = lax.dynamic_slice_in_dim(degree, row_index * blocks_here, blocks_here, 0)
    return (vectors.T, own_degree.reshape(rows_here))


def solution(mesh):
    in_specs = (
        P(("groups", "rows"), "cols"),
        P(("groups", "rows"), "cols"),
        P(("groups", "rows", "tiles"), None, None),
        P(("groups", "rows", "tiles")),
    )
    out_specs = (P(("groups", "rows"), "cols"), P(("groups", "rows")))
    return jax.shard_map(local, mesh=mesh, in_specs=in_specs, out_specs=out_specs, check_vma=False)
```

```python
import functools

import jax
import jax.numpy as jnp
from jax import lax
from jax.experimental import pallas as pl
from jax.experimental.pallas import tpu as pltpu
from jax.sharding import PartitionSpec as P

BLOCK = 128
kernel_gamma = 14.0
CODE_TOP = 32767.0
PART_TOP = 16384.0
CODE_ROWS = 16

VMEM = pl.BlockSpec(memory_space=pltpu.VMEM)
SMEM = pl.BlockSpec(memory_space=pltpu.SMEM)
ANY = pl.BlockSpec(memory_space=pl.ANY)
F32 = jnp.float32
BF16 = jnp.bfloat16
HIGHEST = lax.Precision.HIGHEST
NT = (((1,), (1,)), ((), ()))


def call(body, outs, args, smem_in=(), smem_out=(), any_in=(), scratch=()):
    single = not isinstance(outs, (list, tuple))
    shapes = [outs] if single else list(outs)
    result = pl.pallas_call(
        body,
        out_shape=shapes,
        in_specs=[
            SMEM if i in smem_in else ANY if i in any_in else VMEM for i in range(len(args))
        ],
        out_specs=[SMEM if i in smem_out else VMEM for i in range(len(shapes))],
        scratch_shapes=list(scratch),
        compiler_params=pltpu.CompilerParams(vmem_limit_bytes=48 * 2**20),
    )(*args)
    return result[0] if single else result


def sds(shape, dtype):
    return jax.ShapeDtypeStruct(shape, dtype)


def at_block(index):
    return pl.ds(pl.multiple_of(index * BLOCK, BLOCK), BLOCK)


def eye_mask(size):
    return lax.broadcasted_iota(jnp.int32, (size, size), 0) == lax.broadcasted_iota(
        jnp.int32, (size, size), 1
    )


def halves(value):
    high = value.astype(BF16)
    low = (value - high.astype(F32)).astype(BF16)
    return high, low


def pack(tile):
    return jnp.concatenate(halves(tile), axis=0)


def scale_of(power, part):
    return jnp.exp2(power) * (part * (1.0 / PART_TOP))


def encode(values):
    most = jnp.maximum(jnp.max(jnp.abs(values), axis=0, keepdims=True), 1e-30)
    power = jnp.floor(jnp.log2(most)) + 1.0
    part = jnp.floor(most * jnp.exp2(-power) * PART_TOP) + 1.0
    steps = jnp.floor(values * (CODE_TOP / scale_of(power, part)) + 0.5)
    steps = jnp.minimum(jnp.maximum(steps, -CODE_TOP), CODE_TOP)
    return steps.astype(jnp.int32).astype(jnp.int16), power, part


def decode(steps, scale):
    return steps.astype(jnp.int32).astype(F32) * (scale * (1.0 / CODE_TOP))


def as_rows(powers, parts, count):
    fill = jnp.zeros((count // 2 - len(powers), BLOCK), F32)
    fill = [fill] if fill.shape[0] else []
    rows = jnp.concatenate([*powers, *fill, *parts, *fill], axis=0)
    return rows.astype(jnp.int32).astype(jnp.int16)


def scale_rows(rows):
    rows = rows.astype(jnp.int32).astype(F32)
    half = rows.shape[0] // 2
    return scale_of(rows[:half], rows[half:])


def row_at(rows, place):
    if isinstance(place, int):
        return rows[place : place + 1, :]
    line = rows[:1, :]
    for i in range(1, rows.shape[0]):
        line = jnp.where(place == i, rows[i : i + 1, :], line)
    return line


def product(packed, values):
    left = jnp.concatenate(halves(values), axis=0)
    both = jnp.dot(jnp.concatenate([left, left], axis=1), packed, preferred_element_type=F32)
    count = values.shape[0]
    return both[:count] + both[count:]


def thirds(value):
    high = value.astype(BF16)
    rest = value - high.astype(F32)
    middle = rest.astype(BF16)
    low = (rest - middle.astype(F32)).astype(BF16)
    return jnp.concatenate([high, middle, low], axis=0)


def gram(parts):
    cross = lax.dot_general(parts, parts, NT, preferred_element_type=F32)
    n = parts.shape[0] // 3
    total = None
    for i, j in ((2, 2), (1, 2), (2, 1), (0, 2), (2, 0), (1, 1), (0, 1), (1, 0), (0, 0)):
        piece = cross[i * n : (i + 1) * n, j * n : (j + 1) * n]
        total = piece if total is None else total + piece
    return total


def times(left, parts):
    m = left.shape[0]
    left = jnp.concatenate(halves(left), axis=0)
    both = jnp.dot(jnp.concatenate([left, left], axis=1), parts, preferred_element_type=F32)
    return both[m:] + both[:m]


def lower_inverse(matrix, step=8):
    n = matrix.shape[0]
    state = jnp.concatenate([matrix, eye_mask(n).astype(F32)], axis=1)
    done = []
    for j in range(0, n, step):
        top = j // 8 * 8
        if top > n - state.shape[0]:
            done.append(state[:8])
            state = state[8:]
        base = j - top
        rows = lax.broadcasted_iota(jnp.int32, state.shape, 0)
        columns = [jnp.broadcast_to(state[:, j + i : j + i + 1], state.shape) for i in range(step)]
        lines = [state[base + i : base + i + 1, :] for i in range(step)]
        pivot = [[columns[k][base + i : base + i + 1, :] for k in range(step)] for i in range(step)]
        for i in range(step):
            reciprocal = 1.0 / pivot[i][i]
            scaled = lines[i] * reciprocal
            ratio = [pivot[i][k] * reciprocal for k in range(step)]
            for k in range(i + 1, step):
                lines[k] = lines[k] - pivot[k][i] * scaled
                columns[k] = columns[k] - columns[i] * ratio[k]
                for m in range(i + 1, step):
                    pivot[k][m] = pivot[k][m] - pivot[k][i] * ratio[m]
            state = state - jnp.where(rows > base + i, columns[i], 0.0) * scaled
    state = jnp.concatenate([*done, state], axis=0)
    pivots = jnp.sum(jnp.where(eye_mask(n), state[:, :n], 0.0), axis=1, keepdims=True)
    return state[:, n:] / jnp.sqrt(pivots)


def both_columns(core, own, other):
    first = core == 0
    return jnp.concatenate(
        [jnp.where(first, own, other), jnp.where(first, other, own)], axis=0
    )


def plan_body(dims, me, *refs):
    row_count, capacity, slots, blocks_here = dims
    lists, (emb, after, idx) = refs[:row_count], refs[row_count : row_count + 3]
    sends = refs[row_count + 3 :]
    row = me[0]

    for i in range(slots):
        for line in (0, 1, 2, 4, 5):
            idx[line, i] = 0

    def ranked(listed, want, write):
        count = listed[2, 0]

        def step(s, counts):
            near = listed[0, s]
            far = listed[1, s]
            return write(s, near, far, far // blocks_here, s < count, counts)

        if slots <= 8:
            counts = (0,) * want
            for s in range(slots):
                counts = step(s, counts)
        else:
            lax.fori_loop(0, slots, step, (0,) * want)

    def write_own(s, near, far, owner, live, counts):
        shift = lax.rem(owner - row + row_count, row_count)
        rank = functools.reduce(
            lambda total, k: total + jnp.where(shift == k, counts[k], 0), range(row_count), 0
        )

        @pl.when(live)
        def _():
            slot = shift * capacity + rank
            idx[0, slot] = near - row * blocks_here
            idx[1, slot] = far
            idx[2, slot] = 1

        return tuple(
            counts[k] + (live & (shift == k)).astype(jnp.int32) for k in range(row_count)
        )

    for k in range(row_count):
        if k == 0:
            ranked(lists[k], row_count, write_own)

        def write_in(s, near, far, owner, live, counts, k=k):
            hit = live & (owner == row)

            @pl.when(hit)
            def _():
                slot = k * capacity + counts[0]
                idx[4, slot] = far - row * blocks_here
                idx[5, slot] = near

            return (counts[0] + hit.astype(jnp.int32),)

        ranked(lists[k], 1, write_in)
    for k in range(1, row_count):
        for j in range(capacity):
            sends[k - 1][j * BLOCK : (j + 1) * BLOCK, :] = emb[at_block(idx[4, k * capacity + j]), :]


def squares(block):
    return jnp.sum(jnp.square(block.astype(F32)), axis=1, keepdims=True)


def partial_distance(left, right, left_sq, right_sq):
    inner = lax.dot_general(left, right, NT, preferred_element_type=F32)
    right_row = jnp.sum(jnp.where(eye_mask(BLOCK), right_sq, 0.0), axis=0, keepdims=True)
    return left_sq + right_row - 2.0 * inner


def self_distance_body(own_blocks, tile_count, me, emb, out):
    for i in range(own_blocks):
        block = emb[at_block(i * tile_count + me[1]), :]
        block_sq = squares(block)
        out[i * BLOCK : (i + 1) * BLOCK, :] = partial_distance(block, block, block_sq, block_sq)


def squares_body(emb, after, out):
    for b in range(out.shape[0] // BLOCK):
        part = slice(b * BLOCK, (b + 1) * BLOCK)
        out[part, :] = jnp.broadcast_to(squares(emb[part, :]), (BLOCK, BLOCK))


def pair_distance_body(row_count, capacity, idx, emb, own_squares, *refs):
    out = refs[-1]
    for k in range(row_count):
        for j in range(capacity):
            slot = k * capacity + j
            left = emb[at_block(idx[0, slot]), :]
            left_sq = own_squares[at_block(idx[0, slot]), :]
            if k == 0:
                right = emb[at_block(idx[4, j]), :]
                right_sq = own_squares[at_block(idx[4, j]), :]
            else:
                right = refs[k - 1][j * BLOCK : (j + 1) * BLOCK, :]
                right_sq = squares(right)
            part = slice(slot * BLOCK, (slot + 1) * BLOCK)
            out[part, :] = partial_distance(left, right, left_sq, right_sq)


def self_tile_body(own_blocks, mine, other, packed, sums):
    for i in range(own_blocks):
        part = slice(i * BLOCK, (i + 1) * BLOCK)
        tile = jnp.exp(-kernel_gamma * (mine[part, :] + other[part, :] - 2.0))
        tile = jnp.where(eye_mask(BLOCK), 0.0, tile)
        packed[i] = pack(tile)
        sums[i : i + 1, :] = jnp.sum(tile, axis=0, keepdims=True)


def pair_tile_body(dims, me, idx, mine, other, self_sums, codes, powers, parts, near_tiles, home_tiles, table, *sends):
    row_count, capacity, per_core, blocks_here, tile_count = dims
    row, tile_index, core = me[0], me[1], me[2]
    table[...] = jnp.zeros(table.shape, F32)
    for i in range(self_sums.shape[0]):
        table[pl.ds(row * blocks_here + i * tile_count + tile_index, 1), :] = self_sums[i : i + 1, :]

    def add(block, line):
        place = pl.ds(block, 1)
        table[place, :] = table[place, :] + line

    for k in range(row_count):
        tiles = []
        for j in range(capacity):
            slot = k * capacity + j
            part = slice(slot * BLOCK, (slot + 1) * BLOCK)
            tile = jnp.exp(-kernel_gamma * (mine[part, :] + other[part, :] - 2.0))
            tile = jnp.where(idx[2, slot] > 0, tile, 0.0)
            turned = tile.T
            near_tiles[slot] = pack(turned)
            add(row * blocks_here + idx[0, slot], jnp.sum(turned, axis=0, keepdims=True))
            add(idx[1, slot], jnp.sum(tile, axis=0, keepdims=True))
            if k == 0:
                home_tiles[j] = pack(tile)
            tiles.append(tile)
        if k > 0:
            lines = ([], [])
            for inner in range(per_core):
                at = slice(inner * BLOCK, (inner + 1) * BLOCK)
                steps, power, part = encode(jnp.where(core == 0, tiles[inner], tiles[per_core + inner]))
                sends[k - 1][at, :] = steps
                lines[0].append(power)
                lines[1].append(part)
            pick_columns(idx, k, row_count, capacity, codes, powers, parts, sends[k - 1], per_core * BLOCK, lines)


def encode_blocks(values, codes, powers, parts):
    for b in range(powers.shape[0]):
        at = slice(b * BLOCK, (b + 1) * BLOCK)
        steps, power, part = encode(values[:, at])
        codes[:, at] = steps
        powers[b : b + 1, :] = power
        parts[b : b + 1, :] = part


def start_body(values, codes, powers, parts):
    encode_blocks(values, codes, powers, parts)


def split_body(row_count, per_core, *refs):
    others = row_count - 1
    messages, outs = refs[:others], refs[-others:]
    for message, out in zip(messages, outs):
        scales = scale_rows(message[message.shape[0] - CODE_ROWS :, :])
        for inner in range(per_core):
            steps = message[inner * BLOCK : (inner + 1) * BLOCK, :]
            out[inner] = pack(decode(steps, scales[inner : inner + 1, :]))


def pick_columns(idx, k, row_count, capacity, codes, powers, parts, send, base, lines):
    count = codes.shape[0]
    back = row_count - k
    blocks = [idx[0, k * capacity + j] for j in range(capacity)]
    blocks += [idx[4, back * capacity + j] for j in range(capacity)]
    for place, block in enumerate(blocks):
        send[base + place * count : base + (place + 1) * count, :] = codes[:, at_block(block)]
        lines[0].append(powers[pl.ds(block, 1), :])
        lines[1].append(parts[pl.ds(block, 1), :])
    send[base + len(blocks) * count :, :] = as_rows(*lines, CODE_ROWS)


def add_product(out, block, packed, values):
    place = at_block(block)
    out[:, place] = out[:, place] + product(packed, values)


def apply_own(dims, me, idx, inverse, own, near_tiles, home_tiles, self_tiles, out):
    row_count, capacity, per_core, blocks_here, tile_count = dims
    row, tile_index = me[0], me[1]
    out[...] = jnp.zeros(out.shape, F32)

    def scaled(block):
        return own[:, at_block(block)] * inverse[pl.ds(row * blocks_here + block, 1), :]

    for i in range(blocks_here // tile_count):
        block = i * tile_count + tile_index
        add_product(out, block, self_tiles[i], scaled(block))
    for j in range(capacity):
        add_product(out, idx[0, j], near_tiles[j], scaled(idx[4, j]))
        add_product(out, idx[4, j], home_tiles[j], scaled(idx[0, j]))


def apply_far(dims, me, idx, inverse, received, base, near_tiles, sent, shared, out):
    row_count, capacity, per_core, blocks_here, tile_count = dims
    core = me[2]
    count = out.shape[0]
    lines = [scale_rows(message[message.shape[0] - CODE_ROWS :, :]) for message in received]
    first_line = base // BLOCK

    def arrived(k, place, block):
        steps = received[k - 1][pl.ds(pl.multiple_of(base + place * count, CODE_ROWS), count), :]
        rows = lines[k - 1][first_line : first_line + 2 * capacity, :]
        return decode(steps, row_at(rows, place) * inverse[pl.ds(block, 1), :])

    for k in range(1, row_count):
        for j in range(capacity):
            slot = k * capacity + j
            values = arrived(row_count - k, capacity + j, idx[1, slot])
            add_product(out, idx[0, slot], near_tiles[slot], values)
            inner = j % per_core
            if j < per_core:
                place = core * per_core + inner
                packed = sent[k - 1][inner]
            else:
                place = (1 - core) * per_core + inner
                packed = shared[k - 1][inner]
            slot = k * capacity + place
            add_product(out, idx[4, slot], packed, arrived(k, place, idx[5, slot]))


def first_own_body(dims, me, idx, mine, other, own, near_tiles, home_tiles, self_tiles, out, degree, inverse):
    total = mine[...] + other[...]
    degree[...] = total
    inverse[...] = 1.0 / jnp.sqrt(total)
    apply_own(dims, me, idx, inverse, own, near_tiles, home_tiles, self_tiles, out)


def first_far_body(dims, coded, me, idx, inverse, started, near_tiles, *refs):
    row_count, per_core = dims[0], dims[2]
    others = row_count - 1
    sent, shared, messages = refs[:others], refs[others : 2 * others], refs[2 * others : 3 * others]
    out, total = refs[3 * others :]
    total[...] = started[...]
    apply_far(dims, me, idx, inverse, messages, per_core * BLOCK, near_tiles, sent, shared, total)
    put_sum(coded, total, out)


def second_apply_body(dims, me, idx, inverse, after, own, home_tiles, self_tiles, near_tiles, *refs):
    others = dims[0] - 1
    sent, shared, received = refs[:others], refs[others : 2 * others], refs[2 * others : 3 * others]
    out = refs[-1]
    apply_own(dims, me, idx, inverse, own, near_tiles, home_tiles, self_tiles, out)
    apply_far(dims, me, idx, inverse, received, 0, near_tiles, sent, shared, out)


def gate_body(value, after, out):
    pass


def gate(value, after):
    return pl.pallas_call(
        gate_body,
        out_shape=sds(value.shape, value.dtype),
        in_specs=[ANY, ANY],
        out_specs=ANY,
        input_output_aliases={0: 0},
    )(value, after)


def put_sum(coded, total, out):
    if not coded:
        out[...] = total[...]
        return
    lines = ([], [])
    blocks_here = total.shape[1] // BLOCK
    for b in range(blocks_here):
        at = slice(b * BLOCK, (b + 1) * BLOCK)
        steps, power, part = encode(total[:, at])
        out[:, at] = steps
        lines[0].append(power)
        lines[1].append(part)
    out[:, blocks_here * BLOCK :] = as_rows(*lines, out.shape[0])


def take_sum(coded, me, blocks_here, inverse, mine, other, out):
    if coded:
        tail = blocks_here * BLOCK
        my_scales, other_scales = scale_rows(mine[:, tail:]), scale_rows(other[:, tail:])
    for b in range(blocks_here):
        at = slice(b * BLOCK, (b + 1) * BLOCK)
        row = inverse[pl.ds(me[0] * blocks_here + b, 1), :]
        if coded:
            line = slice(b, b + 1)
            value = decode(mine[:, at], my_scales[line]) + decode(other[:, at], other_scales[line])
        else:
            value = mine[:, at] + other[:, at]
        out[:, at] = value * row


def mapped_body(dims, coded, me, idx, inverse, mine, other, out, *refs):
    row_count, capacity, per_core, blocks_here, tile_count = dims
    sends, (codes, powers, parts) = refs[:-3], refs[-3:]
    take_sum(coded, me, blocks_here, inverse, mine, other, out)
    encode_blocks(out, codes, powers, parts)
    for k in range(1, row_count):
        pick_columns(idx, k, row_count, capacity, codes, powers, parts, sends[k - 1], 0, ([], []))


def last_mapped_body(blocks_here, me, inverse, mine, other, after, out):
    take_sum(False, me, blocks_here, inverse, mine, other, out)


def folded(square):
    half = square.shape[0] // 2
    return jnp.concatenate([square[:half], square[half:]], axis=1)


def unfolded(terms):
    total = functools.reduce(lambda total, term: total + term[...], terms[1:], terms[0][...])
    width = total.shape[1] // 2
    return jnp.concatenate([total[:, :width], total[:, width:]], axis=0)


def gram_body(me, own, other, out):
    out[...] = folded(gram(thirds(both_columns(me[2], own[...], other[...]))))


def factor_body(after, *refs):
    refs[-1][...] = lower_inverse(unfolded(refs[:-1]))


def second_gram_body(me, factor, own, other, mapped, out):
    full = both_columns(me[2], own[...], other[...])
    parts = thirds(times(factor[...], pack(full)))
    mapped[...] = parts[: mapped.shape[0]]
    out[...] = folded(gram(parts))


def final_body(me, mapped, *refs):
    out = refs[-1]
    factor = lower_inverse(unfolded(refs[:-1]))
    own_cols = out.shape[0]
    part = jnp.where(me[2] == 0, factor[:own_cols], factor[own_cols:])
    out[...] = times(part, mapped[...])


def shift_by(value, axes, size, shift):
    return lax.ppermute(value, axes, [(i, (i + shift) % size) for i in range(size)])


def row_terms(value, row_count):
    return [value] + [shift_by(value, "rows", row_count, k) for k in range(1, row_count)]


def pair_step(value, name, flip):
    return lax.ppermute(value, name, [(i, i ^ flip) for i in range(lax.axis_size(name))])


def pair_sum(value, axes):
    terms = None
    steps = [(name, 1 << bit) for name in axes for bit in range((lax.axis_size(name) - 1).bit_length())]
    for name, flip in steps:
        if terms is not None:
            value = terms[0] + terms[1]
        terms = (value, pair_step(value, name, flip))
    return terms


def local(embeddings, start, pair_list, pair_count):
    row_count = lax.axis_size("rows")
    tile_count = lax.axis_size("tiles")
    core_count = lax.axis_size("cols")
    row_index = lax.axis_index("rows")
    tile_index = lax.axis_index("tiles")
    col_index = lax.axis_index("cols")
    me = jnp.stack([row_index, tile_index, col_index]).astype(jnp.int32)
    rows_here, half_features = embeddings.shape
    blocks_here = rows_here // BLOCK
    slots = pair_list.shape[2]
    capacity = slots // row_count
    per_core = capacity // core_count
    own_blocks = blocks_here // tile_count
    own_cols = start.shape[1]
    block_count = row_count * blocks_here
    others = range(1, row_count)

    own_list = jnp.concatenate(
        [pair_list[0], jnp.broadcast_to(pair_count[:, None], (1, slots))], axis=0
    )
    lists = row_terms(own_list, row_count)
    self_part = call(
        functools.partial(self_distance_body, own_blocks, tile_count),
        sds((own_blocks * BLOCK, BLOCK), F32),
        [me, embeddings],
        smem_in=(0,),
    )
    planned = call(
        functools.partial(plan_body, (row_count, capacity, slots, blocks_here)),
        [sds((6, slots), jnp.int32)] + [sds((capacity * BLOCK, half_features), BF16) for _ in others],
        [me, *lists, embeddings, self_part],
        smem_in=range(1 + row_count),
        any_in=(row_count + 2,),
        smem_out=(0,),
    )
    idx, sends = planned[0], planned[1:]
    far = [shift_by(sends[k - 1], "rows", row_count, -k) for k in others]

    self_other = shift_by(self_part, "cols", core_count, 1)
    self_tiles, self_sums = call(
        functools.partial(self_tile_body, own_blocks),
        [sds((own_blocks, 2 * BLOCK, BLOCK), BF16), sds((own_blocks, BLOCK), F32)],
        [self_part, self_other],
    )
    values = start.T
    code_shapes = [((own_cols, rows_here), jnp.int16), ((blocks_here, BLOCK), F32), ((blocks_here, BLOCK), F32)]
    start_codes = call(start_body, [sds(*shape) for shape in code_shapes], [values])
    code_scratch = [pltpu.VMEM(*shape) for shape in code_shapes]
    coded = tile_count == 2
    own_squares = call(squares_body, sds((rows_here, BLOCK), F32), [embeddings, idx], any_in=(1,))
    pair_part = call(
        functools.partial(pair_distance_body, row_count, capacity),
        sds((slots * BLOCK, BLOCK), F32),
        [idx, embeddings, own_squares, *far],
        smem_in=(0,),
    )
    pair_other = shift_by(pair_part, "cols", core_count, 1)

    dims = (row_count, capacity, per_core, blocks_here, tile_count)
    table = sds((block_count, BLOCK), F32)
    picked = 2 * capacity * own_cols
    tiles = call(
        functools.partial(pair_tile_body, dims),
        [sds((slots, 2 * BLOCK, BLOCK), BF16), sds((capacity, 2 * BLOCK, BLOCK), BF16), table]
        + [sds((per_core * BLOCK + picked + CODE_ROWS, BLOCK), jnp.int16) for _ in others],
        [me, idx, pair_part, pair_other, self_sums, *start_codes],
        smem_in=(0, 1),
    )
    near_tiles, home_tiles, degrees, sends = tiles[0], tiles[1], tiles[2], tiles[3:]
    degrees = functools.reduce(jnp.add, row_terms(degrees, row_count))
    degree_terms = pair_sum(degrees, ("tiles",))
    messages = [shift_by(sends[k - 1], "rows", row_count, k) for k in others]
    sent = call(
        functools.partial(split_body, row_count, per_core),
        [sds((per_core, 2 * BLOCK, BLOCK), BF16) for _ in others],
        [*messages, degree_terms[1]],
        any_in=(row_count - 1,),
    )
    shared = [shift_by(tile, "cols", core_count, 1) for tile in sent]

    block_shape = sds((own_cols, rows_here), F32)
    sum_shape = sds((own_cols, rows_here + BLOCK), jnp.int16) if coded else block_shape
    square = sds((2 * own_cols, 2 * own_cols), F32)
    folded_square = sds((own_cols, 4 * own_cols), F32)

    started, degree, inverse = call(
        functools.partial(first_own_body, dims),
        [block_shape, table, table],
        [me, idx, *degree_terms, values, near_tiles, home_tiles, self_tiles],
        smem_in=(0, 1),
    )
    part = call(
        functools.partial(first_far_body, dims, coded),
        sum_shape,
        [me, idx, inverse, started, near_tiles, *sent, *shared, *messages],
        smem_in=(0, 1),
        scratch=[pltpu.VMEM((own_cols, rows_here), F32)],
    )
    mine, other = pair_sum(part, ("tiles",))
    first = call(
        functools.partial(mapped_body, dims, coded),
        [block_shape] + [sds((picked + CODE_ROWS, BLOCK), jnp.int16) for _ in others],
        [me, idx, inverse, mine, other],
        smem_in=(0, 1),
        scratch=code_scratch,
    )
    mapped, sends = first[0], first[1:]
    received = [shift_by(sends[k - 1], "rows", row_count, k) for k in others]

    mapped_other = shift_by(mapped, "cols", core_count, 1)
    first_gram = call(gram_body, folded_square, [me, mapped, mapped_other], smem_in=(0,))
    part = call(
        functools.partial(second_apply_body, dims),
        block_shape,
        [me, idx, inverse, first_gram, mapped, home_tiles, self_tiles, near_tiles, *sent, *shared, *received],
        smem_in=(0, 1),
        any_in=(3,),
    )
    steps = (row_count - 1).bit_length()
    for bit in range(steps - 1):
        first_gram = first_gram + pair_step(first_gram, "rows", 1 << bit)
    part = gate(part, first_gram)
    gram_terms = (first_gram, pair_step(first_gram, "rows", 1 << (steps - 1)))
    mine, other = pair_sum(part, ("tiles",))
    second = call(
        functools.partial(last_mapped_body, blocks_here),
        block_shape,
        [me, inverse, mine, other, gram_terms[1]],
        smem_in=(0,),
        any_in=(4,),
    )
    second_other = shift_by(second, "cols", core_count, 1)
    factor = call(factor_body, square, [second, *gram_terms], any_in=(0,))
    full, second_gram = call(
        second_gram_body,
        [sds((4 * own_cols, rows_here), BF16), folded_square],
        [me, factor, second, second_other],
        smem_in=(0,),
    )
    vectors = call(
        final_body, block_shape, [me, full, *row_terms(second_gram, row_count)], smem_in=(0,)
    )
    own_degree = lax.dynamic_slice_in_dim(degree, row_index * blocks_here, blocks_here, 0)
    return (vectors.T, own_degree.reshape(rows_here))


def solution(mesh):
    in_specs = (
        P(("groups", "rows"), "cols"),
        P(("groups", "rows"), "cols"),
        P(("groups", "rows", "tiles"), None, None),
        P(("groups", "rows", "tiles")),
    )
    out_specs = (P(("groups", "rows"), "cols"), P(("groups", "rows")))
    return jax.shard_map(local, mesh=mesh, in_specs=in_specs, out_specs=out_specs, check_vma=False)
```

```python
import functools

import jax
import jax.numpy as jnp
from jax import lax
from jax.experimental import pallas as pl
from jax.experimental.pallas import tpu as pltpu
from jax.sharding import PartitionSpec as P

BLOCK = 128
kernel_gamma = 14.0
CODE_TOP = 32767.0
PART_TOP = 16384.0
CODE_ROWS = 16

VMEM = pl.BlockSpec(memory_space=pltpu.VMEM)
SMEM = pl.BlockSpec(memory_space=pltpu.SMEM)
ANY = pl.BlockSpec(memory_space=pl.ANY)
F32 = jnp.float32
BF16 = jnp.bfloat16
HIGHEST = lax.Precision.HIGHEST
NT = (((1,), (1,)), ((), ()))


def call(body, outs, args, smem_in=(), smem_out=(), any_in=(), scratch=()):
    single = not isinstance(outs, (list, tuple))
    shapes = [outs] if single else list(outs)
    result = pl.pallas_call(
        body,
        out_shape=shapes,
        in_specs=[
            SMEM if i in smem_in else ANY if i in any_in else VMEM for i in range(len(args))
        ],
        out_specs=[SMEM if i in smem_out else VMEM for i in range(len(shapes))],
        scratch_shapes=list(scratch),
        compiler_params=pltpu.CompilerParams(vmem_limit_bytes=48 * 2**20),
    )(*args)
    return result[0] if single else result


def sds(shape, dtype):
    return jax.ShapeDtypeStruct(shape, dtype)


def at_block(index):
    return pl.ds(pl.multiple_of(index * BLOCK, BLOCK), BLOCK)


def eye_mask(size):
    return lax.broadcasted_iota(jnp.int32, (size, size), 0) == lax.broadcasted_iota(
        jnp.int32, (size, size), 1
    )


def halves(value):
    high = value.astype(BF16)
    low = (value - high.astype(F32)).astype(BF16)
    return high, low


def pack(tile):
    return jnp.concatenate(halves(tile), axis=0)


def scale_of(power, part):
    return jnp.exp2(power) * (part * (1.0 / PART_TOP))


def encode(values):
    most = jnp.maximum(jnp.max(jnp.abs(values), axis=0, keepdims=True), 1e-30)
    power = jnp.floor(jnp.log2(most)) + 1.0
    part = jnp.floor(most * jnp.exp2(-power) * PART_TOP) + 1.0
    steps = jnp.floor(values * (CODE_TOP / scale_of(power, part)) + 0.5)
    steps = jnp.minimum(jnp.maximum(steps, -CODE_TOP), CODE_TOP)
    return steps.astype(jnp.int32).astype(jnp.int16), power, part


def decode(steps, scale):
    return steps.astype(jnp.int32).astype(F32) * (scale * (1.0 / CODE_TOP))


def as_rows(powers, parts, count):
    fill = jnp.zeros((count // 2 - len(powers), BLOCK), F32)
    fill = [fill] if fill.shape[0] else []
    rows = jnp.concatenate([*powers, *fill, *parts, *fill], axis=0)
    return rows.astype(jnp.int32).astype(jnp.int16)


def scale_rows(rows):
    rows = rows.astype(jnp.int32).astype(F32)
    half = rows.shape[0] // 2
    return scale_of(rows[:half], rows[half:])


def row_at(rows, place):
    if isinstance(place, int):
        return rows[place : place + 1, :]
    line = rows[:1, :]
    for i in range(1, rows.shape[0]):
        line = jnp.where(place == i, rows[i : i + 1, :], line)
    return line


def product(packed, values):
    left = jnp.concatenate(halves(values), axis=0)
    both = jnp.dot(jnp.concatenate([left, left], axis=1), packed, preferred_element_type=F32)
    count = values.shape[0]
    return both[:count] + both[count:]


def thirds(value):
    high = value.astype(BF16)
    rest = value - high.astype(F32)
    middle = rest.astype(BF16)
    low = (rest - middle.astype(F32)).astype(BF16)
    return jnp.concatenate([high, middle, low], axis=0)


def gram(parts, n):
    cross = lax.dot_general(parts, parts, NT, preferred_element_type=F32)
    count = parts.shape[0] // n
    pairs = sorted(((i, j) for i in range(count) for j in range(count)), key=lambda p: -p[0] - p[1])
    total = None
    for i, j in pairs:
        piece = cross[i * n : (i + 1) * n, j * n : (j + 1) * n]
        total = piece if total is None else total + piece
    return total


def times(left, parts):
    m = left.shape[0]
    left = jnp.concatenate(halves(left), axis=0)
    both = jnp.dot(jnp.concatenate([left, left], axis=1), parts, preferred_element_type=F32)
    return both[m:] + both[:m]


def lower_inverse(matrix, step=8):
    n = matrix.shape[0]
    state = jnp.concatenate([matrix, eye_mask(n).astype(F32)], axis=1)
    done = []
    for j in range(0, n, step):
        top = j // 8 * 8
        if top > n - state.shape[0]:
            done.append(state[:8])
            state = state[8:]
        base = j - top
        rows = lax.broadcasted_iota(jnp.int32, state.shape, 0)
        columns = [jnp.broadcast_to(state[:, j + i : j + i + 1], state.shape) for i in range(step)]
        lines = [state[base + i : base + i + 1, :] for i in range(step)]
        pivot = [[columns[k][base + i : base + i + 1, :] for k in range(step)] for i in range(step)]
        for i in range(step):
            if i % 2 == 0:
                first, cross, second = pivot[i][i], pivot[i][i + 1], pivot[i + 1][i + 1]
                reciprocals = (1.0 / first, first / (first * second - cross * cross))
            reciprocal = reciprocals[i % 2]
            scaled = lines[i] * reciprocal
            ratio = [pivot[i][k] * reciprocal for k in range(step)]
            for k in range(i + 1, step):
                lines[k] = lines[k] - pivot[k][i] * scaled
                columns[k] = columns[k] - columns[i] * ratio[k]
                for m in range(i + 1, step):
                    pivot[k][m] = pivot[k][m] - pivot[k][i] * ratio[m]
            state = state - jnp.where(rows > base + i, columns[i], 0.0) * scaled
    state = jnp.concatenate([*done, state], axis=0)
    pivots = jnp.sum(jnp.where(eye_mask(n), state[:, :n], 0.0), axis=1, keepdims=True)
    return state[:, n:] / jnp.sqrt(pivots)


def both_columns(core, own, other):
    first = core == 0
    return jnp.concatenate(
        [jnp.where(first, own, other), jnp.where(first, other, own)], axis=0
    )


def plan_body(dims, me, *refs):
    row_count, capacity, slots, blocks_here = dims
    lists, (emb, after, idx) = refs[:row_count], refs[row_count : row_count + 3]
    sends = refs[row_count + 3 :]
    row = me[0]

    for i in range(slots):
        for line in (0, 1, 2, 4, 5):
            idx[line, i] = 0

    def ranked(listed, want, write):
        count = listed[2, 0]

        def step(s, counts):
            near = listed[0, s]
            far = listed[1, s]
            return write(s, near, far, far // blocks_here, s < count, counts)

        if slots <= 8:
            counts = (0,) * want
            for s in range(slots):
                counts = step(s, counts)
        else:
            lax.fori_loop(0, slots, step, (0,) * want)

    def write_own(s, near, far, owner, live, counts):
        shift = lax.rem(owner - row + row_count, row_count)
        rank = functools.reduce(
            lambda total, k: total + jnp.where(shift == k, counts[k], 0), range(row_count), 0
        )

        @pl.when(live)
        def _():
            slot = shift * capacity + rank
            idx[0, slot] = near - row * blocks_here
            idx[1, slot] = far
            idx[2, slot] = 1

        return tuple(
            counts[k] + (live & (shift == k)).astype(jnp.int32) for k in range(row_count)
        )

    for k in range(row_count):
        if k == 0:
            ranked(lists[k], row_count, write_own)

        def write_in(s, near, far, owner, live, counts, k=k):
            hit = live & (owner == row)

            @pl.when(hit)
            def _():
                slot = k * capacity + counts[0]
                idx[4, slot] = far - row * blocks_here
                idx[5, slot] = near

            return (counts[0] + hit.astype(jnp.int32),)

        ranked(lists[k], 1, write_in)
    for k in range(1, row_count):
        for j in range(capacity):
            sends[k - 1][j * BLOCK : (j + 1) * BLOCK, :] = emb[at_block(idx[4, k * capacity + j]), :]


def squares(block):
    return jnp.sum(jnp.square(block.astype(F32)), axis=1, keepdims=True)


def partial_distance(left, right, left_sq, right_sq):
    inner = lax.dot_general(left, right, NT, preferred_element_type=F32)
    right_row = jnp.sum(jnp.where(eye_mask(BLOCK), right_sq, 0.0), axis=0, keepdims=True)
    return left_sq + right_row - 2.0 * inner


def self_distance_body(own_blocks, tile_count, me, emb, out):
    for i in range(own_blocks):
        block = emb[at_block(i * tile_count + me[1]), :]
        block_sq = squares(block)
        out[i * BLOCK : (i + 1) * BLOCK, :] = partial_distance(block, block, block_sq, block_sq)


def squares_body(emb, after, out):
    for b in range(out.shape[0] // BLOCK):
        part = slice(b * BLOCK, (b + 1) * BLOCK)
        out[part, :] = jnp.broadcast_to(squares(emb[part, :]), (BLOCK, BLOCK))


def pair_distance_body(row_count, capacity, idx, emb, own_squares, *refs):
    out = refs[-1]
    for k in range(row_count):
        for j in range(capacity):
            slot = k * capacity + j
            left = emb[at_block(idx[0, slot]), :]
            left_sq = own_squares[at_block(idx[0, slot]), :]
            if k == 0:
                right = emb[at_block(idx[4, j]), :]
                right_sq = own_squares[at_block(idx[4, j]), :]
            else:
                right = refs[k - 1][j * BLOCK : (j + 1) * BLOCK, :]
                right_sq = squares(right)
            part = slice(slot * BLOCK, (slot + 1) * BLOCK)
            out[part, :] = partial_distance(left, right, left_sq, right_sq)


def self_tile_body(own_blocks, mine, other, packed, sums):
    for i in range(own_blocks):
        part = slice(i * BLOCK, (i + 1) * BLOCK)
        tile = jnp.exp(-kernel_gamma * (mine[part, :] + other[part, :] - 2.0))
        tile = jnp.where(eye_mask(BLOCK), 0.0, tile)
        packed[i] = pack(tile)
        sums[i : i + 1, :] = jnp.sum(tile, axis=0, keepdims=True)


def pair_tile_body(dims, me, idx, mine, other, self_sums, codes, powers, parts, near_tiles, home_tiles, table, *sends):
    row_count, capacity, per_core, blocks_here, tile_count = dims
    row, tile_index, core = me[0], me[1], me[2]
    table[...] = jnp.zeros(table.shape, F32)
    for i in range(self_sums.shape[0]):
        table[pl.ds(row * blocks_here + i * tile_count + tile_index, 1), :] = self_sums[i : i + 1, :]

    def add(block, line):
        place = pl.ds(block, 1)
        table[place, :] = table[place, :] + line

    for k in range(row_count):
        tiles = []
        for j in range(capacity):
            slot = k * capacity + j
            part = slice(slot * BLOCK, (slot + 1) * BLOCK)
            tile = jnp.exp(-kernel_gamma * (mine[part, :] + other[part, :] - 2.0))
            tile = jnp.where(idx[2, slot] > 0, tile, 0.0)
            turned = tile.T
            near_tiles[slot] = pack(turned)
            add(row * blocks_here + idx[0, slot], jnp.sum(turned, axis=0, keepdims=True))
            add(idx[1, slot], jnp.sum(tile, axis=0, keepdims=True))
            if k == 0:
                home_tiles[j] = pack(tile)
            tiles.append(tile)
        if k > 0:
            lines = ([], [])
            for inner in range(per_core):
                at = slice(inner * BLOCK, (inner + 1) * BLOCK)
                steps, power, part = encode(jnp.where(core == 0, tiles[inner], tiles[per_core + inner]))
                sends[k - 1][at, :] = steps
                lines[0].append(power)
                lines[1].append(part)
            pick_columns(idx, k, row_count, capacity, codes, powers, parts, sends[k - 1], per_core * BLOCK, lines)


def encode_blocks(values, codes, powers, parts):
    for b in range(powers.shape[0]):
        at = slice(b * BLOCK, (b + 1) * BLOCK)
        steps, power, part = encode(values[:, at])
        codes[:, at] = steps
        powers[b : b + 1, :] = power
        parts[b : b + 1, :] = part


def start_body(values, codes, powers, parts):
    encode_blocks(values, codes, powers, parts)


def split_body(row_count, per_core, *refs):
    others = row_count - 1
    messages, outs = refs[:others], refs[-others:]
    for message, out in zip(messages, outs):
        scales = scale_rows(message[message.shape[0] - CODE_ROWS :, :])
        for inner in range(per_core):
            steps = message[inner * BLOCK : (inner + 1) * BLOCK, :]
            out[inner] = pack(decode(steps, scales[inner : inner + 1, :]))


def pick_columns(idx, k, row_count, capacity, codes, powers, parts, send, base, lines):
    count = codes.shape[0]
    back = row_count - k
    blocks = [idx[0, k * capacity + j] for j in range(capacity)]
    blocks += [idx[4, back * capacity + j] for j in range(capacity)]
    for place, block in enumerate(blocks):
        send[base + place * count : base + (place + 1) * count, :] = codes[:, at_block(block)]
        lines[0].append(powers[pl.ds(block, 1), :])
        lines[1].append(parts[pl.ds(block, 1), :])
    send[base + len(blocks) * count :, :] = as_rows(*lines, CODE_ROWS)


def add_product(out, block, packed, values):
    place = at_block(block)
    out[:, place] = out[:, place] + product(packed, values)


def apply_own(dims, me, idx, inverse, own, near_tiles, home_tiles, self_tiles, out):
    row_count, capacity, per_core, blocks_here, tile_count = dims
    row, tile_index = me[0], me[1]
    out[...] = jnp.zeros(out.shape, F32)

    def scaled(block):
        return own[:, at_block(block)] * inverse[pl.ds(row * blocks_here + block, 1), :]

    for i in range(blocks_here // tile_count):
        block = i * tile_count + tile_index
        add_product(out, block, self_tiles[i], scaled(block))
    for j in range(capacity):
        add_product(out, idx[0, j], near_tiles[j], scaled(idx[4, j]))
        add_product(out, idx[4, j], home_tiles[j], scaled(idx[0, j]))


def apply_far(dims, me, idx, inverse, received, base, near_tiles, sent, shared, out):
    row_count, capacity, per_core, blocks_here, tile_count = dims
    core = me[2]
    count = out.shape[0]
    lines = [scale_rows(message[message.shape[0] - CODE_ROWS :, :]) for message in received]
    first_line = base // BLOCK

    def arrived(k, place, block):
        steps = received[k - 1][pl.ds(pl.multiple_of(base + place * count, CODE_ROWS), count), :]
        rows = lines[k - 1][first_line : first_line + 2 * capacity, :]
        return decode(steps, row_at(rows, place) * inverse[pl.ds(block, 1), :])

    for k in range(1, row_count):
        for j in range(capacity):
            slot = k * capacity + j
            values = arrived(row_count - k, capacity + j, idx[1, slot])
            add_product(out, idx[0, slot], near_tiles[slot], values)
            inner = j % per_core
            if j < per_core:
                place = core * per_core + inner
                packed = sent[k - 1][inner]
            else:
                place = (1 - core) * per_core + inner
                packed = shared[k - 1][inner]
            slot = k * capacity + place
            add_product(out, idx[4, slot], packed, arrived(k, place, idx[5, slot]))


def first_own_body(dims, me, idx, mine, other, own, near_tiles, home_tiles, self_tiles, out, degree, inverse):
    total = mine[...] + other[...]
    degree[...] = total
    inverse[...] = 1.0 / jnp.sqrt(total)
    apply_own(dims, me, idx, inverse, own, near_tiles, home_tiles, self_tiles, out)


def first_far_body(dims, coded, me, idx, inverse, started, near_tiles, *refs):
    row_count, per_core = dims[0], dims[2]
    others = row_count - 1
    sent, shared, messages = refs[:others], refs[others : 2 * others], refs[2 * others : 3 * others]
    out, total = refs[3 * others :]
    total[...] = started[...]
    apply_far(dims, me, idx, inverse, messages, per_core * BLOCK, near_tiles, sent, shared, total)
    put_sum(coded, total, out)


def second_apply_body(dims, me, idx, inverse, after, own, home_tiles, self_tiles, near_tiles, *refs):
    others = dims[0] - 1
    sent, shared, received = refs[:others], refs[others : 2 * others], refs[2 * others : 3 * others]
    out = refs[-1]
    apply_own(dims, me, idx, inverse, own, near_tiles, home_tiles, self_tiles, out)
    apply_far(dims, me, idx, inverse, received, 0, near_tiles, sent, shared, out)


def send_sum_body(coded, total, after, out):
    put_sum(coded, total, out)


def put_sum(coded, total, out):
    if not coded:
        out[...] = total[...]
        return
    lines = ([], [])
    blocks_here = total.shape[1] // BLOCK
    for b in range(blocks_here):
        at = slice(b * BLOCK, (b + 1) * BLOCK)
        steps, power, part = encode(total[:, at])
        out[:, at] = steps
        lines[0].append(power)
        lines[1].append(part)
    out[:, blocks_here * BLOCK :] = as_rows(*lines, out.shape[0])


def take_sum(coded, me, blocks_here, inverse, mine, other, out):
    if coded:
        tail = blocks_here * BLOCK
        my_scales, other_scales = scale_rows(mine[:, tail:]), scale_rows(other[:, tail:])
    for b in range(blocks_here):
        at = slice(b * BLOCK, (b + 1) * BLOCK)
        row = inverse[pl.ds(me[0] * blocks_here + b, 1), :]
        if coded:
            line = slice(b, b + 1)
            value = decode(mine[:, at], my_scales[line]) + decode(other[:, at], other_scales[line])
        else:
            value = mine[:, at] + other[:, at]
        out[:, at] = value * row


def mapped_body(dims, coded, me, idx, inverse, mine, other, out, *refs):
    row_count, capacity, per_core, blocks_here, tile_count = dims
    sends, (codes, powers, parts) = refs[:-3], refs[-3:]
    take_sum(coded, me, blocks_here, inverse, mine, other, out)
    encode_blocks(out, codes, powers, parts)
    for k in range(1, row_count):
        pick_columns(idx, k, row_count, capacity, codes, powers, parts, sends[k - 1], 0, ([], []))


def last_mapped_body(blocks_here, coded, me, inverse, mine, other, after, out):
    take_sum(coded, me, blocks_here, inverse, mine, other, out)


def folded(square):
    half = square.shape[0] // 2
    return jnp.concatenate([square[:half], square[half:]], axis=1)


def unfolded(terms):
    total = functools.reduce(lambda total, term: total + term[...], terms[1:], terms[0][...])
    width = total.shape[1] // 2
    return jnp.concatenate([total[:, :width], total[:, width:]], axis=0)


def gram_body(me, own, other, out):
    full = both_columns(me[2], own[...], other[...])
    out[...] = folded(gram(pack(full), full.shape[0]))


def factor_body(after, *refs):
    refs[-1][...] = lower_inverse(unfolded(refs[:-1]))


def second_gram_body(me, factor, own, other, mapped, out):
    full = both_columns(me[2], own[...], other[...])
    parts = thirds(times(factor[...], pack(full)))
    mapped[...] = parts[: mapped.shape[0]]
    out[...] = folded(gram(parts, full.shape[0]))


def final_body(me, mapped, *refs):
    out = refs[-1]
    factor = lower_inverse(unfolded(refs[:-1]))
    own_cols = out.shape[0]
    part = jnp.where(me[2] == 0, factor[:own_cols], factor[own_cols:])
    out[...] = times(part, mapped[...])


def shift_by(value, axes, size, shift):
    return lax.ppermute(value, axes, [(i, (i + shift) % size) for i in range(size)])


def row_terms(value, row_count):
    return [value] + [shift_by(value, "rows", row_count, k) for k in range(1, row_count)]


def pair_step(value, name, flip):
    return lax.ppermute(value, name, [(i, i ^ flip) for i in range(lax.axis_size(name))])


def pair_sum(value, axes):
    terms = None
    steps = [(name, 1 << bit) for name in axes for bit in range((lax.axis_size(name) - 1).bit_length())]
    for name, flip in steps:
        if terms is not None:
            value = terms[0] + terms[1]
        terms = (value, pair_step(value, name, flip))
    return terms


def local(embeddings, start, pair_list, pair_count):
    row_count = lax.axis_size("rows")
    tile_count = lax.axis_size("tiles")
    core_count = lax.axis_size("cols")
    row_index = lax.axis_index("rows")
    tile_index = lax.axis_index("tiles")
    col_index = lax.axis_index("cols")
    me = jnp.stack([row_index, tile_index, col_index]).astype(jnp.int32)
    rows_here, half_features = embeddings.shape
    blocks_here = rows_here // BLOCK
    slots = pair_list.shape[2]
    capacity = slots // row_count
    per_core = capacity // core_count
    own_blocks = blocks_here // tile_count
    own_cols = start.shape[1]
    block_count = row_count * blocks_here
    others = range(1, row_count)

    own_list = jnp.concatenate(
        [pair_list[0], jnp.broadcast_to(pair_count[:, None], (1, slots))], axis=0
    )
    lists = row_terms(own_list, row_count)
    self_part = call(
        functools.partial(self_distance_body, own_blocks, tile_count),
        sds((own_blocks * BLOCK, BLOCK), F32),
        [me, embeddings],
        smem_in=(0,),
    )
    planned = call(
        functools.partial(plan_body, (row_count, capacity, slots, blocks_here)),
        [sds((6, slots), jnp.int32)] + [sds((capacity * BLOCK, half_features), BF16) for _ in others],
        [me, *lists, embeddings, self_part],
        smem_in=range(1 + row_count),
        any_in=(row_count + 2,),
        smem_out=(0,),
    )
    idx, sends = planned[0], planned[1:]
    far = [shift_by(sends[k - 1], "rows", row_count, -k) for k in others]

    self_other = shift_by(self_part, "cols", core_count, 1)
    self_tiles, self_sums = call(
        functools.partial(self_tile_body, own_blocks),
        [sds((own_blocks, 2 * BLOCK, BLOCK), BF16), sds((own_blocks, BLOCK), F32)],
        [self_part, self_other],
    )
    values = start.T
    code_shapes = [((own_cols, rows_here), jnp.int16), ((blocks_here, BLOCK), F32), ((blocks_here, BLOCK), F32)]
    start_codes = call(start_body, [sds(*shape) for shape in code_shapes], [values])
    code_scratch = [pltpu.VMEM(*shape) for shape in code_shapes]
    coded = tile_count == 2
    own_squares = call(squares_body, sds((rows_here, BLOCK), F32), [embeddings, idx], any_in=(1,))
    pair_part = call(
        functools.partial(pair_distance_body, row_count, capacity),
        sds((slots * BLOCK, BLOCK), F32),
        [idx, embeddings, own_squares, *far],
        smem_in=(0,),
    )
    pair_other = shift_by(pair_part, "cols", core_count, 1)

    dims = (row_count, capacity, per_core, blocks_here, tile_count)
    table = sds((block_count, BLOCK), F32)
    picked = 2 * capacity * own_cols
    tiles = call(
        functools.partial(pair_tile_body, dims),
        [sds((slots, 2 * BLOCK, BLOCK), BF16), sds((capacity, 2 * BLOCK, BLOCK), BF16), table]
        + [sds((per_core * BLOCK + picked + CODE_ROWS, BLOCK), jnp.int16) for _ in others],
        [me, idx, pair_part, pair_other, self_sums, *start_codes],
        smem_in=(0, 1),
    )
    near_tiles, home_tiles, degrees, sends = tiles[0], tiles[1], tiles[2], tiles[3:]
    degrees = functools.reduce(jnp.add, row_terms(degrees, row_count))
    degree_terms = pair_sum(degrees, ("tiles",))
    messages = [shift_by(sends[k - 1], "rows", row_count, k) for k in others]
    sent = call(
        functools.partial(split_body, row_count, per_core),
        [sds((per_core, 2 * BLOCK, BLOCK), BF16) for _ in others],
        [*messages, degree_terms[1]],
        any_in=(row_count - 1,),
    )
    shared = [shift_by(tile, "cols", core_count, 1) for tile in sent]

    block_shape = sds((own_cols, rows_here), F32)
    sum_shape = sds((own_cols, rows_here + BLOCK), jnp.int16) if coded else block_shape
    square = sds((2 * own_cols, 2 * own_cols), F32)
    folded_square = sds((own_cols, 4 * own_cols), F32)

    started, degree, inverse = call(
        functools.partial(first_own_body, dims),
        [block_shape, table, table],
        [me, idx, *degree_terms, values, near_tiles, home_tiles, self_tiles],
        smem_in=(0, 1),
    )
    part = call(
        functools.partial(first_far_body, dims, coded),
        sum_shape,
        [me, idx, inverse, started, near_tiles, *sent, *shared, *messages],
        smem_in=(0, 1),
        scratch=[pltpu.VMEM((own_cols, rows_here), F32)],
    )
    mine, other = pair_sum(part, ("tiles",))
    first = call(
        functools.partial(mapped_body, dims, coded),
        [block_shape] + [sds((picked + CODE_ROWS, BLOCK), jnp.int16) for _ in others],
        [me, idx, inverse, mine, other],
        smem_in=(0, 1),
        scratch=code_scratch,
    )
    mapped, sends = first[0], first[1:]
    received = [shift_by(sends[k - 1], "rows", row_count, k) for k in others]

    mapped_other = shift_by(mapped, "cols", core_count, 1)
    first_gram = call(gram_body, folded_square, [me, mapped, mapped_other], smem_in=(0,))
    part = call(
        functools.partial(second_apply_body, dims),
        block_shape,
        [me, idx, inverse, first_gram, mapped, home_tiles, self_tiles, near_tiles, *sent, *shared, *received],
        smem_in=(0, 1),
        any_in=(3,),
    )
    steps = (row_count - 1).bit_length()
    for bit in range(steps - 1):
        first_gram = first_gram + pair_step(first_gram, "rows", 1 << bit)
    part = call(functools.partial(send_sum_body, coded), sum_shape, [part, first_gram])
    gram_terms = (first_gram, pair_step(first_gram, "rows", 1 << (steps - 1)))
    mine, other = pair_sum(part, ("tiles",))
    second = call(
        functools.partial(last_mapped_body, blocks_here, coded),
        block_shape,
        [me, inverse, mine, other, gram_terms[1]],
        smem_in=(0,),
        any_in=(4,),
    )
    second_other = shift_by(second, "cols", core_count, 1)
    factor = call(factor_body, square, [second, *gram_terms], any_in=(0,))
    full, second_gram = call(
        second_gram_body,
        [sds((4 * own_cols, rows_here), BF16), folded_square],
        [me, factor, second, second_other],
        smem_in=(0,),
    )
    vectors = call(
        final_body, block_shape, [me, full, *row_terms(second_gram, row_count)], smem_in=(0,)
    )
    own_degree = lax.dynamic_slice_in_dim(degree, row_index * blocks_here, blocks_here, 0)
    return (vectors.T, own_degree.reshape(rows_here))


def solution(mesh):
    in_specs = (
        P(("groups", "rows"), "cols"),
        P(("groups", "rows"), "cols"),
        P(("groups", "rows", "tiles"), None, None),
        P(("groups", "rows", "tiles")),
    )
    out_specs = (P(("groups", "rows"), "cols"), P(("groups", "rows")))
    return jax.shard_map(local, mesh=mesh, in_specs=in_specs, out_specs=out_specs, check_vma=False)
```

```python
import functools

import jax
import jax.numpy as jnp
from jax import lax
from jax.experimental import pallas as pl
from jax.experimental.pallas import tpu as pltpu
from jax.sharding import PartitionSpec as P

BLOCK = 128
kernel_gamma = 14.0
CODE_TOP = 32767.0
PART_TOP = 16384.0
CODE_ROWS = 16

VMEM = pl.BlockSpec(memory_space=pltpu.VMEM)
SMEM = pl.BlockSpec(memory_space=pltpu.SMEM)
ANY = pl.BlockSpec(memory_space=pl.ANY)
F32 = jnp.float32
BF16 = jnp.bfloat16
HIGHEST = lax.Precision.HIGHEST
NT = (((1,), (1,)), ((), ()))


def call(body, outs, args, smem_in=(), smem_out=(), any_in=(), scratch=(), cost=0):
    single = not isinstance(outs, (list, tuple))
    shapes = [outs] if single else list(outs)
    result = pl.pallas_call(
        body,
        out_shape=shapes,
        in_specs=[
            SMEM if i in smem_in else ANY if i in any_in else VMEM for i in range(len(args))
        ],
        out_specs=[SMEM if i in smem_out else VMEM for i in range(len(shapes))],
        scratch_shapes=list(scratch),
        cost_estimate=pl.CostEstimate(flops=cost * 10**9, bytes_accessed=0, transcendentals=0)
        if cost
        else None,
        compiler_params=pltpu.CompilerParams(vmem_limit_bytes=48 * 2**20),
    )(*args)
    return result[0] if single else result


def sds(shape, dtype):
    return jax.ShapeDtypeStruct(shape, dtype)


def at_block(index):
    return pl.ds(pl.multiple_of(index * BLOCK, BLOCK), BLOCK)


def eye_mask(size):
    return lax.broadcasted_iota(jnp.int32, (size, size), 0) == lax.broadcasted_iota(
        jnp.int32, (size, size), 1
    )


def halves(value):
    high = value.astype(BF16)
    low = (value - high.astype(F32)).astype(BF16)
    return high, low


def pack(tile):
    return jnp.concatenate(halves(tile), axis=0)


def scale_of(power, part):
    return jnp.exp2(power) * (part * (1.0 / PART_TOP))


def encode(values):
    most = jnp.maximum(jnp.max(jnp.abs(values), axis=0, keepdims=True), 1e-30)
    power = jnp.floor(jnp.log2(most)) + 1.0
    part = jnp.floor(most * jnp.exp2(-power) * PART_TOP) + 1.0
    steps = jnp.floor(values * (CODE_TOP / scale_of(power, part)) + 0.5)
    steps = jnp.minimum(jnp.maximum(steps, -CODE_TOP), CODE_TOP)
    return steps.astype(jnp.int32).astype(jnp.int16), power, part


def decode(steps, scale):
    return steps.astype(jnp.int32).astype(F32) * (scale * (1.0 / CODE_TOP))


def as_rows(powers, parts, count):
    fill = jnp.zeros((count // 2 - len(powers), BLOCK), F32)
    fill = [fill] if fill.shape[0] else []
    rows = jnp.concatenate([*powers, *fill, *parts, *fill], axis=0)
    return rows.astype(jnp.int32).astype(jnp.int16)


def scale_rows(rows):
    rows = rows.astype(jnp.int32).astype(F32)
    half = rows.shape[0] // 2
    return scale_of(rows[:half], rows[half:])


def row_at(rows, place):
    if isinstance(place, int):
        return rows[place : place + 1, :]
    line = rows[:1, :]
    for i in range(1, rows.shape[0]):
        line = jnp.where(place == i, rows[i : i + 1, :], line)
    return line


def product(packed, values):
    left = jnp.concatenate(halves(values), axis=0)
    both = jnp.dot(jnp.concatenate([left, left], axis=1), packed, preferred_element_type=F32)
    count = values.shape[0]
    return both[:count] + both[count:]


def thirds(value):
    high = value.astype(BF16)
    rest = value - high.astype(F32)
    middle = rest.astype(BF16)
    low = (rest - middle.astype(F32)).astype(BF16)
    return jnp.concatenate([high, middle, low], axis=0)


def gram(parts, n):
    cross = lax.dot_general(parts, parts, NT, preferred_element_type=F32)
    count = parts.shape[0] // n
    pairs = sorted(((i, j) for i in range(count) for j in range(count)), key=lambda p: -p[0] - p[1])
    total = None
    for i, j in pairs:
        piece = cross[i * n : (i + 1) * n, j * n : (j + 1) * n]
        total = piece if total is None else total + piece
    return total


def times(left, parts):
    m = left.shape[0]
    left = jnp.concatenate(halves(left), axis=0)
    both = jnp.dot(jnp.concatenate([left, left], axis=1), parts, preferred_element_type=F32)
    return both[m:] + both[:m]


def lower_inverse(matrix, step=8):
    n = matrix.shape[0]
    state = jnp.concatenate([matrix, eye_mask(n).astype(F32)], axis=1)
    done = []
    for j in range(0, n, step):
        top = j // 8 * 8
        if top > n - state.shape[0]:
            done.append(state[:8])
            state = state[8:]
        base = j - top
        rows = lax.broadcasted_iota(jnp.int32, state.shape, 0)
        columns = [jnp.broadcast_to(state[:, j + i : j + i + 1], state.shape) for i in range(step)]
        lines = [state[base + i : base + i + 1, :] for i in range(step)]
        pivot = [[columns[k][base + i : base + i + 1, :] for k in range(step)] for i in range(step)]
        for i in range(step):
            if i % 2 == 0:
                first, cross, second = pivot[i][i], pivot[i][i + 1], pivot[i + 1][i + 1]
                reciprocals = (1.0 / first, first / (first * second - cross * cross))
            reciprocal = reciprocals[i % 2]
            scaled = lines[i] * reciprocal
            ratio = [pivot[i][k] * reciprocal for k in range(step)]
            for k in range(i + 1, step):
                lines[k] = lines[k] - pivot[k][i] * scaled
                columns[k] = columns[k] - columns[i] * ratio[k]
                for m in range(i + 1, step):
                    pivot[k][m] = pivot[k][m] - pivot[k][i] * ratio[m]
            state = state - jnp.where(rows > base + i, columns[i], 0.0) * scaled
    state = jnp.concatenate([*done, state], axis=0)
    pivots = jnp.sum(jnp.where(eye_mask(n), state[:, :n], 0.0), axis=1, keepdims=True)
    return state[:, n:] / jnp.sqrt(pivots)


def both_columns(core, own, other):
    first = core == 0
    return jnp.concatenate(
        [jnp.where(first, own, other), jnp.where(first, other, own)], axis=0
    )


def plan_body(dims, me, *refs):
    row_count, capacity, slots, blocks_here = dims
    lists, idx = refs[:row_count], refs[row_count]
    row = me[0]

    for i in range(slots):
        for line in (0, 1, 2, 4, 5):
            idx[line, i] = 0

    def ranked(listed, want, write):
        count = listed[2, 0]

        def step(s, counts):
            near = listed[0, s]
            far = listed[1, s]
            return write(s, near, far, far // blocks_here, s < count, counts)

        if slots <= 8:
            counts = (0,) * want
            for s in range(slots):
                counts = step(s, counts)
        else:
            lax.fori_loop(0, slots, step, (0,) * want)

    def write_own(s, near, far, owner, live, counts):
        shift = lax.rem(owner - row + row_count, row_count)
        rank = functools.reduce(
            lambda total, k: total + jnp.where(shift == k, counts[k], 0), range(row_count), 0
        )

        @pl.when(live)
        def _():
            slot = shift * capacity + rank
            idx[0, slot] = near - row * blocks_here
            idx[1, slot] = far
            idx[2, slot] = 1

        return tuple(
            counts[k] + (live & (shift == k)).astype(jnp.int32) for k in range(row_count)
        )

    for k in range(row_count):
        if k == 0:
            ranked(lists[k], row_count, write_own)

        def write_in(s, near, far, owner, live, counts, k=k):
            hit = live & (owner == row)

            @pl.when(hit)
            def _():
                slot = k * capacity + counts[0]
                idx[4, slot] = far - row * blocks_here
                idx[5, slot] = near

            return (counts[0] + hit.astype(jnp.int32),)

        ranked(lists[k], 1, write_in)

def pick_body(row_count, capacity, idx, emb, *sends):
    for k in range(1, row_count):
        for j in range(capacity):
            sends[k - 1][j * BLOCK : (j + 1) * BLOCK, :] = emb[at_block(idx[4, k * capacity + j]), :]


def squares(block):
    return jnp.sum(jnp.square(block.astype(F32)), axis=1, keepdims=True)


def partial_distance(left, right, left_sq, right_sq):
    inner = lax.dot_general(left, right, NT, preferred_element_type=F32)
    right_row = jnp.sum(jnp.where(eye_mask(BLOCK), right_sq, 0.0), axis=0, keepdims=True)
    return left_sq + right_row - 2.0 * inner


def self_distance_body(own_blocks, tile_count, me, emb, after, out):
    for i in range(own_blocks):
        block = emb[at_block(i * tile_count + me[1]), :]
        block_sq = squares(block)
        out[i * BLOCK : (i + 1) * BLOCK, :] = partial_distance(block, block, block_sq, block_sq)


def squares_body(emb, after, out):
    for b in range(out.shape[0] // BLOCK):
        part = slice(b * BLOCK, (b + 1) * BLOCK)
        out[part, :] = jnp.broadcast_to(squares(emb[part, :]), (BLOCK, BLOCK))


def pair_distance_body(row_count, capacity, idx, emb, own_squares, *refs):
    out = refs[-1]
    for k in range(row_count):
        for j in range(capacity):
            slot = k * capacity + j
            left = emb[at_block(idx[0, slot]), :]
            left_sq = own_squares[at_block(idx[0, slot]), :]
            if k == 0:
                right = emb[at_block(idx[4, j]), :]
                right_sq = own_squares[at_block(idx[4, j]), :]
            else:
                right = refs[k - 1][j * BLOCK : (j + 1) * BLOCK, :]
                right_sq = squares(right)
            part = slice(slot * BLOCK, (slot + 1) * BLOCK)
            out[part, :] = partial_distance(left, right, left_sq, right_sq)


def self_tile_body(own_blocks, mine, other, packed, sums):
    for i in range(own_blocks):
        part = slice(i * BLOCK, (i + 1) * BLOCK)
        tile = jnp.exp(-kernel_gamma * (mine[part, :] + other[part, :] - 2.0))
        tile = jnp.where(eye_mask(BLOCK), 0.0, tile)
        packed[i] = pack(tile)
        sums[i : i + 1, :] = jnp.sum(tile, axis=0, keepdims=True)


def pair_tile_body(dims, me, idx, mine, other, self_sums, codes, powers, parts, near_tiles, home_tiles, table, *sends):
    row_count, capacity, per_core, blocks_here, tile_count = dims
    row, tile_index, core = me[0], me[1], me[2]
    table[...] = jnp.zeros(table.shape, F32)
    for i in range(self_sums.shape[0]):
        table[pl.ds(row * blocks_here + i * tile_count + tile_index, 1), :] = self_sums[i : i + 1, :]

    def add(block, line):
        place = pl.ds(block, 1)
        table[place, :] = table[place, :] + line

    for k in range(row_count):
        tiles = []
        for j in range(capacity):
            slot = k * capacity + j
            part = slice(slot * BLOCK, (slot + 1) * BLOCK)
            tile = jnp.exp(-kernel_gamma * (mine[part, :] + other[part, :] - 2.0))
            tile = jnp.where(idx[2, slot] > 0, tile, 0.0)
            turned = tile.T
            near_tiles[slot] = pack(turned)
            add(row * blocks_here + idx[0, slot], jnp.sum(turned, axis=0, keepdims=True))
            add(idx[1, slot], jnp.sum(tile, axis=0, keepdims=True))
            if k == 0:
                home_tiles[j] = pack(tile)
            tiles.append(tile)
        if k > 0:
            lines = ([], [])
            for inner in range(per_core):
                at = slice(inner * BLOCK, (inner + 1) * BLOCK)
                steps, power, part = encode(jnp.where(core == 0, tiles[inner], tiles[per_core + inner]))
                sends[k - 1][at, :] = steps
                lines[0].append(power)
                lines[1].append(part)
            pick_columns(idx, k, row_count, capacity, codes, powers, parts, sends[k - 1], per_core * BLOCK, lines)


def encode_blocks(values, codes, powers, parts):
    for b in range(powers.shape[0]):
        at = slice(b * BLOCK, (b + 1) * BLOCK)
        steps, power, part = encode(values[:, at])
        codes[:, at] = steps
        powers[b : b + 1, :] = power
        parts[b : b + 1, :] = part


def start_body(values, codes, powers, parts):
    encode_blocks(values, codes, powers, parts)


def split_body(row_count, per_core, *refs):
    others = row_count - 1
    messages, outs = refs[:others], refs[-others:]
    for message, out in zip(messages, outs):
        scales = scale_rows(message[message.shape[0] - CODE_ROWS :, :])
        for inner in range(per_core):
            steps = message[inner * BLOCK : (inner + 1) * BLOCK, :]
            out[inner] = pack(decode(steps, scales[inner : inner + 1, :]))


def pick_columns(idx, k, row_count, capacity, codes, powers, parts, send, base, lines):
    count = codes.shape[0]
    back = row_count - k
    blocks = [idx[0, k * capacity + j] for j in range(capacity)]
    blocks += [idx[4, back * capacity + j] for j in range(capacity)]
    for place, block in enumerate(blocks):
        send[base + place * count : base + (place + 1) * count, :] = codes[:, at_block(block)]
        lines[0].append(powers[pl.ds(block, 1), :])
        lines[1].append(parts[pl.ds(block, 1), :])
    send[base + len(blocks) * count :, :] = as_rows(*lines, CODE_ROWS)


def add_product(out, block, packed, values):
    place = at_block(block)
    out[:, place] = out[:, place] + product(packed, values)


def apply_own(dims, me, idx, inverse, own, near_tiles, home_tiles, self_tiles, out):
    row_count, capacity, per_core, blocks_here, tile_count = dims
    row, tile_index = me[0], me[1]
    out[...] = jnp.zeros(out.shape, F32)

    def scaled(block):
        return own[:, at_block(block)] * inverse[pl.ds(row * blocks_here + block, 1), :]

    for i in range(blocks_here // tile_count):
        block = i * tile_count + tile_index
        add_product(out, block, self_tiles[i], scaled(block))
    for j in range(capacity):
        add_product(out, idx[0, j], near_tiles[j], scaled(idx[4, j]))
        add_product(out, idx[4, j], home_tiles[j], scaled(idx[0, j]))


def apply_far(dims, me, idx, inverse, received, base, near_tiles, sent, shared, out):
    row_count, capacity, per_core, blocks_here, tile_count = dims
    core = me[2]
    count = out.shape[0]
    lines = [scale_rows(message[message.shape[0] - CODE_ROWS :, :]) for message in received]
    first_line = base // BLOCK

    def arrived(k, place, block):
        steps = received[k - 1][pl.ds(pl.multiple_of(base + place * count, CODE_ROWS), count), :]
        rows = lines[k - 1][first_line : first_line + 2 * capacity, :]
        return decode(steps, row_at(rows, place) * inverse[pl.ds(block, 1), :])

    for k in range(1, row_count):
        for j in range(capacity):
            slot = k * capacity + j
            values = arrived(row_count - k, capacity + j, idx[1, slot])
            add_product(out, idx[0, slot], near_tiles[slot], values)
            inner = j % per_core
            if j < per_core:
                place = core * per_core + inner
                packed = sent[k - 1][inner]
            else:
                place = (1 - core) * per_core + inner
                packed = shared[k - 1][inner]
            slot = k * capacity + place
            add_product(out, idx[4, slot], packed, arrived(k, place, idx[5, slot]))


def first_own_body(dims, me, idx, mine, other, own, near_tiles, home_tiles, self_tiles, out, degree, inverse):
    total = mine[...] + other[...]
    degree[...] = total
    inverse[...] = 1.0 / jnp.sqrt(total)
    apply_own(dims, me, idx, inverse, own, near_tiles, home_tiles, self_tiles, out)


def first_far_body(dims, coded, me, idx, inverse, started, near_tiles, *refs):
    row_count, per_core = dims[0], dims[2]
    others = row_count - 1
    sent, shared, messages = refs[:others], refs[others : 2 * others], refs[2 * others : 3 * others]
    out, total = refs[3 * others :]
    total[...] = started[...]
    apply_far(dims, me, idx, inverse, messages, per_core * BLOCK, near_tiles, sent, shared, total)
    put_sum(coded, total, out)


def second_apply_body(dims, me, idx, inverse, after, own, home_tiles, self_tiles, near_tiles, *refs):
    others = dims[0] - 1
    sent, shared, received = refs[:others], refs[others : 2 * others], refs[2 * others : 3 * others]
    out = refs[-1]
    apply_own(dims, me, idx, inverse, own, near_tiles, home_tiles, self_tiles, out)
    apply_far(dims, me, idx, inverse, received, 0, near_tiles, sent, shared, out)


def send_sum_body(coded, total, after, out):
    put_sum(coded, total, out)


def put_sum(coded, total, out):
    if not coded:
        out[...] = total[...]
        return
    lines = ([], [])
    blocks_here = total.shape[1] // BLOCK
    for b in range(blocks_here):
        at = slice(b * BLOCK, (b + 1) * BLOCK)
        steps, power, part = encode(total[:, at])
        out[:, at] = steps
        lines[0].append(power)
        lines[1].append(part)
    out[:, blocks_here * BLOCK :] = as_rows(*lines, out.shape[0])


def take_sum(coded, me, blocks_here, inverse, mine, other, out):
    if coded:
        tail = blocks_here * BLOCK
        my_scales, other_scales = scale_rows(mine[:, tail:]), scale_rows(other[:, tail:])
    for b in range(blocks_here):
        at = slice(b * BLOCK, (b + 1) * BLOCK)
        row = inverse[pl.ds(me[0] * blocks_here + b, 1), :]
        if coded:
            line = slice(b, b + 1)
            value = decode(mine[:, at], my_scales[line]) + decode(other[:, at], other_scales[line])
        else:
            value = mine[:, at] + other[:, at]
        out[:, at] = value * row


def mapped_body(dims, coded, me, idx, inverse, mine, other, out, *refs):
    row_count, capacity, per_core, blocks_here, tile_count = dims
    sends, (codes, powers, parts) = refs[:-3], refs[-3:]
    take_sum(coded, me, blocks_here, inverse, mine, other, out)
    encode_blocks(out, codes, powers, parts)
    for k in range(1, row_count):
        pick_columns(idx, k, row_count, capacity, codes, powers, parts, sends[k - 1], 0, ([], []))


def last_mapped_body(blocks_here, coded, me, inverse, mine, other, after, out):
    take_sum(coded, me, blocks_here, inverse, mine, other, out)


def folded(square):
    half = square.shape[0] // 2
    return jnp.concatenate([square[:half], square[half:]], axis=1)


def unfolded(terms):
    total = functools.reduce(lambda total, term: total + term[...], terms[1:], terms[0][...])
    width = total.shape[1] // 2
    return jnp.concatenate([total[:, :width], total[:, width:]], axis=0)


def gram_body(me, own, other, out):
    full = both_columns(me[2], own[...], other[...])
    out[...] = folded(gram(pack(full), full.shape[0]))


def factor_body(after, *refs):
    refs[-1][...] = lower_inverse(unfolded(refs[:-1]))


def second_gram_body(me, factor, own, other, mapped, out):
    full = both_columns(me[2], own[...], other[...])
    parts = thirds(times(factor[...], pack(full)))
    mapped[...] = parts[: mapped.shape[0]]
    out[...] = folded(gram(parts, full.shape[0]))


def final_body(me, mapped, *refs):
    out = refs[-1]
    factor = lower_inverse(unfolded(refs[:-1]))
    own_cols = out.shape[0]
    part = jnp.where(me[2] == 0, factor[:own_cols], factor[own_cols:])
    out[...] = times(part, mapped[...])


def shift_by(value, axes, size, shift):
    return lax.ppermute(value, axes, [(i, (i + shift) % size) for i in range(size)])


def row_terms(value, row_count):
    return [value] + [shift_by(value, "rows", row_count, k) for k in range(1, row_count)]


def pair_step(value, name, flip):
    return lax.ppermute(value, name, [(i, i ^ flip) for i in range(lax.axis_size(name))])


def pair_sum(value, axes):
    terms = None
    steps = [(name, 1 << bit) for name in axes for bit in range((lax.axis_size(name) - 1).bit_length())]
    for name, flip in steps:
        if terms is not None:
            value = terms[0] + terms[1]
        terms = (value, pair_step(value, name, flip))
    return terms


def local(embeddings, start, pair_list, pair_count):
    row_count = lax.axis_size("rows")
    tile_count = lax.axis_size("tiles")
    core_count = lax.axis_size("cols")
    row_index = lax.axis_index("rows")
    tile_index = lax.axis_index("tiles")
    col_index = lax.axis_index("cols")
    me = jnp.stack([row_index, tile_index, col_index]).astype(jnp.int32)
    rows_here, half_features = embeddings.shape
    blocks_here = rows_here // BLOCK
    slots = pair_list.shape[2]
    capacity = slots // row_count
    per_core = capacity // core_count
    own_blocks = blocks_here // tile_count
    own_cols = start.shape[1]
    block_count = row_count * blocks_here
    others = range(1, row_count)

    own_list = jnp.concatenate(
        [pair_list[0], jnp.broadcast_to(pair_count[:, None], (1, slots))], axis=0
    )
    lists = row_terms(own_list, row_count)
    idx = call(
        functools.partial(plan_body, (row_count, capacity, slots, blocks_here)),
        sds((6, slots), jnp.int32),
        [me, *lists],
        smem_in=range(1 + row_count),
        smem_out=(0,),
        cost=3,
    )
    sends = call(
        functools.partial(pick_body, row_count, capacity),
        [sds((capacity * BLOCK, half_features), BF16) for _ in others],
        [idx, embeddings],
        smem_in=(0,),
    )
    far = [shift_by(sends[k - 1], "rows", row_count, -k) for k in others]

    self_part = call(
        functools.partial(self_distance_body, own_blocks, tile_count),
        sds((own_blocks * BLOCK, BLOCK), F32),
        [me, embeddings, idx],
        smem_in=(0,),
        any_in=(2,),
    )
    self_other = shift_by(self_part, "cols", core_count, 1)
    self_tiles, self_sums = call(
        functools.partial(self_tile_body, own_blocks),
        [sds((own_blocks, 2 * BLOCK, BLOCK), BF16), sds((own_blocks, BLOCK), F32)],
        [self_part, self_other],
    )
    values = start.T
    code_shapes = [((own_cols, rows_here), jnp.int16), ((blocks_here, BLOCK), F32), ((blocks_here, BLOCK), F32)]
    start_codes = call(start_body, [sds(*shape) for shape in code_shapes], [values])
    code_scratch = [pltpu.VMEM(*shape) for shape in code_shapes]
    coded = tile_count == 2
    own_squares = call(squares_body, sds((rows_here, BLOCK), F32), [embeddings, idx], any_in=(1,))
    pair_part = call(
        functools.partial(pair_distance_body, row_count, capacity),
        sds((slots * BLOCK, BLOCK), F32),
        [idx, embeddings, own_squares, *far],
        smem_in=(0,),
    )
    pair_other = shift_by(pair_part, "cols", core_count, 1)

    dims = (row_count, capacity, per_core, blocks_here, tile_count)
    table = sds((block_count, BLOCK), F32)
    picked = 2 * capacity * own_cols
    tiles = call(
        functools.partial(pair_tile_body, dims),
        [sds((slots, 2 * BLOCK, BLOCK), BF16), sds((capacity, 2 * BLOCK, BLOCK), BF16), table]
        + [sds((per_core * BLOCK + picked + CODE_ROWS, BLOCK), jnp.int16) for _ in others],
        [me, idx, pair_part, pair_other, self_sums, *start_codes],
        smem_in=(0, 1),
    )
    near_tiles, home_tiles, degrees, sends = tiles[0], tiles[1], tiles[2], tiles[3:]
    degrees = functools.reduce(jnp.add, row_terms(degrees, row_count))
    degree_terms = pair_sum(degrees, ("tiles",))
    messages = [shift_by(sends[k - 1], "rows", row_count, k) for k in others]
    sent = call(
        functools.partial(split_body, row_count, per_core),
        [sds((per_core, 2 * BLOCK, BLOCK), BF16) for _ in others],
        [*messages, degree_terms[1]],
        any_in=(row_count - 1,),
    )
    shared = [shift_by(tile, "cols", core_count, 1) for tile in sent]

    block_shape = sds((own_cols, rows_here), F32)
    sum_shape = sds((own_cols, rows_here + BLOCK), jnp.int16) if coded else block_shape
    square = sds((2 * own_cols, 2 * own_cols), F32)
    folded_square = sds((own_cols, 4 * own_cols), F32)

    started, degree, inverse = call(
        functools.partial(first_own_body, dims),
        [block_shape, table, table],
        [me, idx, *degree_terms, values, near_tiles, home_tiles, self_tiles],
        smem_in=(0, 1),
    )
    part = call(
        functools.partial(first_far_body, dims, coded),
        sum_shape,
        [me, idx, inverse, started, near_tiles, *sent, *shared, *messages],
        smem_in=(0, 1),
        scratch=[pltpu.VMEM((own_cols, rows_here), F32)],
    )
    mine, other = pair_sum(part, ("tiles",))
    first = call(
        functools.partial(mapped_body, dims, coded),
        [block_shape] + [sds((picked + CODE_ROWS, BLOCK), jnp.int16) for _ in others],
        [me, idx, inverse, mine, other],
        smem_in=(0, 1),
        scratch=code_scratch,
    )
    mapped, sends = first[0], first[1:]
    received = [shift_by(sends[k - 1], "rows", row_count, k) for k in others]

    mapped_other = shift_by(mapped, "cols", core_count, 1)
    first_gram = call(gram_body, folded_square, [me, mapped, mapped_other], smem_in=(0,))
    part = call(
        functools.partial(second_apply_body, dims),
        block_shape,
        [me, idx, inverse, first_gram, mapped, home_tiles, self_tiles, near_tiles, *sent, *shared, *received],
        smem_in=(0, 1),
        any_in=(3,),
    )
    steps = (row_count - 1).bit_length()
    for bit in range(steps - 1):
        first_gram = first_gram + pair_step(first_gram, "rows", 1 << bit)
    part = call(functools.partial(send_sum_body, coded), sum_shape, [part, first_gram])
    gram_terms = (first_gram, pair_step(first_gram, "rows", 1 << (steps - 1)))
    mine, other = pair_sum(part, ("tiles",))
    second = call(
        functools.partial(last_mapped_body, blocks_here, coded),
        block_shape,
        [me, inverse, mine, other, gram_terms[1]],
        smem_in=(0,),
        any_in=(4,),
    )
    second_other = shift_by(second, "cols", core_count, 1)
    factor = call(factor_body, square, [second, *gram_terms], any_in=(0,))
    full, second_gram = call(
        second_gram_body,
        [sds((4 * own_cols, rows_here), BF16), folded_square],
        [me, factor, second, second_other],
        smem_in=(0,),
    )
    vectors = call(
        final_body, block_shape, [me, full, *row_terms(second_gram, row_count)], smem_in=(0,)
    )
    own_degree = lax.dynamic_slice_in_dim(degree, row_index * blocks_here, blocks_here, 0)
    return (vectors.T, own_degree.reshape(rows_here))


def solution(mesh):
    in_specs = (
        P(("groups", "rows"), "cols"),
        P(("groups", "rows"), "cols"),
        P(("groups", "rows", "tiles"), None, None),
        P(("groups", "rows", "tiles")),
    )
    out_specs = (P(("groups", "rows"), "cols"), P(("groups", "rows")))
    return jax.shard_map(local, mesh=mesh, in_specs=in_specs, out_specs=out_specs, check_vma=False)
```

```python
import functools

import jax
import jax.numpy as jnp
from jax import lax
from jax.experimental import pallas as pl
from jax.experimental.pallas import tpu as pltpu
from jax.sharding import PartitionSpec as P

BLOCK = 128
kernel_gamma = 14.0
CODE_TOP = 32767.0
PART_TOP = 16384.0
CODE_ROWS = 16

VMEM = pl.BlockSpec(memory_space=pltpu.VMEM)
SMEM = pl.BlockSpec(memory_space=pltpu.SMEM)
ANY = pl.BlockSpec(memory_space=pl.ANY)
F32 = jnp.float32
BF16 = jnp.bfloat16
HIGHEST = lax.Precision.HIGHEST
NT = (((1,), (1,)), ((), ()))


def call(body, outs, args, smem_in=(), smem_out=(), any_in=(), scratch=(), vmem=48):
    single = not isinstance(outs, (list, tuple))
    shapes = [outs] if single else list(outs)
    result = pl.pallas_call(
        body,
        out_shape=shapes,
        in_specs=[
            SMEM if i in smem_in else ANY if i in any_in else VMEM for i in range(len(args))
        ],
        out_specs=[SMEM if i in smem_out else VMEM for i in range(len(shapes))],
        scratch_shapes=list(scratch),
        compiler_params=pltpu.CompilerParams(vmem_limit_bytes=vmem * 2**20),
    )(*args)
    return result[0] if single else result


def sds(shape, dtype):
    return jax.ShapeDtypeStruct(shape, dtype)


def at_block(index):
    return pl.ds(pl.multiple_of(index * BLOCK, BLOCK), BLOCK)


def eye_mask(size):
    return lax.broadcasted_iota(jnp.int32, (size, size), 0) == lax.broadcasted_iota(
        jnp.int32, (size, size), 1
    )


def halves(value):
    high = value.astype(BF16)
    low = (value - high.astype(F32)).astype(BF16)
    return high, low


def pack(tile):
    return jnp.concatenate(halves(tile), axis=0)


def scale_of(power, part):
    return jnp.exp2(power) * (part * (1.0 / PART_TOP))


def encode(values):
    most = jnp.maximum(jnp.max(jnp.abs(values), axis=0, keepdims=True), 1e-30)
    power = jnp.floor(jnp.log2(most)) + 1.0
    part = jnp.floor(most * jnp.exp2(-power) * PART_TOP) + 1.0
    steps = jnp.floor(values * (CODE_TOP / scale_of(power, part)) + 0.5)
    steps = jnp.minimum(jnp.maximum(steps, -CODE_TOP), CODE_TOP)
    return steps.astype(jnp.int32).astype(jnp.int16), power, part


def decode(steps, scale):
    return steps.astype(jnp.int32).astype(F32) * (scale * (1.0 / CODE_TOP))


def as_rows(powers, parts, count):
    fill = jnp.zeros((count // 2 - len(powers), BLOCK), F32)
    fill = [fill] if fill.shape[0] else []
    rows = jnp.concatenate([*powers, *fill, *parts, *fill], axis=0)
    return rows.astype(jnp.int32).astype(jnp.int16)


def scale_rows(rows):
    rows = rows.astype(jnp.int32).astype(F32)
    half = rows.shape[0] // 2
    return scale_of(rows[:half], rows[half:])


def row_at(rows, place):
    if isinstance(place, int):
        return rows[place : place + 1, :]
    line = rows[:1, :]
    for i in range(1, rows.shape[0]):
        line = jnp.where(place == i, rows[i : i + 1, :], line)
    return line


def product(packed, values):
    left = jnp.concatenate(halves(values), axis=0)
    both = jnp.dot(jnp.concatenate([left, left], axis=1), packed, preferred_element_type=F32)
    count = values.shape[0]
    return both[:count] + both[count:]


def thirds(value):
    high = value.astype(BF16)
    rest = value - high.astype(F32)
    middle = rest.astype(BF16)
    low = (rest - middle.astype(F32)).astype(BF16)
    return jnp.concatenate([high, middle, low], axis=0)


def gram(parts, n):
    cross = lax.dot_general(parts, parts, NT, preferred_element_type=F32)
    count = parts.shape[0] // n
    pairs = sorted(((i, j) for i in range(count) for j in range(count)), key=lambda p: -p[0] - p[1])
    total = None
    for i, j in pairs:
        piece = cross[i * n : (i + 1) * n, j * n : (j + 1) * n]
        total = piece if total is None else total + piece
    return total


def times(left, parts):
    m = left.shape[0]
    left = jnp.concatenate(halves(left), axis=0)
    both = jnp.dot(jnp.concatenate([left, left], axis=1), parts, preferred_element_type=F32)
    return both[m:] + both[:m]


def lower_inverse(matrix, step=8):
    n = matrix.shape[0]
    state = jnp.concatenate([matrix, eye_mask(n).astype(F32)], axis=1)
    done = []
    for j in range(0, n, step):
        top = j // 8 * 8
        if top > n - state.shape[0]:
            done.append(state[:8])
            state = state[8:]
        base = j - top
        rows = lax.broadcasted_iota(jnp.int32, state.shape, 0)
        columns = [jnp.broadcast_to(state[:, j + i : j + i + 1], state.shape) for i in range(step)]
        lines = [state[base + i : base + i + 1, :] for i in range(step)]
        pivot = [[columns[k][base + i : base + i + 1, :] for k in range(step)] for i in range(step)]
        for i in range(step):
            if i % 2 == 0:
                first, cross, second = pivot[i][i], pivot[i][i + 1], pivot[i + 1][i + 1]
                reciprocals = (1.0 / first, first / (first * second - cross * cross))
            reciprocal = reciprocals[i % 2]
            scaled = lines[i] * reciprocal
            ratio = [pivot[i][k] * reciprocal for k in range(step)]
            for k in range(i + 1, step):
                lines[k] = lines[k] - pivot[k][i] * scaled
                columns[k] = columns[k] - columns[i] * ratio[k]
                for m in range(i + 1, step):
                    pivot[k][m] = pivot[k][m] - pivot[k][i] * ratio[m]
            state = state - jnp.where(rows > base + i, columns[i], 0.0) * scaled
    state = jnp.concatenate([*done, state], axis=0)
    pivots = jnp.sum(jnp.where(eye_mask(n), state[:, :n], 0.0), axis=1, keepdims=True)
    return state[:, n:] / jnp.sqrt(pivots)


def both_columns(core, own, other):
    first = core == 0
    return jnp.concatenate(
        [jnp.where(first, own, other), jnp.where(first, other, own)], axis=0
    )


def quotient(value, size):
    if size & (size - 1) == 0:
        return lax.shift_right_logical(value, jnp.int32(size.bit_length() - 1))
    return lax.div(value, jnp.int32(size))


def remainder(value, size):
    if size & (size - 1) == 0:
        return lax.bitwise_and(value, jnp.int32(size - 1))
    return lax.rem(value, jnp.int32(size))


def plan_body(dims, me, lists, emb, idx, *refs):
    sends, arrived = refs[:-1], refs[-1]
    row_count, capacity, slots, blocks_here = dims
    row = me[0]
    for i in range(slots):
        for line in (0, 1, 2, 4, 5):
            idx[line, i] = 0

    def each(count, step, start):
        if slots <= 8:
            for s in range(slots):
                start = step(s, start)
        else:
            lax.fori_loop(0, slots, step, start)

    for k in range(row_count):
        source = remainder(row - k + row_count, row_count)
        live_count = lists[source, 2, 0]

        def step(s, counts, k=k, source=source, live_count=live_count):
            near = lists[source, 0, s]
            far = lists[source, 1, s]
            owner = quotient(far, blocks_here)
            live = s < live_count
            hit = live & (owner == row)
            slot = jnp.where(hit, k * capacity + counts[0], slots)
            idx[4, slot] = far - row * blocks_here
            idx[5, slot] = near
            if k > 0:
                return (counts[0] + hit.astype(jnp.int32),)
            shift = remainder(owner - row + row_count, row_count)
            rank = counts[1]
            for d in range(1, row_count):
                rank = jnp.where(shift == d, counts[1 + d], rank)
            slot = jnp.where(live, shift * capacity + rank, slots)
            idx[0, slot] = near - row * blocks_here
            idx[1, slot] = far
            idx[2, slot] = 1
            more = tuple(
                counts[1 + d] + (live & (shift == d)).astype(jnp.int32) for d in range(row_count)
            )
            return (counts[0] + hit.astype(jnp.int32), *more)

        each(slots, step, (jnp.int32(0),) * (1 + row_count if k == 0 else 1))
    copies = []
    for k in range(1, row_count):
        for j in range(capacity):
            slot = k * capacity + j
            copies.append(
                pltpu.make_async_copy(
                    emb.at[at_block(idx[4, slot]), :],
                    sends[k - 1].at[j * BLOCK : (j + 1) * BLOCK, :],
                    arrived.at[slot - capacity],
                )
            )
    for copy in copies:
        copy.start()
    for copy in copies:
        copy.wait()


def squares(block):
    return jnp.sum(jnp.square(block.astype(F32)), axis=1, keepdims=True)


def partial_distance(left, right, left_sq, right_sq):
    inner = lax.dot_general(left, right, NT, preferred_element_type=F32)
    right_row = jnp.sum(jnp.where(eye_mask(BLOCK), right_sq, 0.0), axis=0, keepdims=True)
    return left_sq + right_row - 2.0 * inner


def self_distance_body(own_blocks, tile_count, me, emb, after, out):
    for i in range(own_blocks):
        block = emb[at_block(i * tile_count + me[1]), :]
        block_sq = squares(block)
        out[i * BLOCK : (i + 1) * BLOCK, :] = partial_distance(block, block, block_sq, block_sq)


def squares_body(emb, after, out):
    for b in range(out.shape[0] // BLOCK):
        part = slice(b * BLOCK, (b + 1) * BLOCK)
        out[part, :] = jnp.broadcast_to(squares(emb[part, :]), (BLOCK, BLOCK))


def pair_distance_body(row_count, capacity, idx, emb, own_squares, *refs):
    out = refs[-1]
    for k in range(row_count):
        for j in range(capacity):
            slot = k * capacity + j
            left = emb[at_block(idx[0, slot]), :]
            left_sq = own_squares[at_block(idx[0, slot]), :]
            if k == 0:
                right = emb[at_block(idx[4, j]), :]
                right_sq = own_squares[at_block(idx[4, j]), :]
            else:
                right = refs[k - 1][j * BLOCK : (j + 1) * BLOCK, :]
                right_sq = squares(right)
            part = slice(slot * BLOCK, (slot + 1) * BLOCK)
            out[part, :] = partial_distance(left, right, left_sq, right_sq)


def self_tile_body(own_blocks, mine, other, packed, sums):
    for i in range(own_blocks):
        part = slice(i * BLOCK, (i + 1) * BLOCK)
        tile = jnp.exp(-kernel_gamma * (mine[part, :] + other[part, :] - 2.0))
        tile = jnp.where(eye_mask(BLOCK), 0.0, tile)
        packed[i] = pack(tile)
        sums[i : i + 1, :] = jnp.sum(tile, axis=0, keepdims=True)


def pair_tile_body(dims, me, idx, mine, other, self_sums, codes, powers, parts, near_tiles, home_tiles, table, *sends):
    row_count, capacity, per_core, blocks_here, tile_count = dims
    row, tile_index, core = me[0], me[1], me[2]
    table[...] = jnp.zeros(table.shape, F32)
    for i in range(self_sums.shape[0]):
        table[pl.ds(row * blocks_here + i * tile_count + tile_index, 1), :] = self_sums[i : i + 1, :]

    def add(block, line):
        place = pl.ds(block, 1)
        table[place, :] = table[place, :] + line

    for k in range(row_count):
        tiles = []
        for j in range(capacity):
            slot = k * capacity + j
            part = slice(slot * BLOCK, (slot + 1) * BLOCK)
            tile = jnp.exp(-kernel_gamma * (mine[part, :] + other[part, :] - 2.0))
            tile = jnp.where(idx[2, slot] > 0, tile, 0.0)
            turned = tile.T
            near_tiles[slot] = pack(turned)
            add(row * blocks_here + idx[0, slot], jnp.sum(turned, axis=0, keepdims=True))
            add(idx[1, slot], jnp.sum(tile, axis=0, keepdims=True))
            if k == 0:
                home_tiles[j] = pack(tile)
            tiles.append(tile)
        if k > 0:
            lines = ([], [])
            for inner in range(per_core):
                at = slice(inner * BLOCK, (inner + 1) * BLOCK)
                steps, power, part = encode(jnp.where(core == 0, tiles[inner], tiles[per_core + inner]))
                sends[k - 1][at, :] = steps
                lines[0].append(power)
                lines[1].append(part)
            pick_columns(idx, k, row_count, capacity, codes, powers, parts, sends[k - 1], per_core * BLOCK, lines)


def encode_blocks(values, codes, powers, parts):
    for b in range(powers.shape[0]):
        at = slice(b * BLOCK, (b + 1) * BLOCK)
        steps, power, part = encode(values[:, at])
        codes[:, at] = steps
        powers[b : b + 1, :] = power
        parts[b : b + 1, :] = part


def start_body(values, codes, powers, parts):
    encode_blocks(values, codes, powers, parts)


def split_body(row_count, per_core, *refs):
    others = row_count - 1
    messages, outs = refs[:others], refs[-others:]
    for message, out in zip(messages, outs):
        scales = scale_rows(message[message.shape[0] - CODE_ROWS :, :])
        for inner in range(per_core):
            steps = message[inner * BLOCK : (inner + 1) * BLOCK, :]
            out[inner] = pack(decode(steps, scales[inner : inner + 1, :]))


def pick_columns(idx, k, row_count, capacity, codes, powers, parts, send, base, lines):
    count = codes.shape[0]
    back = row_count - k
    blocks = [idx[0, k * capacity + j] for j in range(capacity)]
    blocks += [idx[4, back * capacity + j] for j in range(capacity)]
    for place, block in enumerate(blocks):
        send[base + place * count : base + (place + 1) * count, :] = codes[:, at_block(block)]
        lines[0].append(powers[pl.ds(block, 1), :])
        lines[1].append(parts[pl.ds(block, 1), :])
    send[base + len(blocks) * count :, :] = as_rows(*lines, CODE_ROWS)


def add_product(out, block, packed, values):
    place = at_block(block)
    out[:, place] = out[:, place] + product(packed, values)


def apply_own(dims, me, idx, inverse, own, near_tiles, home_tiles, self_tiles, out):
    row_count, capacity, per_core, blocks_here, tile_count = dims
    row, tile_index = me[0], me[1]
    out[...] = jnp.zeros(out.shape, F32)

    def scaled(block):
        return own[:, at_block(block)] * inverse[pl.ds(row * blocks_here + block, 1), :]

    for i in range(blocks_here // tile_count):
        block = i * tile_count + tile_index
        add_product(out, block, self_tiles[i], scaled(block))
    for j in range(capacity):
        add_product(out, idx[0, j], near_tiles[j], scaled(idx[4, j]))
        add_product(out, idx[4, j], home_tiles[j], scaled(idx[0, j]))


def apply_far(dims, me, idx, inverse, received, base, near_tiles, sent, shared, out):
    row_count, capacity, per_core, blocks_here, tile_count = dims
    core = me[2]
    count = out.shape[0]
    lines = [scale_rows(message[message.shape[0] - CODE_ROWS :, :]) for message in received]
    first_line = base // BLOCK

    def arrived(k, place, block):
        steps = received[k - 1][pl.ds(pl.multiple_of(base + place * count, CODE_ROWS), count), :]
        rows = lines[k - 1][first_line : first_line + 2 * capacity, :]
        return decode(steps, row_at(rows, place) * inverse[pl.ds(block, 1), :])

    for k in range(1, row_count):
        for j in range(capacity):
            slot = k * capacity + j
            values = arrived(row_count - k, capacity + j, idx[1, slot])
            add_product(out, idx[0, slot], near_tiles[slot], values)
            inner = j % per_core
            if j < per_core:
                place = core * per_core + inner
                packed = sent[k - 1][inner]
            else:
                place = (1 - core) * per_core + inner
                packed = shared[k - 1][inner]
            slot = k * capacity + place
            add_product(out, idx[4, slot], packed, arrived(k, place, idx[5, slot]))


def first_own_body(dims, me, idx, mine, other, own, near_tiles, home_tiles, self_tiles, out, degree, inverse):
    total = mine[...] + other[...]
    degree[...] = total
    inverse[...] = 1.0 / jnp.sqrt(total)
    apply_own(dims, me, idx, inverse, own, near_tiles, home_tiles, self_tiles, out)


def first_far_body(dims, coded, me, idx, inverse, started, near_tiles, *refs):
    row_count, per_core = dims[0], dims[2]
    others = row_count - 1
    sent, shared, messages = refs[:others], refs[others : 2 * others], refs[2 * others : 3 * others]
    out, total = refs[3 * others :]
    total[...] = started[...]
    apply_far(dims, me, idx, inverse, messages, per_core * BLOCK, near_tiles, sent, shared, total)
    put_sum(coded, total, out)


def second_apply_body(dims, me, idx, inverse, after, own, home_tiles, self_tiles, near_tiles, *refs):
    others = dims[0] - 1
    sent, shared, received = refs[:others], refs[others : 2 * others], refs[2 * others : 3 * others]
    out = refs[-1]
    apply_own(dims, me, idx, inverse, own, near_tiles, home_tiles, self_tiles, out)
    apply_far(dims, me, idx, inverse, received, 0, near_tiles, sent, shared, out)


def send_sum_body(coded, total, after, out):
    put_sum(coded, total, out)


def put_sum(coded, total, out):
    if not coded:
        out[...] = total[...]
        return
    lines = ([], [])
    blocks_here = total.shape[1] // BLOCK
    for b in range(blocks_here):
        at = slice(b * BLOCK, (b + 1) * BLOCK)
        steps, power, part = encode(total[:, at])
        out[:, at] = steps
        lines[0].append(power)
        lines[1].append(part)
    out[:, blocks_here * BLOCK :] = as_rows(*lines, out.shape[0])


def take_sum(coded, me, blocks_here, inverse, mine, other, out):
    if coded:
        tail = blocks_here * BLOCK
        my_scales, other_scales = scale_rows(mine[:, tail:]), scale_rows(other[:, tail:])
    for b in range(blocks_here):
        at = slice(b * BLOCK, (b + 1) * BLOCK)
        row = inverse[pl.ds(me[0] * blocks_here + b, 1), :]
        if coded:
            line = slice(b, b + 1)
            value = decode(mine[:, at], my_scales[line]) + decode(other[:, at], other_scales[line])
        else:
            value = mine[:, at] + other[:, at]
        out[:, at] = value * row


def mapped_body(dims, coded, me, idx, inverse, mine, other, out, *refs):
    row_count, capacity, per_core, blocks_here, tile_count = dims
    sends, (codes, powers, parts) = refs[:-3], refs[-3:]
    take_sum(coded, me, blocks_here, inverse, mine, other, out)
    encode_blocks(out, codes, powers, parts)
    for k in range(1, row_count):
        pick_columns(idx, k, row_count, capacity, codes, powers, parts, sends[k - 1], 0, ([], []))


def last_mapped_body(blocks_here, coded, me, inverse, mine, other, after, out):
    take_sum(coded, me, blocks_here, inverse, mine, other, out)


def folded(square):
    half = square.shape[0] // 2
    return jnp.concatenate([square[:half], square[half:]], axis=1)


def unfolded(terms):
    total = functools.reduce(lambda total, term: total + term[...], terms[1:], terms[0][...])
    width = total.shape[1] // 2
    return jnp.concatenate([total[:, :width], total[:, width:]], axis=0)


def gram_body(me, own, other, out):
    full = both_columns(me[2], own[...], other[...])
    out[...] = folded(gram(pack(full), full.shape[0]))


def factor_body(after, *refs):
    refs[-1][...] = lower_inverse(unfolded(refs[:-1]))


def second_gram_body(me, factor, own, other, mapped, out):
    full = both_columns(me[2], own[...], other[...])
    parts = thirds(times(factor[...], pack(full)))
    mapped[...] = parts[: mapped.shape[0]]
    out[...] = folded(gram(parts, full.shape[0]))


def final_body(me, mapped, *refs):
    out = refs[-1]
    factor = lower_inverse(unfolded(refs[:-1]))
    own_cols = out.shape[0]
    part = jnp.where(me[2] == 0, factor[:own_cols], factor[own_cols:])
    out[...] = times(part, mapped[...])


def shift_by(value, axes, size, shift):
    return lax.ppermute(value, axes, [(i, (i + shift) % size) for i in range(size)])


def exchange(value):
    return lax.all_to_all(value, "rows", split_axis=0, concat_axis=0, tiled=True)


def row_terms(value, row_count):
    return [value] + [shift_by(value, "rows", row_count, k) for k in range(1, row_count)]


def pair_step(value, name, flip):
    return lax.ppermute(value, name, [(i, i ^ flip) for i in range(lax.axis_size(name))])


def pair_sum(value, axes):
    terms = None
    steps = [(name, 1 << bit) for name in axes for bit in range((lax.axis_size(name) - 1).bit_length())]
    for name, flip in steps:
        if terms is not None:
            value = terms[0] + terms[1]
        terms = (value, pair_step(value, name, flip))
    return terms


def local(embeddings, start, pair_list, pair_count):
    row_count = lax.axis_size("rows")
    tile_count = lax.axis_size("tiles")
    core_count = lax.axis_size("cols")
    row_index = lax.axis_index("rows")
    tile_index = lax.axis_index("tiles")
    col_index = lax.axis_index("cols")
    me = jnp.stack([row_index, tile_index, col_index]).astype(jnp.int32)
    rows_here, half_features = embeddings.shape
    blocks_here = rows_here // BLOCK
    slots = pair_list.shape[2]
    capacity = slots // row_count
    per_core = capacity // core_count
    own_blocks = blocks_here // tile_count
    own_cols = start.shape[1]
    block_count = row_count * blocks_here
    others = range(1, row_count)

    own_list = jnp.concatenate(
        [pair_list[0], jnp.broadcast_to(pair_count[:, None], (1, slots))], axis=0
    )
    own_list = jnp.pad(own_list, ((0, 5), (0, BLOCK - slots)))
    lists = exchange(jnp.broadcast_to(own_list[None], (row_count, 8, BLOCK)))
    planned = call(
        functools.partial(plan_body, (row_count, capacity, slots, blocks_here)),
        [sds((6, slots + 1), jnp.int32)] + [sds((capacity * BLOCK, half_features), BF16) for _ in others],
        [me, lists, embeddings],
        smem_in=(0, 1),
        any_in=(2,),
        smem_out=(0,),
        scratch=[pltpu.SemaphoreType.DMA((slots - capacity,))],
        vmem=53,
    )
    idx, sends = planned[0], planned[1:]
    far = [shift_by(sends[k - 1], "rows", row_count, -k) for k in others]

    self_part = call(
        functools.partial(self_distance_body, own_blocks, tile_count),
        sds((own_blocks * BLOCK, BLOCK), F32),
        [me, embeddings, idx],
        smem_in=(0,),
        any_in=(2,),
    )
    self_other = shift_by(self_part, "cols", core_count, 1)
    self_tiles, self_sums = call(
        functools.partial(self_tile_body, own_blocks),
        [sds((own_blocks, 2 * BLOCK, BLOCK), BF16), sds((own_blocks, BLOCK), F32)],
        [self_part, self_other],
    )
    values = start.T
    code_shapes = [((own_cols, rows_here), jnp.int16), ((blocks_here, BLOCK), F32), ((blocks_here, BLOCK), F32)]
    start_codes = call(start_body, [sds(*shape) for shape in code_shapes], [values])
    code_scratch = [pltpu.VMEM(*shape) for shape in code_shapes]
    coded = tile_count == 2
    own_squares = call(squares_body, sds((rows_here, BLOCK), F32), [embeddings, idx], any_in=(1,))
    pair_part = call(
        functools.partial(pair_distance_body, row_count, capacity),
        sds((slots * BLOCK, BLOCK), F32),
        [idx, embeddings, own_squares, *far],
        smem_in=(0,),
    )
    pair_other = shift_by(pair_part, "cols", core_count, 1)

    dims = (row_count, capacity, per_core, blocks_here, tile_count)
    table = sds((block_count, BLOCK), F32)
    picked = 2 * capacity * own_cols
    tiles = call(
        functools.partial(pair_tile_body, dims),
        [sds((slots, 2 * BLOCK, BLOCK), BF16), sds((capacity, 2 * BLOCK, BLOCK), BF16), table]
        + [sds((per_core * BLOCK + picked + CODE_ROWS, BLOCK), jnp.int16) for _ in others],
        [me, idx, pair_part, pair_other, self_sums, *start_codes],
        smem_in=(0, 1),
    )
    near_tiles, home_tiles, degrees, sends = tiles[0], tiles[1], tiles[2], tiles[3:]
    degrees = functools.reduce(jnp.add, row_terms(degrees, row_count))
    degree_terms = pair_sum(degrees, ("tiles",))
    messages = [shift_by(sends[k - 1], "rows", row_count, k) for k in others]
    sent = call(
        functools.partial(split_body, row_count, per_core),
        [sds((per_core, 2 * BLOCK, BLOCK), BF16) for _ in others],
        [*messages, degree_terms[1]],
        any_in=(row_count - 1,),
    )
    shared = [shift_by(tile, "cols", core_count, 1) for tile in sent]

    block_shape = sds((own_cols, rows_here), F32)
    sum_shape = sds((own_cols, rows_here + BLOCK), jnp.int16) if coded else block_shape
    square = sds((2 * own_cols, 2 * own_cols), F32)
    folded_square = sds((own_cols, 4 * own_cols), F32)

    started, degree, inverse = call(
        functools.partial(first_own_body, dims),
        [block_shape, table, table],
        [me, idx, *degree_terms, values, near_tiles, home_tiles, self_tiles],
        smem_in=(0, 1),
    )
    part = call(
        functools.partial(first_far_body, dims, coded),
        sum_shape,
        [me, idx, inverse, started, near_tiles, *sent, *shared, *messages],
        smem_in=(0, 1),
        scratch=[pltpu.VMEM((own_cols, rows_here), F32)],
    )
    mine, other = pair_sum(part, ("tiles",))
    first = call(
        functools.partial(mapped_body, dims, coded),
        [block_shape] + [sds((picked + CODE_ROWS, BLOCK), jnp.int16) for _ in others],
        [me, idx, inverse, mine, other],
        smem_in=(0, 1),
        scratch=code_scratch,
    )
    mapped, sends = first[0], first[1:]
    received = [shift_by(sends[k - 1], "rows", row_count, k) for k in others]

    mapped_other = shift_by(mapped, "cols", core_count, 1)
    first_gram = call(gram_body, folded_square, [me, mapped, mapped_other], smem_in=(0,))
    part = call(
        functools.partial(second_apply_body, dims),
        block_shape,
        [me, idx, inverse, first_gram, mapped, home_tiles, self_tiles, near_tiles, *sent, *shared, *received],
        smem_in=(0, 1),
        any_in=(3,),
    )
    steps = (row_count - 1).bit_length()
    for bit in range(steps - 1):
        first_gram = first_gram + pair_step(first_gram, "rows", 1 << bit)
    part = call(functools.partial(send_sum_body, coded), sum_shape, [part, first_gram])
    gram_terms = (first_gram, pair_step(first_gram, "rows", 1 << (steps - 1)))
    mine, other = pair_sum(part, ("tiles",))
    second = call(
        functools.partial(last_mapped_body, blocks_here, coded),
        block_shape,
        [me, inverse, mine, other, gram_terms[1]],
        smem_in=(0,),
        any_in=(4,),
    )
    second_other = shift_by(second, "cols", core_count, 1)
    factor = call(factor_body, square, [second, *gram_terms], any_in=(0,))
    full, second_gram = call(
        second_gram_body,
        [sds((4 * own_cols, rows_here), BF16), folded_square],
        [me, factor, second, second_other],
        smem_in=(0,),
    )
    vectors = call(
        final_body, block_shape, [me, full, *row_terms(second_gram, row_count)], smem_in=(0,)
    )
    own_degree = lax.dynamic_slice_in_dim(degree, row_index * blocks_here, blocks_here, 0)
    return (vectors.T, own_degree.reshape(rows_here))


def solution(mesh):
    in_specs = (
        P(("groups", "rows"), "cols"),
        P(("groups", "rows"), "cols"),
        P(("groups", "rows", "tiles"), None, None),
        P(("groups", "rows", "tiles")),
    )
    out_specs = (P(("groups", "rows"), "cols"), P(("groups", "rows")))
    return jax.shard_map(local, mesh=mesh, in_specs=in_specs, out_specs=out_specs, check_vma=False)
```

```python
import functools

import jax
import jax.numpy as jnp
from jax import lax
from jax.experimental import pallas as pl
from jax.experimental.pallas import tpu as pltpu
from jax.sharding import PartitionSpec as P

BLOCK = 128
kernel_gamma = 14.0
CODE_TOP = 32767.0
PART_TOP = 16384.0
CODE_ROWS = 16

VMEM = pl.BlockSpec(memory_space=pltpu.VMEM)
SMEM = pl.BlockSpec(memory_space=pltpu.SMEM)
ANY = pl.BlockSpec(memory_space=pl.ANY)
F32 = jnp.float32
BF16 = jnp.bfloat16
HIGHEST = lax.Precision.HIGHEST
NT = (((1,), (1,)), ((), ()))


def call(body, outs, args, smem_in=(), smem_out=(), any_in=(), scratch=()):
    single = not isinstance(outs, (list, tuple))
    shapes = [outs] if single else list(outs)
    result = pl.pallas_call(
        body,
        out_shape=shapes,
        in_specs=[
            SMEM if i in smem_in else ANY if i in any_in else VMEM for i in range(len(args))
        ],
        out_specs=[SMEM if i in smem_out else VMEM for i in range(len(shapes))],
        scratch_shapes=list(scratch),
        compiler_params=pltpu.CompilerParams(vmem_limit_bytes=48 * 2**20),
    )(*args)
    return result[0] if single else result


def sds(shape, dtype):
    return jax.ShapeDtypeStruct(shape, dtype)


def at_block(index):
    return pl.ds(pl.multiple_of(index * BLOCK, BLOCK), BLOCK)


def eye_mask(size):
    return lax.broadcasted_iota(jnp.int32, (size, size), 0) == lax.broadcasted_iota(
        jnp.int32, (size, size), 1
    )


def halves(value):
    high = value.astype(BF16)
    low = (value - high.astype(F32)).astype(BF16)
    return high, low


def pack(tile):
    return jnp.concatenate(halves(tile), axis=0)


def scale_of(power, part):
    return jnp.exp2(power) * (part * (1.0 / PART_TOP))


def encode(values):
    most = jnp.maximum(jnp.max(jnp.abs(values), axis=0, keepdims=True), 1e-30)
    power = jnp.floor(jnp.log2(most)) + 1.0
    part = jnp.floor(most * jnp.exp2(-power) * PART_TOP) + 1.0
    steps = jnp.floor(values * (CODE_TOP / scale_of(power, part)) + 0.5)
    steps = jnp.minimum(jnp.maximum(steps, -CODE_TOP), CODE_TOP)
    return steps.astype(jnp.int32).astype(jnp.int16), power, part


def decode(steps, scale):
    return steps.astype(jnp.int32).astype(F32) * (scale * (1.0 / CODE_TOP))


def as_rows(powers, parts, count):
    fill = jnp.zeros((count // 2 - len(powers), BLOCK), F32)
    fill = [fill] if fill.shape[0] else []
    rows = jnp.concatenate([*powers, *fill, *parts, *fill], axis=0)
    return rows.astype(jnp.int32).astype(jnp.int16)


def scale_rows(rows):
    rows = rows.astype(jnp.int32).astype(F32)
    half = rows.shape[0] // 2
    return scale_of(rows[:half], rows[half:])


def row_at(rows, place):
    if isinstance(place, int):
        return rows[place : place + 1, :]
    line = rows[:1, :]
    for i in range(1, rows.shape[0]):
        line = jnp.where(place == i, rows[i : i + 1, :], line)
    return line


def product(packed, values):
    left = jnp.concatenate(halves(values), axis=0)
    both = jnp.dot(jnp.concatenate([left, left], axis=1), packed, preferred_element_type=F32)
    count = values.shape[0]
    return both[:count] + both[count:]


def thirds(value):
    high = value.astype(BF16)
    rest = value - high.astype(F32)
    middle = rest.astype(BF16)
    low = (rest - middle.astype(F32)).astype(BF16)
    return jnp.concatenate([high, middle, low], axis=0)


def gram(parts, n):
    cross = lax.dot_general(parts, parts, NT, preferred_element_type=F32)
    count = parts.shape[0] // n
    pairs = sorted(((i, j) for i in range(count) for j in range(count)), key=lambda p: -p[0] - p[1])
    total = None
    for i, j in pairs:
        piece = cross[i * n : (i + 1) * n, j * n : (j + 1) * n]
        total = piece if total is None else total + piece
    return total


def times(left, parts):
    m = left.shape[0]
    left = jnp.concatenate(halves(left), axis=0)
    both = jnp.dot(jnp.concatenate([left, left], axis=1), parts, preferred_element_type=F32)
    return both[m:] + both[:m]


def lower_inverse(matrix, step=8):
    n = matrix.shape[0]
    state = jnp.concatenate([matrix, eye_mask(n).astype(F32)], axis=1)
    done = []
    for j in range(0, n, step):
        top = j // 8 * 8
        if top > n - state.shape[0]:
            done.append(state[:8])
            state = state[8:]
        base = j - top
        rows = lax.broadcasted_iota(jnp.int32, state.shape, 0)
        columns = [jnp.broadcast_to(state[:, j + i : j + i + 1], state.shape) for i in range(step)]
        lines = [state[base + i : base + i + 1, :] for i in range(step)]
        pivot = [[columns[k][base + i : base + i + 1, :] for k in range(step)] for i in range(step)]
        for i in range(step):
            if i % 2 == 0:
                first, cross, second = pivot[i][i], pivot[i][i + 1], pivot[i + 1][i + 1]
                reciprocals = (1.0 / first, first / (first * second - cross * cross))
            reciprocal = reciprocals[i % 2]
            scaled = lines[i] * reciprocal
            ratio = [pivot[i][k] * reciprocal for k in range(step)]
            for k in range(i + 1, step):
                lines[k] = lines[k] - pivot[k][i] * scaled
                columns[k] = columns[k] - columns[i] * ratio[k]
                for m in range(i + 1, step):
                    pivot[k][m] = pivot[k][m] - pivot[k][i] * ratio[m]
            state = state - jnp.where(rows > base + i, columns[i], 0.0) * scaled
    state = jnp.concatenate([*done, state], axis=0)
    pivots = jnp.sum(jnp.where(eye_mask(n), state[:, :n], 0.0), axis=1, keepdims=True)
    return state[:, n:] / jnp.sqrt(pivots)


def both_columns(core, own, other):
    first = core == 0
    return jnp.concatenate(
        [jnp.where(first, own, other), jnp.where(first, other, own)], axis=0
    )


def quotient(value, size):
    if size & (size - 1) == 0:
        return lax.shift_right_logical(value, jnp.int32(size.bit_length() - 1))
    return lax.div(value, jnp.int32(size))


def remainder(value, size):
    if size & (size - 1) == 0:
        return lax.bitwise_and(value, jnp.int32(size - 1))
    return lax.rem(value, jnp.int32(size))


def plan_body(dims, me, *refs):
    row_count, capacity, slots, blocks_here = dims
    lists, (emb, after, idx) = refs[:row_count], refs[row_count : row_count + 3]
    sends = refs[row_count + 3 :]
    row = me[0]
    for i in range(slots):
        for line in (0, 1, 2, 4, 5):
            idx[line, i] = 0

    def each(step, start):
        if slots <= 8:
            for s in range(slots):
                start = step(s, start)
        else:
            lax.fori_loop(0, slots, step, start)

    for k in range(row_count):
        live_count = lists[k][2, 0]

        def step(s, counts, k=k, live_count=live_count):
            near = lists[k][0, s]
            far = lists[k][1, s]
            owner = quotient(far, blocks_here)
            live = s < live_count
            hit = live & (owner == row)
            slot = jnp.where(hit, k * capacity + counts[0], slots)
            idx[4, slot] = far - row * blocks_here
            idx[5, slot] = near
            if k > 0:
                return (counts[0] + hit.astype(jnp.int32),)
            shift = remainder(owner - row + row_count, row_count)
            rank = counts[1]
            for d in range(1, row_count):
                rank = jnp.where(shift == d, counts[1 + d], rank)
            slot = jnp.where(live, shift * capacity + rank, slots)
            idx[0, slot] = near - row * blocks_here
            idx[1, slot] = far
            idx[2, slot] = 1
            more = tuple(
                counts[1 + d] + (live & (shift == d)).astype(jnp.int32) for d in range(row_count)
            )
            return (counts[0] + hit.astype(jnp.int32), *more)

        each(step, (jnp.int32(0),) * (1 + row_count if k == 0 else 1))
    for k in range(1, row_count):
        for j in range(capacity):
            sends[k - 1][j * BLOCK : (j + 1) * BLOCK, :] = emb[at_block(idx[4, k * capacity + j]), :]


def squares(block):
    return jnp.sum(jnp.square(block.astype(F32)), axis=1, keepdims=True)


def partial_distance(left, right, left_sq, right_sq):
    inner = lax.dot_general(left, right, NT, preferred_element_type=F32)
    right_row = jnp.sum(jnp.where(eye_mask(BLOCK), right_sq, 0.0), axis=0, keepdims=True)
    return left_sq + right_row - 2.0 * inner


def self_distance_body(own_blocks, tile_count, me, emb, out):
    for i in range(own_blocks):
        block = emb[at_block(i * tile_count + me[1]), :]
        block_sq = squares(block)
        out[i * BLOCK : (i + 1) * BLOCK, :] = partial_distance(block, block, block_sq, block_sq)


def squares_body(emb, after, out):
    for b in range(out.shape[0] // BLOCK):
        part = slice(b * BLOCK, (b + 1) * BLOCK)
        out[part, :] = jnp.broadcast_to(squares(emb[part, :]), (BLOCK, BLOCK))


def pair_distance_body(order, capacity, idx, emb, own_squares, *refs):
    far, out = dict(zip(order, refs)), refs[-1]
    row_count = len(order) + 1
    for k in range(row_count):
        for j in range(capacity):
            slot = k * capacity + j
            left = emb[at_block(idx[0, slot]), :]
            left_sq = own_squares[at_block(idx[0, slot]), :]
            if k == 0:
                right = emb[at_block(idx[4, j]), :]
                right_sq = own_squares[at_block(idx[4, j]), :]
            else:
                right = far[k][j * BLOCK : (j + 1) * BLOCK, :]
                right_sq = squares(right)
            part = slice(slot * BLOCK, (slot + 1) * BLOCK)
            out[part, :] = partial_distance(left, right, left_sq, right_sq)


def self_tile_body(own_blocks, mine, other, packed, sums):
    for i in range(own_blocks):
        part = slice(i * BLOCK, (i + 1) * BLOCK)
        tile = jnp.exp(-kernel_gamma * (mine[part, :] + other[part, :] - 2.0))
        tile = jnp.where(eye_mask(BLOCK), 0.0, tile)
        packed[i] = pack(tile)
        sums[i : i + 1, :] = jnp.sum(tile, axis=0, keepdims=True)


def pair_tile_body(dims, me, idx, mine, other, self_sums, codes, powers, parts, near_tiles, home_tiles, table, *sends):
    row_count, capacity, per_core, blocks_here, tile_count = dims
    row, tile_index, core = me[0], me[1], me[2]
    table[...] = jnp.zeros(table.shape, F32)
    for i in range(self_sums.shape[0]):
        table[pl.ds(row * blocks_here + i * tile_count + tile_index, 1), :] = self_sums[i : i + 1, :]

    def add(block, line):
        place = pl.ds(block, 1)
        table[place, :] = table[place, :] + line

    for k in range(row_count):
        tiles = []
        for j in range(capacity):
            slot = k * capacity + j
            part = slice(slot * BLOCK, (slot + 1) * BLOCK)
            tile = jnp.exp(-kernel_gamma * (mine[part, :] + other[part, :] - 2.0))
            tile = jnp.where(idx[2, slot] > 0, tile, 0.0)
            turned = tile.T
            near_tiles[slot] = pack(turned)
            add(row * blocks_here + idx[0, slot], jnp.sum(turned, axis=0, keepdims=True))
            add(idx[1, slot], jnp.sum(tile, axis=0, keepdims=True))
            if k == 0:
                home_tiles[j] = pack(tile)
            tiles.append(tile)
        if k > 0:
            lines = ([], [])
            for inner in range(per_core):
                at = slice(inner * BLOCK, (inner + 1) * BLOCK)
                steps, power, part = encode(jnp.where(core == 0, tiles[inner], tiles[per_core + inner]))
                sends[k - 1][at, :] = steps
                lines[0].append(power)
                lines[1].append(part)
            pick_columns(idx, k, row_count, capacity, codes, powers, parts, sends[k - 1], per_core * BLOCK, lines)


def encode_blocks(values, codes, powers, parts):
    for b in range(powers.shape[0]):
        at = slice(b * BLOCK, (b + 1) * BLOCK)
        steps, power, part = encode(values[:, at])
        codes[:, at] = steps
        powers[b : b + 1, :] = power
        parts[b : b + 1, :] = part


def start_body(values, codes, powers, parts):
    encode_blocks(values, codes, powers, parts)


def split_body(row_count, per_core, *refs):
    others = row_count - 1
    messages, outs = refs[:others], refs[-others:]
    for message, out in zip(messages, outs):
        scales = scale_rows(message[message.shape[0] - CODE_ROWS :, :])
        for inner in range(per_core):
            steps = message[inner * BLOCK : (inner + 1) * BLOCK, :]
            out[inner] = pack(decode(steps, scales[inner : inner + 1, :]))


def pick_columns(idx, k, row_count, capacity, codes, powers, parts, send, base, lines):
    count = codes.shape[0]
    back = row_count - k
    blocks = [idx[0, k * capacity + j] for j in range(capacity)]
    blocks += [idx[4, back * capacity + j] for j in range(capacity)]
    for place, block in enumerate(blocks):
        send[base + place * count : base + (place + 1) * count, :] = codes[:, at_block(block)]
        lines[0].append(powers[pl.ds(block, 1), :])
        lines[1].append(parts[pl.ds(block, 1), :])
    send[base + len(blocks) * count :, :] = as_rows(*lines, CODE_ROWS)


def add_product(out, block, packed, values):
    place = at_block(block)
    out[:, place] = out[:, place] + product(packed, values)


def apply_own(dims, me, idx, inverse, own, near_tiles, home_tiles, self_tiles, out):
    row_count, capacity, per_core, blocks_here, tile_count = dims
    row, tile_index = me[0], me[1]
    out[...] = jnp.zeros(out.shape, F32)

    def scaled(block):
        return own[:, at_block(block)] * inverse[pl.ds(row * blocks_here + block, 1), :]

    for i in range(blocks_here // tile_count):
        block = i * tile_count + tile_index
        add_product(out, block, self_tiles[i], scaled(block))
    for j in range(capacity):
        add_product(out, idx[0, j], near_tiles[j], scaled(idx[4, j]))
        add_product(out, idx[4, j], home_tiles[j], scaled(idx[0, j]))


def apply_far(dims, me, idx, inverse, received, base, near_tiles, sent, shared, out):
    row_count, capacity, per_core, blocks_here, tile_count = dims
    core = me[2]
    count = out.shape[0]
    lines = [scale_rows(message[message.shape[0] - CODE_ROWS :, :]) for message in received]
    first_line = base // BLOCK

    def arrived(k, place, block):
        steps = received[k - 1][pl.ds(pl.multiple_of(base + place * count, CODE_ROWS), count), :]
        rows = lines[k - 1][first_line : first_line + 2 * capacity, :]
        return decode(steps, row_at(rows, place) * inverse[pl.ds(block, 1), :])

    for k in range(1, row_count):
        for j in range(capacity):
            slot = k * capacity + j
            values = arrived(row_count - k, capacity + j, idx[1, slot])
            add_product(out, idx[0, slot], near_tiles[slot], values)
            inner = j % per_core
            if j < per_core:
                place = core * per_core + inner
                packed = sent[k - 1][inner]
            else:
                place = (1 - core) * per_core + inner
                packed = shared[k - 1][inner]
            slot = k * capacity + place
            add_product(out, idx[4, slot], packed, arrived(k, place, idx[5, slot]))


def first_own_body(dims, me, idx, mine, other, own, near_tiles, home_tiles, self_tiles, out, degree, inverse):
    total = mine[...] + other[...]
    degree[...] = total
    inverse[...] = 1.0 / jnp.sqrt(total)
    apply_own(dims, me, idx, inverse, own, near_tiles, home_tiles, self_tiles, out)


def first_far_body(dims, coded, me, idx, inverse, started, near_tiles, *refs):
    row_count, per_core = dims[0], dims[2]
    others = row_count - 1
    sent, shared, messages = refs[:others], refs[others : 2 * others], refs[2 * others : 3 * others]
    out, total = refs[3 * others :]
    total[...] = started[...]
    apply_far(dims, me, idx, inverse, messages, per_core * BLOCK, near_tiles, sent, shared, total)
    put_sum(coded, total, out)


def second_apply_body(dims, me, idx, inverse, after, own, home_tiles, self_tiles, near_tiles, *refs):
    others = dims[0] - 1
    sent, shared, received = refs[:others], refs[others : 2 * others], refs[2 * others : 3 * others]
    out = refs[-1]
    apply_own(dims, me, idx, inverse, own, near_tiles, home_tiles, self_tiles, out)
    apply_far(dims, me, idx, inverse, received, 0, near_tiles, sent, shared, out)


def send_sum_body(coded, total, after, out):
    put_sum(coded, total, out)


def put_sum(coded, total, out):
    if not coded:
        out[...] = total[...]
        return
    lines = ([], [])
    blocks_here = total.shape[1] // BLOCK
    for b in range(blocks_here):
        at = slice(b * BLOCK, (b + 1) * BLOCK)
        steps, power, part = encode(total[:, at])
        out[:, at] = steps
        lines[0].append(power)
        lines[1].append(part)
    out[:, blocks_here * BLOCK :] = as_rows(*lines, out.shape[0])


def take_sum(coded, me, blocks_here, inverse, mine, other, out):
    if coded:
        tail = blocks_here * BLOCK
        my_scales, other_scales = scale_rows(mine[:, tail:]), scale_rows(other[:, tail:])
    for b in range(blocks_here):
        at = slice(b * BLOCK, (b + 1) * BLOCK)
        row = inverse[pl.ds(me[0] * blocks_here + b, 1), :]
        if coded:
            line = slice(b, b + 1)
            value = decode(mine[:, at], my_scales[line]) + decode(other[:, at], other_scales[line])
        else:
            value = mine[:, at] + other[:, at]
        out[:, at] = value * row


def mapped_body(dims, coded, me, idx, inverse, mine, other, out, *refs):
    row_count, capacity, per_core, blocks_here, tile_count = dims
    sends, (codes, powers, parts) = refs[:-3], refs[-3:]
    take_sum(coded, me, blocks_here, inverse, mine, other, out)
    encode_blocks(out, codes, powers, parts)
    for k in range(1, row_count):
        pick_columns(idx, k, row_count, capacity, codes, powers, parts, sends[k - 1], 0, ([], []))


def last_mapped_body(blocks_here, coded, me, inverse, mine, other, after, out):
    take_sum(coded, me, blocks_here, inverse, mine, other, out)


def folded(square):
    half = square.shape[0] // 2
    return jnp.concatenate([square[:half], square[half:]], axis=1)


def unfolded(terms):
    total = functools.reduce(lambda total, term: total + term[...], terms[1:], terms[0][...])
    width = total.shape[1] // 2
    return jnp.concatenate([total[:, :width], total[:, width:]], axis=0)


def gram_body(me, own, other, out):
    full = both_columns(me[2], own[...], other[...])
    out[...] = folded(gram(pack(full), full.shape[0]))


def factor_body(after, *refs):
    refs[-1][...] = lower_inverse(unfolded(refs[:-1]))


def second_gram_body(me, factor, own, other, mapped, out):
    full = both_columns(me[2], own[...], other[...])
    parts = thirds(times(factor[...], pack(full)))
    mapped[...] = parts[: mapped.shape[0]]
    out[...] = folded(gram(parts, full.shape[0]))


def final_body(me, mapped, *refs):
    out = refs[-1]
    factor = lower_inverse(unfolded(refs[:-1]))
    own_cols = out.shape[0]
    part = jnp.where(me[2] == 0, factor[:own_cols], factor[own_cols:])
    out[...] = times(part, mapped[...])


def shift_by(value, axes, size, shift):
    return lax.ppermute(value, axes, [(i, (i + shift) % size) for i in range(size)])


def row_terms(value, row_count):
    return [value] + [shift_by(value, "rows", row_count, k) for k in range(1, row_count)]


def pair_step(value, name, flip):
    return lax.ppermute(value, name, [(i, i ^ flip) for i in range(lax.axis_size(name))])


def pair_sum(value, axes):
    terms = None
    steps = [(name, 1 << bit) for name in axes for bit in range((lax.axis_size(name) - 1).bit_length())]
    for name, flip in steps:
        if terms is not None:
            value = terms[0] + terms[1]
        terms = (value, pair_step(value, name, flip))
    return terms


def local(embeddings, start, pair_list, pair_count):
    row_count = lax.axis_size("rows")
    tile_count = lax.axis_size("tiles")
    core_count = lax.axis_size("cols")
    row_index = lax.axis_index("rows")
    tile_index = lax.axis_index("tiles")
    col_index = lax.axis_index("cols")
    me = jnp.stack([row_index, tile_index, col_index]).astype(jnp.int32)
    rows_here, half_features = embeddings.shape
    blocks_here = rows_here // BLOCK
    slots = pair_list.shape[2]
    capacity = slots // row_count
    per_core = capacity // core_count
    own_blocks = blocks_here // tile_count
    own_cols = start.shape[1]
    block_count = row_count * blocks_here
    others = range(1, row_count)

    own_list = jnp.concatenate(
        [pair_list[0], jnp.broadcast_to(pair_count[:, None], (1, slots))], axis=0
    )
    lists = row_terms(own_list, row_count)
    self_part = call(
        functools.partial(self_distance_body, own_blocks, tile_count),
        sds((own_blocks * BLOCK, BLOCK), F32),
        [me, embeddings],
        smem_in=(0,),
    )
    planned = call(
        functools.partial(plan_body, (row_count, capacity, slots, blocks_here)),
        [sds((6, slots + 1), jnp.int32)] + [sds((capacity * BLOCK, half_features), BF16) for _ in others],
        [me, *lists, embeddings, self_part],
        smem_in=range(1 + row_count),
        any_in=(row_count + 2,),
        smem_out=(0,),
    )
    idx, sends = planned[0], planned[1:]
    order = sorted(others, key=lambda k: abs(k - row_count // 2))
    far = [shift_by(sends[k - 1], "rows", row_count, -k) for k in order]

    self_other = shift_by(self_part, "cols", core_count, 1)
    self_tiles, self_sums = call(
        functools.partial(self_tile_body, own_blocks),
        [sds((own_blocks, 2 * BLOCK, BLOCK), BF16), sds((own_blocks, BLOCK), F32)],
        [self_part, self_other],
    )
    values = start.T
    code_shapes = [((own_cols, rows_here), jnp.int16), ((blocks_here, BLOCK), F32), ((blocks_here, BLOCK), F32)]
    start_codes = call(start_body, [sds(*shape) for shape in code_shapes], [values])
    code_scratch = [pltpu.VMEM(*shape) for shape in code_shapes]
    coded = tile_count == 2
    own_squares = call(squares_body, sds((rows_here, BLOCK), F32), [embeddings, idx], any_in=(1,))
    pair_part = call(
        functools.partial(pair_distance_body, order, capacity),
        sds((slots * BLOCK, BLOCK), F32),
        [idx, embeddings, own_squares, *far],
        smem_in=(0,),
    )
    pair_other = shift_by(pair_part, "cols", core_count, 1)

    dims = (row_count, capacity, per_core, blocks_here, tile_count)
    table = sds((block_count, BLOCK), F32)
    picked = 2 * capacity * own_cols
    tiles = call(
        functools.partial(pair_tile_body, dims),
        [sds((slots, 2 * BLOCK, BLOCK), BF16), sds((capacity, 2 * BLOCK, BLOCK), BF16), table]
        + [sds((per_core * BLOCK + picked + CODE_ROWS, BLOCK), jnp.int16) for _ in others],
        [me, idx, pair_part, pair_other, self_sums, *start_codes],
        smem_in=(0, 1),
    )
    near_tiles, home_tiles, degrees, sends = tiles[0], tiles[1], tiles[2], tiles[3:]
    degrees = functools.reduce(jnp.add, row_terms(degrees, row_count))
    degree_terms = pair_sum(degrees, ("tiles",))
    messages = [shift_by(sends[k - 1], "rows", row_count, k) for k in others]
    sent = call(
        functools.partial(split_body, row_count, per_core),
        [sds((per_core, 2 * BLOCK, BLOCK), BF16) for _ in others],
        [*messages, degree_terms[1]],
        any_in=(row_count - 1,),
    )
    shared = [shift_by(tile, "cols", core_count, 1) for tile in sent]

    block_shape = sds((own_cols, rows_here), F32)
    sum_shape = sds((own_cols, rows_here + BLOCK), jnp.int16) if coded else block_shape
    square = sds((2 * own_cols, 2 * own_cols), F32)
    folded_square = sds((own_cols, 4 * own_cols), F32)

    started, degree, inverse = call(
        functools.partial(first_own_body, dims),
        [block_shape, table, table],
        [me, idx, *degree_terms, values, near_tiles, home_tiles, self_tiles],
        smem_in=(0, 1),
    )
    part = call(
        functools.partial(first_far_body, dims, coded),
        sum_shape,
        [me, idx, inverse, started, near_tiles, *sent, *shared, *messages],
        smem_in=(0, 1),
        scratch=[pltpu.VMEM((own_cols, rows_here), F32)],
    )
    mine, other = pair_sum(part, ("tiles",))
    first = call(
        functools.partial(mapped_body, dims, coded),
        [block_shape] + [sds((picked + CODE_ROWS, BLOCK), jnp.int16) for _ in others],
        [me, idx, inverse, mine, other],
        smem_in=(0, 1),
        scratch=code_scratch,
    )
    mapped, sends = first[0], first[1:]
    received = [shift_by(sends[k - 1], "rows", row_count, k) for k in others]

    mapped_other = shift_by(mapped, "cols", core_count, 1)
    first_gram = call(gram_body, folded_square, [me, mapped, mapped_other], smem_in=(0,))
    part = call(
        functools.partial(second_apply_body, dims),
        block_shape,
        [me, idx, inverse, first_gram, mapped, home_tiles, self_tiles, near_tiles, *sent, *shared, *received],
        smem_in=(0, 1),
        any_in=(3,),
    )
    steps = (row_count - 1).bit_length()
    for bit in range(steps - 1):
        first_gram = first_gram + pair_step(first_gram, "rows", 1 << bit)
    part = call(functools.partial(send_sum_body, coded), sum_shape, [part, first_gram])
    gram_terms = (first_gram, pair_step(first_gram, "rows", 1 << (steps - 1)))
    mine, other = pair_sum(part, ("tiles",))
    second = call(
        functools.partial(last_mapped_body, blocks_here, coded),
        block_shape,
        [me, inverse, mine, other, gram_terms[1]],
        smem_in=(0,),
        any_in=(4,),
    )
    second_other = shift_by(second, "cols", core_count, 1)
    factor = call(factor_body, square, [second, *gram_terms], any_in=(0,))
    full, second_gram = call(
        second_gram_body,
        [sds((4 * own_cols, rows_here), BF16), folded_square],
        [me, factor, second, second_other],
        smem_in=(0,),
    )
    vectors = call(
        final_body, block_shape, [me, full, *row_terms(second_gram, row_count)], smem_in=(0,)
    )
    own_degree = lax.dynamic_slice_in_dim(degree, row_index * blocks_here, blocks_here, 0)
    return (vectors.T, own_degree.reshape(rows_here))


def solution(mesh):
    in_specs = (
        P(("groups", "rows"), "cols"),
        P(("groups", "rows"), "cols"),
        P(("groups", "rows", "tiles"), None, None),
        P(("groups", "rows", "tiles")),
    )
    out_specs = (P(("groups", "rows"), "cols"), P(("groups", "rows")))
    return jax.shard_map(local, mesh=mesh, in_specs=in_specs, out_specs=out_specs, check_vma=False)
```

```python
import functools

import jax
import jax.numpy as jnp
from jax import lax
from jax.experimental import pallas as pl
from jax.experimental.pallas import tpu as pltpu
from jax.sharding import PartitionSpec as P

BLOCK = 128
kernel_gamma = 14.0
CODE_TOP = 32767.0
PART_TOP = 16384.0
CODE_ROWS = 16

VMEM = pl.BlockSpec(memory_space=pltpu.VMEM)
SMEM = pl.BlockSpec(memory_space=pltpu.SMEM)
ANY = pl.BlockSpec(memory_space=pl.ANY)
F32 = jnp.float32
BF16 = jnp.bfloat16
HIGHEST = lax.Precision.HIGHEST
NT = (((1,), (1,)), ((), ()))


ME = None


def with_position(body):
    def inner(*refs):
        body([lax.axis_index(name) for name in ("rows", "tiles", "cols")], *refs)

    return inner


def call(body, outs, args, smem_in=(), smem_out=(), any_in=(), scratch=(), any_out=()):
    if args[0] is ME:
        body, args = with_position(body), args[1:]
        smem_in, any_in = [[i - 1 for i in places] for places in (smem_in, any_in)]
    single = not isinstance(outs, (list, tuple))
    shapes = [outs] if single else list(outs)
    result = pl.pallas_call(
        body,
        out_shape=shapes,
        in_specs=[
            SMEM if i in smem_in else ANY if i in any_in else VMEM for i in range(len(args))
        ],
        out_specs=[
            SMEM if i in smem_out else ANY if i in any_out else VMEM for i in range(len(shapes))
        ],
        scratch_shapes=list(scratch),
        compiler_params=pltpu.CompilerParams(vmem_limit_bytes=48 * 2**20),
    )(*args)
    return result[0] if single else result


def sds(shape, dtype):
    return jax.ShapeDtypeStruct(shape, dtype)


def at_block(index):
    return pl.ds(pl.multiple_of(index * BLOCK, BLOCK), BLOCK)


def eye_mask(size):
    return lax.broadcasted_iota(jnp.int32, (size, size), 0) == lax.broadcasted_iota(
        jnp.int32, (size, size), 1
    )


def halves(value):
    high = value.astype(BF16)
    low = (value - high.astype(F32)).astype(BF16)
    return high, low


def pack(tile):
    return jnp.concatenate(halves(tile), axis=0)


def scale_of(power, part):
    return jnp.exp2(power) * (part * (1.0 / PART_TOP))


def encode(values):
    most = jnp.maximum(jnp.max(jnp.abs(values), axis=0, keepdims=True), 1e-30)
    power = jnp.floor(jnp.log2(most)) + 1.0
    part = jnp.floor(most * jnp.exp2(-power) * PART_TOP) + 1.0
    steps = jnp.floor(values * (CODE_TOP / scale_of(power, part)) + 0.5)
    steps = jnp.minimum(jnp.maximum(steps, -CODE_TOP), CODE_TOP)
    return steps.astype(jnp.int32).astype(jnp.int16), power, part


def decode(steps, scale):
    return steps.astype(jnp.int32).astype(F32) * (scale * (1.0 / CODE_TOP))


def as_rows(powers, parts, count):
    fill = jnp.zeros((count // 2 - len(powers), BLOCK), F32)
    fill = [fill] if fill.shape[0] else []
    rows = jnp.concatenate([*powers, *fill, *parts, *fill], axis=0)
    return rows.astype(jnp.int32).astype(jnp.int16)


def scale_rows(rows):
    rows = rows.astype(jnp.int32).astype(F32)
    half = rows.shape[0] // 2
    return scale_of(rows[:half], rows[half:])


def row_at(rows, place):
    if isinstance(place, int):
        return rows[place : place + 1, :]
    line = rows[:1, :]
    for i in range(1, rows.shape[0]):
        line = jnp.where(place == i, rows[i : i + 1, :], line)
    return line


def product(packed, values):
    left = jnp.concatenate(halves(values), axis=0)
    both = jnp.dot(jnp.concatenate([left, left], axis=1), packed, preferred_element_type=F32)
    count = values.shape[0]
    return both[:count] + both[count:]


def thirds(value):
    high = value.astype(BF16)
    rest = value - high.astype(F32)
    middle = rest.astype(BF16)
    low = (rest - middle.astype(F32)).astype(BF16)
    return jnp.concatenate([high, middle, low], axis=0)


def gram(parts, n):
    cross = lax.dot_general(parts, parts, NT, preferred_element_type=F32)
    count = parts.shape[0] // n
    pairs = sorted(((i, j) for i in range(count) for j in range(count)), key=lambda p: -p[0] - p[1])
    total = None
    for i, j in pairs:
        piece = cross[i * n : (i + 1) * n, j * n : (j + 1) * n]
        total = piece if total is None else total + piece
    return total


def times(left, parts):
    m = left.shape[0]
    left = jnp.concatenate(halves(left), axis=0)
    both = jnp.dot(jnp.concatenate([left, left], axis=1), parts, preferred_element_type=F32)
    return both[m:] + both[:m]


def lower_inverse(matrix, step=8):
    n = matrix.shape[0]
    state = jnp.concatenate([matrix, eye_mask(n).astype(F32)], axis=1)
    done = []
    for j in range(0, n, step):
        top = j // 8 * 8
        if top > n - state.shape[0]:
            done.append(state[:8])
            state = state[8:]
        base = j - top
        rows = lax.broadcasted_iota(jnp.int32, state.shape, 0)
        columns = [jnp.broadcast_to(state[:, j + i : j + i + 1], state.shape) for i in range(step)]
        lines = [state[base + i : base + i + 1, :] for i in range(step)]
        pivot = [[columns[k][base + i : base + i + 1, :] for k in range(step)] for i in range(step)]
        for i in range(step):
            if i % 2 == 0:
                first, cross, second = pivot[i][i], pivot[i][i + 1], pivot[i + 1][i + 1]
                reciprocals = (1.0 / first, first / (first * second - cross * cross))
            reciprocal = reciprocals[i % 2]
            scaled = lines[i] * reciprocal
            ratio = [pivot[i][k] * reciprocal for k in range(step)]
            for k in range(i + 1, step):
                lines[k] = lines[k] - pivot[k][i] * scaled
                columns[k] = columns[k] - columns[i] * ratio[k]
                for m in range(i + 1, step):
                    pivot[k][m] = pivot[k][m] - pivot[k][i] * ratio[m]
            state = state - jnp.where(rows > base + i, columns[i], 0.0) * scaled
    state = jnp.concatenate([*done, state], axis=0)
    pivots = jnp.sum(jnp.where(eye_mask(n), state[:, :n], 0.0), axis=1, keepdims=True)
    return state[:, n:] / jnp.sqrt(pivots)


def both_columns(core, own, other):
    first = core == 0
    return jnp.concatenate(
        [jnp.where(first, own, other), jnp.where(first, other, own)], axis=0
    )


def quotient(value, size):
    if size & (size - 1) == 0:
        return lax.shift_right_logical(value, jnp.int32(size.bit_length() - 1))
    return lax.div(value, jnp.int32(size))


def remainder(value, size):
    if size & (size - 1) == 0:
        return lax.bitwise_and(value, jnp.int32(size - 1))
    return lax.rem(value, jnp.int32(size))


def plan_body(dims, list_order, me, *refs):
    row_count, capacity, slots, blocks_here = dims
    lists, (emb, after, idx) = refs[:row_count], refs[row_count : row_count + 3]
    lists = dict(zip(list_order, lists))
    sends = refs[row_count + 3 :]
    row = me[0]
    for i in range(slots):
        for line in (0, 1, 2, 4, 5):
            idx[line, i] = 0

    def each(step, start):
        if slots <= 8:
            for s in range(slots):
                start = step(s, start)
        else:
            lax.fori_loop(0, slots, step, start)

    for k in range(row_count):
        live_count = lists[k][2, 0]

        def step(s, counts, k=k, live_count=live_count):
            near = lists[k][0, s]
            far = lists[k][1, s]
            owner = quotient(far, blocks_here)
            live = s < live_count
            hit = live & (owner == row)
            slot = jnp.where(hit, k * capacity + counts[0], slots)
            idx[4, slot] = far - row * blocks_here
            idx[5, slot] = near
            if k > 0:
                return (counts[0] + hit.astype(jnp.int32),)
            shift = remainder(owner - row + row_count, row_count)
            rank = counts[1]
            for d in range(1, row_count):
                rank = jnp.where(shift == d, counts[1 + d], rank)
            slot = jnp.where(live, shift * capacity + rank, slots)
            idx[0, slot] = near - row * blocks_here
            idx[1, slot] = far
            idx[2, slot] = 1
            more = tuple(
                counts[1 + d] + (live & (shift == d)).astype(jnp.int32) for d in range(row_count)
            )
            return (counts[0] + hit.astype(jnp.int32), *more)

        each(step, (jnp.int32(0),) * (1 + row_count if k == 0 else 1))
    for k in range(1, row_count):
        for j in range(capacity):
            sends[k - 1][j * BLOCK : (j + 1) * BLOCK, :] = emb[at_block(idx[4, k * capacity + j]), :]


def squares(block):
    return jnp.sum(jnp.square(block.astype(F32)), axis=1, keepdims=True)


def partial_distance(left, right, left_sq, right_sq):
    inner = lax.dot_general(left, right, NT, preferred_element_type=F32)
    right_row = jnp.sum(jnp.where(eye_mask(BLOCK), right_sq, 0.0), axis=0, keepdims=True)
    return left_sq + right_row - 2.0 * inner


def self_distance_body(own_blocks, tile_count, me, emb, out):
    for i in range(own_blocks):
        block = emb[at_block(i * tile_count + me[1]), :]
        block_sq = squares(block)
        out[i * BLOCK : (i + 1) * BLOCK, :] = partial_distance(block, block, block_sq, block_sq)


def squares_body(emb, after, out):
    for b in range(out.shape[0] // BLOCK):
        part = slice(b * BLOCK, (b + 1) * BLOCK)
        out[part, :] = jnp.broadcast_to(squares(emb[part, :]), (BLOCK, BLOCK))


def pair_distance_body(order, capacity, idx, emb, own_squares, *refs):
    far, out = dict(zip(order, refs)), refs[-1]
    row_count = len(order) + 1
    for k in range(row_count):
        for j in range(capacity):
            slot = k * capacity + j
            left = emb[at_block(idx[0, slot]), :]
            left_sq = own_squares[at_block(idx[0, slot]), :]
            if k == 0:
                right = emb[at_block(idx[4, j]), :]
                right_sq = own_squares[at_block(idx[4, j]), :]
            else:
                right = far[k][j * BLOCK : (j + 1) * BLOCK, :]
                right_sq = squares(right)
            part = slice(slot * BLOCK, (slot + 1) * BLOCK)
            out[part, :] = partial_distance(left, right, left_sq, right_sq)


def self_tile_body(own_blocks, mine, other, packed, sums):
    for i in range(own_blocks):
        part = slice(i * BLOCK, (i + 1) * BLOCK)
        tile = jnp.exp(-kernel_gamma * (mine[part, :] + other[part, :] - 2.0))
        tile = jnp.where(eye_mask(BLOCK), 0.0, tile)
        packed[i] = pack(tile)
        sums[i : i + 1, :] = jnp.sum(tile, axis=0, keepdims=True)


def pair_tile_body(dims, me, idx, mine, other, self_sums, codes, powers, parts, near_tiles, home_tiles, table, *sends):
    row_count, capacity, per_core, blocks_here, tile_count = dims
    row, tile_index, core = me[0], me[1], me[2]
    table[...] = jnp.zeros(table.shape, F32)
    for i in range(self_sums.shape[0]):
        table[pl.ds(row * blocks_here + i * tile_count + tile_index, 1), :] = self_sums[i : i + 1, :]

    def add(block, line):
        place = pl.ds(block, 1)
        table[place, :] = table[place, :] + line

    for k in range(row_count):
        tiles = []
        for j in range(capacity):
            slot = k * capacity + j
            part = slice(slot * BLOCK, (slot + 1) * BLOCK)
            tile = jnp.exp(-kernel_gamma * (mine[part, :] + other[part, :] - 2.0))
            tile = jnp.where(idx[2, slot] > 0, tile, 0.0)
            turned = tile.T
            near_tiles[slot] = pack(turned)
            add(row * blocks_here + idx[0, slot], jnp.sum(turned, axis=0, keepdims=True))
            add(idx[1, slot], jnp.sum(tile, axis=0, keepdims=True))
            if k == 0:
                home_tiles[j] = pack(tile)
            tiles.append(tile)
        if k > 0:
            lines = ([], [])
            for inner in range(per_core):
                at = slice(inner * BLOCK, (inner + 1) * BLOCK)
                steps, power, part = encode(jnp.where(core == 0, tiles[inner], tiles[per_core + inner]))
                sends[k - 1][at, :] = steps
                lines[0].append(power)
                lines[1].append(part)
            pick_columns(idx, k, row_count, capacity, codes, powers, parts, sends[k - 1], per_core * BLOCK, lines)


def encode_blocks(values, codes, powers, parts):
    for b in range(powers.shape[0]):
        at = slice(b * BLOCK, (b + 1) * BLOCK)
        steps, power, part = encode(values[:, at])
        codes[:, at] = steps
        powers[b : b + 1, :] = power
        parts[b : b + 1, :] = part


def start_body(values, codes, powers, parts):
    encode_blocks(values, codes, powers, parts)


def split_body(row_count, per_core, *refs):
    others = row_count - 1
    messages, outs = refs[:others], refs[-others:]
    for message, out in zip(messages, outs):
        scales = scale_rows(message[message.shape[0] - CODE_ROWS :, :])
        for inner in range(per_core):
            steps = message[inner * BLOCK : (inner + 1) * BLOCK, :]
            out[inner] = pack(decode(steps, scales[inner : inner + 1, :]))


def pick_columns(idx, k, row_count, capacity, codes, powers, parts, send, base, lines):
    count = codes.shape[0]
    back = row_count - k
    blocks = [idx[0, k * capacity + j] for j in range(capacity)]
    blocks += [idx[4, back * capacity + j] for j in range(capacity)]
    for place, block in enumerate(blocks):
        send[base + place * count : base + (place + 1) * count, :] = codes[:, at_block(block)]
        lines[0].append(powers[pl.ds(block, 1), :])
        lines[1].append(parts[pl.ds(block, 1), :])
    send[base + len(blocks) * count :, :] = as_rows(*lines, CODE_ROWS)


def add_product(out, block, packed, values):
    place = at_block(block)
    out[:, place] = out[:, place] + product(packed, values)


def apply_own(dims, me, idx, inverse, own, near_tiles, home_tiles, self_tiles, out):
    row_count, capacity, per_core, blocks_here, tile_count = dims
    row, tile_index = me[0], me[1]
    out[...] = jnp.zeros(out.shape, F32)

    def scaled(block):
        return own[:, at_block(block)] * inverse[pl.ds(row * blocks_here + block, 1), :]

    for i in range(blocks_here // tile_count):
        block = i * tile_count + tile_index
        add_product(out, block, self_tiles[i], scaled(block))
    for j in range(capacity):
        add_product(out, idx[0, j], near_tiles[j], scaled(idx[4, j]))
        add_product(out, idx[4, j], home_tiles[j], scaled(idx[0, j]))


def apply_far(dims, me, idx, inverse, received, base, near_tiles, sent, shared, out):
    row_count, capacity, per_core, blocks_here, tile_count = dims
    core = me[2]
    count = out.shape[0]
    lines = [scale_rows(message[message.shape[0] - CODE_ROWS :, :]) for message in received]
    first_line = base // BLOCK

    def arrived(k, place, block):
        steps = received[k - 1][pl.ds(pl.multiple_of(base + place * count, CODE_ROWS), count), :]
        rows = lines[k - 1][first_line : first_line + 2 * capacity, :]
        return decode(steps, row_at(rows, place) * inverse[pl.ds(block, 1), :])

    for k in range(1, row_count):
        for j in range(capacity):
            slot = k * capacity + j
            values = arrived(row_count - k, capacity + j, idx[1, slot])
            add_product(out, idx[0, slot], near_tiles[slot], values)
            inner = j % per_core
            if j < per_core:
                place = core * per_core + inner
                packed = sent[k - 1][inner]
            else:
                place = (1 - core) * per_core + inner
                packed = shared[k - 1][inner]
            slot = k * capacity + place
            add_product(out, idx[4, slot], packed, arrived(k, place, idx[5, slot]))


def first_own_body(dims, me, idx, mine, other, own, near_tiles, home_tiles, self_tiles, out, degree, inverse):
    total = mine[...] + other[...]
    degree[...] = total
    inverse[...] = 1.0 / jnp.sqrt(total)
    apply_own(dims, me, idx, inverse, own, near_tiles, home_tiles, self_tiles, out)


def first_far_body(dims, coded, me, idx, inverse, started, near_tiles, *refs):
    row_count, per_core = dims[0], dims[2]
    others = row_count - 1
    sent, shared, messages = refs[:others], refs[others : 2 * others], refs[2 * others : 3 * others]
    out, total = refs[3 * others :]
    total[...] = started[...]
    apply_far(dims, me, idx, inverse, messages, per_core * BLOCK, near_tiles, sent, shared, total)
    put_sum(coded, total, out)


def second_apply_body(dims, me, idx, inverse, after, own, home_tiles, self_tiles, near_tiles, *refs):
    others = dims[0] - 1
    sent, shared, received = refs[:others], refs[others : 2 * others], refs[2 * others : 3 * others]
    out = refs[-1]
    apply_own(dims, me, idx, inverse, own, near_tiles, home_tiles, self_tiles, out)
    apply_far(dims, me, idx, inverse, received, 0, near_tiles, sent, shared, out)


def send_sum_body(coded, total, after, out):
    put_sum(coded, total, out)


def put_sum(coded, total, out):
    if not coded:
        out[...] = total[...]
        return
    lines = ([], [])
    blocks_here = total.shape[1] // BLOCK
    for b in range(blocks_here):
        at = slice(b * BLOCK, (b + 1) * BLOCK)
        steps, power, part = encode(total[:, at])
        out[:, at] = steps
        lines[0].append(power)
        lines[1].append(part)
    out[:, blocks_here * BLOCK :] = as_rows(*lines, out.shape[0])


def take_sum(coded, me, blocks_here, inverse, mine, other, out):
    if coded:
        tail = blocks_here * BLOCK
        my_scales, other_scales = scale_rows(mine[:, tail:]), scale_rows(other[:, tail:])
    for b in range(blocks_here):
        at = slice(b * BLOCK, (b + 1) * BLOCK)
        row = inverse[pl.ds(me[0] * blocks_here + b, 1), :]
        if coded:
            line = slice(b, b + 1)
            value = decode(mine[:, at], my_scales[line]) + decode(other[:, at], other_scales[line])
        else:
            value = mine[:, at] + other[:, at]
        out[:, at] = value * row


def mapped_body(dims, coded, me, idx, inverse, mine, other, out, *refs):
    row_count, capacity, per_core, blocks_here, tile_count = dims
    sends, (codes, powers, parts) = refs[:-3], refs[-3:]
    take_sum(coded, me, blocks_here, inverse, mine, other, out)
    encode_blocks(out, codes, powers, parts)
    for k in range(1, row_count):
        pick_columns(idx, k, row_count, capacity, codes, powers, parts, sends[k - 1], 0, ([], []))


def last_mapped_body(blocks_here, coded, me, inverse, mine, other, after, out):
    take_sum(coded, me, blocks_here, inverse, mine, other, out)


def folded(square):
    half = square.shape[0] // 2
    return jnp.concatenate([square[:half], square[half:]], axis=1)


def unfolded(terms):
    total = functools.reduce(lambda total, term: total + term[...], terms[1:], terms[0][...])
    width = total.shape[1] // 2
    return jnp.concatenate([total[:, :width], total[:, width:]], axis=0)


def gram_body(me, own, other, out):
    full = both_columns(me[2], own[...], other[...])
    out[...] = folded(gram(pack(full), full.shape[0]))


def factor_body(after, *refs):
    refs[-1][...] = lower_inverse(unfolded(refs[:-1]))


def second_gram_body(me, factor, own, other, mapped, out):
    full = both_columns(me[2], own[...], other[...])
    parts = thirds(times(factor[...], pack(full)))
    mapped[...] = parts[: mapped.shape[0]]
    out[...] = folded(gram(parts, full.shape[0]))


def final_body(me, mapped, *refs):
    terms, (out, value, sent) = refs[:-3], refs[-3:]
    factor = lower_inverse(unfolded(terms))
    own_cols = value.shape[0]
    part = jnp.where(me[2] == 0, factor[:own_cols], factor[own_cols:])
    copies = []
    chunk = value.shape[1] // sent.shape[0]
    for i in range(sent.shape[0]):
        at = slice(i * chunk, (i + 1) * chunk)
        value[:, at] = times(part, mapped[:, at])
        copies.append(pltpu.make_async_copy(value.at[:, at], out.at[:, at], sent.at[i]))
        copies[-1].start()
    for copy in copies:
        copy.wait()


def shift_by(value, axes, size, shift):
    return lax.ppermute(value, axes, [(i, (i + shift) % size) for i in range(size)])


def row_terms(value, row_count):
    return [value] + [shift_by(value, "rows", row_count, k) for k in range(1, row_count)]


def pair_step(value, name, flip):
    return lax.ppermute(value, name, [(i, i ^ flip) for i in range(lax.axis_size(name))])


def pair_sum(value, axes):
    terms = None
    steps = [(name, 1 << bit) for name in axes for bit in range((lax.axis_size(name) - 1).bit_length())]
    for name, flip in steps:
        if terms is not None:
            value = terms[0] + terms[1]
        terms = (value, pair_step(value, name, flip))
    return terms


def local(embeddings, start, pair_list, pair_count):
    row_count = lax.axis_size("rows")
    tile_count = lax.axis_size("tiles")
    core_count = lax.axis_size("cols")
    row_index = lax.axis_index("rows")
    tile_index = lax.axis_index("tiles")
    col_index = lax.axis_index("cols")
    rows_here, half_features = embeddings.shape
    blocks_here = rows_here // BLOCK
    slots = pair_list.shape[2]
    capacity = slots // row_count
    per_core = capacity // core_count
    own_blocks = blocks_here // tile_count
    own_cols = start.shape[1]
    block_count = row_count * blocks_here
    others = range(1, row_count)

    own_list = jnp.concatenate(
        [pair_list[0], jnp.broadcast_to(pair_count[:, None], (1, slots))], axis=0
    )
    lists = row_terms(own_list, row_count)
    list_order = [0, *sorted(others, key=lambda k: k * (row_count - k))]
    self_part = call(
        functools.partial(self_distance_body, own_blocks, tile_count),
        sds((own_blocks * BLOCK, BLOCK), F32),
        [ME, embeddings],
        smem_in=(0,),
    )
    planned = call(
        functools.partial(plan_body, (row_count, capacity, slots, blocks_here), list_order),
        [sds((6, slots + 1), jnp.int32)] + [sds((capacity * BLOCK, half_features), BF16) for _ in others],
        [ME, *[lists[k] for k in list_order], embeddings, self_part],
        smem_in=range(1 + row_count),
        any_in=(row_count + 2,),
        smem_out=(0,),
    )
    idx, sends = planned[0], planned[1:]
    order = sorted(others, key=lambda k: abs(k - row_count // 2))
    far = [shift_by(sends[k - 1], "rows", row_count, -k) for k in order]

    self_other = shift_by(self_part, "cols", core_count, 1)
    self_tiles, self_sums = call(
        functools.partial(self_tile_body, own_blocks),
        [sds((own_blocks, 2 * BLOCK, BLOCK), BF16), sds((own_blocks, BLOCK), F32)],
        [self_part, self_other],
    )
    values = start.T
    code_shapes = [((own_cols, rows_here), jnp.int16), ((blocks_here, BLOCK), F32), ((blocks_here, BLOCK), F32)]
    start_codes = call(start_body, [sds(*shape) for shape in code_shapes], [values])
    code_scratch = [pltpu.VMEM(*shape) for shape in code_shapes]
    coded = tile_count == 2
    own_squares = call(squares_body, sds((rows_here, BLOCK), F32), [embeddings, idx], any_in=(1,))
    pair_part = call(
        functools.partial(pair_distance_body, order, capacity),
        sds((slots * BLOCK, BLOCK), F32),
        [idx, embeddings, own_squares, *far],
        smem_in=(0,),
    )
    pair_other = shift_by(pair_part, "cols", core_count, 1)

    dims = (row_count, capacity, per_core, blocks_here, tile_count)
    table = sds((block_count, BLOCK), F32)
    picked = 2 * capacity * own_cols
    tiles = call(
        functools.partial(pair_tile_body, dims),
        [sds((slots, 2 * BLOCK, BLOCK), BF16), sds((capacity, 2 * BLOCK, BLOCK), BF16), table]
        + [sds((per_core * BLOCK + picked + CODE_ROWS, BLOCK), jnp.int16) for _ in others],
        [ME, idx, pair_part, pair_other, self_sums, *start_codes],
        smem_in=(0, 1),
    )
    near_tiles, home_tiles, degrees, sends = tiles[0], tiles[1], tiles[2], tiles[3:]
    degrees = functools.reduce(jnp.add, row_terms(degrees, row_count))
    degree_terms = pair_sum(degrees, ("tiles",))
    messages = [shift_by(sends[k - 1], "rows", row_count, k) for k in others]
    sent = call(
        functools.partial(split_body, row_count, per_core),
        [sds((per_core, 2 * BLOCK, BLOCK), BF16) for _ in others],
        [*messages, degree_terms[1]],
        any_in=(row_count - 1,),
    )
    shared = [shift_by(tile, "cols", core_count, 1) for tile in sent]

    block_shape = sds((own_cols, rows_here), F32)
    sum_shape = sds((own_cols, rows_here + BLOCK), jnp.int16) if coded else block_shape
    square = sds((2 * own_cols, 2 * own_cols), F32)
    folded_square = sds((own_cols, 4 * own_cols), F32)

    started, degree, inverse = call(
        functools.partial(first_own_body, dims),
        [block_shape, table, table],
        [ME, idx, *degree_terms, values, near_tiles, home_tiles, self_tiles],
        smem_in=(0, 1),
    )
    part = call(
        functools.partial(first_far_body, dims, coded),
        sum_shape,
        [ME, idx, inverse, started, near_tiles, *sent, *shared, *messages],
        smem_in=(0, 1),
        scratch=[pltpu.VMEM((own_cols, rows_here), F32)],
    )
    mine, other = pair_sum(part, ("tiles",))
    first = call(
        functools.partial(mapped_body, dims, coded),
        [block_shape] + [sds((picked + CODE_ROWS, BLOCK), jnp.int16) for _ in others],
        [ME, idx, inverse, mine, other],
        smem_in=(0, 1),
        scratch=code_scratch,
    )
    mapped, sends = first[0], first[1:]
    received = [shift_by(sends[k - 1], "rows", row_count, k) for k in others]

    mapped_other = shift_by(mapped, "cols", core_count, 1)
    first_gram = call(gram_body, folded_square, [ME, mapped, mapped_other], smem_in=(0,))
    part = call(
        functools.partial(second_apply_body, dims),
        block_shape,
        [ME, idx, inverse, first_gram, mapped, home_tiles, self_tiles, near_tiles, *sent, *shared, *received],
        smem_in=(0, 1),
        any_in=(3,),
    )
    steps = (row_count - 1).bit_length()
    for bit in range(steps - 1):
        first_gram = first_gram + pair_step(first_gram, "rows", 1 << bit)
    part = call(functools.partial(send_sum_body, coded), sum_shape, [part, first_gram])
    gram_terms = (first_gram, pair_step(first_gram, "rows", 1 << (steps - 1)))
    mine, other = pair_sum(part, ("tiles",))
    second = call(
        functools.partial(last_mapped_body, blocks_here, coded),
        block_shape,
        [ME, inverse, mine, other, gram_terms[1]],
        smem_in=(0,),
        any_in=(4,),
    )
    second_other = shift_by(second, "cols", core_count, 1)
    factor = call(factor_body, square, [second, *gram_terms], any_in=(0,))
    full, second_gram = call(
        second_gram_body,
        [sds((4 * own_cols, rows_here), BF16), folded_square],
        [ME, factor, second, second_other],
        smem_in=(0,),
    )
    vectors = call(
        final_body,
        block_shape,
        [ME, full, *row_terms(second_gram, row_count)],
        any_out=(0,),
        scratch=[pltpu.VMEM((own_cols, rows_here), F32), pltpu.SemaphoreType.DMA((4,))],
    )
    own_degree = lax.dynamic_slice_in_dim(degree, row_index * blocks_here, blocks_here, 0)
    return (vectors.T, own_degree.reshape(rows_here))


def solution(mesh):
    in_specs = (
        P(("groups", "rows"), "cols"),
        P(("groups", "rows"), "cols"),
        P(("groups", "rows", "tiles"), None, None),
        P(("groups", "rows", "tiles")),
    )
    out_specs = (P(("groups", "rows"), "cols"), P(("groups", "rows")))
    return jax.shard_map(local, mesh=mesh, in_specs=in_specs, out_specs=out_specs, check_vma=False)
```

```python
import functools

import jax
import jax.numpy as jnp
from jax import lax
from jax.experimental import pallas as pl
from jax.experimental.pallas import tpu as pltpu
from jax.sharding import PartitionSpec as P

BLOCK = 128
kernel_gamma = 14.0
CODE_TOP = 32767.0
PART_TOP = 16384.0
CODE_ROWS = 16

VMEM = pl.BlockSpec(memory_space=pltpu.VMEM)
ANY = pl.BlockSpec(memory_space=pl.ANY)
F32 = jnp.float32
BF16 = jnp.bfloat16
HIGHEST = lax.Precision.HIGHEST
NT = (((1,), (1,)), ((), ()))


ME = None


def with_position(body):
    def inner(*refs):
        return body([lax.axis_index(name) for name in ("rows", "tiles", "cols")], *refs)

    return inner


class Late:
    def __init__(self, source, table, arrived):
        self.table = table
        self.copy = pltpu.make_async_copy(source, table, arrived)
        self.copy.start()

    def ready(self):
        self.copy.wait()
        return self.table


def with_late(body, places, count):
    def inner(*refs):
        refs, tables, arrived = refs[:-1 - count], refs[-1 - count : -1], refs[-1]
        refs = list(refs)
        for i, place in enumerate(places):
            refs[place] = Late(refs[place], tables[i], arrived.at[i])
        body(*refs)

    return inner


def call(body, outs, args, late=(), any_in=(), scratch=(), any_out=()):
    if args[0] is ME:
        body, args = with_position(body), args[1:]
        late, any_in = [[i - 1 for i in places] for places in (late, any_in)]
    if late:
        scratch = [
            *scratch,
            *[pltpu.SMEM(args[i].shape, args[i].dtype) for i in late],
            pltpu.SemaphoreType.DMA((len(late),)),
        ]
        any_in = [*any_in, *late]
        body = with_late(body, late, len(late))
    single = not isinstance(outs, (list, tuple))
    shapes = [outs] if single else list(outs)
    result = pl.pallas_call(
        body,
        out_shape=shapes,
        in_specs=[ANY if i in any_in else VMEM for i in range(len(args))],
        out_specs=[ANY if i in any_out else VMEM for i in range(len(shapes))],
        scratch_shapes=list(scratch),
        compiler_params=pltpu.CompilerParams(vmem_limit_bytes=48 * 2**20),
    )(*args)
    return result[0] if single else result


def sds(shape, dtype):
    return jax.ShapeDtypeStruct(shape, dtype)


def at_block(index):
    return pl.ds(pl.multiple_of(index * BLOCK, BLOCK), BLOCK)


def eye_mask(size):
    return lax.broadcasted_iota(jnp.int32, (size, size), 0) == lax.broadcasted_iota(
        jnp.int32, (size, size), 1
    )


def halves(value):
    high = value.astype(BF16)
    low = (value - high.astype(F32)).astype(BF16)
    return high, low


def pack(tile):
    return jnp.concatenate(halves(tile), axis=0)


def scale_of(power, part):
    return jnp.exp2(power) * (part * (1.0 / PART_TOP))


def encode(values):
    most = jnp.maximum(jnp.max(jnp.abs(values), axis=0, keepdims=True), 1e-30)
    power = jnp.floor(jnp.log2(most)) + 1.0
    part = jnp.floor(most * jnp.exp2(-power) * PART_TOP) + 1.0
    steps = jnp.floor(values * (CODE_TOP / scale_of(power, part)) + 0.5)
    steps = jnp.minimum(jnp.maximum(steps, -CODE_TOP), CODE_TOP)
    return steps.astype(jnp.int32).astype(jnp.int16), power, part


def decode(steps, scale):
    return steps.astype(jnp.int32).astype(F32) * (scale * (1.0 / CODE_TOP))


def as_rows(powers, parts, count):
    fill = jnp.zeros((count // 2 - len(powers), BLOCK), F32)
    fill = [fill] if fill.shape[0] else []
    rows = jnp.concatenate([*powers, *fill, *parts, *fill], axis=0)
    return rows.astype(jnp.int32).astype(jnp.int16)


def scale_rows(rows):
    rows = rows.astype(jnp.int32).astype(F32)
    half = rows.shape[0] // 2
    return scale_of(rows[:half], rows[half:])


def row_at(rows, place):
    if isinstance(place, int):
        return rows[place : place + 1, :]
    line = rows[:1, :]
    for i in range(1, rows.shape[0]):
        line = jnp.where(place == i, rows[i : i + 1, :], line)
    return line


def product(packed, values):
    left = jnp.concatenate(halves(values), axis=0)
    both = jnp.dot(jnp.concatenate([left, left], axis=1), packed, preferred_element_type=F32)
    count = values.shape[0]
    return both[:count] + both[count:]


def thirds(value):
    high = value.astype(BF16)
    rest = value - high.astype(F32)
    middle = rest.astype(BF16)
    low = (rest - middle.astype(F32)).astype(BF16)
    return jnp.concatenate([high, middle, low], axis=0)


def gram(parts, n):
    cross = lax.dot_general(parts, parts, NT, preferred_element_type=F32)
    count = parts.shape[0] // n
    pairs = sorted(((i, j) for i in range(count) for j in range(count)), key=lambda p: -p[0] - p[1])
    total = None
    for i, j in pairs:
        piece = cross[i * n : (i + 1) * n, j * n : (j + 1) * n]
        total = piece if total is None else total + piece
    return total


def times(left, parts):
    m = left.shape[0]
    left = jnp.concatenate(halves(left), axis=0)
    both = jnp.dot(jnp.concatenate([left, left], axis=1), parts, preferred_element_type=F32)
    return both[m:] + both[:m]


def lower_inverse(matrix, step=8):
    n = matrix.shape[0]
    state = jnp.concatenate([matrix, eye_mask(n).astype(F32)], axis=1)
    done = []
    for j in range(0, n, step):
        top = j // 8 * 8
        if top > n - state.shape[0]:
            done.append(state[:8])
            state = state[8:]
        base = j - top
        rows = lax.broadcasted_iota(jnp.int32, state.shape, 0)
        columns = [jnp.broadcast_to(state[:, j + i : j + i + 1], state.shape) for i in range(step)]
        lines = [state[base + i : base + i + 1, :] for i in range(step)]
        pivot = [[columns[k][base + i : base + i + 1, :] for k in range(step)] for i in range(step)]
        for i in range(step):
            if i % 2 == 0:
                first, cross, second = pivot[i][i], pivot[i][i + 1], pivot[i + 1][i + 1]
                reciprocals = (1.0 / first, first / (first * second - cross * cross))
            reciprocal = reciprocals[i % 2]
            scaled = lines[i] * reciprocal
            ratio = [pivot[i][k] * reciprocal for k in range(step)]
            for k in range(i + 1, step):
                lines[k] = lines[k] - pivot[k][i] * scaled
                columns[k] = columns[k] - columns[i] * ratio[k]
                for m in range(i + 1, step):
                    pivot[k][m] = pivot[k][m] - pivot[k][i] * ratio[m]
            state = state - jnp.where(rows > base + i, columns[i], 0.0) * scaled
    state = jnp.concatenate([*done, state], axis=0)
    pivots = jnp.sum(jnp.where(eye_mask(n), state[:, :n], 0.0), axis=1, keepdims=True)
    return state[:, n:] / jnp.sqrt(pivots)


def both_columns(core, own, other):
    first = core == 0
    return jnp.concatenate(
        [jnp.where(first, own, other), jnp.where(first, other, own)], axis=0
    )


def quotient(value, size):
    if size & (size - 1) == 0:
        return lax.shift_right_logical(value, jnp.int32(size.bit_length() - 1))
    return lax.div(value, jnp.int32(size))


def remainder(value, size):
    if size & (size - 1) == 0:
        return lax.bitwise_and(value, jnp.int32(size - 1))
    return lax.rem(value, jnp.int32(size))


def plan_body(dims, list_order, me, *refs):
    row_count, capacity, slots, blocks_here = dims
    lists, (emb, after, idx_out) = refs[:row_count], refs[row_count : row_count + 3]
    sends, (idx, left) = refs[row_count + 3 : -2], refs[-2:]
    row = me[0]
    for i in range(slots):
        for line in (0, 1, 2, 4, 5):
            idx[line, i] = 0
    lists = dict(zip(list_order, [one.ready() for one in lists]))

    def each(step, start):
        if slots <= 8:
            for s in range(slots):
                start = step(s, start)
        else:
            lax.fori_loop(0, slots, step, start)

    for k in range(row_count):
        live_count = lists[k][2, 0]

        def step(s, counts, k=k, live_count=live_count):
            near = lists[k][0, s]
            far = lists[k][1, s]
            owner = quotient(far, blocks_here)
            live = s < live_count
            hit = live & (owner == row)
            slot = jnp.where(hit, k * capacity + counts[0], slots)
            idx[4, slot] = far - row * blocks_here
            idx[5, slot] = near
            if k > 0:
                return (counts[0] + hit.astype(jnp.int32),)
            shift = remainder(owner - row + row_count, row_count)
            rank = counts[1]
            for d in range(1, row_count):
                rank = jnp.where(shift == d, counts[1 + d], rank)
            slot = jnp.where(live, shift * capacity + rank, slots)
            idx[0, slot] = near - row * blocks_here
            idx[1, slot] = far
            idx[2, slot] = 1
            more = tuple(
                counts[1 + d] + (live & (shift == d)).astype(jnp.int32) for d in range(row_count)
            )
            return (counts[0] + hit.astype(jnp.int32), *more)

        each(step, (jnp.int32(0),) * (1 + row_count if k == 0 else 1))
    leave = pltpu.make_async_copy(idx, idx_out, left)
    leave.start()
    for k in range(1, row_count):
        for j in range(capacity):
            sends[k - 1][j * BLOCK : (j + 1) * BLOCK, :] = emb[at_block(idx[4, k * capacity + j]), :]
    leave.wait()


def squares(block):
    return jnp.sum(jnp.square(block.astype(F32)), axis=1, keepdims=True)


def as_row(column):
    return jnp.sum(jnp.where(eye_mask(BLOCK), column, 0.0), axis=0, keepdims=True)


def partial_distance(left, right, left_sq, right_row):
    inner = lax.dot_general(left, right, NT, preferred_element_type=F32)
    return left_sq + right_row - 2.0 * inner


def self_distance_body(own_blocks, tile_count, me, emb, out):
    for i in range(own_blocks):
        block = emb[at_block(i * tile_count + me[1]), :]
        block_sq = squares(block)
        out[i * BLOCK : (i + 1) * BLOCK, :] = partial_distance(
            block, block, block_sq, as_row(block_sq)
        )


def squares_body(emb, after, out):
    for b in range(out.shape[0] // BLOCK):
        part = slice(b * BLOCK, (b + 1) * BLOCK)
        out[part, :] = jnp.broadcast_to(squares(emb[part, :]), (BLOCK, BLOCK))


def pair_distance_body(order, capacity, idx, emb, own_squares, *refs):
    far, out = dict(zip(order, refs)), refs[-1]
    rows = {}
    for k in order:
        for j in range(capacity):
            rows[k, j] = as_row(squares(far[k][j * BLOCK : (j + 1) * BLOCK, :]))
    idx = idx.ready()
    for k in range(len(order) + 1):
        for j in range(capacity):
            slot = k * capacity + j
            left = emb[at_block(idx[0, slot]), :]
            left_sq = own_squares[at_block(idx[0, slot]), :]
            if k == 0:
                right = emb[at_block(idx[4, j]), :]
                right_row = as_row(own_squares[at_block(idx[4, j]), :])
            else:
                right = far[k][j * BLOCK : (j + 1) * BLOCK, :]
                right_row = rows[k, j]
            part = slice(slot * BLOCK, (slot + 1) * BLOCK)
            out[part, :] = partial_distance(left, right, left_sq, right_row)


def self_tile_body(own_blocks, mine, other, packed, sums):
    for i in range(own_blocks):
        part = slice(i * BLOCK, (i + 1) * BLOCK)
        tile = jnp.exp(-kernel_gamma * (mine[part, :] + other[part, :] - 2.0))
        tile = jnp.where(eye_mask(BLOCK), 0.0, tile)
        packed[i] = pack(tile)
        sums[i : i + 1, :] = jnp.sum(tile, axis=0, keepdims=True)


def pair_tile_body(dims, me, idx, mine, other, self_sums, codes, powers, parts, near_tiles, home_tiles, table, *sends):
    row_count, capacity, per_core, blocks_here, tile_count = dims
    row, tile_index, core = me[0], me[1], me[2]
    table[...] = jnp.zeros(table.shape, F32)
    for i in range(self_sums.shape[0]):
        table[pl.ds(row * blocks_here + i * tile_count + tile_index, 1), :] = self_sums[i : i + 1, :]

    def add(block, line):
        place = pl.ds(block, 1)
        table[place, :] = table[place, :] + line

    all_tiles = jnp.exp(-kernel_gamma * (mine[...] + other[...] - 2.0))
    idx = idx.ready()
    for k in range(row_count):
        tiles = []
        for j in range(capacity):
            slot = k * capacity + j
            tile = all_tiles[slot * BLOCK : (slot + 1) * BLOCK]
            tile = jnp.where(idx[2, slot] > 0, tile, 0.0)
            turned = tile.T
            near_tiles[slot] = pack(turned)
            add(row * blocks_here + idx[0, slot], jnp.sum(turned, axis=0, keepdims=True))
            add(idx[1, slot], jnp.sum(tile, axis=0, keepdims=True))
            if k == 0:
                home_tiles[j] = pack(tile)
            tiles.append(tile)
        if k > 0:
            lines = ([], [])
            for inner in range(per_core):
                at = slice(inner * BLOCK, (inner + 1) * BLOCK)
                steps, power, part = encode(jnp.where(core == 0, tiles[inner], tiles[per_core + inner]))
                sends[k - 1][at, :] = steps
                lines[0].append(power)
                lines[1].append(part)
            pick_columns(idx, k, row_count, capacity, codes, powers, parts, sends[k - 1], per_core * BLOCK, lines)


def encode_blocks(values, codes, powers, parts):
    for b in range(powers.shape[0]):
        at = slice(b * BLOCK, (b + 1) * BLOCK)
        steps, power, part = encode(values[:, at])
        codes[:, at] = steps
        powers[b : b + 1, :] = power
        parts[b : b + 1, :] = part


def start_body(values, codes, powers, parts):
    encode_blocks(values, codes, powers, parts)


def split_body(row_count, per_core, *refs):
    others = row_count - 1
    messages, outs = refs[:others], refs[-others:]
    for message, out in zip(messages, outs):
        scales = scale_rows(message[message.shape[0] - CODE_ROWS :, :])
        for inner in range(per_core):
            steps = message[inner * BLOCK : (inner + 1) * BLOCK, :]
            out[inner] = pack(decode(steps, scales[inner : inner + 1, :]))


def pick_columns(idx, k, row_count, capacity, codes, powers, parts, send, base, lines):
    count = codes.shape[0]
    back = row_count - k
    blocks = [idx[0, k * capacity + j] for j in range(capacity)]
    blocks += [idx[4, back * capacity + j] for j in range(capacity)]
    for place, block in enumerate(blocks):
        send[base + place * count : base + (place + 1) * count, :] = codes[:, at_block(block)]
        lines[0].append(powers[pl.ds(block, 1), :])
        lines[1].append(parts[pl.ds(block, 1), :])
    send[base + len(blocks) * count :, :] = as_rows(*lines, CODE_ROWS)


def add_product(out, block, packed, values):
    place = at_block(block)
    out[:, place] = out[:, place] + product(packed, values)


def apply_own(dims, me, idx, inverse, own, near_tiles, home_tiles, self_tiles, out):
    row_count, capacity, per_core, blocks_here, tile_count = dims
    row, tile_index = me[0], me[1]
    out[...] = jnp.zeros(out.shape, F32)

    def scaled(block):
        return own[:, at_block(block)] * inverse[pl.ds(row * blocks_here + block, 1), :]

    for i in range(blocks_here // tile_count):
        block = i * tile_count + tile_index
        add_product(out, block, self_tiles[i], scaled(block))
    idx = idx.ready()
    for j in range(capacity):
        add_product(out, idx[0, j], near_tiles[j], scaled(idx[4, j]))
        add_product(out, idx[4, j], home_tiles[j], scaled(idx[0, j]))
    return idx


def apply_far(dims, me, idx, inverse, received, base, near_tiles, sent, shared, out):
    row_count, capacity, per_core, blocks_here, tile_count = dims
    core = me[2]
    count = out.shape[0]
    lines = [scale_rows(message[message.shape[0] - CODE_ROWS :, :]) for message in received]
    first_line = base // BLOCK

    def arrived(k, place, block):
        steps = received[k - 1][pl.ds(pl.multiple_of(base + place * count, CODE_ROWS), count), :]
        rows = lines[k - 1][first_line : first_line + 2 * capacity, :]
        return decode(steps, row_at(rows, place) * inverse[pl.ds(block, 1), :])

    for k in range(1, row_count):
        for j in range(capacity):
            slot = k * capacity + j
            values = arrived(row_count - k, capacity + j, idx[1, slot])
            add_product(out, idx[0, slot], near_tiles[slot], values)
            inner = j % per_core
            if j < per_core:
                place = core * per_core + inner
                packed = sent[k - 1][inner]
            else:
                place = (1 - core) * per_core + inner
                packed = shared[k - 1][inner]
            slot = k * capacity + place
            add_product(out, idx[4, slot], packed, arrived(k, place, idx[5, slot]))


def first_own_body(dims, me, idx, mine, other, own, near_tiles, home_tiles, self_tiles, out, degree, inverse):
    total = mine[...] + other[...]
    degree[...] = total
    inverse[...] = 1.0 / jnp.sqrt(total)
    apply_own(dims, me, idx, inverse, own, near_tiles, home_tiles, self_tiles, out)


def first_far_body(dims, coded, me, idx, inverse, started, near_tiles, *refs):
    row_count, per_core = dims[0], dims[2]
    others = row_count - 1
    sent, shared, messages = refs[:others], refs[others : 2 * others], refs[2 * others : 3 * others]
    out, total = refs[3 * others :]
    total[...] = started[...]
    apply_far(dims, me, idx.ready(), inverse, messages, per_core * BLOCK, near_tiles, sent, shared, total)
    put_sum(coded, total, out)


def second_apply_body(dims, me, idx, inverse, after, own, home_tiles, self_tiles, near_tiles, *refs):
    others = dims[0] - 1
    sent, shared, received = refs[:others], refs[others : 2 * others], refs[2 * others : 3 * others]
    out = refs[-1]
    idx = apply_own(dims, me, idx, inverse, own, near_tiles, home_tiles, self_tiles, out)
    apply_far(dims, me, idx, inverse, received, 0, near_tiles, sent, shared, out)


def send_sum_body(coded, total, after, out):
    put_sum(coded, total, out)


def put_sum(coded, total, out):
    if not coded:
        out[...] = total[...]
        return
    lines = ([], [])
    blocks_here = total.shape[1] // BLOCK
    for b in range(blocks_here):
        at = slice(b * BLOCK, (b + 1) * BLOCK)
        steps, power, part = encode(total[:, at])
        out[:, at] = steps
        lines[0].append(power)
        lines[1].append(part)
    out[:, blocks_here * BLOCK :] = as_rows(*lines, out.shape[0])


def take_sum(coded, me, blocks_here, inverse, mine, other, out):
    if coded:
        tail = blocks_here * BLOCK
        my_scales, other_scales = scale_rows(mine[:, tail:]), scale_rows(other[:, tail:])
    for b in range(blocks_here):
        at = slice(b * BLOCK, (b + 1) * BLOCK)
        row = inverse[pl.ds(me[0] * blocks_here + b, 1), :]
        if coded:
            line = slice(b, b + 1)
            value = decode(mine[:, at], my_scales[line]) + decode(other[:, at], other_scales[line])
        else:
            value = mine[:, at] + other[:, at]
        out[:, at] = value * row


def mapped_body(dims, coded, me, idx, inverse, mine, other, out, *refs):
    row_count, capacity, per_core, blocks_here, tile_count = dims
    sends, (codes, powers, parts) = refs[:-3], refs[-3:]
    take_sum(coded, me, blocks_here, inverse, mine, other, out)
    encode_blocks(out, codes, powers, parts)
    idx = idx.ready()
    for k in range(1, row_count):
        pick_columns(idx, k, row_count, capacity, codes, powers, parts, sends[k - 1], 0, ([], []))


def last_mapped_body(blocks_here, coded, me, inverse, mine, other, after, out):
    take_sum(coded, me, blocks_here, inverse, mine, other, out)


def folded(square):
    half = square.shape[0] // 2
    return jnp.concatenate([square[:half], square[half:]], axis=1)


def unfolded(terms):
    total = functools.reduce(lambda total, term: total + term[...], terms[1:], terms[0][...])
    width = total.shape[1] // 2
    return jnp.concatenate([total[:, :width], total[:, width:]], axis=0)


def gram_body(me, own, other, out):
    full = both_columns(me[2], own[...], other[...])
    out[...] = folded(gram(pack(full), full.shape[0]))


def factor_body(after, *refs):
    refs[-1][...] = lower_inverse(unfolded(refs[:-1]))


def second_gram_body(me, factor, own, other, mapped, out):
    full = both_columns(me[2], own[...], other[...])
    parts = thirds(times(factor[...], pack(full)))
    mapped[...] = parts[: mapped.shape[0]]
    out[...] = folded(gram(parts, full.shape[0]))


def final_body(me, mapped, *refs):
    terms, (out, value, sent) = refs[:-3], refs[-3:]
    factor = lower_inverse(unfolded(terms))
    own_cols = value.shape[0]
    part = jnp.where(me[2] == 0, factor[:own_cols], factor[own_cols:])
    copies = []
    chunk = value.shape[1] // sent.shape[0]
    for i in range(sent.shape[0]):
        at = slice(i * chunk, (i + 1) * chunk)
        value[:, at] = times(part, mapped[:, at])
        copies.append(pltpu.make_async_copy(value.at[:, at], out.at[:, at], sent.at[i]))
        copies[-1].start()
    for copy in copies:
        copy.wait()


def shift_by(value, axes, size, shift):
    return lax.ppermute(value, axes, [(i, (i + shift) % size) for i in range(size)])


def row_terms(value, row_count):
    return [value] + [shift_by(value, "rows", row_count, k) for k in range(1, row_count)]


def pair_step(value, name, flip):
    return lax.ppermute(value, name, [(i, i ^ flip) for i in range(lax.axis_size(name))])


def pair_sum(value, axes):
    terms = None
    steps = [(name, 1 << bit) for name in axes for bit in range((lax.axis_size(name) - 1).bit_length())]
    for name, flip in steps:
        if terms is not None:
            value = terms[0] + terms[1]
        terms = (value, pair_step(value, name, flip))
    return terms


def local(embeddings, start, pair_list, pair_count):
    row_count = lax.axis_size("rows")
    tile_count = lax.axis_size("tiles")
    core_count = lax.axis_size("cols")
    row_index = lax.axis_index("rows")
    tile_index = lax.axis_index("tiles")
    col_index = lax.axis_index("cols")
    rows_here, half_features = embeddings.shape
    blocks_here = rows_here // BLOCK
    slots = pair_list.shape[2]
    capacity = slots // row_count
    per_core = capacity // core_count
    own_blocks = blocks_here // tile_count
    own_cols = start.shape[1]
    block_count = row_count * blocks_here
    others = range(1, row_count)

    own_list = jnp.concatenate(
        [pair_list[0], jnp.broadcast_to(pair_count[:, None], (1, slots))], axis=0
    )
    lists = row_terms(own_list, row_count)
    list_order = [0, *sorted(others, key=lambda k: k * (row_count - k))]
    self_part = call(
        functools.partial(self_distance_body, own_blocks, tile_count),
        sds((own_blocks * BLOCK, BLOCK), F32),
        [ME, embeddings],
    )
    planned = call(
        functools.partial(plan_body, (row_count, capacity, slots, blocks_here), list_order),
        [sds((6, slots + 1), jnp.int32)] + [sds((capacity * BLOCK, half_features), BF16) for _ in others],
        [ME, *[lists[k] for k in list_order], embeddings, self_part],
        late=range(1, 1 + row_count),
        any_in=(row_count + 2,),
        any_out=(0,),
        scratch=[pltpu.SMEM((6, slots + 1), jnp.int32), pltpu.SemaphoreType.DMA],
    )
    idx, sends = planned[0], planned[1:]
    order = sorted(others, key=lambda k: abs(k - row_count // 2))
    far = [shift_by(sends[k - 1], "rows", row_count, -k) for k in order]

    self_other = shift_by(self_part, "cols", core_count, 1)
    self_tiles, self_sums = call(
        functools.partial(self_tile_body, own_blocks),
        [sds((own_blocks, 2 * BLOCK, BLOCK), BF16), sds((own_blocks, BLOCK), F32)],
        [self_part, self_other],
    )
    values = start.T
    code_shapes = [((own_cols, rows_here), jnp.int16), ((blocks_here, BLOCK), F32), ((blocks_here, BLOCK), F32)]
    start_codes = call(start_body, [sds(*shape) for shape in code_shapes], [values])
    code_scratch = [pltpu.VMEM(*shape) for shape in code_shapes]
    coded = tile_count == 2
    own_squares = call(squares_body, sds((rows_here, BLOCK), F32), [embeddings, idx], any_in=(1,))
    pair_part = call(
        functools.partial(pair_distance_body, order, capacity),
        sds((slots * BLOCK, BLOCK), F32),
        [idx, embeddings, own_squares, *far],
        late=(0,),
    )
    pair_other = shift_by(pair_part, "cols", core_count, 1)

    dims = (row_count, capacity, per_core, blocks_here, tile_count)
    table = sds((block_count, BLOCK), F32)
    picked = 2 * capacity * own_cols
    tiles = call(
        functools.partial(pair_tile_body, dims),
        [sds((slots, 2 * BLOCK, BLOCK), BF16), sds((capacity, 2 * BLOCK, BLOCK), BF16), table]
        + [sds((per_core * BLOCK + picked + CODE_ROWS, BLOCK), jnp.int16) for _ in others],
        [ME, idx, pair_part, pair_other, self_sums, *start_codes],
        late=(1,),
    )
    near_tiles, home_tiles, degrees, sends = tiles[0], tiles[1], tiles[2], tiles[3:]
    degrees = functools.reduce(jnp.add, row_terms(degrees, row_count))
    degree_terms = pair_sum(degrees, ("tiles",))
    messages = [shift_by(sends[k - 1], "rows", row_count, k) for k in others]
    sent = call(
        functools.partial(split_body, row_count, per_core),
        [sds((per_core, 2 * BLOCK, BLOCK), BF16) for _ in others],
        [*messages, degree_terms[1]],
        any_in=(row_count - 1,),
    )
    shared = [shift_by(tile, "cols", core_count, 1) for tile in sent]

    block_shape = sds((own_cols, rows_here), F32)
    sum_shape = sds((own_cols, rows_here + BLOCK), jnp.int16) if coded else block_shape
    square = sds((2 * own_cols, 2 * own_cols), F32)
    folded_square = sds((own_cols, 4 * own_cols), F32)

    started, degree, inverse = call(
        functools.partial(first_own_body, dims),
        [block_shape, table, table],
        [ME, idx, *degree_terms, values, near_tiles, home_tiles, self_tiles],
        late=(1,),
    )
    part = call(
        functools.partial(first_far_body, dims, coded),
        sum_shape,
        [ME, idx, inverse, started, near_tiles, *sent, *shared, *messages],
        late=(1,),
        scratch=[pltpu.VMEM((own_cols, rows_here), F32)],
    )
    mine, other = pair_sum(part, ("tiles",))
    first = call(
        functools.partial(mapped_body, dims, coded),
        [block_shape] + [sds((picked + CODE_ROWS, BLOCK), jnp.int16) for _ in others],
        [ME, idx, inverse, mine, other],
        late=(1,),
        scratch=code_scratch,
    )
    mapped, sends = first[0], first[1:]
    received = [shift_by(sends[k - 1], "rows", row_count, k) for k in others]

    mapped_other = shift_by(mapped, "cols", core_count, 1)
    first_gram = call(gram_body, folded_square, [ME, mapped, mapped_other])
    part = call(
        functools.partial(second_apply_body, dims),
        block_shape,
        [ME, idx, inverse, first_gram, mapped, home_tiles, self_tiles, near_tiles, *sent, *shared, *received],
        late=(1,),
        any_in=(3,),
    )
    steps = (row_count - 1).bit_length()
    for bit in range(steps - 1):
        first_gram = first_gram + pair_step(first_gram, "rows", 1 << bit)
    part = call(functools.partial(send_sum_body, coded), sum_shape, [part, first_gram])
    gram_terms = (first_gram, pair_step(first_gram, "rows", 1 << (steps - 1)))
    mine, other = pair_sum(part, ("tiles",))
    second = call(
        functools.partial(last_mapped_body, blocks_here, coded),
        block_shape,
        [ME, inverse, mine, other, gram_terms[1]],
        any_in=(4,),
    )
    second_other = shift_by(second, "cols", core_count, 1)
    factor = call(factor_body, square, [second, *gram_terms], any_in=(0,))
    full, second_gram = call(
        second_gram_body,
        [sds((4 * own_cols, rows_here), BF16), folded_square],
        [ME, factor, second, second_other],
    )
    vectors = call(
        final_body,
        block_shape,
        [ME, full, *row_terms(second_gram, row_count)],
        any_out=(0,),
        scratch=[pltpu.VMEM((own_cols, rows_here), F32), pltpu.SemaphoreType.DMA((4,))],
    )
    own_degree = lax.dynamic_slice_in_dim(degree, row_index * blocks_here, blocks_here, 0)
    return (vectors.T, own_degree.reshape(rows_here))


def solution(mesh):
    in_specs = (
        P(("groups", "rows"), "cols"),
        P(("groups", "rows"), "cols"),
        P(("groups", "rows", "tiles"), None, None),
        P(("groups", "rows", "tiles")),
    )
    out_specs = (P(("groups", "rows"), "cols"), P(("groups", "rows")))
    return jax.shard_map(local, mesh=mesh, in_specs=in_specs, out_specs=out_specs, check_vma=False)
```

```python
import functools

import jax
import jax.numpy as jnp
from jax import lax
from jax.experimental import pallas as pl
from jax.experimental.pallas import tpu as pltpu
from jax.sharding import PartitionSpec as P

BLOCK = 128
kernel_gamma = 14.0
CODE_TOP = 32767.0
PART_TOP = 16384.0
CODE_ROWS = 16

VMEM = pl.BlockSpec(memory_space=pltpu.VMEM)
ANY = pl.BlockSpec(memory_space=pl.ANY)
F32 = jnp.float32
BF16 = jnp.bfloat16
HIGHEST = lax.Precision.HIGHEST
NT = (((1,), (1,)), ((), ()))


ME = None


def with_position(body):
    def inner(*refs):
        return body([lax.axis_index(name) for name in ("rows", "tiles", "cols")], *refs)

    return inner


class Late:
    def __init__(self, source, table, arrived):
        self.table = table
        self.copy = pltpu.make_async_copy(source, table, arrived)
        self.copy.start()

    def ready(self):
        self.copy.wait()
        return self.table


def with_late(body, places, count):
    def inner(*refs):
        refs, tables, arrived = refs[:-1 - count], refs[-1 - count : -1], refs[-1]
        refs = list(refs)
        for i, place in enumerate(places):
            refs[place] = Late(refs[place], tables[i], arrived.at[i])
        body(*refs)

    return inner


def call(body, outs, args, late=(), any_in=(), scratch=(), any_out=()):
    if args[0] is ME:
        body, args = with_position(body), args[1:]
        late, any_in = [[i - 1 for i in places] for places in (late, any_in)]
    if late:
        scratch = [
            *scratch,
            *[pltpu.SMEM(args[i].shape, args[i].dtype) for i in late],
            pltpu.SemaphoreType.DMA((len(late),)),
        ]
        any_in = [*any_in, *late]
        body = with_late(body, late, len(late))
    single = not isinstance(outs, (list, tuple))
    shapes = [outs] if single else list(outs)
    result = pl.pallas_call(
        body,
        out_shape=shapes,
        in_specs=[ANY if i in any_in else VMEM for i in range(len(args))],
        out_specs=[ANY if i in any_out else VMEM for i in range(len(shapes))],
        scratch_shapes=list(scratch),
        compiler_params=pltpu.CompilerParams(vmem_limit_bytes=48 * 2**20),
    )(*args)
    return result[0] if single else result


def sds(shape, dtype):
    return jax.ShapeDtypeStruct(shape, dtype)


def at_block(index):
    return pl.ds(pl.multiple_of(index * BLOCK, BLOCK), BLOCK)


def eye_mask(size):
    return lax.broadcasted_iota(jnp.int32, (size, size), 0) == lax.broadcasted_iota(
        jnp.int32, (size, size), 1
    )


def halves(value):
    high = value.astype(BF16)
    low = (value - high.astype(F32)).astype(BF16)
    return high, low


def pack(tile):
    return jnp.concatenate(halves(tile), axis=0)


def scale_of(power, part):
    return jnp.exp2(power) * (part * (1.0 / PART_TOP))


def encode(values):
    most = jnp.maximum(jnp.max(jnp.abs(values), axis=0, keepdims=True), 1e-30)
    power = jnp.floor(jnp.log2(most)) + 1.0
    part = jnp.floor(most * jnp.exp2(-power) * PART_TOP) + 1.0
    steps = jnp.floor(values * (CODE_TOP / scale_of(power, part)) + 0.5)
    steps = jnp.minimum(jnp.maximum(steps, -CODE_TOP), CODE_TOP)
    return steps.astype(jnp.int32).astype(jnp.int16), power, part


def decode(steps, scale):
    return steps.astype(jnp.int32).astype(F32) * (scale * (1.0 / CODE_TOP))


def as_rows(powers, parts, count):
    fill = jnp.zeros((count // 2 - len(powers), BLOCK), F32)
    fill = [fill] if fill.shape[0] else []
    rows = jnp.concatenate([*powers, *fill, *parts, *fill], axis=0)
    return rows.astype(jnp.int32).astype(jnp.int16)


def scale_rows(rows):
    rows = rows.astype(jnp.int32).astype(F32)
    half = rows.shape[0] // 2
    return scale_of(rows[:half], rows[half:])


def row_at(rows, place):
    if isinstance(place, int):
        return rows[place : place + 1, :]
    line = rows[:1, :]
    for i in range(1, rows.shape[0]):
        line = jnp.where(place == i, rows[i : i + 1, :], line)
    return line


def product(packed, values):
    left = jnp.concatenate(halves(values), axis=0)
    both = jnp.dot(jnp.concatenate([left, left], axis=1), packed, preferred_element_type=F32)
    count = values.shape[0]
    return both[:count] + both[count:]


def thirds(value):
    high = value.astype(BF16)
    rest = value - high.astype(F32)
    middle = rest.astype(BF16)
    low = (rest - middle.astype(F32)).astype(BF16)
    return jnp.concatenate([high, middle, low], axis=0)


def gram(parts, n):
    cross = lax.dot_general(parts, parts, NT, preferred_element_type=F32)
    count = parts.shape[0] // n
    pairs = sorted(((i, j) for i in range(count) for j in range(count)), key=lambda p: -p[0] - p[1])
    total = None
    for i, j in pairs:
        piece = cross[i * n : (i + 1) * n, j * n : (j + 1) * n]
        total = piece if total is None else total + piece
    return total


def times(left, parts):
    m = left.shape[0]
    left = jnp.concatenate(halves(left), axis=0)
    both = jnp.dot(jnp.concatenate([left, left], axis=1), parts, preferred_element_type=F32)
    return both[m:] + both[:m]


def lower_inverse(matrix, step=8):
    n = matrix.shape[0]
    state = jnp.concatenate([matrix, eye_mask(n).astype(F32)], axis=1)
    done = []
    for j in range(0, n, step):
        top = j // 8 * 8
        if top > n - state.shape[0]:
            done.append(state[:8])
            state = state[8:]
        base = j - top
        rows = lax.broadcasted_iota(jnp.int32, state.shape, 0)
        columns = [jnp.broadcast_to(state[:, j + i : j + i + 1], state.shape) for i in range(step)]
        lines = [state[base + i : base + i + 1, :] for i in range(step)]
        pivot = [[columns[k][base + i : base + i + 1, :] for k in range(step)] for i in range(step)]
        for i in range(step):
            if i % 2 == 0:
                first, cross, second = pivot[i][i], pivot[i][i + 1], pivot[i + 1][i + 1]
                reciprocals = (1.0 / first, first / (first * second - cross * cross))
            reciprocal = reciprocals[i % 2]
            scaled = lines[i] * reciprocal
            ratio = [pivot[i][k] * reciprocal for k in range(step)]
            for k in range(i + 1, step):
                lines[k] = lines[k] - pivot[k][i] * scaled
                columns[k] = columns[k] - columns[i] * ratio[k]
                for m in range(i + 1, step):
                    pivot[k][m] = pivot[k][m] - pivot[k][i] * ratio[m]
            state = state - jnp.where(rows > base + i, columns[i], 0.0) * scaled
    state = jnp.concatenate([*done, state], axis=0)
    pivots = jnp.sum(jnp.where(eye_mask(n), state[:, :n], 0.0), axis=1, keepdims=True)
    return state[:, n:] / jnp.sqrt(pivots)


def both_columns(core, own, other):
    first = core == 0
    return jnp.concatenate(
        [jnp.where(first, own, other), jnp.where(first, other, own)], axis=0
    )


def quotient(value, size):
    if size & (size - 1) == 0:
        return lax.shift_right_logical(value, jnp.int32(size.bit_length() - 1))
    return lax.div(value, jnp.int32(size))


def remainder(value, size):
    if size & (size - 1) == 0:
        return lax.bitwise_and(value, jnp.int32(size - 1))
    return lax.rem(value, jnp.int32(size))


def plan_body(dims, list_order, me, *refs):
    row_count, capacity, slots, blocks_here = dims
    lists, (emb, after, idx_out) = refs[:row_count], refs[row_count : row_count + 3]
    sends, (idx, left) = refs[row_count + 3 : -2], refs[-2:]
    row = me[0]
    for i in range(slots):
        for line in (0, 1, 2, 4, 5):
            idx[line, i] = 0
    lists = dict(zip(list_order, [one.ready() for one in lists]))

    def each(step, start):
        if slots <= 8:
            for s in range(slots):
                start = step(s, start)
        else:
            lax.fori_loop(0, slots, step, start)

    for k in range(row_count):
        live_count = lists[k][2, 0]

        def step(s, counts, k=k, live_count=live_count):
            near = lists[k][0, s]
            far = lists[k][1, s]
            owner = quotient(far, blocks_here)
            live = s < live_count
            hit = live & (owner == row)
            slot = jnp.where(hit, k * capacity + counts[0], slots)
            idx[4, slot] = far - row * blocks_here
            idx[5, slot] = near
            if k > 0:
                return (counts[0] + hit.astype(jnp.int32),)
            shift = remainder(owner - row + row_count, row_count)
            rank = counts[1]
            for d in range(1, row_count):
                rank = jnp.where(shift == d, counts[1 + d], rank)
            slot = jnp.where(live, shift * capacity + rank, slots)
            idx[0, slot] = near - row * blocks_here
            idx[1, slot] = far
            idx[2, slot] = 1
            more = tuple(
                counts[1 + d] + (live & (shift == d)).astype(jnp.int32) for d in range(row_count)
            )
            return (counts[0] + hit.astype(jnp.int32), *more)

        each(step, (jnp.int32(0),) * (1 + row_count if k == 0 else 1))
    leave = pltpu.make_async_copy(idx, idx_out, left)
    leave.start()
    for k in range(1, row_count):
        for j in range(capacity):
            sends[k - 1][j * BLOCK : (j + 1) * BLOCK, :] = emb[at_block(idx[4, k * capacity + j]), :]
    leave.wait()


def squares(block):
    return jnp.sum(jnp.square(block.astype(F32)), axis=1, keepdims=True)


def as_row(column):
    return jnp.sum(jnp.where(eye_mask(BLOCK), column, 0.0), axis=0, keepdims=True)


def partial_distance(left, right, left_sq, right_row):
    inner = lax.dot_general(left, right, NT, preferred_element_type=F32)
    return left_sq + right_row - 2.0 * inner


def self_distance_body(own_blocks, tile_count, me, emb, out):
    for i in range(own_blocks):
        block = emb[at_block(i * tile_count + me[1]), :]
        block_sq = squares(block)
        out[i * BLOCK : (i + 1) * BLOCK, :] = partial_distance(
            block, block, block_sq, as_row(block_sq)
        )


def squares_body(emb, after, out):
    for b in range(out.shape[0] // BLOCK):
        part = slice(b * BLOCK, (b + 1) * BLOCK)
        out[part, :] = jnp.broadcast_to(squares(emb[part, :]), (BLOCK, BLOCK))


def pair_distance_body(order, capacity, idx, emb, own_squares, *refs):
    far, out = dict(zip(order, refs)), refs[-1]
    rows = {}
    for k in order:
        for j in range(capacity):
            rows[k, j] = as_row(squares(far[k][j * BLOCK : (j + 1) * BLOCK, :]))
    idx = idx.ready()
    for k in range(len(order) + 1):
        for j in range(capacity):
            slot = k * capacity + j
            left = emb[at_block(idx[0, slot]), :]
            left_sq = own_squares[at_block(idx[0, slot]), :]
            if k == 0:
                right = emb[at_block(idx[4, j]), :]
                right_row = as_row(own_squares[at_block(idx[4, j]), :])
            else:
                right = far[k][j * BLOCK : (j + 1) * BLOCK, :]
                right_row = rows[k, j]
            part = slice(slot * BLOCK, (slot + 1) * BLOCK)
            out[part, :] = partial_distance(left, right, left_sq, right_row)


def self_tile_body(own_blocks, mine, other, packed, sums):
    for i in range(own_blocks):
        part = slice(i * BLOCK, (i + 1) * BLOCK)
        tile = jnp.exp(-kernel_gamma * (mine[part, :] + other[part, :] - 2.0))
        tile = jnp.where(eye_mask(BLOCK), 0.0, tile)
        packed[i] = pack(tile)
        sums[i : i + 1, :] = jnp.sum(tile, axis=0, keepdims=True)


def pair_tile_body(dims, me, idx, mine, other, self_sums, codes, powers, parts, near_tiles, home_tiles, table, *sends):
    row_count, capacity, per_core, blocks_here, tile_count = dims
    row, tile_index, core = me[0], me[1], me[2]
    table[...] = jnp.zeros(table.shape, F32)
    for i in range(self_sums.shape[0]):
        table[pl.ds(row * blocks_here + i * tile_count + tile_index, 1), :] = self_sums[i : i + 1, :]

    def add(block, line):
        place = pl.ds(block, 1)
        table[place, :] = table[place, :] + line

    all_tiles = jnp.exp(-kernel_gamma * (mine[...] + other[...] - 2.0))
    idx = idx.ready()
    for k in range(row_count):
        tiles = []
        for j in range(capacity):
            slot = k * capacity + j
            tile = all_tiles[slot * BLOCK : (slot + 1) * BLOCK]
            tile = jnp.where(idx[2, slot] > 0, tile, 0.0)
            turned = tile.T
            near_tiles[slot] = pack(turned)
            add(row * blocks_here + idx[0, slot], jnp.sum(turned, axis=0, keepdims=True))
            add(idx[1, slot], jnp.sum(tile, axis=0, keepdims=True))
            if k == 0:
                home_tiles[j] = pack(tile)
            tiles.append(tile)
        if k > 0:
            lines = ([], [])
            for inner in range(per_core):
                at = slice(inner * BLOCK, (inner + 1) * BLOCK)
                steps, power, part = encode(jnp.where(core == 0, tiles[inner], tiles[per_core + inner]))
                sends[k - 1][at, :] = steps
                lines[0].append(power)
                lines[1].append(part)
            pick_columns(idx, k, row_count, capacity, codes, powers, parts, sends[k - 1], per_core * BLOCK, lines)


def encode_blocks(values, codes, powers, parts):
    for b in range(powers.shape[0]):
        at = slice(b * BLOCK, (b + 1) * BLOCK)
        steps, power, part = encode(values[:, at])
        codes[:, at] = steps
        powers[b : b + 1, :] = power
        parts[b : b + 1, :] = part


def start_body(values, codes, powers, parts):
    encode_blocks(values, codes, powers, parts)


def split_body(row_count, per_core, *refs):
    others = row_count - 1
    messages, outs = refs[:others], refs[-others:]
    for message, out in zip(messages, outs):
        scales = scale_rows(message[message.shape[0] - CODE_ROWS :, :])
        for inner in range(per_core):
            steps = message[inner * BLOCK : (inner + 1) * BLOCK, :]
            out[inner] = pack(decode(steps, scales[inner : inner + 1, :]))


def pick_columns(idx, k, row_count, capacity, codes, powers, parts, send, base, lines):
    count = codes.shape[0]
    back = row_count - k
    blocks = [idx[0, k * capacity + j] for j in range(capacity)]
    blocks += [idx[4, back * capacity + j] for j in range(capacity)]
    for place, block in enumerate(blocks):
        send[base + place * count : base + (place + 1) * count, :] = codes[:, at_block(block)]
        lines[0].append(powers[pl.ds(block, 1), :])
        lines[1].append(parts[pl.ds(block, 1), :])
    send[base + len(blocks) * count :, :] = as_rows(*lines, CODE_ROWS)


def add_product(out, block, packed, values):
    place = at_block(block)
    out[:, place] = out[:, place] + product(packed, values)


def apply_own(dims, me, idx, inverse, own, near_tiles, home_tiles, self_tiles, out):
    row_count, capacity, per_core, blocks_here, tile_count = dims
    row, tile_index = me[0], me[1]
    out[...] = jnp.zeros(out.shape, F32)

    def scaled(block):
        return own[:, at_block(block)] * inverse[pl.ds(row * blocks_here + block, 1), :]

    for i in range(blocks_here // tile_count):
        block = i * tile_count + tile_index
        add_product(out, block, self_tiles[i], scaled(block))
    idx = idx.ready()
    for j in range(capacity):
        add_product(out, idx[0, j], near_tiles[j], scaled(idx[4, j]))
        add_product(out, idx[4, j], home_tiles[j], scaled(idx[0, j]))
    return idx


def apply_far(dims, me, idx, inverse, received, base, near_tiles, sent, shared, out):
    row_count, capacity, per_core, blocks_here, tile_count = dims
    core = me[2]
    count = out.shape[0]
    order = way_order(row_count)
    received, sent, shared = [dict(zip(order, refs)) for refs in (received, sent, shared)]
    lines = {k: scale_rows(received[k][received[k].shape[0] - CODE_ROWS :, :]) for k in order}
    first_line = base // BLOCK

    def arrived(k, place, block):
        steps = received[k][pl.ds(pl.multiple_of(base + place * count, CODE_ROWS), count), :]
        rows = lines[k][first_line : first_line + 2 * capacity, :]
        return decode(steps, row_at(rows, place) * inverse[pl.ds(block, 1), :])

    for k in range(1, row_count):
        for j in range(capacity):
            slot = k * capacity + j
            values = arrived(row_count - k, capacity + j, idx[1, slot])
            add_product(out, idx[0, slot], near_tiles[slot], values)
            inner = j % per_core
            if j < per_core:
                place = core * per_core + inner
                packed = sent[k][inner]
            else:
                place = (1 - core) * per_core + inner
                packed = shared[k][inner]
            slot = k * capacity + place
            add_product(out, idx[4, slot], packed, arrived(k, place, idx[5, slot]))


def first_own_body(dims, me, idx, mine, other, own, near_tiles, home_tiles, self_tiles, out, degree, inverse):
    total = mine[...] + other[...]
    degree[...] = total
    inverse[...] = 1.0 / jnp.sqrt(total)
    apply_own(dims, me, idx, inverse, own, near_tiles, home_tiles, self_tiles, out)


def first_far_body(dims, coded, me, idx, inverse, started, near_tiles, *refs):
    row_count, per_core = dims[0], dims[2]
    others = row_count - 1
    sent, shared, messages = refs[:others], refs[others : 2 * others], refs[2 * others : 3 * others]
    out, total = refs[3 * others :]
    total[...] = started[...]
    apply_far(dims, me, idx.ready(), inverse, messages, per_core * BLOCK, near_tiles, sent, shared, total)
    put_sum(coded, total, out)


def second_apply_body(dims, me, idx, inverse, after, own, home_tiles, self_tiles, near_tiles, *refs):
    others = dims[0] - 1
    sent, shared, received = refs[:others], refs[others : 2 * others], refs[2 * others : 3 * others]
    out = refs[-1]
    idx = apply_own(dims, me, idx, inverse, own, near_tiles, home_tiles, self_tiles, out)
    apply_far(dims, me, idx, inverse, received, 0, near_tiles, sent, shared, out)


def send_sum_body(coded, total, after, out):
    put_sum(coded, total, out)


def put_sum(coded, total, out):
    if not coded:
        out[...] = total[...]
        return
    lines = ([], [])
    blocks_here = total.shape[1] // BLOCK
    for b in range(blocks_here):
        at = slice(b * BLOCK, (b + 1) * BLOCK)
        steps, power, part = encode(total[:, at])
        out[:, at] = steps
        lines[0].append(power)
        lines[1].append(part)
    out[:, blocks_here * BLOCK :] = as_rows(*lines, out.shape[0])


def take_sum(coded, me, blocks_here, inverse, mine, other, out):
    if coded:
        tail = blocks_here * BLOCK
        my_scales, other_scales = scale_rows(mine[:, tail:]), scale_rows(other[:, tail:])
    for b in range(blocks_here):
        at = slice(b * BLOCK, (b + 1) * BLOCK)
        row = inverse[pl.ds(me[0] * blocks_here + b, 1), :]
        if coded:
            line = slice(b, b + 1)
            value = decode(mine[:, at], my_scales[line]) + decode(other[:, at], other_scales[line])
        else:
            value = mine[:, at] + other[:, at]
        out[:, at] = value * row


def mapped_body(dims, coded, me, idx, inverse, mine, other, out, *refs):
    row_count, capacity, per_core, blocks_here, tile_count = dims
    sends, (codes, powers, parts) = refs[:-3], refs[-3:]
    take_sum(coded, me, blocks_here, inverse, mine, other, out)
    encode_blocks(out, codes, powers, parts)
    idx = idx.ready()
    for k in range(1, row_count):
        pick_columns(idx, k, row_count, capacity, codes, powers, parts, sends[k - 1], 0, ([], []))


def last_mapped_body(blocks_here, coded, me, inverse, mine, other, after, out):
    take_sum(coded, me, blocks_here, inverse, mine, other, out)


def folded(square):
    half = square.shape[0] // 2
    return jnp.concatenate([square[:half], square[half:]], axis=1)


def unfolded(terms):
    total = functools.reduce(lambda total, term: total + term[...], terms[1:], terms[0][...])
    width = total.shape[1] // 2
    return jnp.concatenate([total[:, :width], total[:, width:]], axis=0)


def gram_body(me, own, other, out):
    full = both_columns(me[2], own[...], other[...])
    out[...] = folded(gram(pack(full), full.shape[0]))


def factor_body(after, *refs):
    refs[-1][...] = lower_inverse(unfolded(refs[:-1]))


def second_gram_body(me, factor, own, other, mapped, out):
    full = both_columns(me[2], own[...], other[...])
    parts = thirds(times(factor[...], pack(full)))
    mapped[...] = parts[: mapped.shape[0]]
    out[...] = folded(gram(parts, full.shape[0]))


def final_body(me, mapped, *refs):
    terms, (out, value, sent) = refs[:-3], refs[-3:]
    factor = lower_inverse(unfolded(terms))
    own_cols = value.shape[0]
    part = jnp.where(me[2] == 0, factor[:own_cols], factor[own_cols:])
    copies = []
    chunk = value.shape[1] // sent.shape[0]
    for i in range(sent.shape[0]):
        at = slice(i * chunk, (i + 1) * chunk)
        value[:, at] = times(part, mapped[:, at])
        copies.append(pltpu.make_async_copy(value.at[:, at], out.at[:, at], sent.at[i]))
        copies[-1].start()
    for copy in copies:
        copy.wait()


def shift_by(value, axes, size, shift):
    return lax.ppermute(value, axes, [(i, (i + shift) % size) for i in range(size)])


def way_order(row_count):
    return sorted(range(1, row_count), key=lambda k: abs(k - row_count // 2))


def row_terms(value, row_count):
    return [value] + [shift_by(value, "rows", row_count, k) for k in way_order(row_count)]


def pair_step(value, name, flip):
    return lax.ppermute(value, name, [(i, i ^ flip) for i in range(lax.axis_size(name))])


def pair_sum(value, axes):
    terms = None
    steps = [(name, 1 << bit) for name in axes for bit in range((lax.axis_size(name) - 1).bit_length())]
    for name, flip in steps:
        if terms is not None:
            value = terms[0] + terms[1]
        terms = (value, pair_step(value, name, flip))
    return terms


def local(embeddings, start, pair_list, pair_count):
    row_count = lax.axis_size("rows")
    tile_count = lax.axis_size("tiles")
    core_count = lax.axis_size("cols")
    row_index = lax.axis_index("rows")
    tile_index = lax.axis_index("tiles")
    col_index = lax.axis_index("cols")
    rows_here, half_features = embeddings.shape
    blocks_here = rows_here // BLOCK
    slots = pair_list.shape[2]
    capacity = slots // row_count
    per_core = capacity // core_count
    own_blocks = blocks_here // tile_count
    own_cols = start.shape[1]
    block_count = row_count * blocks_here
    others = range(1, row_count)
    order = way_order(row_count)

    own_list = jnp.concatenate(
        [pair_list[0], jnp.broadcast_to(pair_count[:, None], (1, slots))], axis=0
    )
    list_order = [0, *sorted(others, key=lambda k: k * (row_count - k))]
    lists = [shift_by(own_list, "rows", row_count, k) if k else own_list for k in list_order]
    self_part = call(
        functools.partial(self_distance_body, own_blocks, tile_count),
        sds((own_blocks * BLOCK, BLOCK), F32),
        [ME, embeddings],
    )
    planned = call(
        functools.partial(plan_body, (row_count, capacity, slots, blocks_here), list_order),
        [sds((6, slots + 1), jnp.int32)] + [sds((capacity * BLOCK, half_features), BF16) for _ in others],
        [ME, *lists, embeddings, self_part],
        late=range(1, 1 + row_count),
        any_in=(row_count + 2,),
        any_out=(0,),
        scratch=[pltpu.SMEM((6, slots + 1), jnp.int32), pltpu.SemaphoreType.DMA],
    )
    idx, sends = planned[0], planned[1:]
    far = [shift_by(sends[k - 1], "rows", row_count, -k) for k in order]

    self_other = shift_by(self_part, "cols", core_count, 1)
    self_tiles, self_sums = call(
        functools.partial(self_tile_body, own_blocks),
        [sds((own_blocks, 2 * BLOCK, BLOCK), BF16), sds((own_blocks, BLOCK), F32)],
        [self_part, self_other],
    )
    values = start.T
    code_shapes = [((own_cols, rows_here), jnp.int16), ((blocks_here, BLOCK), F32), ((blocks_here, BLOCK), F32)]
    start_codes = call(start_body, [sds(*shape) for shape in code_shapes], [values])
    code_scratch = [pltpu.VMEM(*shape) for shape in code_shapes]
    coded = tile_count == 2
    own_squares = call(squares_body, sds((rows_here, BLOCK), F32), [embeddings, idx], any_in=(1,))
    pair_part = call(
        functools.partial(pair_distance_body, order, capacity),
        sds((slots * BLOCK, BLOCK), F32),
        [idx, embeddings, own_squares, *far],
        late=(0,),
    )
    pair_other = shift_by(pair_part, "cols", core_count, 1)

    dims = (row_count, capacity, per_core, blocks_here, tile_count)
    table = sds((block_count, BLOCK), F32)
    picked = 2 * capacity * own_cols
    tiles = call(
        functools.partial(pair_tile_body, dims),
        [sds((slots, 2 * BLOCK, BLOCK), BF16), sds((capacity, 2 * BLOCK, BLOCK), BF16), table]
        + [sds((per_core * BLOCK + picked + CODE_ROWS, BLOCK), jnp.int16) for _ in others],
        [ME, idx, pair_part, pair_other, self_sums, *start_codes],
        late=(1,),
    )
    near_tiles, home_tiles, degrees, sends = tiles[0], tiles[1], tiles[2], tiles[3:]
    degrees = functools.reduce(
        jnp.add, [degrees] + [shift_by(degrees, "rows", row_count, k) for k in reversed(order)]
    )
    degree_terms = pair_sum(degrees, ("tiles",))
    messages = [shift_by(sends[k - 1], "rows", row_count, k) for k in order]
    sent = call(
        functools.partial(split_body, row_count, per_core),
        [sds((per_core, 2 * BLOCK, BLOCK), BF16) for _ in others],
        [*messages, degree_terms[1]],
        any_in=(row_count - 1,),
    )
    shared = [shift_by(tile, "cols", core_count, 1) for tile in sent]

    block_shape = sds((own_cols, rows_here), F32)
    sum_shape = sds((own_cols, rows_here + BLOCK), jnp.int16) if coded else block_shape
    square = sds((2 * own_cols, 2 * own_cols), F32)
    folded_square = sds((own_cols, 4 * own_cols), F32)

    started, degree, inverse = call(
        functools.partial(first_own_body, dims),
        [block_shape, table, table],
        [ME, idx, *degree_terms, values, near_tiles, home_tiles, self_tiles],
        late=(1,),
    )
    part = call(
        functools.partial(first_far_body, dims, coded),
        sum_shape,
        [ME, idx, inverse, started, near_tiles, *sent, *shared, *messages],
        late=(1,),
        scratch=[pltpu.VMEM((own_cols, rows_here), F32)],
    )
    mine, other = pair_sum(part, ("tiles",))
    first = call(
        functools.partial(mapped_body, dims, coded),
        [block_shape] + [sds((picked + CODE_ROWS, BLOCK), jnp.int16) for _ in others],
        [ME, idx, inverse, mine, other],
        late=(1,),
        scratch=code_scratch,
    )
    mapped, sends = first[0], first[1:]
    received = [shift_by(sends[k - 1], "rows", row_count, k) for k in order]

    mapped_other = shift_by(mapped, "cols", core_count, 1)
    first_gram = call(gram_body, folded_square, [ME, mapped, mapped_other])
    part = call(
        functools.partial(second_apply_body, dims),
        block_shape,
        [ME, idx, inverse, first_gram, mapped, home_tiles, self_tiles, near_tiles, *sent, *shared, *received],
        late=(1,),
        any_in=(3,),
    )
    steps = (row_count - 1).bit_length()
    for bit in range(steps - 1):
        first_gram = first_gram + pair_step(first_gram, "rows", 1 << bit)
    part = call(functools.partial(send_sum_body, coded), sum_shape, [part, first_gram])
    gram_terms = (first_gram, pair_step(first_gram, "rows", 1 << (steps - 1)))
    mine, other = pair_sum(part, ("tiles",))
    second = call(
        functools.partial(last_mapped_body, blocks_here, coded),
        block_shape,
        [ME, inverse, mine, other, gram_terms[1]],
        any_in=(4,),
    )
    second_other = shift_by(second, "cols", core_count, 1)
    factor = call(factor_body, square, [second, *gram_terms], any_in=(0,))
    full, second_gram = call(
        second_gram_body,
        [sds((4 * own_cols, rows_here), BF16), folded_square],
        [ME, factor, second, second_other],
    )
    vectors = call(
        final_body,
        block_shape,
        [ME, full, *row_terms(second_gram, row_count)],
        any_out=(0,),
        scratch=[pltpu.VMEM((own_cols, rows_here), F32), pltpu.SemaphoreType.DMA((4,))],
    )
    own_degree = lax.dynamic_slice_in_dim(degree, row_index * blocks_here, blocks_here, 0)
    return (vectors.T, own_degree.reshape(rows_here))


def solution(mesh):
    in_specs = (
        P(("groups", "rows"), "cols"),
        P(("groups", "rows"), "cols"),
        P(("groups", "rows", "tiles"), None, None),
        P(("groups", "rows", "tiles")),
    )
    out_specs = (P(("groups", "rows"), "cols"), P(("groups", "rows")))
    return jax.shard_map(local, mesh=mesh, in_specs=in_specs, out_specs=out_specs, check_vma=False)
```

```python
import functools

import jax
import jax.numpy as jnp
from jax import lax
from jax.experimental import pallas as pl
from jax.experimental.pallas import tpu as pltpu
from jax.sharding import PartitionSpec as P

BLOCK = 128
kernel_gamma = 14.0
CODE_TOP = 32767.0
PART_TOP = 16384.0
CODE_ROWS = 16

VMEM = pl.BlockSpec(memory_space=pltpu.VMEM)
ANY = pl.BlockSpec(memory_space=pl.ANY)
F32 = jnp.float32
BF16 = jnp.bfloat16
HIGHEST = lax.Precision.HIGHEST
NT = (((1,), (1,)), ((), ()))


ME = None


def with_position(body):
    def inner(*refs):
        return body([lax.axis_index(name) for name in ("rows", "tiles", "cols")], *refs)

    return inner


class Late:
    def __init__(self, source, table, arrived):
        self.table = table
        self.copy = pltpu.make_async_copy(source, table, arrived)
        self.copy.start()

    def ready(self):
        self.copy.wait()
        return self.table


def with_late(body, places, count):
    def inner(*refs):
        refs, tables, arrived = refs[:-1 - count], refs[-1 - count : -1], refs[-1]
        refs = list(refs)
        for i, place in enumerate(places):
            refs[place] = Late(refs[place], tables[i], arrived.at[i])
        body(*refs)

    return inner


def call(body, outs, args, late=(), any_in=(), scratch=(), any_out=()):
    if args[0] is ME:
        body, args = with_position(body), args[1:]
        late, any_in = [[i - 1 for i in places] for places in (late, any_in)]
    if late:
        scratch = [
            *scratch,
            *[pltpu.SMEM(args[i].shape, args[i].dtype) for i in late],
            pltpu.SemaphoreType.DMA((len(late),)),
        ]
        any_in = [*any_in, *late]
        body = with_late(body, late, len(late))
    single = not isinstance(outs, (list, tuple))
    shapes = [outs] if single else list(outs)
    result = pl.pallas_call(
        body,
        out_shape=shapes,
        in_specs=[ANY if i in any_in else VMEM for i in range(len(args))],
        out_specs=[ANY if i in any_out else VMEM for i in range(len(shapes))],
        scratch_shapes=list(scratch),
        compiler_params=pltpu.CompilerParams(vmem_limit_bytes=48 * 2**20),
    )(*args)
    return result[0] if single else result


def sds(shape, dtype):
    return jax.ShapeDtypeStruct(shape, dtype)


def at_block(index):
    return pl.ds(pl.multiple_of(index * BLOCK, BLOCK), BLOCK)


def eye_mask(size):
    return lax.broadcasted_iota(jnp.int32, (size, size), 0) == lax.broadcasted_iota(
        jnp.int32, (size, size), 1
    )


def halves(value):
    high = value.astype(BF16)
    low = (value - high.astype(F32)).astype(BF16)
    return high, low


def pack(tile):
    return jnp.concatenate(halves(tile), axis=0)


def scale_of(power, part):
    return jnp.exp2(power) * (part * (1.0 / PART_TOP))


def encode(values):
    most = jnp.maximum(jnp.max(jnp.abs(values), axis=0, keepdims=True), 1e-30)
    power = jnp.floor(jnp.log2(most)) + 1.0
    part = jnp.floor(most * jnp.exp2(-power) * PART_TOP) + 1.0
    steps = jnp.floor(values * (CODE_TOP / scale_of(power, part)) + 0.5)
    steps = jnp.minimum(jnp.maximum(steps, -CODE_TOP), CODE_TOP)
    return steps.astype(jnp.int32).astype(jnp.int16), power, part


def decode(steps, scale):
    return steps.astype(jnp.int32).astype(F32) * (scale * (1.0 / CODE_TOP))


def as_rows(powers, parts, count):
    fill = jnp.zeros((count // 2 - len(powers), BLOCK), F32)
    fill = [fill] if fill.shape[0] else []
    rows = jnp.concatenate([*powers, *fill, *parts, *fill], axis=0)
    return rows.astype(jnp.int32).astype(jnp.int16)


def scale_rows(rows):
    rows = rows.astype(jnp.int32).astype(F32)
    half = rows.shape[0] // 2
    return scale_of(rows[:half], rows[half:])


def row_at(rows, place):
    if isinstance(place, int):
        return rows[place : place + 1, :]
    line = rows[:1, :]
    for i in range(1, rows.shape[0]):
        line = jnp.where(place == i, rows[i : i + 1, :], line)
    return line


def product(packed, values):
    left = jnp.concatenate(halves(values), axis=0)
    both = jnp.dot(jnp.concatenate([left, left], axis=1), packed, preferred_element_type=F32)
    count = values.shape[0]
    return both[:count] + both[count:]


def thirds(value):
    high = value.astype(BF16)
    rest = value - high.astype(F32)
    middle = rest.astype(BF16)
    low = (rest - middle.astype(F32)).astype(BF16)
    return jnp.concatenate([high, middle, low], axis=0)


def gram(parts, n):
    cross = lax.dot_general(parts, parts, NT, preferred_element_type=F32)
    count = parts.shape[0] // n
    pairs = sorted(((i, j) for i in range(count) for j in range(count)), key=lambda p: -p[0] - p[1])
    total = None
    for i, j in pairs:
        piece = cross[i * n : (i + 1) * n, j * n : (j + 1) * n]
        total = piece if total is None else total + piece
    return total


def times(left, parts):
    m = left.shape[0]
    left = jnp.concatenate(halves(left), axis=0)
    both = jnp.dot(jnp.concatenate([left, left], axis=1), parts, preferred_element_type=F32)
    return both[m:] + both[:m]


def lower_inverse(matrix):
    n = matrix.shape[0]
    step = 8
    state = jnp.concatenate([matrix, eye_mask(n).astype(F32)], axis=1)
    tiles = [state[i : i + step] for i in range(0, n, step)]
    shape = tiles[0].shape
    rows = lax.broadcasted_iota(jnp.int32, shape, 0)
    done = []
    for j in range(0, n, step):
        columns = [
            [jnp.broadcast_to(tile[:, j + i : j + i + 1], shape) for tile in tiles] for i in range(step)
        ]
        lines = [jnp.broadcast_to(tiles[0][i : i + 1, :], shape) for i in range(step)]
        pivot = {
            (i, k): jnp.broadcast_to(columns[k][0][i : i + 1, :], shape)
            for i in range(step)
            for k in range(i, step)
        }
        for i in range(step):
            if i % 2 == 0:
                first, cross, second = pivot[i, i], pivot[i, i + 1], pivot[i + 1, i + 1]
                reciprocals = (1.0 / first, first / (first * second - cross * cross))
            reciprocal = reciprocals[i % 2]
            scaled = lines[i] * reciprocal
            ratio = {k: pivot[i, k] * reciprocal for k in range(i + 1, step)}
            for k in range(i + 1, step):
                lines[k] = lines[k] - pivot[i, k] * scaled
                columns[k] = [one - other * ratio[k] for one, other in zip(columns[k], columns[i])]
                for m in range(k, step):
                    pivot[k, m] = pivot[k, m] - pivot[i, k] * ratio[m]
            left = [jnp.where(rows > i, columns[i][0], 0.0), *columns[i][1:]]
            tiles = [tile - one * scaled for tile, one in zip(tiles, left)]
        done.append(tiles[0])
        tiles = tiles[1:]
    state = jnp.concatenate(done, axis=0)
    pivots = jnp.sum(jnp.where(eye_mask(n), state[:, :n], 0.0), axis=1, keepdims=True)
    return state[:, n:] / jnp.sqrt(pivots)


def both_columns(core, own, other):
    first = core == 0
    return jnp.concatenate(
        [jnp.where(first, own, other), jnp.where(first, other, own)], axis=0
    )


def quotient(value, size):
    if size & (size - 1) == 0:
        return lax.shift_right_logical(value, jnp.int32(size.bit_length() - 1))
    return lax.div(value, jnp.int32(size))


def remainder(value, size):
    if size & (size - 1) == 0:
        return lax.bitwise_and(value, jnp.int32(size - 1))
    return lax.rem(value, jnp.int32(size))


def plan_body(dims, list_order, me, *refs):
    row_count, capacity, slots, blocks_here = dims
    lists, (emb, after, idx_out) = refs[:row_count], refs[row_count : row_count + 3]
    sends, (idx, left) = refs[row_count + 3 : -2], refs[-2:]
    row = me[0]
    for i in range(slots):
        for line in (0, 1, 2, 4, 5):
            idx[line, i] = 0
    lists = dict(zip(list_order, [one.ready() for one in lists]))

    def each(step, start):
        if slots <= 8:
            for s in range(slots):
                start = step(s, start)
        else:
            lax.fori_loop(0, slots, step, start)

    for k in range(row_count):
        live_count = lists[k][2, 0]

        def step(s, counts, k=k, live_count=live_count):
            near = lists[k][0, s]
            far = lists[k][1, s]
            owner = quotient(far, blocks_here)
            live = s < live_count
            hit = live & (owner == row)
            slot = jnp.where(hit, k * capacity + counts[0], slots)
            idx[4, slot] = far - row * blocks_here
            idx[5, slot] = near
            if k > 0:
                return (counts[0] + hit.astype(jnp.int32),)
            shift = remainder(owner - row + row_count, row_count)
            rank = counts[1]
            for d in range(1, row_count):
                rank = jnp.where(shift == d, counts[1 + d], rank)
            slot = jnp.where(live, shift * capacity + rank, slots)
            idx[0, slot] = near - row * blocks_here
            idx[1, slot] = far
            idx[2, slot] = 1
            more = tuple(
                counts[1 + d] + (live & (shift == d)).astype(jnp.int32) for d in range(row_count)
            )
            return (counts[0] + hit.astype(jnp.int32), *more)

        each(step, (jnp.int32(0),) * (1 + row_count if k == 0 else 1))
    leave = pltpu.make_async_copy(idx, idx_out, left)
    leave.start()
    for k in range(1, row_count):
        for j in range(capacity):
            sends[k - 1][j * BLOCK : (j + 1) * BLOCK, :] = emb[at_block(idx[4, k * capacity + j]), :]
    leave.wait()


def squares(block):
    return jnp.sum(jnp.square(block.astype(F32)), axis=1, keepdims=True)


def as_row(column):
    return jnp.sum(jnp.where(eye_mask(BLOCK), column, 0.0), axis=0, keepdims=True)


def partial_distance(left, right, left_sq, right_row):
    inner = lax.dot_general(left, right, NT, preferred_element_type=F32)
    return left_sq + right_row - 2.0 * inner


def self_distance_body(own_blocks, tile_count, me, emb, out):
    for i in range(own_blocks):
        block = emb[at_block(i * tile_count + me[1]), :]
        block_sq = squares(block)
        out[i * BLOCK : (i + 1) * BLOCK, :] = partial_distance(
            block, block, block_sq, as_row(block_sq)
        )


def squares_body(emb, after, out):
    for b in range(out.shape[0] // BLOCK):
        part = slice(b * BLOCK, (b + 1) * BLOCK)
        out[part, :] = jnp.broadcast_to(squares(emb[part, :]), (BLOCK, BLOCK))


def pair_distance_body(order, capacity, idx, emb, own_squares, *refs):
    far, out = dict(zip(order, refs)), refs[-1]
    rows = {}
    for k in order:
        for j in range(capacity):
            rows[k, j] = as_row(squares(far[k][j * BLOCK : (j + 1) * BLOCK, :]))
    idx = idx.ready()
    for k in range(len(order) + 1):
        for j in range(capacity):
            slot = k * capacity + j
            left = emb[at_block(idx[0, slot]), :]
            left_sq = own_squares[at_block(idx[0, slot]), :]
            if k == 0:
                right = emb[at_block(idx[4, j]), :]
                right_row = as_row(own_squares[at_block(idx[4, j]), :])
            else:
                right = far[k][j * BLOCK : (j + 1) * BLOCK, :]
                right_row = rows[k, j]
            part = slice(slot * BLOCK, (slot + 1) * BLOCK)
            out[part, :] = partial_distance(left, right, left_sq, right_row)


def self_tile_body(own_blocks, mine, other, packed, sums):
    for i in range(own_blocks):
        part = slice(i * BLOCK, (i + 1) * BLOCK)
        tile = jnp.exp(-kernel_gamma * (mine[part, :] + other[part, :] - 2.0))
        tile = jnp.where(eye_mask(BLOCK), 0.0, tile)
        packed[i] = pack(tile)
        sums[i : i + 1, :] = jnp.sum(tile, axis=0, keepdims=True)


def pair_tile_body(dims, me, idx, mine, other, self_sums, codes, powers, parts, near_tiles, home_tiles, table, *sends):
    row_count, capacity, per_core, blocks_here, tile_count = dims
    row, tile_index, core = me[0], me[1], me[2]
    table[...] = jnp.zeros(table.shape, F32)
    for i in range(self_sums.shape[0]):
        table[pl.ds(row * blocks_here + i * tile_count + tile_index, 1), :] = self_sums[i : i + 1, :]

    def add(block, line):
        place = pl.ds(block, 1)
        table[place, :] = table[place, :] + line

    all_tiles = jnp.exp(-kernel_gamma * (mine[...] + other[...] - 2.0))
    idx = idx.ready()
    for k in range(row_count):
        tiles = []
        for j in range(capacity):
            slot = k * capacity + j
            tile = all_tiles[slot * BLOCK : (slot + 1) * BLOCK]
            tile = jnp.where(idx[2, slot] > 0, tile, 0.0)
            turned = tile.T
            near_tiles[slot] = pack(turned)
            add(row * blocks_here + idx[0, slot], jnp.sum(turned, axis=0, keepdims=True))
            add(idx[1, slot], jnp.sum(tile, axis=0, keepdims=True))
            if k == 0:
                home_tiles[j] = pack(tile)
            tiles.append(tile)
        if k > 0:
            lines = ([], [])
            for inner in range(per_core):
                at = slice(inner * BLOCK, (inner + 1) * BLOCK)
                steps, power, part = encode(jnp.where(core == 0, tiles[inner], tiles[per_core + inner]))
                sends[k - 1][at, :] = steps
                lines[0].append(power)
                lines[1].append(part)
            pick_columns(idx, k, row_count, capacity, codes, powers, parts, sends[k - 1], per_core * BLOCK, lines)


def encode_blocks(values, codes, powers, parts):
    for b in range(powers.shape[0]):
        at = slice(b * BLOCK, (b + 1) * BLOCK)
        steps, power, part = encode(values[:, at])
        codes[:, at] = steps
        powers[b : b + 1, :] = power
        parts[b : b + 1, :] = part


def start_body(values, codes, powers, parts):
    encode_blocks(values, codes, powers, parts)


def split_body(row_count, per_core, *refs):
    others = row_count - 1
    messages, outs = refs[:others], refs[-others:]
    for message, out in zip(messages, outs):
        scales = scale_rows(message[message.shape[0] - CODE_ROWS :, :])
        for inner in range(per_core):
            steps = message[inner * BLOCK : (inner + 1) * BLOCK, :]
            out[inner] = pack(decode(steps, scales[inner : inner + 1, :]))


def pick_columns(idx, k, row_count, capacity, codes, powers, parts, send, base, lines):
    count = codes.shape[0]
    back = row_count - k
    blocks = [idx[0, k * capacity + j] for j in range(capacity)]
    blocks += [idx[4, back * capacity + j] for j in range(capacity)]
    for place, block in enumerate(blocks):
        send[base + place * count : base + (place + 1) * count, :] = codes[:, at_block(block)]
        lines[0].append(powers[pl.ds(block, 1), :])
        lines[1].append(parts[pl.ds(block, 1), :])
    send[base + len(blocks) * count :, :] = as_rows(*lines, CODE_ROWS)


def add_product(out, block, packed, values):
    place = at_block(block)
    out[:, place] = out[:, place] + product(packed, values)


def apply_own(dims, me, idx, inverse, own, near_tiles, home_tiles, self_tiles, out):
    row_count, capacity, per_core, blocks_here, tile_count = dims
    row, tile_index = me[0], me[1]
    out[...] = jnp.zeros(out.shape, F32)

    def scaled(block):
        return own[:, at_block(block)] * inverse[pl.ds(row * blocks_here + block, 1), :]

    for i in range(blocks_here // tile_count):
        block = i * tile_count + tile_index
        add_product(out, block, self_tiles[i], scaled(block))
    idx = idx.ready()
    for j in range(capacity):
        add_product(out, idx[0, j], near_tiles[j], scaled(idx[4, j]))
        add_product(out, idx[4, j], home_tiles[j], scaled(idx[0, j]))
    return idx


def apply_far(dims, me, idx, inverse, received, base, near_tiles, sent, shared, out):
    row_count, capacity, per_core, blocks_here, tile_count = dims
    core = me[2]
    count = out.shape[0]
    lines = [scale_rows(message[message.shape[0] - CODE_ROWS :, :]) for message in received]
    first_line = base // BLOCK

    def arrived(k, place, block):
        steps = received[k - 1][pl.ds(pl.multiple_of(base + place * count, CODE_ROWS), count), :]
        rows = lines[k - 1][first_line : first_line + 2 * capacity, :]
        return decode(steps, row_at(rows, place) * inverse[pl.ds(block, 1), :])

    for k in range(1, row_count):
        for j in range(capacity):
            slot = k * capacity + j
            values = arrived(row_count - k, capacity + j, idx[1, slot])
            add_product(out, idx[0, slot], near_tiles[slot], values)
            inner = j % per_core
            if j < per_core:
                place = core * per_core + inner
                packed = sent[k - 1][inner]
            else:
                place = (1 - core) * per_core + inner
                packed = shared[k - 1][inner]
            slot = k * capacity + place
            add_product(out, idx[4, slot], packed, arrived(k, place, idx[5, slot]))


def first_own_body(dims, me, idx, mine, other, own, near_tiles, home_tiles, self_tiles, out, degree, inverse):
    total = mine[...] + other[...]
    degree[...] = total
    inverse[...] = 1.0 / jnp.sqrt(total)
    apply_own(dims, me, idx, inverse, own, near_tiles, home_tiles, self_tiles, out)


def first_far_body(dims, coded, me, idx, inverse, started, near_tiles, *refs):
    row_count, per_core = dims[0], dims[2]
    others = row_count - 1
    sent, shared, messages = refs[:others], refs[others : 2 * others], refs[2 * others : 3 * others]
    out, total = refs[3 * others :]
    total[...] = started[...]
    apply_far(dims, me, idx.ready(), inverse, messages, per_core * BLOCK, near_tiles, sent, shared, total)
    put_sum(coded, total, out)


def second_apply_body(dims, me, idx, inverse, after, own, home_tiles, self_tiles, near_tiles, *refs):
    others = dims[0] - 1
    sent, shared, received = refs[:others], refs[others : 2 * others], refs[2 * others : 3 * others]
    out = refs[-1]
    idx = apply_own(dims, me, idx, inverse, own, near_tiles, home_tiles, self_tiles, out)
    apply_far(dims, me, idx, inverse, received, 0, near_tiles, sent, shared, out)


def send_sum_body(coded, total, after, out):
    put_sum(coded, total, out)


def put_sum(coded, total, out):
    if not coded:
        out[...] = total[...]
        return
    lines = ([], [])
    blocks_here = total.shape[1] // BLOCK
    for b in range(blocks_here):
        at = slice(b * BLOCK, (b + 1) * BLOCK)
        steps, power, part = encode(total[:, at])
        out[:, at] = steps
        lines[0].append(power)
        lines[1].append(part)
    out[:, blocks_here * BLOCK :] = as_rows(*lines, out.shape[0])


def take_sum(coded, me, blocks_here, inverse, mine, other, out):
    if coded:
        tail = blocks_here * BLOCK
        my_scales, other_scales = scale_rows(mine[:, tail:]), scale_rows(other[:, tail:])
    for b in range(blocks_here):
        at = slice(b * BLOCK, (b + 1) * BLOCK)
        row = inverse[pl.ds(me[0] * blocks_here + b, 1), :]
        if coded:
            line = slice(b, b + 1)
            value = decode(mine[:, at], my_scales[line]) + decode(other[:, at], other_scales[line])
        else:
            value = mine[:, at] + other[:, at]
        out[:, at] = value * row


def mapped_body(dims, coded, me, idx, inverse, mine, other, out, *refs):
    row_count, capacity, per_core, blocks_here, tile_count = dims
    sends, (codes, powers, parts) = refs[:-3], refs[-3:]
    take_sum(coded, me, blocks_here, inverse, mine, other, out)
    encode_blocks(out, codes, powers, parts)
    idx = idx.ready()
    for k in range(1, row_count):
        pick_columns(idx, k, row_count, capacity, codes, powers, parts, sends[k - 1], 0, ([], []))


def last_mapped_body(blocks_here, coded, me, inverse, mine, other, after, out):
    take_sum(coded, me, blocks_here, inverse, mine, other, out)


def folded(square):
    half = square.shape[0] // 2
    return jnp.concatenate([square[:half], square[half:]], axis=1)


def unfolded(terms):
    total = functools.reduce(lambda total, term: total + term[...], terms[1:], terms[0][...])
    width = total.shape[1] // 2
    return jnp.concatenate([total[:, :width], total[:, width:]], axis=0)


def gram_body(me, own, other, out):
    full = both_columns(me[2], own[...], other[...])
    out[...] = folded(gram(pack(full), full.shape[0]))


def factor_body(after, *refs):
    refs[-1][...] = lower_inverse(unfolded(refs[:-1]))


def second_gram_body(me, factor, own, other, mapped, out):
    full = both_columns(me[2], own[...], other[...])
    parts = thirds(times(factor[...], pack(full)))
    mapped[...] = parts[: mapped.shape[0]]
    out[...] = folded(gram(parts, full.shape[0]))


def final_body(me, mapped, *refs):
    terms, (out, value, sent) = refs[:-3], refs[-3:]
    factor = lower_inverse(unfolded(terms))
    own_cols = value.shape[0]
    part = jnp.where(me[2] == 0, factor[:own_cols], factor[own_cols:])
    copies = []
    chunk = value.shape[1] // sent.shape[0]
    for i in range(sent.shape[0]):
        at = slice(i * chunk, (i + 1) * chunk)
        value[:, at] = times(part, mapped[:, at])
        copies.append(pltpu.make_async_copy(value.at[:, at], out.at[:, at], sent.at[i]))
        copies[-1].start()
    for copy in copies:
        copy.wait()


def shift_by(value, axes, size, shift):
    return lax.ppermute(value, axes, [(i, (i + shift) % size) for i in range(size)])


def row_terms(value, row_count):
    return [value] + [shift_by(value, "rows", row_count, k) for k in range(1, row_count)]


def pair_step(value, name, flip):
    return lax.ppermute(value, name, [(i, i ^ flip) for i in range(lax.axis_size(name))])


def pair_sum(value, axes):
    terms = None
    steps = [(name, 1 << bit) for name in axes for bit in range((lax.axis_size(name) - 1).bit_length())]
    for name, flip in steps:
        if terms is not None:
            value = terms[0] + terms[1]
        terms = (value, pair_step(value, name, flip))
    return terms


def local(embeddings, start, pair_list, pair_count):
    row_count = lax.axis_size("rows")
    tile_count = lax.axis_size("tiles")
    core_count = lax.axis_size("cols")
    row_index = lax.axis_index("rows")
    tile_index = lax.axis_index("tiles")
    col_index = lax.axis_index("cols")
    rows_here, half_features = embeddings.shape
    blocks_here = rows_here // BLOCK
    slots = pair_list.shape[2]
    capacity = slots // row_count
    per_core = capacity // core_count
    own_blocks = blocks_here // tile_count
    own_cols = start.shape[1]
    block_count = row_count * blocks_here
    others = range(1, row_count)

    own_list = jnp.concatenate(
        [pair_list[0], jnp.broadcast_to(pair_count[:, None], (1, slots))], axis=0
    )
    lists = row_terms(own_list, row_count)
    list_order = [0, *sorted(others, key=lambda k: k * (row_count - k))]
    self_part = call(
        functools.partial(self_distance_body, own_blocks, tile_count),
        sds((own_blocks * BLOCK, BLOCK), F32),
        [ME, embeddings],
    )
    planned = call(
        functools.partial(plan_body, (row_count, capacity, slots, blocks_here), list_order),
        [sds((6, slots + 1), jnp.int32)] + [sds((capacity * BLOCK, half_features), BF16) for _ in others],
        [ME, *[lists[k] for k in list_order], embeddings, self_part],
        late=range(1, 1 + row_count),
        any_in=(row_count + 2,),
        any_out=(0,),
        scratch=[pltpu.SMEM((6, slots + 1), jnp.int32), pltpu.SemaphoreType.DMA],
    )
    idx, sends = planned[0], planned[1:]
    order = sorted(others, key=lambda k: abs(k - row_count // 2))
    far = [shift_by(sends[k - 1], "rows", row_count, -k) for k in order]

    self_other = shift_by(self_part, "cols", core_count, 1)
    self_tiles, self_sums = call(
        functools.partial(self_tile_body, own_blocks),
        [sds((own_blocks, 2 * BLOCK, BLOCK), BF16), sds((own_blocks, BLOCK), F32)],
        [self_part, self_other],
    )
    values = start.T
    code_shapes = [((own_cols, rows_here), jnp.int16), ((blocks_here, BLOCK), F32), ((blocks_here, BLOCK), F32)]
    start_codes = call(start_body, [sds(*shape) for shape in code_shapes], [values])
    code_scratch = [pltpu.VMEM(*shape) for shape in code_shapes]
    coded = tile_count == 2
    own_squares = call(squares_body, sds((rows_here, BLOCK), F32), [embeddings, idx], any_in=(1,))
    pair_part = call(
        functools.partial(pair_distance_body, order, capacity),
        sds((slots * BLOCK, BLOCK), F32),
        [idx, embeddings, own_squares, *far],
        late=(0,),
    )
    pair_other = shift_by(pair_part, "cols", core_count, 1)

    dims = (row_count, capacity, per_core, blocks_here, tile_count)
    table = sds((block_count, BLOCK), F32)
    picked = 2 * capacity * own_cols
    tiles = call(
        functools.partial(pair_tile_body, dims),
        [sds((slots, 2 * BLOCK, BLOCK), BF16), sds((capacity, 2 * BLOCK, BLOCK), BF16), table]
        + [sds((per_core * BLOCK + picked + CODE_ROWS, BLOCK), jnp.int16) for _ in others],
        [ME, idx, pair_part, pair_other, self_sums, *start_codes],
        late=(1,),
    )
    near_tiles, home_tiles, degrees, sends = tiles[0], tiles[1], tiles[2], tiles[3:]
    degrees = functools.reduce(jnp.add, row_terms(degrees, row_count))
    degree_terms = pair_sum(degrees, ("tiles",))
    messages = [shift_by(sends[k - 1], "rows", row_count, k) for k in others]
    sent = call(
        functools.partial(split_body, row_count, per_core),
        [sds((per_core, 2 * BLOCK, BLOCK), BF16) for _ in others],
        [*messages, degree_terms[1]],
        any_in=(row_count - 1,),
    )
    shared = [shift_by(tile, "cols", core_count, 1) for tile in sent]

    block_shape = sds((own_cols, rows_here), F32)
    sum_shape = sds((own_cols, rows_here + BLOCK), jnp.int16) if coded else block_shape
    square = sds((2 * own_cols, 2 * own_cols), F32)
    folded_square = sds((own_cols, 4 * own_cols), F32)

    started, degree, inverse = call(
        functools.partial(first_own_body, dims),
        [block_shape, table, table],
        [ME, idx, *degree_terms, values, near_tiles, home_tiles, self_tiles],
        late=(1,),
    )
    part = call(
        functools.partial(first_far_body, dims, coded),
        sum_shape,
        [ME, idx, inverse, started, near_tiles, *sent, *shared, *messages],
        late=(1,),
        scratch=[pltpu.VMEM((own_cols, rows_here), F32)],
    )
    mine, other = pair_sum(part, ("tiles",))
    first = call(
        functools.partial(mapped_body, dims, coded),
        [block_shape] + [sds((picked + CODE_ROWS, BLOCK), jnp.int16) for _ in others],
        [ME, idx, inverse, mine, other],
        late=(1,),
        scratch=code_scratch,
    )
    mapped, sends = first[0], first[1:]
    received = [shift_by(sends[k - 1], "rows", row_count, k) for k in others]

    mapped_other = shift_by(mapped, "cols", core_count, 1)
    first_gram = call(gram_body, folded_square, [ME, mapped, mapped_other])
    part = call(
        functools.partial(second_apply_body, dims),
        block_shape,
        [ME, idx, inverse, first_gram, mapped, home_tiles, self_tiles, near_tiles, *sent, *shared, *received],
        late=(1,),
        any_in=(3,),
    )
    steps = (row_count - 1).bit_length()
    for bit in range(steps - 1):
        first_gram = first_gram + pair_step(first_gram, "rows", 1 << bit)
    part = call(functools.partial(send_sum_body, coded), sum_shape, [part, first_gram])
    gram_terms = (first_gram, pair_step(first_gram, "rows", 1 << (steps - 1)))
    mine, other = pair_sum(part, ("tiles",))
    second = call(
        functools.partial(last_mapped_body, blocks_here, coded),
        block_shape,
        [ME, inverse, mine, other, gram_terms[1]],
        any_in=(4,),
    )
    second_other = shift_by(second, "cols", core_count, 1)
    factor = call(factor_body, square, [second, *gram_terms], any_in=(0,))
    full, second_gram = call(
        second_gram_body,
        [sds((4 * own_cols, rows_here), BF16), folded_square],
        [ME, factor, second, second_other],
    )
    vectors = call(
        final_body,
        block_shape,
        [ME, full, *row_terms(second_gram, row_count)],
        any_out=(0,),
        scratch=[pltpu.VMEM((own_cols, rows_here), F32), pltpu.SemaphoreType.DMA((4,))],
    )
    own_degree = lax.dynamic_slice_in_dim(degree, row_index * blocks_here, blocks_here, 0)
    return (vectors.T, own_degree.reshape(rows_here))


def solution(mesh):
    in_specs = (
        P(("groups", "rows"), "cols"),
        P(("groups", "rows"), "cols"),
        P(("groups", "rows", "tiles"), None, None),
        P(("groups", "rows", "tiles")),
    )
    out_specs = (P(("groups", "rows"), "cols"), P(("groups", "rows")))
    return jax.shard_map(local, mesh=mesh, in_specs=in_specs, out_specs=out_specs, check_vma=False)
```

```python
import functools

import jax
import jax.numpy as jnp
from jax import lax
from jax.experimental import pallas as pl
from jax.experimental.pallas import tpu as pltpu
from jax.sharding import PartitionSpec as P

BLOCK = 128
kernel_gamma = 14.0
CODE_TOP = 32767.0
PART_TOP = 16384.0
CODE_ROWS = 16

VMEM = pl.BlockSpec(memory_space=pltpu.VMEM)
ANY = pl.BlockSpec(memory_space=pl.ANY)
F32 = jnp.float32
BF16 = jnp.bfloat16
HIGHEST = lax.Precision.HIGHEST
NT = (((1,), (1,)), ((), ()))


ME = None


def with_position(body):
    def inner(*refs):
        return body([lax.axis_index(name) for name in ("rows", "tiles", "cols")], *refs)

    return inner


class Late:
    def __init__(self, source, table, arrived):
        self.table = table
        self.copy = pltpu.make_async_copy(source, table, arrived)
        self.copy.start()

    def ready(self):
        self.copy.wait()
        return self.table


def with_late(body, places, count):
    def inner(*refs):
        refs, tables, arrived = refs[:-1 - count], refs[-1 - count : -1], refs[-1]
        refs = list(refs)
        for i, place in enumerate(places):
            refs[place] = Late(refs[place], tables[i], arrived.at[i])
        body(*refs)

    return inner


def call(body, outs, args, late=(), any_in=(), scratch=(), any_out=()):
    if args[0] is ME:
        body, args = with_position(body), args[1:]
        late, any_in = [[i - 1 for i in places] for places in (late, any_in)]
    if late:
        scratch = [
            *scratch,
            *[pltpu.SMEM(args[i].shape, args[i].dtype) for i in late],
            pltpu.SemaphoreType.DMA((len(late),)),
        ]
        any_in = [*any_in, *late]
        body = with_late(body, late, len(late))
    single = not isinstance(outs, (list, tuple))
    shapes = [outs] if single else list(outs)
    result = pl.pallas_call(
        body,
        out_shape=shapes,
        in_specs=[ANY if i in any_in else VMEM for i in range(len(args))],
        out_specs=[ANY if i in any_out else VMEM for i in range(len(shapes))],
        scratch_shapes=list(scratch),
        compiler_params=pltpu.CompilerParams(vmem_limit_bytes=48 * 2**20),
    )(*args)
    return result[0] if single else result


def sds(shape, dtype):
    return jax.ShapeDtypeStruct(shape, dtype)


def at_block(index):
    return pl.ds(pl.multiple_of(index * BLOCK, BLOCK), BLOCK)


def eye_mask(size):
    return lax.broadcasted_iota(jnp.int32, (size, size), 0) == lax.broadcasted_iota(
        jnp.int32, (size, size), 1
    )


def halves(value):
    high = value.astype(BF16)
    low = (value - high.astype(F32)).astype(BF16)
    return high, low


def pack(tile):
    return jnp.concatenate(halves(tile), axis=0)


def scale_of(power, part):
    return jnp.exp2(power) * (part * (1.0 / PART_TOP))


def encode(values):
    most = jnp.maximum(jnp.max(jnp.abs(values), axis=0, keepdims=True), 1e-30)
    power = jnp.floor(jnp.log2(most)) + 1.0
    part = jnp.floor(most * jnp.exp2(-power) * PART_TOP) + 1.0
    steps = jnp.floor(values * (CODE_TOP / scale_of(power, part)) + 0.5)
    steps = jnp.minimum(jnp.maximum(steps, -CODE_TOP), CODE_TOP)
    return steps.astype(jnp.int32).astype(jnp.int16), power, part


def decode(steps, scale):
    return steps.astype(jnp.int32).astype(F32) * (scale * (1.0 / CODE_TOP))


def as_rows(powers, parts, count):
    fill = jnp.zeros((count // 2 - len(powers), BLOCK), F32)
    fill = [fill] if fill.shape[0] else []
    rows = jnp.concatenate([*powers, *fill, *parts, *fill], axis=0)
    return rows.astype(jnp.int32).astype(jnp.int16)


def scale_rows(rows):
    rows = rows.astype(jnp.int32).astype(F32)
    half = rows.shape[0] // 2
    return scale_of(rows[:half], rows[half:])


def row_at(rows, place):
    if isinstance(place, int):
        return rows[place : place + 1, :]
    line = rows[:1, :]
    for i in range(1, rows.shape[0]):
        line = jnp.where(place == i, rows[i : i + 1, :], line)
    return line


def product(packed, values):
    left = jnp.concatenate(halves(values), axis=0)
    both = jnp.dot(jnp.concatenate([left, left], axis=1), packed, preferred_element_type=F32)
    count = values.shape[0]
    return both[:count] + both[count:]


def thirds(value):
    high = value.astype(BF16)
    rest = value - high.astype(F32)
    middle = rest.astype(BF16)
    low = (rest - middle.astype(F32)).astype(BF16)
    return jnp.concatenate([high, middle, low], axis=0)


def gram(parts, n):
    cross = lax.dot_general(parts, parts, NT, preferred_element_type=F32)
    count = parts.shape[0] // n
    pairs = sorted(((i, j) for i in range(count) for j in range(count)), key=lambda p: -p[0] - p[1])
    total = None
    for i, j in pairs:
        piece = cross[i * n : (i + 1) * n, j * n : (j + 1) * n]
        total = piece if total is None else total + piece
    return total


def times(left, parts):
    m = left.shape[0]
    left = jnp.concatenate(halves(left), axis=0)
    both = jnp.dot(jnp.concatenate([left, left], axis=1), parts, preferred_element_type=F32)
    return both[m:] + both[:m]


def lower_inverse(matrix, step=8):
    n = matrix.shape[0]
    state = jnp.concatenate([matrix, eye_mask(n).astype(F32)], axis=1)
    done = []
    for j in range(0, n, step):
        top = j // 8 * 8
        if top > n - state.shape[0]:
            done.append(state[:8])
            state = state[8:]
        base = j - top
        rows = lax.broadcasted_iota(jnp.int32, state.shape, 0)
        columns = [jnp.broadcast_to(state[:, j + i : j + i + 1], state.shape) for i in range(step)]
        lines = [state[base + i : base + i + 1, :] for i in range(step)]
        pivot = [[columns[k][base + i : base + i + 1, :] for k in range(step)] for i in range(step)]
        for i in range(step):
            if i % 2 == 0:
                first, cross, second = pivot[i][i], pivot[i][i + 1], pivot[i + 1][i + 1]
                reciprocals = (1.0 / first, first / (first * second - cross * cross))
            reciprocal = reciprocals[i % 2]
            scaled = lines[i] * reciprocal
            ratio = [pivot[i][k] * reciprocal for k in range(step)]
            for k in range(i + 1, step):
                lines[k] = lines[k] - pivot[k][i] * scaled
                columns[k] = columns[k] - columns[i] * ratio[k]
                for m in range(i + 1, step):
                    pivot[k][m] = pivot[k][m] - pivot[k][i] * ratio[m]
            state = state - jnp.where(rows > base + i, columns[i], 0.0) * scaled
    state = jnp.concatenate([*done, state], axis=0)
    pivots = jnp.sum(jnp.where(eye_mask(n), state[:, :n], 0.0), axis=1, keepdims=True)
    return state[:, n:] / jnp.sqrt(pivots)


def both_columns(core, own, other):
    first = core == 0
    return jnp.concatenate(
        [jnp.where(first, own, other), jnp.where(first, other, own)], axis=0
    )


def quotient(value, size):
    if size & (size - 1) == 0:
        return lax.shift_right_logical(value, jnp.int32(size.bit_length() - 1))
    return lax.div(value, jnp.int32(size))


def remainder(value, size):
    if size & (size - 1) == 0:
        return lax.bitwise_and(value, jnp.int32(size - 1))
    return lax.rem(value, jnp.int32(size))


def plan_body(dims, list_order, me, live_count, *refs):
    row_count, capacity, slots, blocks_here = dims
    lists, (emb, after, idx_out) = refs[:row_count], refs[row_count : row_count + 3]
    sends, (idx, left) = refs[row_count + 3 : -2], refs[-2:]
    row = me[0]
    for i in range(slots):
        for line in (0, 1, 2, 4, 5):
            idx[line, i] = 0
    lists = dict(zip(list_order, [one.ready() for one in lists]))
    live_count = live_count.ready()[0]

    def each(step, start):
        if slots <= 8:
            for s in range(slots):
                start = step(s, start)
        else:
            lax.fori_loop(0, slots, step, start)

    for k in range(row_count):

        def step(s, counts, k=k):
            near = lists[k][0, s]
            far = lists[k][1, s]
            owner = quotient(far, blocks_here)
            hit = owner == row
            if k > 0:
                hit = hit & (counts[0] < capacity)
            else:
                live = s < live_count
                hit = hit & live
            slot = jnp.where(hit, k * capacity + counts[0], slots)
            idx[4, slot] = far - row * blocks_here
            idx[5, slot] = near
            if k > 0:
                return (counts[0] + hit.astype(jnp.int32),)
            shift = remainder(owner - row + row_count, row_count)
            rank = counts[1]
            for d in range(1, row_count):
                rank = jnp.where(shift == d, counts[1 + d], rank)
            slot = jnp.where(live, shift * capacity + rank, slots)
            idx[0, slot] = near - row * blocks_here
            idx[1, slot] = far
            idx[2, slot] = 1
            more = tuple(
                counts[1 + d] + (live & (shift == d)).astype(jnp.int32) for d in range(row_count)
            )
            return (counts[0] + hit.astype(jnp.int32), *more)

        each(step, (jnp.int32(0),) * (1 + row_count if k == 0 else 1))
    leave = pltpu.make_async_copy(idx, idx_out, left)
    leave.start()
    for k in range(1, row_count):
        for j in range(capacity):
            sends[k - 1][j * BLOCK : (j + 1) * BLOCK, :] = emb[at_block(idx[4, k * capacity + j]), :]
    leave.wait()


def squares(block):
    return jnp.sum(jnp.square(block.astype(F32)), axis=1, keepdims=True)


def as_row(column):
    return jnp.sum(jnp.where(eye_mask(BLOCK), column, 0.0), axis=0, keepdims=True)


def partial_distance(left, right, left_sq, right_row):
    inner = lax.dot_general(left, right, NT, preferred_element_type=F32)
    return left_sq + right_row - 2.0 * inner


def self_distance_body(own_blocks, tile_count, me, emb, out):
    for i in range(own_blocks):
        block = emb[at_block(i * tile_count + me[1]), :]
        block_sq = squares(block)
        out[i * BLOCK : (i + 1) * BLOCK, :] = partial_distance(
            block, block, block_sq, as_row(block_sq)
        )


def squares_body(emb, after, out):
    for b in range(out.shape[0] // BLOCK):
        part = slice(b * BLOCK, (b + 1) * BLOCK)
        out[part, :] = jnp.broadcast_to(squares(emb[part, :]), (BLOCK, BLOCK))


def pair_distance_body(order, capacity, idx, emb, own_squares, *refs):
    far, out = dict(zip(order, refs)), refs[-1]
    rows = {}
    for k in order:
        for j in range(capacity):
            rows[k, j] = as_row(squares(far[k][j * BLOCK : (j + 1) * BLOCK, :]))
    idx = idx.ready()
    for k in range(len(order) + 1):
        for j in range(capacity):
            slot = k * capacity + j
            left = emb[at_block(idx[0, slot]), :]
            left_sq = own_squares[at_block(idx[0, slot]), :]
            if k == 0:
                right = emb[at_block(idx[4, j]), :]
                right_row = as_row(own_squares[at_block(idx[4, j]), :])
            else:
                right = far[k][j * BLOCK : (j + 1) * BLOCK, :]
                right_row = rows[k, j]
            part = slice(slot * BLOCK, (slot + 1) * BLOCK)
            out[part, :] = partial_distance(left, right, left_sq, right_row)


def self_tile_body(own_blocks, mine, other, packed, sums):
    for i in range(own_blocks):
        part = slice(i * BLOCK, (i + 1) * BLOCK)
        tile = jnp.exp(-kernel_gamma * (mine[part, :] + other[part, :] - 2.0))
        tile = jnp.where(eye_mask(BLOCK), 0.0, tile)
        packed[i] = pack(tile)
        sums[i : i + 1, :] = jnp.sum(tile, axis=0, keepdims=True)


def pair_tile_body(dims, me, idx, mine, other, self_sums, codes, powers, parts, near_tiles, home_tiles, table, *sends):
    row_count, capacity, per_core, blocks_here, tile_count = dims
    row, tile_index, core = me[0], me[1], me[2]
    table[...] = jnp.zeros(table.shape, F32)
    for i in range(self_sums.shape[0]):
        table[pl.ds(row * blocks_here + i * tile_count + tile_index, 1), :] = self_sums[i : i + 1, :]

    def add(block, line):
        place = pl.ds(block, 1)
        table[place, :] = table[place, :] + line

    all_tiles = jnp.exp(-kernel_gamma * (mine[...] + other[...] - 2.0))
    idx = idx.ready()
    for k in range(row_count):
        tiles = []
        for j in range(capacity):
            slot = k * capacity + j
            tile = all_tiles[slot * BLOCK : (slot + 1) * BLOCK]
            tile = jnp.where(idx[2, slot] > 0, tile, 0.0)
            turned = tile.T
            near_tiles[slot] = pack(turned)
            add(row * blocks_here + idx[0, slot], jnp.sum(turned, axis=0, keepdims=True))
            add(idx[1, slot], jnp.sum(tile, axis=0, keepdims=True))
            if k == 0:
                home_tiles[j] = pack(tile)
            tiles.append(tile)
        if k > 0:
            lines = ([], [])
            for inner in range(per_core):
                at = slice(inner * BLOCK, (inner + 1) * BLOCK)
                steps, power, part = encode(jnp.where(core == 0, tiles[inner], tiles[per_core + inner]))
                sends[k - 1][at, :] = steps
                lines[0].append(power)
                lines[1].append(part)
            pick_columns(idx, k, row_count, capacity, codes, powers, parts, sends[k - 1], per_core * BLOCK, lines)


def encode_blocks(values, codes, powers, parts):
    for b in range(powers.shape[0]):
        at = slice(b * BLOCK, (b + 1) * BLOCK)
        steps, power, part = encode(values[:, at])
        codes[:, at] = steps
        powers[b : b + 1, :] = power
        parts[b : b + 1, :] = part


def start_body(values, codes, powers, parts):
    encode_blocks(values, codes, powers, parts)


def split_body(row_count, per_core, *refs):
    others = row_count - 1
    messages, outs = refs[:others], refs[-others:]
    for message, out in zip(messages, outs):
        scales = scale_rows(message[message.shape[0] - CODE_ROWS :, :])
        for inner in range(per_core):
            steps = message[inner * BLOCK : (inner + 1) * BLOCK, :]
            out[inner] = pack(decode(steps, scales[inner : inner + 1, :]))


def pick_columns(idx, k, row_count, capacity, codes, powers, parts, send, base, lines):
    count = codes.shape[0]
    back = row_count - k
    blocks = [idx[0, k * capacity + j] for j in range(capacity)]
    blocks += [idx[4, back * capacity + j] for j in range(capacity)]
    for place, block in enumerate(blocks):
        send[base + place * count : base + (place + 1) * count, :] = codes[:, at_block(block)]
        lines[0].append(powers[pl.ds(block, 1), :])
        lines[1].append(parts[pl.ds(block, 1), :])
    send[base + len(blocks) * count :, :] = as_rows(*lines, CODE_ROWS)


def add_product(out, block, packed, values):
    place = at_block(block)
    out[:, place] = out[:, place] + product(packed, values)


def apply_own(dims, me, idx, inverse, own, near_tiles, home_tiles, self_tiles, out):
    row_count, capacity, per_core, blocks_here, tile_count = dims
    row, tile_index = me[0], me[1]
    out[...] = jnp.zeros(out.shape, F32)

    def scaled(block):
        return own[:, at_block(block)] * inverse[pl.ds(row * blocks_here + block, 1), :]

    for i in range(blocks_here // tile_count):
        block = i * tile_count + tile_index
        add_product(out, block, self_tiles[i], scaled(block))
    idx = idx.ready()
    for j in range(capacity):
        add_product(out, idx[0, j], near_tiles[j], scaled(idx[4, j]))
        add_product(out, idx[4, j], home_tiles[j], scaled(idx[0, j]))
    return idx


def apply_far(dims, me, idx, inverse, received, base, near_tiles, sent, shared, out):
    row_count, capacity, per_core, blocks_here, tile_count = dims
    core = me[2]
    count = out.shape[0]
    lines = [scale_rows(message[message.shape[0] - CODE_ROWS :, :]) for message in received]
    first_line = base // BLOCK

    def arrived(k, place, block):
        steps = received[k - 1][pl.ds(pl.multiple_of(base + place * count, CODE_ROWS), count), :]
        rows = lines[k - 1][first_line : first_line + 2 * capacity, :]
        return decode(steps, row_at(rows, place) * inverse[pl.ds(block, 1), :])

    for k in range(1, row_count):
        for j in range(capacity):
            slot = k * capacity + j
            values = arrived(row_count - k, capacity + j, idx[1, slot])
            add_product(out, idx[0, slot], near_tiles[slot], values)
            inner = j % per_core
            if j < per_core:
                place = core * per_core + inner
                packed = sent[k - 1][inner]
            else:
                place = (1 - core) * per_core + inner
                packed = shared[k - 1][inner]
            slot = k * capacity + place
            add_product(out, idx[4, slot], packed, arrived(k, place, idx[5, slot]))


def first_own_body(dims, me, idx, mine, other, own, near_tiles, home_tiles, self_tiles, out, degree, inverse):
    total = mine[...] + other[...]
    degree[...] = total
    inverse[...] = 1.0 / jnp.sqrt(total)
    apply_own(dims, me, idx, inverse, own, near_tiles, home_tiles, self_tiles, out)


def first_far_body(dims, coded, me, idx, inverse, started, near_tiles, *refs):
    row_count, per_core = dims[0], dims[2]
    others = row_count - 1
    sent, shared, messages = refs[:others], refs[others : 2 * others], refs[2 * others : 3 * others]
    out, total = refs[3 * others :]
    total[...] = started[...]
    apply_far(dims, me, idx.ready(), inverse, messages, per_core * BLOCK, near_tiles, sent, shared, total)
    put_sum(coded, total, out)


def second_apply_body(dims, me, idx, inverse, after, own, home_tiles, self_tiles, near_tiles, *refs):
    others = dims[0] - 1
    sent, shared, received = refs[:others], refs[others : 2 * others], refs[2 * others : 3 * others]
    out = refs[-1]
    idx = apply_own(dims, me, idx, inverse, own, near_tiles, home_tiles, self_tiles, out)
    apply_far(dims, me, idx, inverse, received, 0, near_tiles, sent, shared, out)


def send_sum_body(coded, total, after, out):
    put_sum(coded, total, out)


def put_sum(coded, total, out):
    if not coded:
        out[...] = total[...]
        return
    lines = ([], [])
    blocks_here = total.shape[1] // BLOCK
    for b in range(blocks_here):
        at = slice(b * BLOCK, (b + 1) * BLOCK)
        steps, power, part = encode(total[:, at])
        out[:, at] = steps
        lines[0].append(power)
        lines[1].append(part)
    out[:, blocks_here * BLOCK :] = as_rows(*lines, out.shape[0])


def take_sum(coded, me, blocks_here, inverse, mine, other, out):
    if coded:
        tail = blocks_here * BLOCK
        my_scales, other_scales = scale_rows(mine[:, tail:]), scale_rows(other[:, tail:])
    for b in range(blocks_here):
        at = slice(b * BLOCK, (b + 1) * BLOCK)
        row = inverse[pl.ds(me[0] * blocks_here + b, 1), :]
        if coded:
            line = slice(b, b + 1)
            value = decode(mine[:, at], my_scales[line]) + decode(other[:, at], other_scales[line])
        else:
            value = mine[:, at] + other[:, at]
        out[:, at] = value * row


def mapped_body(dims, coded, me, idx, inverse, mine, other, out, *refs):
    row_count, capacity, per_core, blocks_here, tile_count = dims
    sends, (codes, powers, parts) = refs[:-3], refs[-3:]
    take_sum(coded, me, blocks_here, inverse, mine, other, out)
    encode_blocks(out, codes, powers, parts)
    idx = idx.ready()
    for k in range(1, row_count):
        pick_columns(idx, k, row_count, capacity, codes, powers, parts, sends[k - 1], 0, ([], []))


def last_mapped_body(blocks_here, coded, me, inverse, mine, other, after, out):
    take_sum(coded, me, blocks_here, inverse, mine, other, out)


def folded(square):
    half = square.shape[0] // 2
    return jnp.concatenate([square[:half], square[half:]], axis=1)


def unfolded(terms):
    total = functools.reduce(lambda total, term: total + term[...], terms[1:], terms[0][...])
    width = total.shape[1] // 2
    return jnp.concatenate([total[:, :width], total[:, width:]], axis=0)


def gram_body(me, own, other, out):
    full = both_columns(me[2], own[...], other[...])
    out[...] = folded(gram(pack(full), full.shape[0]))


def factor_body(after, *refs):
    refs[-1][...] = lower_inverse(unfolded(refs[:-1]))


def second_gram_body(me, factor, own, other, mapped, out):
    full = both_columns(me[2], own[...], other[...])
    parts = thirds(times(factor[...], pack(full)))
    mapped[...] = parts[: mapped.shape[0]]
    out[...] = folded(gram(parts, full.shape[0]))


def final_body(me, mapped, *refs):
    terms, (out, value, sent) = refs[:-3], refs[-3:]
    factor = lower_inverse(unfolded(terms))
    own_cols = value.shape[0]
    part = jnp.where(me[2] == 0, factor[:own_cols], factor[own_cols:])
    copies = []
    chunk = value.shape[1] // sent.shape[0]
    for i in range(sent.shape[0]):
        at = slice(i * chunk, (i + 1) * chunk)
        value[:, at] = times(part, mapped[:, at])
        copies.append(pltpu.make_async_copy(value.at[:, at], out.at[:, at], sent.at[i]))
        copies[-1].start()
    for copy in copies:
        copy.wait()


def shift_by(value, axes, size, shift):
    return lax.ppermute(value, axes, [(i, (i + shift) % size) for i in range(size)])


def row_terms(value, row_count):
    return [value] + [shift_by(value, "rows", row_count, k) for k in range(1, row_count)]


def pair_step(value, name, flip):
    return lax.ppermute(value, name, [(i, i ^ flip) for i in range(lax.axis_size(name))])


def pair_sum(value, axes):
    terms = None
    steps = [(name, 1 << bit) for name in axes for bit in range((lax.axis_size(name) - 1).bit_length())]
    for name, flip in steps:
        if terms is not None:
            value = terms[0] + terms[1]
        terms = (value, pair_step(value, name, flip))
    return terms


def local(embeddings, start, pair_list, pair_count):
    row_count = lax.axis_size("rows")
    tile_count = lax.axis_size("tiles")
    core_count = lax.axis_size("cols")
    row_index = lax.axis_index("rows")
    tile_index = lax.axis_index("tiles")
    col_index = lax.axis_index("cols")
    rows_here, half_features = embeddings.shape
    blocks_here = rows_here // BLOCK
    slots = pair_list.shape[2]
    capacity = slots // row_count
    per_core = capacity // core_count
    own_blocks = blocks_here // tile_count
    own_cols = start.shape[1]
    block_count = row_count * blocks_here
    others = range(1, row_count)

    list_order = [0, *sorted(others, key=lambda k: k * (row_count - k))]
    lists = [shift_by(pair_list[0], "rows", row_count, k) if k else pair_list[0] for k in list_order]
    self_part = call(
        functools.partial(self_distance_body, own_blocks, tile_count),
        sds((own_blocks * BLOCK, BLOCK), F32),
        [ME, embeddings],
    )
    planned = call(
        functools.partial(plan_body, (row_count, capacity, slots, blocks_here), list_order),
        [sds((6, slots + 1), jnp.int32)] + [sds((capacity * BLOCK, half_features), BF16) for _ in others],
        [ME, pair_count, *lists, embeddings, self_part],
        late=range(1, 2 + row_count),
        any_in=(row_count + 3,),
        any_out=(0,),
        scratch=[pltpu.SMEM((6, slots + 1), jnp.int32), pltpu.SemaphoreType.DMA],
    )
    idx, sends = planned[0], planned[1:]
    order = sorted(others, key=lambda k: abs(k - row_count // 2))
    far = [shift_by(sends[k - 1], "rows", row_count, -k) for k in order]

    self_other = shift_by(self_part, "cols", core_count, 1)
    self_tiles, self_sums = call(
        functools.partial(self_tile_body, own_blocks),
        [sds((own_blocks, 2 * BLOCK, BLOCK), BF16), sds((own_blocks, BLOCK), F32)],
        [self_part, self_other],
    )
    values = start.T
    code_shapes = [((own_cols, rows_here), jnp.int16), ((blocks_here, BLOCK), F32), ((blocks_here, BLOCK), F32)]
    start_codes = call(start_body, [sds(*shape) for shape in code_shapes], [values])
    code_scratch = [pltpu.VMEM(*shape) for shape in code_shapes]
    coded = tile_count == 2
    own_squares = call(squares_body, sds((rows_here, BLOCK), F32), [embeddings, idx], any_in=(1,))
    pair_part = call(
        functools.partial(pair_distance_body, order, capacity),
        sds((slots * BLOCK, BLOCK), F32),
        [idx, embeddings, own_squares, *far],
        late=(0,),
    )
    pair_other = shift_by(pair_part, "cols", core_count, 1)

    dims = (row_count, capacity, per_core, blocks_here, tile_count)
    table = sds((block_count, BLOCK), F32)
    picked = 2 * capacity * own_cols
    tiles = call(
        functools.partial(pair_tile_body, dims),
        [sds((slots, 2 * BLOCK, BLOCK), BF16), sds((capacity, 2 * BLOCK, BLOCK), BF16), table]
        + [sds((per_core * BLOCK + picked + CODE_ROWS, BLOCK), jnp.int16) for _ in others],
        [ME, idx, pair_part, pair_other, self_sums, *start_codes],
        late=(1,),
    )
    near_tiles, home_tiles, degrees, sends = tiles[0], tiles[1], tiles[2], tiles[3:]
    degrees = functools.reduce(jnp.add, row_terms(degrees, row_count))
    degree_terms = pair_sum(degrees, ("tiles",))
    messages = [shift_by(sends[k - 1], "rows", row_count, k) for k in others]
    sent = call(
        functools.partial(split_body, row_count, per_core),
        [sds((per_core, 2 * BLOCK, BLOCK), BF16) for _ in others],
        [*messages, degree_terms[1]],
        any_in=(row_count - 1,),
    )
    shared = [shift_by(tile, "cols", core_count, 1) for tile in sent]

    block_shape = sds((own_cols, rows_here), F32)
    sum_shape = sds((own_cols, rows_here + BLOCK), jnp.int16) if coded else block_shape
    square = sds((2 * own_cols, 2 * own_cols), F32)
    folded_square = sds((own_cols, 4 * own_cols), F32)

    started, degree, inverse = call(
        functools.partial(first_own_body, dims),
        [block_shape, table, table],
        [ME, idx, *degree_terms, values, near_tiles, home_tiles, self_tiles],
        late=(1,),
    )
    part = call(
        functools.partial(first_far_body, dims, coded),
        sum_shape,
        [ME, idx, inverse, started, near_tiles, *sent, *shared, *messages],
        late=(1,),
        scratch=[pltpu.VMEM((own_cols, rows_here), F32)],
    )
    mine, other = pair_sum(part, ("tiles",))
    first = call(
        functools.partial(mapped_body, dims, coded),
        [block_shape] + [sds((picked + CODE_ROWS, BLOCK), jnp.int16) for _ in others],
        [ME, idx, inverse, mine, other],
        late=(1,),
        scratch=code_scratch,
    )
    mapped, sends = first[0], first[1:]
    received = [shift_by(sends[k - 1], "rows", row_count, k) for k in others]

    mapped_other = shift_by(mapped, "cols", core_count, 1)
    first_gram = call(gram_body, folded_square, [ME, mapped, mapped_other])
    part = call(
        functools.partial(second_apply_body, dims),
        block_shape,
        [ME, idx, inverse, first_gram, mapped, home_tiles, self_tiles, near_tiles, *sent, *shared, *received],
        late=(1,),
        any_in=(3,),
    )
    steps = (row_count - 1).bit_length()
    for bit in range(steps - 1):
        first_gram = first_gram + pair_step(first_gram, "rows", 1 << bit)
    part = call(functools.partial(send_sum_body, coded), sum_shape, [part, first_gram])
    gram_terms = (first_gram, pair_step(first_gram, "rows", 1 << (steps - 1)))
    mine, other = pair_sum(part, ("tiles",))
    second = call(
        functools.partial(last_mapped_body, blocks_here, coded),
        block_shape,
        [ME, inverse, mine, other, gram_terms[1]],
        any_in=(4,),
    )
    second_other = shift_by(second, "cols", core_count, 1)
    factor = call(factor_body, square, [second, *gram_terms], any_in=(0,))
    full, second_gram = call(
        second_gram_body,
        [sds((4 * own_cols, rows_here), BF16), folded_square],
        [ME, factor, second, second_other],
    )
    vectors = call(
        final_body,
        block_shape,
        [ME, full, *row_terms(second_gram, row_count)],
        any_out=(0,),
        scratch=[pltpu.VMEM((own_cols, rows_here), F32), pltpu.SemaphoreType.DMA((4,))],
    )
    own_degree = lax.dynamic_slice_in_dim(degree, row_index * blocks_here, blocks_here, 0)
    return (vectors.T, own_degree.reshape(rows_here))


def solution(mesh):
    in_specs = (
        P(("groups", "rows"), "cols"),
        P(("groups", "rows"), "cols"),
        P(("groups", "rows", "tiles"), None, None),
        P(("groups", "rows", "tiles")),
    )
    out_specs = (P(("groups", "rows"), "cols"), P(("groups", "rows")))
    return jax.shard_map(local, mesh=mesh, in_specs=in_specs, out_specs=out_specs, check_vma=False)
```

```python
import functools

import jax
import jax.numpy as jnp
from jax import lax
from jax.experimental import pallas as pl
from jax.experimental.pallas import tpu as pltpu
from jax.sharding import PartitionSpec as P

BLOCK = 128
kernel_gamma = 14.0
CODE_TOP = 32767.0
PART_TOP = 16384.0
CODE_ROWS = 16

VMEM = pl.BlockSpec(memory_space=pltpu.VMEM)
ANY = pl.BlockSpec(memory_space=pl.ANY)
F32 = jnp.float32
BF16 = jnp.bfloat16
HIGHEST = lax.Precision.HIGHEST
NT = (((1,), (1,)), ((), ()))


ME = None


def with_position(body):
    def inner(*refs):
        return body([lax.axis_index(name) for name in ("rows", "tiles", "cols")], *refs)

    return inner


class Late:
    def __init__(self, source, table, arrived):
        self.table = table
        self.copy = pltpu.make_async_copy(source, table, arrived)
        self.copy.start()

    def ready(self):
        self.copy.wait()
        return self.table


def with_late(body, places, count):
    def inner(*refs):
        refs, tables, arrived = refs[:-1 - count], refs[-1 - count : -1], refs[-1]
        refs = list(refs)
        for i, place in enumerate(places):
            refs[place] = Late(refs[place], tables[i], arrived.at[i])
        body(*refs)

    return inner


def call(body, outs, args, late=(), any_in=(), scratch=(), any_out=()):
    if args[0] is ME:
        body, args = with_position(body), args[1:]
        late, any_in = [[i - 1 for i in places] for places in (late, any_in)]
    if late:
        scratch = [
            *scratch,
            *[pltpu.SMEM(args[i].shape, args[i].dtype) for i in late],
            pltpu.SemaphoreType.DMA((len(late),)),
        ]
        any_in = [*any_in, *late]
        body = with_late(body, late, len(late))
    single = not isinstance(outs, (list, tuple))
    shapes = [outs] if single else list(outs)
    result = pl.pallas_call(
        body,
        out_shape=shapes,
        in_specs=[ANY if i in any_in else VMEM for i in range(len(args))],
        out_specs=[ANY if i in any_out else VMEM for i in range(len(shapes))],
        scratch_shapes=list(scratch),
        compiler_params=pltpu.CompilerParams(vmem_limit_bytes=48 * 2**20),
    )(*args)
    return result[0] if single else result


def sds(shape, dtype):
    return jax.ShapeDtypeStruct(shape, dtype)


def at_block(index):
    return pl.ds(pl.multiple_of(index * BLOCK, BLOCK), BLOCK)


def eye_mask(size):
    return lax.broadcasted_iota(jnp.int32, (size, size), 0) == lax.broadcasted_iota(
        jnp.int32, (size, size), 1
    )


def halves(value):
    high = value.astype(BF16)
    low = (value - high.astype(F32)).astype(BF16)
    return high, low


def pack(tile):
    return jnp.concatenate(halves(tile), axis=0)


def scale_of(power, part):
    return jnp.exp2(power) * (part * (1.0 / PART_TOP))


def encode(values):
    most = jnp.maximum(jnp.max(jnp.abs(values), axis=0, keepdims=True), 1e-30)
    power = jnp.floor(jnp.log2(most)) + 1.0
    part = jnp.floor(most * jnp.exp2(-power) * PART_TOP) + 1.0
    steps = jnp.floor(values * (CODE_TOP / scale_of(power, part)) + 0.5)
    steps = jnp.minimum(jnp.maximum(steps, -CODE_TOP), CODE_TOP)
    return steps.astype(jnp.int32).astype(jnp.int16), power, part


def decode(steps, scale):
    return steps.astype(jnp.int32).astype(F32) * (scale * (1.0 / CODE_TOP))


def as_rows(powers, parts, count):
    fill = jnp.zeros((count // 2 - len(powers), BLOCK), F32)
    fill = [fill] if fill.shape[0] else []
    rows = jnp.concatenate([*powers, *fill, *parts, *fill], axis=0)
    return rows.astype(jnp.int32).astype(jnp.int16)


def scale_rows(rows):
    rows = rows.astype(jnp.int32).astype(F32)
    half = rows.shape[0] // 2
    return scale_of(rows[:half], rows[half:])


def row_at(rows, place):
    if isinstance(place, int):
        return rows[place : place + 1, :]
    line = rows[:1, :]
    for i in range(1, rows.shape[0]):
        line = jnp.where(place == i, rows[i : i + 1, :], line)
    return line


def product(packed, values):
    left = jnp.concatenate(halves(values), axis=0)
    both = jnp.dot(jnp.concatenate([left, left], axis=1), packed, preferred_element_type=F32)
    count = values.shape[0]
    return both[:count] + both[count:]


def thirds(value):
    high = value.astype(BF16)
    rest = value - high.astype(F32)
    middle = rest.astype(BF16)
    low = (rest - middle.astype(F32)).astype(BF16)
    return jnp.concatenate([high, middle, low], axis=0)


def gram(parts, n):
    cross = lax.dot_general(parts, parts, NT, preferred_element_type=F32)
    count = parts.shape[0] // n
    pairs = sorted(((i, j) for i in range(count) for j in range(count)), key=lambda p: -p[0] - p[1])
    total = None
    for i, j in pairs:
        piece = cross[i * n : (i + 1) * n, j * n : (j + 1) * n]
        total = piece if total is None else total + piece
    return total


def times(left, parts):
    m = left.shape[0]
    left = jnp.concatenate(halves(left), axis=0)
    both = jnp.dot(jnp.concatenate([left, left], axis=1), parts, preferred_element_type=F32)
    return both[m:] + both[:m]


def lower_inverse(matrix, step=8):
    n = matrix.shape[0]
    state = jnp.concatenate([matrix, eye_mask(n).astype(F32)], axis=1)
    done = []
    for j in range(0, n, step):
        top = j // 8 * 8
        if top > n - state.shape[0]:
            done.append(state[:8])
            state = state[8:]
        base = j - top
        rows = lax.broadcasted_iota(jnp.int32, state.shape, 0)
        columns = [jnp.broadcast_to(state[:, j + i : j + i + 1], state.shape) for i in range(step)]
        lines = [state[base + i : base + i + 1, :] for i in range(step)]
        pivot = [[columns[k][base + i : base + i + 1, :] for k in range(step)] for i in range(step)]
        for i in range(step):
            if i % 2 == 0:
                first, cross, second = pivot[i][i], pivot[i][i + 1], pivot[i + 1][i + 1]
                reciprocals = (1.0 / first, first / (first * second - cross * cross))
            reciprocal = reciprocals[i % 2]
            scaled = lines[i] * reciprocal
            ratio = [pivot[i][k] * reciprocal for k in range(step)]
            for k in range(i + 1, step):
                lines[k] = lines[k] - pivot[k][i] * scaled
                columns[k] = columns[k] - columns[i] * ratio[k]
                for m in range(i + 1, step):
                    pivot[k][m] = pivot[k][m] - pivot[k][i] * ratio[m]
            state = state - jnp.where(rows > base + i, columns[i], 0.0) * scaled
    state = jnp.concatenate([*done, state], axis=0)
    pivots = jnp.sum(jnp.where(eye_mask(n), state[:, :n], 0.0), axis=1, keepdims=True)
    return state[:, n:] / jnp.sqrt(pivots)


def both_columns(core, own, other):
    first = core == 0
    return jnp.concatenate(
        [jnp.where(first, own, other), jnp.where(first, other, own)], axis=0
    )


def quotient(value, size):
    if size & (size - 1) == 0:
        return lax.shift_right_logical(value, jnp.int32(size.bit_length() - 1))
    return lax.div(value, jnp.int32(size))


def remainder(value, size):
    if size & (size - 1) == 0:
        return lax.bitwise_and(value, jnp.int32(size - 1))
    return lax.rem(value, jnp.int32(size))


def plan_body(dims, list_order, me, *refs):
    row_count, capacity, slots, blocks_here = dims
    lists, (emb, after, idx_out) = refs[:row_count], refs[row_count : row_count + 3]
    sends, (idx, left) = refs[row_count + 3 : -2], refs[-2:]
    row = me[0]
    for i in range(slots):
        for line in (0, 1, 4, 5):
            idx[line, i] = 0
        idx[3, i] = slots
    lists = dict(zip(list_order, [one.ready() for one in lists]))

    def each(step, start):
        if slots <= 8:
            for s in range(slots):
                start = step(s, start)
        else:
            lax.fori_loop(0, slots, step, start)

    for k in range(row_count):

        def step(s, counts, k=k):
            near = lists[k][0, s]
            far = lists[k][1, s]
            owner = quotient(far, blocks_here)
            if k > 0:
                hit = (owner == row) & (counts[0] < capacity)
                slot = jnp.where(hit, k * capacity + counts[0], slots)
                idx[4, slot] = far - row * blocks_here
                idx[5, slot] = near
                return (counts[0] + hit.astype(jnp.int32),)
            shift = remainder(owner - row + row_count, row_count)
            rank = counts[0]
            for d in range(1, row_count):
                rank = jnp.where(shift == d, counts[d], rank)
            slot = jnp.where(rank < capacity, shift * capacity + rank, slots)
            idx[0, slot] = near - row * blocks_here
            idx[1, slot] = far
            idx[3, slot] = s
            slot = jnp.where(shift == 0, slot, slots)
            idx[4, slot] = far - row * blocks_here
            idx[5, slot] = near
            return tuple(counts[d] + (shift == d).astype(jnp.int32) for d in range(row_count))

        each(step, (jnp.int32(0),) * (row_count if k == 0 else 1))
    leave = pltpu.make_async_copy(idx, idx_out, left)
    leave.start()
    for k in range(1, row_count):
        for j in range(capacity):
            sends[k - 1][j * BLOCK : (j + 1) * BLOCK, :] = emb[at_block(idx[4, k * capacity + j]), :]
    leave.wait()


def squares(block):
    return jnp.sum(jnp.square(block.astype(F32)), axis=1, keepdims=True)


def as_row(column):
    return jnp.sum(jnp.where(eye_mask(BLOCK), column, 0.0), axis=0, keepdims=True)


def partial_distance(left, right, left_sq, right_row):
    inner = lax.dot_general(left, right, NT, preferred_element_type=F32)
    return left_sq + right_row - 2.0 * inner


def self_distance_body(own_blocks, tile_count, me, emb, out):
    for i in range(own_blocks):
        block = emb[at_block(i * tile_count + me[1]), :]
        block_sq = squares(block)
        out[i * BLOCK : (i + 1) * BLOCK, :] = partial_distance(
            block, block, block_sq, as_row(block_sq)
        )


def squares_body(emb, after, out):
    for b in range(out.shape[0] // BLOCK):
        part = slice(b * BLOCK, (b + 1) * BLOCK)
        out[part, :] = jnp.broadcast_to(squares(emb[part, :]), (BLOCK, BLOCK))


def pair_distance_body(order, capacity, idx, emb, own_squares, *refs):
    far, out = dict(zip(order, refs)), refs[-1]
    rows = {}
    for k in order:
        for j in range(capacity):
            rows[k, j] = as_row(squares(far[k][j * BLOCK : (j + 1) * BLOCK, :]))
    idx = idx.ready()
    for k in range(len(order) + 1):
        for j in range(capacity):
            slot = k * capacity + j
            left = emb[at_block(idx[0, slot]), :]
            left_sq = own_squares[at_block(idx[0, slot]), :]
            if k == 0:
                right = emb[at_block(idx[4, j]), :]
                right_row = as_row(own_squares[at_block(idx[4, j]), :])
            else:
                right = far[k][j * BLOCK : (j + 1) * BLOCK, :]
                right_row = rows[k, j]
            part = slice(slot * BLOCK, (slot + 1) * BLOCK)
            out[part, :] = partial_distance(left, right, left_sq, right_row)


def self_tile_body(own_blocks, mine, other, packed, sums):
    for i in range(own_blocks):
        part = slice(i * BLOCK, (i + 1) * BLOCK)
        tile = jnp.exp(-kernel_gamma * (mine[part, :] + other[part, :] - 2.0))
        tile = jnp.where(eye_mask(BLOCK), 0.0, tile)
        packed[i] = pack(tile)
        sums[i : i + 1, :] = jnp.sum(tile, axis=0, keepdims=True)


def pair_tile_body(dims, me, idx, live_count, mine, other, self_sums, codes, powers, parts, near_tiles, home_tiles, table, *sends):
    row_count, capacity, per_core, blocks_here, tile_count = dims
    row, tile_index, core = me[0], me[1], me[2]
    table[...] = jnp.zeros(table.shape, F32)
    for i in range(self_sums.shape[0]):
        table[pl.ds(row * blocks_here + i * tile_count + tile_index, 1), :] = self_sums[i : i + 1, :]

    def add(block, line):
        place = pl.ds(block, 1)
        table[place, :] = table[place, :] + line

    all_tiles = jnp.exp(-kernel_gamma * (mine[...] + other[...] - 2.0))
    idx = idx.ready()
    live_count = live_count.ready()[0]
    for k in range(row_count):
        tiles = []
        for j in range(capacity):
            slot = k * capacity + j
            tile = all_tiles[slot * BLOCK : (slot + 1) * BLOCK]
            tile = jnp.where(idx[3, slot] < live_count, tile, 0.0)
            turned = tile.T
            near_tiles[slot] = pack(turned)
            add(row * blocks_here + idx[0, slot], jnp.sum(turned, axis=0, keepdims=True))
            add(idx[1, slot], jnp.sum(tile, axis=0, keepdims=True))
            if k == 0:
                home_tiles[j] = pack(tile)
            tiles.append(tile)
        if k > 0:
            lines = ([], [])
            for inner in range(per_core):
                at = slice(inner * BLOCK, (inner + 1) * BLOCK)
                steps, power, part = encode(jnp.where(core == 0, tiles[inner], tiles[per_core + inner]))
                sends[k - 1][at, :] = steps
                lines[0].append(power)
                lines[1].append(part)
            pick_columns(idx, k, row_count, capacity, codes, powers, parts, sends[k - 1], per_core * BLOCK, lines)


def encode_blocks(values, codes, powers, parts):
    for b in range(powers.shape[0]):
        at = slice(b * BLOCK, (b + 1) * BLOCK)
        steps, power, part = encode(values[:, at])
        codes[:, at] = steps
        powers[b : b + 1, :] = power
        parts[b : b + 1, :] = part


def start_body(values, codes, powers, parts):
    encode_blocks(values, codes, powers, parts)


def split_body(row_count, per_core, *refs):
    others = row_count - 1
    messages, outs = refs[:others], refs[-others:]
    for message, out in zip(messages, outs):
        scales = scale_rows(message[message.shape[0] - CODE_ROWS :, :])
        for inner in range(per_core):
            steps = message[inner * BLOCK : (inner + 1) * BLOCK, :]
            out[inner] = pack(decode(steps, scales[inner : inner + 1, :]))


def pick_columns(idx, k, row_count, capacity, codes, powers, parts, send, base, lines):
    count = codes.shape[0]
    back = row_count - k
    blocks = [idx[0, k * capacity + j] for j in range(capacity)]
    blocks += [idx[4, back * capacity + j] for j in range(capacity)]
    for place, block in enumerate(blocks):
        send[base + place * count : base + (place + 1) * count, :] = codes[:, at_block(block)]
        lines[0].append(powers[pl.ds(block, 1), :])
        lines[1].append(parts[pl.ds(block, 1), :])
    send[base + len(blocks) * count :, :] = as_rows(*lines, CODE_ROWS)


def add_product(out, block, packed, values):
    place = at_block(block)
    out[:, place] = out[:, place] + product(packed, values)


def apply_own(dims, me, idx, inverse, own, near_tiles, home_tiles, self_tiles, out):
    row_count, capacity, per_core, blocks_here, tile_count = dims
    row, tile_index = me[0], me[1]
    out[...] = jnp.zeros(out.shape, F32)

    def scaled(block):
        return own[:, at_block(block)] * inverse[pl.ds(row * blocks_here + block, 1), :]

    for i in range(blocks_here // tile_count):
        block = i * tile_count + tile_index
        add_product(out, block, self_tiles[i], scaled(block))
    idx = idx.ready()
    for j in range(capacity):
        add_product(out, idx[0, j], near_tiles[j], scaled(idx[4, j]))
        add_product(out, idx[4, j], home_tiles[j], scaled(idx[0, j]))
    return idx


def apply_far(dims, me, idx, inverse, received, base, near_tiles, sent, shared, out):
    row_count, capacity, per_core, blocks_here, tile_count = dims
    core = me[2]
    count = out.shape[0]
    lines = [scale_rows(message[message.shape[0] - CODE_ROWS :, :]) for message in received]
    first_line = base // BLOCK

    def arrived(k, place, block):
        steps = received[k - 1][pl.ds(pl.multiple_of(base + place * count, CODE_ROWS), count), :]
        rows = lines[k - 1][first_line : first_line + 2 * capacity, :]
        return decode(steps, row_at(rows, place) * inverse[pl.ds(block, 1), :])

    for k in range(1, row_count):
        for j in range(capacity):
            slot = k * capacity + j
            values = arrived(row_count - k, capacity + j, idx[1, slot])
            add_product(out, idx[0, slot], near_tiles[slot], values)
            inner = j % per_core
            if j < per_core:
                place = core * per_core + inner
                packed = sent[k - 1][inner]
            else:
                place = (1 - core) * per_core + inner
                packed = shared[k - 1][inner]
            slot = k * capacity + place
            add_product(out, idx[4, slot], packed, arrived(k, place, idx[5, slot]))


def first_own_body(dims, me, idx, mine, other, own, near_tiles, home_tiles, self_tiles, out, degree, inverse):
    total = mine[...] + other[...]
    degree[...] = total
    inverse[...] = 1.0 / jnp.sqrt(total)
    apply_own(dims, me, idx, inverse, own, near_tiles, home_tiles, self_tiles, out)


def first_far_body(dims, coded, me, idx, inverse, started, near_tiles, *refs):
    row_count, per_core = dims[0], dims[2]
    others = row_count - 1
    sent, shared, messages = refs[:others], refs[others : 2 * others], refs[2 * others : 3 * others]
    out, total = refs[3 * others :]
    total[...] = started[...]
    apply_far(dims, me, idx.ready(), inverse, messages, per_core * BLOCK, near_tiles, sent, shared, total)
    put_sum(coded, total, out)


def second_apply_body(dims, me, idx, inverse, after, own, home_tiles, self_tiles, near_tiles, *refs):
    others = dims[0] - 1
    sent, shared, received = refs[:others], refs[others : 2 * others], refs[2 * others : 3 * others]
    out = refs[-1]
    idx = apply_own(dims, me, idx, inverse, own, near_tiles, home_tiles, self_tiles, out)
    apply_far(dims, me, idx, inverse, received, 0, near_tiles, sent, shared, out)


def send_sum_body(coded, total, after, out):
    put_sum(coded, total, out)


def put_sum(coded, total, out):
    if not coded:
        out[...] = total[...]
        return
    lines = ([], [])
    blocks_here = total.shape[1] // BLOCK
    for b in range(blocks_here):
        at = slice(b * BLOCK, (b + 1) * BLOCK)
        steps, power, part = encode(total[:, at])
        out[:, at] = steps
        lines[0].append(power)
        lines[1].append(part)
    out[:, blocks_here * BLOCK :] = as_rows(*lines, out.shape[0])


def take_sum(coded, me, blocks_here, inverse, mine, other, out):
    if coded:
        tail = blocks_here * BLOCK
        my_scales, other_scales = scale_rows(mine[:, tail:]), scale_rows(other[:, tail:])
    for b in range(blocks_here):
        at = slice(b * BLOCK, (b + 1) * BLOCK)
        row = inverse[pl.ds(me[0] * blocks_here + b, 1), :]
        if coded:
            line = slice(b, b + 1)
            value = decode(mine[:, at], my_scales[line]) + decode(other[:, at], other_scales[line])
        else:
            value = mine[:, at] + other[:, at]
        out[:, at] = value * row


def mapped_body(dims, coded, me, idx, inverse, mine, other, out, *refs):
    row_count, capacity, per_core, blocks_here, tile_count = dims
    sends, (codes, powers, parts) = refs[:-3], refs[-3:]
    take_sum(coded, me, blocks_here, inverse, mine, other, out)
    encode_blocks(out, codes, powers, parts)
    idx = idx.ready()
    for k in range(1, row_count):
        pick_columns(idx, k, row_count, capacity, codes, powers, parts, sends[k - 1], 0, ([], []))


def last_mapped_body(blocks_here, coded, me, inverse, mine, other, after, out):
    take_sum(coded, me, blocks_here, inverse, mine, other, out)


def folded(square):
    half = square.shape[0] // 2
    return jnp.concatenate([square[:half], square[half:]], axis=1)


def unfolded(terms):
    total = functools.reduce(lambda total, term: total + term[...], terms[1:], terms[0][...])
    width = total.shape[1] // 2
    return jnp.concatenate([total[:, :width], total[:, width:]], axis=0)


def gram_body(me, own, other, out):
    full = both_columns(me[2], own[...], other[...])
    out[...] = folded(gram(pack(full), full.shape[0]))


def factor_body(after, *refs):
    refs[-1][...] = lower_inverse(unfolded(refs[:-1]))


def second_gram_body(me, factor, own, other, mapped, out):
    full = both_columns(me[2], own[...], other[...])
    parts = thirds(times(factor[...], pack(full)))
    mapped[...] = parts[: mapped.shape[0]]
    out[...] = folded(gram(parts, full.shape[0]))


def final_body(me, mapped, *refs):
    terms, (out, value, sent) = refs[:-3], refs[-3:]
    factor = lower_inverse(unfolded(terms))
    own_cols = value.shape[0]
    part = jnp.where(me[2] == 0, factor[:own_cols], factor[own_cols:])
    copies = []
    chunk = value.shape[1] // sent.shape[0]
    for i in range(sent.shape[0]):
        at = slice(i * chunk, (i + 1) * chunk)
        value[:, at] = times(part, mapped[:, at])
        copies.append(pltpu.make_async_copy(value.at[:, at], out.at[:, at], sent.at[i]))
        copies[-1].start()
    for copy in copies:
        copy.wait()


def shift_by(value, axes, size, shift):
    return lax.ppermute(value, axes, [(i, (i + shift) % size) for i in range(size)])


def row_terms(value, row_count):
    return [value] + [shift_by(value, "rows", row_count, k) for k in range(1, row_count)]


def pair_step(value, name, flip):
    return lax.ppermute(value, name, [(i, i ^ flip) for i in range(lax.axis_size(name))])


def pair_sum(value, axes):
    terms = None
    steps = [(name, 1 << bit) for name in axes for bit in range((lax.axis_size(name) - 1).bit_length())]
    for name, flip in steps:
        if terms is not None:
            value = terms[0] + terms[1]
        terms = (value, pair_step(value, name, flip))
    return terms


def local(embeddings, start, pair_list, pair_count):
    row_count = lax.axis_size("rows")
    tile_count = lax.axis_size("tiles")
    core_count = lax.axis_size("cols")
    row_index = lax.axis_index("rows")
    tile_index = lax.axis_index("tiles")
    col_index = lax.axis_index("cols")
    rows_here, half_features = embeddings.shape
    blocks_here = rows_here // BLOCK
    slots = pair_list.shape[2]
    capacity = slots // row_count
    per_core = capacity // core_count
    own_blocks = blocks_here // tile_count
    own_cols = start.shape[1]
    block_count = row_count * blocks_here
    others = range(1, row_count)

    list_order = [0, *sorted(others, key=lambda k: k * (row_count - k))]
    lists = [shift_by(pair_list[0], "rows", row_count, k) if k else pair_list[0] for k in list_order]
    self_part = call(
        functools.partial(self_distance_body, own_blocks, tile_count),
        sds((own_blocks * BLOCK, BLOCK), F32),
        [ME, embeddings],
    )
    planned = call(
        functools.partial(plan_body, (row_count, capacity, slots, blocks_here), list_order),
        [sds((6, slots + 1), jnp.int32)] + [sds((capacity * BLOCK, half_features), BF16) for _ in others],
        [ME, *lists, embeddings, self_part],
        late=range(1, 1 + row_count),
        any_in=(row_count + 2,),
        any_out=(0,),
        scratch=[pltpu.SMEM((6, slots + 1), jnp.int32), pltpu.SemaphoreType.DMA],
    )
    idx, sends = planned[0], planned[1:]
    order = sorted(others, key=lambda k: abs(k - row_count // 2))
    far = [shift_by(sends[k - 1], "rows", row_count, -k) for k in order]

    self_other = shift_by(self_part, "cols", core_count, 1)
    self_tiles, self_sums = call(
        functools.partial(self_tile_body, own_blocks),
        [sds((own_blocks, 2 * BLOCK, BLOCK), BF16), sds((own_blocks, BLOCK), F32)],
        [self_part, self_other],
    )
    values = start.T
    code_shapes = [((own_cols, rows_here), jnp.int16), ((blocks_here, BLOCK), F32), ((blocks_here, BLOCK), F32)]
    start_codes = call(start_body, [sds(*shape) for shape in code_shapes], [values])
    code_scratch = [pltpu.VMEM(*shape) for shape in code_shapes]
    coded = tile_count == 2
    own_squares = call(squares_body, sds((rows_here, BLOCK), F32), [embeddings, idx], any_in=(1,))
    pair_part = call(
        functools.partial(pair_distance_body, order, capacity),
        sds((slots * BLOCK, BLOCK), F32),
        [idx, embeddings, own_squares, *far],
        late=(0,),
    )
    pair_other = shift_by(pair_part, "cols", core_count, 1)

    dims = (row_count, capacity, per_core, blocks_here, tile_count)
    table = sds((block_count, BLOCK), F32)
    picked = 2 * capacity * own_cols
    tiles = call(
        functools.partial(pair_tile_body, dims),
        [sds((slots, 2 * BLOCK, BLOCK), BF16), sds((capacity, 2 * BLOCK, BLOCK), BF16), table]
        + [sds((per_core * BLOCK + picked + CODE_ROWS, BLOCK), jnp.int16) for _ in others],
        [ME, idx, pair_count, pair_part, pair_other, self_sums, *start_codes],
        late=(1, 2),
    )
    near_tiles, home_tiles, degrees, sends = tiles[0], tiles[1], tiles[2], tiles[3:]
    degrees = functools.reduce(jnp.add, row_terms(degrees, row_count))
    degree_terms = pair_sum(degrees, ("tiles",))
    messages = [shift_by(sends[k - 1], "rows", row_count, k) for k in others]
    sent = call(
        functools.partial(split_body, row_count, per_core),
        [sds((per_core, 2 * BLOCK, BLOCK), BF16) for _ in others],
        [*messages, degree_terms[1]],
        any_in=(row_count - 1,),
    )
    shared = [shift_by(tile, "cols", core_count, 1) for tile in sent]

    block_shape = sds((own_cols, rows_here), F32)
    sum_shape = sds((own_cols, rows_here + BLOCK), jnp.int16) if coded else block_shape
    square = sds((2 * own_cols, 2 * own_cols), F32)
    folded_square = sds((own_cols, 4 * own_cols), F32)

    started, degree, inverse = call(
        functools.partial(first_own_body, dims),
        [block_shape, table, table],
        [ME, idx, *degree_terms, values, near_tiles, home_tiles, self_tiles],
        late=(1,),
    )
    part = call(
        functools.partial(first_far_body, dims, coded),
        sum_shape,
        [ME, idx, inverse, started, near_tiles, *sent, *shared, *messages],
        late=(1,),
        scratch=[pltpu.VMEM((own_cols, rows_here), F32)],
    )
    mine, other = pair_sum(part, ("tiles",))
    first = call(
        functools.partial(mapped_body, dims, coded),
        [block_shape] + [sds((picked + CODE_ROWS, BLOCK), jnp.int16) for _ in others],
        [ME, idx, inverse, mine, other],
        late=(1,),
        scratch=code_scratch,
    )
    mapped, sends = first[0], first[1:]
    received = [shift_by(sends[k - 1], "rows", row_count, k) for k in others]

    mapped_other = shift_by(mapped, "cols", core_count, 1)
    first_gram = call(gram_body, folded_square, [ME, mapped, mapped_other])
    part = call(
        functools.partial(second_apply_body, dims),
        block_shape,
        [ME, idx, inverse, first_gram, mapped, home_tiles, self_tiles, near_tiles, *sent, *shared, *received],
        late=(1,),
        any_in=(3,),
    )
    steps = (row_count - 1).bit_length()
    for bit in range(steps - 1):
        first_gram = first_gram + pair_step(first_gram, "rows", 1 << bit)
    part = call(functools.partial(send_sum_body, coded), sum_shape, [part, first_gram])
    gram_terms = (first_gram, pair_step(first_gram, "rows", 1 << (steps - 1)))
    mine, other = pair_sum(part, ("tiles",))
    second = call(
        functools.partial(last_mapped_body, blocks_here, coded),
        block_shape,
        [ME, inverse, mine, other, gram_terms[1]],
        any_in=(4,),
    )
    second_other = shift_by(second, "cols", core_count, 1)
    factor = call(factor_body, square, [second, *gram_terms], any_in=(0,))
    full, second_gram = call(
        second_gram_body,
        [sds((4 * own_cols, rows_here), BF16), folded_square],
        [ME, factor, second, second_other],
    )
    vectors = call(
        final_body,
        block_shape,
        [ME, full, *row_terms(second_gram, row_count)],
        any_out=(0,),
        scratch=[pltpu.VMEM((own_cols, rows_here), F32), pltpu.SemaphoreType.DMA((4,))],
    )
    own_degree = lax.dynamic_slice_in_dim(degree, row_index * blocks_here, blocks_here, 0)
    return (vectors.T, own_degree.reshape(rows_here))


def solution(mesh):
    in_specs = (
        P(("groups", "rows"), "cols"),
        P(("groups", "rows"), "cols"),
        P(("groups", "rows", "tiles"), None, None),
        P(("groups", "rows", "tiles")),
    )
    out_specs = (P(("groups", "rows"), "cols"), P(("groups", "rows")))
    return jax.shard_map(local, mesh=mesh, in_specs=in_specs, out_specs=out_specs, check_vma=False)
```

```python
import functools

import jax
import jax.numpy as jnp
from jax import lax
from jax.experimental import pallas as pl
from jax.experimental.pallas import tpu as pltpu
from jax.sharding import PartitionSpec as P

BLOCK = 128
kernel_gamma = 14.0
CODE_TOP = 32767.0
PART_TOP = 16384.0
CODE_ROWS = 16

VMEM = pl.BlockSpec(memory_space=pltpu.VMEM)
ANY = pl.BlockSpec(memory_space=pl.ANY)
F32 = jnp.float32
BF16 = jnp.bfloat16
HIGHEST = lax.Precision.HIGHEST
NT = (((1,), (1,)), ((), ()))


ME = None


def with_position(body):
    def inner(*refs):
        return body([lax.axis_index(name) for name in ("rows", "tiles", "cols")], *refs)

    return inner


class Late:
    def __init__(self, source, table, arrived):
        self.table = table
        self.copy = pltpu.make_async_copy(source, table, arrived)
        self.copy.start()

    def ready(self):
        self.copy.wait()
        return self.table


def with_late(body, places, count):
    def inner(*refs):
        refs, tables, arrived = refs[:-1 - count], refs[-1 - count : -1], refs[-1]
        refs = list(refs)
        for i, place in enumerate(places):
            refs[place] = Late(refs[place], tables[i], arrived.at[i])
        body(*refs)

    return inner


def call(body, outs, args, late=(), any_in=(), scratch=(), any_out=()):
    if args[0] is ME:
        body, args = with_position(body), args[1:]
        late, any_in = [[i - 1 for i in places] for places in (late, any_in)]
    if late:
        scratch = [
            *scratch,
            *[pltpu.SMEM(args[i].shape, args[i].dtype) for i in late],
            pltpu.SemaphoreType.DMA((len(late),)),
        ]
        any_in = [*any_in, *late]
        body = with_late(body, late, len(late))
    single = not isinstance(outs, (list, tuple))
    shapes = [outs] if single else list(outs)
    result = pl.pallas_call(
        body,
        out_shape=shapes,
        in_specs=[ANY if i in any_in else VMEM for i in range(len(args))],
        out_specs=[ANY if i in any_out else VMEM for i in range(len(shapes))],
        scratch_shapes=list(scratch),
        compiler_params=pltpu.CompilerParams(vmem_limit_bytes=48 * 2**20),
    )(*args)
    return result[0] if single else result


def sds(shape, dtype):
    return jax.ShapeDtypeStruct(shape, dtype)


def at_block(index):
    return pl.ds(pl.multiple_of(index * BLOCK, BLOCK), BLOCK)


def eye_mask(size):
    return lax.broadcasted_iota(jnp.int32, (size, size), 0) == lax.broadcasted_iota(
        jnp.int32, (size, size), 1
    )


def halves(value):
    high = value.astype(BF16)
    low = (value - high.astype(F32)).astype(BF16)
    return high, low


def pack(tile):
    return jnp.concatenate(halves(tile), axis=0)


def scale_of(power, part):
    return jnp.exp2(power) * (part * (1.0 / PART_TOP))


def encode(values):
    most = jnp.maximum(jnp.max(jnp.abs(values), axis=0, keepdims=True), 1e-30)
    power = jnp.floor(jnp.log2(most)) + 1.0
    part = jnp.floor(most * jnp.exp2(-power) * PART_TOP) + 1.0
    steps = jnp.floor(values * (CODE_TOP / scale_of(power, part)) + 0.5)
    steps = jnp.minimum(jnp.maximum(steps, -CODE_TOP), CODE_TOP)
    return steps.astype(jnp.int32).astype(jnp.int16), power, part


def decode(steps, scale):
    return steps.astype(jnp.int32).astype(F32) * (scale * (1.0 / CODE_TOP))


def as_rows(powers, parts, count):
    fill = jnp.zeros((count // 2 - len(powers), BLOCK), F32)
    fill = [fill] if fill.shape[0] else []
    rows = jnp.concatenate([*powers, *fill, *parts, *fill], axis=0)
    return rows.astype(jnp.int32).astype(jnp.int16)


def scale_rows(rows):
    rows = rows.astype(jnp.int32).astype(F32)
    half = rows.shape[0] // 2
    return scale_of(rows[:half], rows[half:])


def row_at(rows, place):
    if isinstance(place, int):
        return rows[place : place + 1, :]
    line = rows[:1, :]
    for i in range(1, rows.shape[0]):
        line = jnp.where(place == i, rows[i : i + 1, :], line)
    return line


def product(packed, values):
    left = jnp.concatenate(halves(values), axis=0)
    both = jnp.dot(jnp.concatenate([left, left], axis=1), packed, preferred_element_type=F32)
    count = values.shape[0]
    return both[:count] + both[count:]


def thirds(value):
    high = value.astype(BF16)
    rest = value - high.astype(F32)
    middle = rest.astype(BF16)
    low = (rest - middle.astype(F32)).astype(BF16)
    return jnp.concatenate([high, middle, low], axis=0)


def gram(parts, n):
    cross = lax.dot_general(parts, parts, NT, preferred_element_type=F32)
    count = parts.shape[0] // n
    pairs = sorted(((i, j) for i in range(count) for j in range(count)), key=lambda p: -p[0] - p[1])
    total = None
    for i, j in pairs:
        piece = cross[i * n : (i + 1) * n, j * n : (j + 1) * n]
        total = piece if total is None else total + piece
    return total


def times(left, parts):
    m = left.shape[0]
    left = jnp.concatenate(halves(left), axis=0)
    both = jnp.dot(jnp.concatenate([left, left], axis=1), parts, preferred_element_type=F32)
    return both[m:] + both[:m]


def lower_inverse(matrix, step=8):
    n = matrix.shape[0]
    state = jnp.concatenate([matrix, eye_mask(n).astype(F32)], axis=1)
    done = []
    for j in range(0, n, step):
        top = j // 8 * 8
        if top > n - state.shape[0]:
            done.append(state[:8])
            state = state[8:]
        base = j - top
        rows = lax.broadcasted_iota(jnp.int32, state.shape, 0)
        columns = [jnp.broadcast_to(state[:, j + i : j + i + 1], state.shape) for i in range(step)]
        lines = [state[base + i : base + i + 1, :] for i in range(step)]
        pivot = [[columns[k][base + i : base + i + 1, :] for k in range(step)] for i in range(step)]
        for i in range(step):
            if i % 2 == 0:
                first, cross, second = pivot[i][i], pivot[i][i + 1], pivot[i + 1][i + 1]
                reciprocals = (1.0 / first, first / (first * second - cross * cross))
            reciprocal = reciprocals[i % 2]
            scaled = lines[i] * reciprocal
            ratio = [pivot[i][k] * reciprocal for k in range(step)]
            for k in range(i + 1, step):
                lines[k] = lines[k] - pivot[k][i] * scaled
                columns[k] = columns[k] - columns[i] * ratio[k]
                for m in range(i + 1, step):
                    pivot[k][m] = pivot[k][m] - pivot[k][i] * ratio[m]
            state = state - jnp.where(rows > base + i, columns[i], 0.0) * scaled
    state = jnp.concatenate([*done, state], axis=0)
    pivots = jnp.sum(jnp.where(eye_mask(n), state[:, :n], 0.0), axis=1, keepdims=True)
    return state[:, n:] / jnp.sqrt(pivots)


def both_columns(core, own, other):
    first = core == 0
    return jnp.concatenate(
        [jnp.where(first, own, other), jnp.where(first, other, own)], axis=0
    )


def quotient(value, size):
    if size & (size - 1) == 0:
        return lax.shift_right_logical(value, jnp.int32(size.bit_length() - 1))
    return lax.div(value, jnp.int32(size))


def remainder(value, size):
    if size & (size - 1) == 0:
        return lax.bitwise_and(value, jnp.int32(size - 1))
    return lax.rem(value, jnp.int32(size))


def plan_body(dims, list_order, me, *refs):
    row_count, capacity, slots, blocks_here = dims
    lists, (emb, after, idx_out) = refs[:row_count], refs[row_count : row_count + 3]
    sends, (idx, left) = refs[row_count + 3 : -2], refs[-2:]
    row = me[0]
    for i in range(slots):
        for line in (0, 1, 4, 5):
            idx[line, i] = 0
        idx[3, i] = slots
    lists = dict(zip(list_order, [one.ready() for one in lists]))

    def each(step, start):
        if slots <= 8:
            for s in range(slots):
                start = step(s, start)
        else:
            lax.fori_loop(0, slots, step, start)

    for k in range(row_count):

        def step(s, counts, k=k):
            near = lists[k][0, s]
            far = lists[k][1, s]
            owner = quotient(far, blocks_here)
            if k > 0:
                hit = (owner == row) & (counts[0] < capacity)
                slot = jnp.where(hit, k * capacity + counts[0], slots)
                idx[4, slot] = far - row * blocks_here
                idx[5, slot] = near
                return (counts[0] + hit.astype(jnp.int32),)
            shift = remainder(owner - row + row_count, row_count)
            rank = counts[0]
            for d in range(1, row_count):
                rank = jnp.where(shift == d, counts[d], rank)
            slot = jnp.where(rank < capacity, shift * capacity + rank, slots)
            idx[0, slot] = near - row * blocks_here
            idx[1, slot] = far
            idx[3, slot] = s
            slot = jnp.where(shift == 0, slot, slots)
            idx[4, slot] = far - row * blocks_here
            idx[5, slot] = near
            return tuple(counts[d] + (shift == d).astype(jnp.int32) for d in range(row_count))

        each(step, (jnp.int32(0),) * (row_count if k == 0 else 1))
    leave = pltpu.make_async_copy(idx, idx_out, left)
    leave.start()
    for k in range(1, row_count):
        for j in range(capacity):
            sends[k - 1][j * BLOCK : (j + 1) * BLOCK, :] = emb[at_block(idx[4, k * capacity + j]), :]
    leave.wait()


def squares(block):
    return jnp.sum(jnp.square(block.astype(F32)), axis=1, keepdims=True)


def as_row(column):
    return jnp.sum(jnp.where(eye_mask(BLOCK), column, 0.0), axis=0, keepdims=True)


def partial_distance(left, right, left_sq, right_row):
    inner = lax.dot_general(left, right, NT, preferred_element_type=F32)
    return left_sq + right_row - 2.0 * inner


def self_distance_body(own_blocks, tile_count, me, emb, out):
    for i in range(own_blocks):
        block = emb[at_block(i * tile_count + me[1]), :]
        block_sq = squares(block)
        out[i * BLOCK : (i + 1) * BLOCK, :] = partial_distance(
            block, block, block_sq, as_row(block_sq)
        )


def squares_body(capacity, idx, emb, out, home):
    for b in range(out.shape[0] // BLOCK):
        part = slice(b * BLOCK, (b + 1) * BLOCK)
        out[part, :] = jnp.broadcast_to(squares(emb[part, :]), (BLOCK, BLOCK))
    idx = idx.ready()
    for j in range(capacity):
        left, right = at_block(idx[0, j]), at_block(idx[4, j])
        home[j * BLOCK : (j + 1) * BLOCK, :] = partial_distance(
            emb[left, :], emb[right, :], out[left, :], as_row(out[right, :])
        )


def pair_distance_body(order, capacity, idx, emb, own_squares, home, *refs):
    far, out = dict(zip(order, refs)), refs[-1]
    rows = {}
    for k in order:
        for j in range(capacity):
            rows[k, j] = as_row(squares(far[k][j * BLOCK : (j + 1) * BLOCK, :]))
    idx = idx.ready()
    out[: capacity * BLOCK, :] = home[...]
    for k in range(1, len(order) + 1):
        for j in range(capacity):
            slot = k * capacity + j
            left = emb[at_block(idx[0, slot]), :]
            left_sq = own_squares[at_block(idx[0, slot]), :]
            right = far[k][j * BLOCK : (j + 1) * BLOCK, :]
            part = slice(slot * BLOCK, (slot + 1) * BLOCK)
            out[part, :] = partial_distance(left, right, left_sq, rows[k, j])


def self_tile_body(own_blocks, mine, other, packed, sums):
    for i in range(own_blocks):
        part = slice(i * BLOCK, (i + 1) * BLOCK)
        tile = jnp.exp(-kernel_gamma * (mine[part, :] + other[part, :] - 2.0))
        tile = jnp.where(eye_mask(BLOCK), 0.0, tile)
        packed[i] = pack(tile)
        sums[i : i + 1, :] = jnp.sum(tile, axis=0, keepdims=True)


def pair_tile_body(dims, me, idx, live_count, mine, other, self_sums, codes, powers, parts, near_tiles, home_tiles, table, *sends):
    row_count, capacity, per_core, blocks_here, tile_count = dims
    row, tile_index, core = me[0], me[1], me[2]
    table[...] = jnp.zeros(table.shape, F32)
    for i in range(self_sums.shape[0]):
        table[pl.ds(row * blocks_here + i * tile_count + tile_index, 1), :] = self_sums[i : i + 1, :]

    def add(block, line):
        place = pl.ds(block, 1)
        table[place, :] = table[place, :] + line

    all_tiles = jnp.exp(-kernel_gamma * (mine[...] + other[...] - 2.0))
    idx = idx.ready()
    live_count = live_count.ready()[0]
    for k in range(row_count):
        tiles = []
        for j in range(capacity):
            slot = k * capacity + j
            tile = all_tiles[slot * BLOCK : (slot + 1) * BLOCK]
            tile = jnp.where(idx[3, slot] < live_count, tile, 0.0)
            turned = tile.T
            near_tiles[slot] = pack(turned)
            add(row * blocks_here + idx[0, slot], jnp.sum(turned, axis=0, keepdims=True))
            add(idx[1, slot], jnp.sum(tile, axis=0, keepdims=True))
            if k == 0:
                home_tiles[j] = pack(tile)
            tiles.append(tile)
        if k > 0:
            lines = ([], [])
            for inner in range(per_core):
                at = slice(inner * BLOCK, (inner + 1) * BLOCK)
                steps, power, part = encode(jnp.where(core == 0, tiles[inner], tiles[per_core + inner]))
                sends[k - 1][at, :] = steps
                lines[0].append(power)
                lines[1].append(part)
            pick_columns(idx, k, row_count, capacity, codes, powers, parts, sends[k - 1], per_core * BLOCK, lines)


def encode_blocks(values, codes, powers, parts):
    for b in range(powers.shape[0]):
        at = slice(b * BLOCK, (b + 1) * BLOCK)
        steps, power, part = encode(values[:, at])
        codes[:, at] = steps
        powers[b : b + 1, :] = power
        parts[b : b + 1, :] = part


def start_body(values, codes, powers, parts):
    encode_blocks(values, codes, powers, parts)


def split_body(row_count, per_core, *refs):
    others = row_count - 1
    messages, outs = refs[:others], refs[-others:]
    for message, out in zip(messages, outs):
        scales = scale_rows(message[message.shape[0] - CODE_ROWS :, :])
        for inner in range(per_core):
            steps = message[inner * BLOCK : (inner + 1) * BLOCK, :]
            out[inner] = pack(decode(steps, scales[inner : inner + 1, :]))


def pick_columns(idx, k, row_count, capacity, codes, powers, parts, send, base, lines):
    count = codes.shape[0]
    back = row_count - k
    blocks = [idx[0, k * capacity + j] for j in range(capacity)]
    blocks += [idx[4, back * capacity + j] for j in range(capacity)]
    for place, block in enumerate(blocks):
        send[base + place * count : base + (place + 1) * count, :] = codes[:, at_block(block)]
        lines[0].append(powers[pl.ds(block, 1), :])
        lines[1].append(parts[pl.ds(block, 1), :])
    send[base + len(blocks) * count :, :] = as_rows(*lines, CODE_ROWS)


def add_product(out, block, packed, values):
    place = at_block(block)
    out[:, place] = out[:, place] + product(packed, values)


def apply_own(dims, me, idx, inverse, own, near_tiles, home_tiles, self_tiles, out):
    row_count, capacity, per_core, blocks_here, tile_count = dims
    row, tile_index = me[0], me[1]
    out[...] = jnp.zeros(out.shape, F32)

    def scaled(block):
        return own[:, at_block(block)] * inverse[pl.ds(row * blocks_here + block, 1), :]

    for i in range(blocks_here // tile_count):
        block = i * tile_count + tile_index
        add_product(out, block, self_tiles[i], scaled(block))
    idx = idx.ready()
    for j in range(capacity):
        add_product(out, idx[0, j], near_tiles[j], scaled(idx[4, j]))
        add_product(out, idx[4, j], home_tiles[j], scaled(idx[0, j]))
    return idx


def apply_far(dims, me, idx, inverse, received, base, near_tiles, sent, shared, out):
    row_count, capacity, per_core, blocks_here, tile_count = dims
    core = me[2]
    count = out.shape[0]
    lines = [scale_rows(message[message.shape[0] - CODE_ROWS :, :]) for message in received]
    first_line = base // BLOCK

    def arrived(k, place, block):
        steps = received[k - 1][pl.ds(pl.multiple_of(base + place * count, CODE_ROWS), count), :]
        rows = lines[k - 1][first_line : first_line + 2 * capacity, :]
        return decode(steps, row_at(rows, place) * inverse[pl.ds(block, 1), :])

    for k in range(1, row_count):
        for j in range(capacity):
            slot = k * capacity + j
            values = arrived(row_count - k, capacity + j, idx[1, slot])
            add_product(out, idx[0, slot], near_tiles[slot], values)
            inner = j % per_core
            if j < per_core:
                place = core * per_core + inner
                packed = sent[k - 1][inner]
            else:
                place = (1 - core) * per_core + inner
                packed = shared[k - 1][inner]
            slot = k * capacity + place
            add_product(out, idx[4, slot], packed, arrived(k, place, idx[5, slot]))


def first_own_body(dims, me, idx, mine, other, own, near_tiles, home_tiles, self_tiles, out, degree, inverse):
    total = mine[...] + other[...]
    degree[...] = total
    inverse[...] = 1.0 / jnp.sqrt(total)
    apply_own(dims, me, idx, inverse, own, near_tiles, home_tiles, self_tiles, out)


def first_far_body(dims, coded, me, idx, inverse, started, near_tiles, *refs):
    row_count, per_core = dims[0], dims[2]
    others = row_count - 1
    sent, shared, messages = refs[:others], refs[others : 2 * others], refs[2 * others : 3 * others]
    out, total = refs[3 * others :]
    total[...] = started[...]
    apply_far(dims, me, idx.ready(), inverse, messages, per_core * BLOCK, near_tiles, sent, shared, total)
    put_sum(coded, total, out)


def second_apply_body(dims, me, idx, inverse, after, own, home_tiles, self_tiles, near_tiles, *refs):
    others = dims[0] - 1
    sent, shared, received = refs[:others], refs[others : 2 * others], refs[2 * others : 3 * others]
    out = refs[-1]
    idx = apply_own(dims, me, idx, inverse, own, near_tiles, home_tiles, self_tiles, out)
    apply_far(dims, me, idx, inverse, received, 0, near_tiles, sent, shared, out)


def send_sum_body(coded, total, after, out):
    put_sum(coded, total, out)


def put_sum(coded, total, out):
    if not coded:
        out[...] = total[...]
        return
    lines = ([], [])
    blocks_here = total.shape[1] // BLOCK
    for b in range(blocks_here):
        at = slice(b * BLOCK, (b + 1) * BLOCK)
        steps, power, part = encode(total[:, at])
        out[:, at] = steps
        lines[0].append(power)
        lines[1].append(part)
    out[:, blocks_here * BLOCK :] = as_rows(*lines, out.shape[0])


def take_sum(coded, me, blocks_here, inverse, mine, other, out):
    if coded:
        tail = blocks_here * BLOCK
        my_scales, other_scales = scale_rows(mine[:, tail:]), scale_rows(other[:, tail:])
    for b in range(blocks_here):
        at = slice(b * BLOCK, (b + 1) * BLOCK)
        row = inverse[pl.ds(me[0] * blocks_here + b, 1), :]
        if coded:
            line = slice(b, b + 1)
            value = decode(mine[:, at], my_scales[line]) + decode(other[:, at], other_scales[line])
        else:
            value = mine[:, at] + other[:, at]
        out[:, at] = value * row


def mapped_body(dims, coded, me, idx, inverse, mine, other, out, *refs):
    row_count, capacity, per_core, blocks_here, tile_count = dims
    sends, (codes, powers, parts) = refs[:-3], refs[-3:]
    take_sum(coded, me, blocks_here, inverse, mine, other, out)
    encode_blocks(out, codes, powers, parts)
    idx = idx.ready()
    for k in range(1, row_count):
        pick_columns(idx, k, row_count, capacity, codes, powers, parts, sends[k - 1], 0, ([], []))


def last_mapped_body(blocks_here, coded, me, inverse, mine, other, after, out):
    take_sum(coded, me, blocks_here, inverse, mine, other, out)


def folded(square):
    half = square.shape[0] // 2
    return jnp.concatenate([square[:half], square[half:]], axis=1)


def unfolded(terms):
    total = functools.reduce(lambda total, term: total + term[...], terms[1:], terms[0][...])
    width = total.shape[1] // 2
    return jnp.concatenate([total[:, :width], total[:, width:]], axis=0)


def gram_body(me, own, other, out):
    full = both_columns(me[2], own[...], other[...])
    out[...] = folded(gram(pack(full), full.shape[0]))


def factor_body(after, *refs):
    refs[-1][...] = lower_inverse(unfolded(refs[:-1]))


def second_gram_body(me, factor, own, other, mapped, out):
    full = both_columns(me[2], own[...], other[...])
    parts = thirds(times(factor[...], pack(full)))
    mapped[...] = parts[: mapped.shape[0]]
    out[...] = folded(gram(parts, full.shape[0]))


def final_body(me, mapped, *refs):
    terms, (out, value, sent) = refs[:-3], refs[-3:]
    factor = lower_inverse(unfolded(terms))
    own_cols = value.shape[0]
    part = jnp.where(me[2] == 0, factor[:own_cols], factor[own_cols:])
    copies = []
    chunk = value.shape[1] // sent.shape[0]
    for i in range(sent.shape[0]):
        at = slice(i * chunk, (i + 1) * chunk)
        value[:, at] = times(part, mapped[:, at])
        copies.append(pltpu.make_async_copy(value.at[:, at], out.at[:, at], sent.at[i]))
        copies[-1].start()
    for copy in copies:
        copy.wait()


def shift_by(value, axes, size, shift):
    return lax.ppermute(value, axes, [(i, (i + shift) % size) for i in range(size)])


def row_terms(value, row_count):
    return [value] + [shift_by(value, "rows", row_count, k) for k in range(1, row_count)]


def pair_step(value, name, flip):
    return lax.ppermute(value, name, [(i, i ^ flip) for i in range(lax.axis_size(name))])


def pair_sum(value, axes):
    terms = None
    steps = [(name, 1 << bit) for name in axes for bit in range((lax.axis_size(name) - 1).bit_length())]
    for name, flip in steps:
        if terms is not None:
            value = terms[0] + terms[1]
        terms = (value, pair_step(value, name, flip))
    return terms


def local(embeddings, start, pair_list, pair_count):
    row_count = lax.axis_size("rows")
    tile_count = lax.axis_size("tiles")
    core_count = lax.axis_size("cols")
    row_index = lax.axis_index("rows")
    tile_index = lax.axis_index("tiles")
    col_index = lax.axis_index("cols")
    rows_here, half_features = embeddings.shape
    blocks_here = rows_here // BLOCK
    slots = pair_list.shape[2]
    capacity = slots // row_count
    per_core = capacity // core_count
    own_blocks = blocks_here // tile_count
    own_cols = start.shape[1]
    block_count = row_count * blocks_here
    others = range(1, row_count)

    list_order = [0, *sorted(others, key=lambda k: abs(k - row_count // 2))]
    lists = [shift_by(pair_list[0], "rows", row_count, k) if k else pair_list[0] for k in list_order]
    self_part = call(
        functools.partial(self_distance_body, own_blocks, tile_count),
        sds((own_blocks * BLOCK, BLOCK), F32),
        [ME, embeddings],
    )
    planned = call(
        functools.partial(plan_body, (row_count, capacity, slots, blocks_here), list_order),
        [sds((6, slots + 1), jnp.int32)] + [sds((capacity * BLOCK, half_features), BF16) for _ in others],
        [ME, *lists, embeddings, self_part],
        late=range(1, 1 + row_count),
        any_in=(row_count + 2,),
        any_out=(0,),
        scratch=[pltpu.SMEM((6, slots + 1), jnp.int32), pltpu.SemaphoreType.DMA],
    )
    idx, sends = planned[0], planned[1:]
    order = sorted(others, key=lambda k: abs(k - row_count // 2))
    far = [shift_by(sends[k - 1], "rows", row_count, -k) for k in order]

    self_other = shift_by(self_part, "cols", core_count, 1)
    self_tiles, self_sums = call(
        functools.partial(self_tile_body, own_blocks),
        [sds((own_blocks, 2 * BLOCK, BLOCK), BF16), sds((own_blocks, BLOCK), F32)],
        [self_part, self_other],
    )
    values = start.T
    code_shapes = [((own_cols, rows_here), jnp.int16), ((blocks_here, BLOCK), F32), ((blocks_here, BLOCK), F32)]
    start_codes = call(start_body, [sds(*shape) for shape in code_shapes], [values])
    code_scratch = [pltpu.VMEM(*shape) for shape in code_shapes]
    coded = tile_count == 2
    own_squares, home = call(
        functools.partial(squares_body, capacity),
        [sds((rows_here, BLOCK), F32), sds((capacity * BLOCK, BLOCK), F32)],
        [idx, embeddings],
        late=(0,),
    )
    pair_part = call(
        functools.partial(pair_distance_body, order, capacity),
        sds((slots * BLOCK, BLOCK), F32),
        [idx, embeddings, own_squares, home, *far],
        late=(0,),
    )
    pair_other = shift_by(pair_part, "cols", core_count, 1)

    dims = (row_count, capacity, per_core, blocks_here, tile_count)
    table = sds((block_count, BLOCK), F32)
    picked = 2 * capacity * own_cols
    tiles = call(
        functools.partial(pair_tile_body, dims),
        [sds((slots, 2 * BLOCK, BLOCK), BF16), sds((capacity, 2 * BLOCK, BLOCK), BF16), table]
        + [sds((per_core * BLOCK + picked + CODE_ROWS, BLOCK), jnp.int16) for _ in others],
        [ME, idx, pair_count, pair_part, pair_other, self_sums, *start_codes],
        late=(1, 2),
    )
    near_tiles, home_tiles, degrees, sends = tiles[0], tiles[1], tiles[2], tiles[3:]
    degrees = functools.reduce(jnp.add, row_terms(degrees, row_count))
    degree_terms = pair_sum(degrees, ("tiles",))
    messages = [shift_by(sends[k - 1], "rows", row_count, k) for k in others]
    sent = call(
        functools.partial(split_body, row_count, per_core),
        [sds((per_core, 2 * BLOCK, BLOCK), BF16) for _ in others],
        [*messages, degree_terms[1]],
        any_in=(row_count - 1,),
    )
    shared = [shift_by(tile, "cols", core_count, 1) for tile in sent]

    block_shape = sds((own_cols, rows_here), F32)
    sum_shape = sds((own_cols, rows_here + BLOCK), jnp.int16) if coded else block_shape
    square = sds((2 * own_cols, 2 * own_cols), F32)
    folded_square = sds((own_cols, 4 * own_cols), F32)

    started, degree, inverse = call(
        functools.partial(first_own_body, dims),
        [block_shape, table, table],
        [ME, idx, *degree_terms, values, near_tiles, home_tiles, self_tiles],
        late=(1,),
    )
    part = call(
        functools.partial(first_far_body, dims, coded),
        sum_shape,
        [ME, idx, inverse, started, near_tiles, *sent, *shared, *messages],
        late=(1,),
        scratch=[pltpu.VMEM((own_cols, rows_here), F32)],
    )
    mine, other = pair_sum(part, ("tiles",))
    first = call(
        functools.partial(mapped_body, dims, coded),
        [block_shape] + [sds((picked + CODE_ROWS, BLOCK), jnp.int16) for _ in others],
        [ME, idx, inverse, mine, other],
        late=(1,),
        scratch=code_scratch,
    )
    mapped, sends = first[0], first[1:]
    received = [shift_by(sends[k - 1], "rows", row_count, k) for k in others]

    mapped_other = shift_by(mapped, "cols", core_count, 1)
    first_gram = call(gram_body, folded_square, [ME, mapped, mapped_other])
    part = call(
        functools.partial(second_apply_body, dims),
        block_shape,
        [ME, idx, inverse, first_gram, mapped, home_tiles, self_tiles, near_tiles, *sent, *shared, *received],
        late=(1,),
        any_in=(3,),
    )
    steps = (row_count - 1).bit_length()
    for bit in range(steps - 1):
        first_gram = first_gram + pair_step(first_gram, "rows", 1 << bit)
    part = call(functools.partial(send_sum_body, coded), sum_shape, [part, first_gram])
    gram_terms = (first_gram, pair_step(first_gram, "rows", 1 << (steps - 1)))
    mine, other = pair_sum(part, ("tiles",))
    second = call(
        functools.partial(last_mapped_body, blocks_here, coded),
        block_shape,
        [ME, inverse, mine, other, gram_terms[1]],
        any_in=(4,),
    )
    second_other = shift_by(second, "cols", core_count, 1)
    factor = call(factor_body, square, [second, *gram_terms], any_in=(0,))
    full, second_gram = call(
        second_gram_body,
        [sds((4 * own_cols, rows_here), BF16), folded_square],
        [ME, factor, second, second_other],
    )
    vectors = call(
        final_body,
        block_shape,
        [ME, full, *row_terms(second_gram, row_count)],
        any_out=(0,),
        scratch=[pltpu.VMEM((own_cols, rows_here), F32), pltpu.SemaphoreType.DMA((4,))],
    )
    own_degree = lax.dynamic_slice_in_dim(degree, row_index * blocks_here, blocks_here, 0)
    return (vectors.T, own_degree.reshape(rows_here))


def solution(mesh):
    in_specs = (
        P(("groups", "rows"), "cols"),
        P(("groups", "rows"), "cols"),
        P(("groups", "rows", "tiles"), None, None),
        P(("groups", "rows", "tiles")),
    )
    out_specs = (P(("groups", "rows"), "cols"), P(("groups", "rows")))
    return jax.shard_map(local, mesh=mesh, in_specs=in_specs, out_specs=out_specs, check_vma=False)
```

```python
import functools

import jax
import jax.numpy as jnp
from jax import lax
from jax.experimental import pallas as pl
from jax.experimental.pallas import tpu as pltpu
from jax.sharding import PartitionSpec as P

BLOCK = 128
kernel_gamma = 14.0
CODE_TOP = 32767.0
PART_TOP = 16384.0
CODE_ROWS = 16

VMEM = pl.BlockSpec(memory_space=pltpu.VMEM)
ANY = pl.BlockSpec(memory_space=pl.ANY)
F32 = jnp.float32
BF16 = jnp.bfloat16
HIGHEST = lax.Precision.HIGHEST
NT = (((1,), (1,)), ((), ()))


ME = None


def with_position(body):
    def inner(*refs):
        return body([lax.axis_index(name) for name in ("rows", "tiles", "cols")], *refs)

    return inner


class Late:
    def __init__(self, source, table, arrived):
        self.table = table
        self.copy = pltpu.make_async_copy(source, table, arrived)
        self.copy.start()

    def ready(self):
        self.copy.wait()
        return self.table


def with_late(body, places, count):
    def inner(*refs):
        refs, tables, arrived = refs[:-1 - count], refs[-1 - count : -1], refs[-1]
        refs = list(refs)
        for i, place in enumerate(places):
            refs[place] = Late(refs[place], tables[i], arrived.at[i])
        body(*refs)

    return inner


def call(body, outs, args, late=(), any_in=(), scratch=(), any_out=()):
    if args[0] is ME:
        body, args = with_position(body), args[1:]
        late, any_in = [[i - 1 for i in places] for places in (late, any_in)]
    if late:
        scratch = [
            *scratch,
            *[pltpu.SMEM(args[i].shape, args[i].dtype) for i in late],
            pltpu.SemaphoreType.DMA((len(late),)),
        ]
        any_in = [*any_in, *late]
        body = with_late(body, late, len(late))
    single = not isinstance(outs, (list, tuple))
    shapes = [outs] if single else list(outs)
    result = pl.pallas_call(
        body,
        out_shape=shapes,
        in_specs=[ANY if i in any_in else VMEM for i in range(len(args))],
        out_specs=[ANY if i in any_out else VMEM for i in range(len(shapes))],
        scratch_shapes=list(scratch),
        compiler_params=pltpu.CompilerParams(vmem_limit_bytes=48 * 2**20),
    )(*args)
    return result[0] if single else result


def sds(shape, dtype):
    return jax.ShapeDtypeStruct(shape, dtype)


def at_block(index):
    return pl.ds(pl.multiple_of(index * BLOCK, BLOCK), BLOCK)


def eye_mask(size):
    return lax.broadcasted_iota(jnp.int32, (size, size), 0) == lax.broadcasted_iota(
        jnp.int32, (size, size), 1
    )


def halves(value):
    high = value.astype(BF16)
    low = (value - high.astype(F32)).astype(BF16)
    return high, low


def pack(tile):
    return jnp.concatenate(halves(tile), axis=0)


def scale_of(power, part):
    return jnp.exp2(power) * (part * (1.0 / PART_TOP))


def encode(values):
    most = jnp.maximum(jnp.max(jnp.abs(values), axis=0, keepdims=True), 1e-30)
    power = jnp.floor(jnp.log2(most)) + 1.0
    part = jnp.floor(most * jnp.exp2(-power) * PART_TOP) + 1.0
    steps = jnp.floor(values * (CODE_TOP / scale_of(power, part)) + 0.5)
    steps = jnp.minimum(jnp.maximum(steps, -CODE_TOP), CODE_TOP)
    return steps.astype(jnp.int32).astype(jnp.int16), power, part


def decode(steps, scale):
    return steps.astype(jnp.int32).astype(F32) * (scale * (1.0 / CODE_TOP))


def as_rows(powers, parts, count):
    fill = jnp.zeros((count // 2 - len(powers), BLOCK), F32)
    fill = [fill] if fill.shape[0] else []
    rows = jnp.concatenate([*powers, *fill, *parts, *fill], axis=0)
    return rows.astype(jnp.int32).astype(jnp.int16)


def scale_rows(rows):
    rows = rows.astype(jnp.int32).astype(F32)
    half = rows.shape[0] // 2
    return scale_of(rows[:half], rows[half:])


def row_at(rows, place):
    if isinstance(place, int):
        return rows[place : place + 1, :]
    line = rows[:1, :]
    for i in range(1, rows.shape[0]):
        line = jnp.where(place == i, rows[i : i + 1, :], line)
    return line


def product(packed, values):
    left = jnp.concatenate(halves(values), axis=0)
    both = jnp.dot(jnp.concatenate([left, left], axis=1), packed, preferred_element_type=F32)
    count = values.shape[0]
    return both[:count] + both[count:]


def thirds(value):
    high = value.astype(BF16)
    rest = value - high.astype(F32)
    middle = rest.astype(BF16)
    low = (rest - middle.astype(F32)).astype(BF16)
    return jnp.concatenate([high, middle, low], axis=0)


def gram(parts, n):
    cross = lax.dot_general(parts, parts, NT, preferred_element_type=F32)
    count = parts.shape[0] // n
    pairs = sorted(((i, j) for i in range(count) for j in range(count)), key=lambda p: -p[0] - p[1])
    total = None
    for i, j in pairs:
        piece = cross[i * n : (i + 1) * n, j * n : (j + 1) * n]
        total = piece if total is None else total + piece
    return total


def times(left, parts):
    m = left.shape[0]
    left = jnp.concatenate(halves(left), axis=0)
    both = jnp.dot(jnp.concatenate([left, left], axis=1), parts, preferred_element_type=F32)
    return both[m:] + both[:m]


def lower_inverse(matrix, step=8):
    n = matrix.shape[0]
    state = jnp.concatenate([matrix, eye_mask(n).astype(F32)], axis=1)
    done = []
    for j in range(0, n, step):
        top = j // 8 * 8
        if top > n - state.shape[0]:
            done.append(state[:8])
            state = state[8:]
        base = j - top
        rows = lax.broadcasted_iota(jnp.int32, state.shape, 0)
        columns = [jnp.broadcast_to(state[:, j + i : j + i + 1], state.shape) for i in range(step)]
        lines = [state[base + i : base + i + 1, :] for i in range(step)]
        pivot = [[columns[k][base + i : base + i + 1, :] for k in range(step)] for i in range(step)]
        for i in range(step):
            if i % 2 == 0:
                first, cross, second = pivot[i][i], pivot[i][i + 1], pivot[i + 1][i + 1]
                reciprocals = (1.0 / first, first / (first * second - cross * cross))
            reciprocal = reciprocals[i % 2]
            scaled = lines[i] * reciprocal
            ratio = [pivot[i][k] * reciprocal for k in range(step)]
            for k in range(i + 1, step):
                lines[k] = lines[k] - pivot[k][i] * scaled
                columns[k] = columns[k] - columns[i] * ratio[k]
                for m in range(i + 1, step):
                    pivot[k][m] = pivot[k][m] - pivot[k][i] * ratio[m]
            state = state - jnp.where(rows > base + i, columns[i], 0.0) * scaled
    state = jnp.concatenate([*done, state], axis=0)
    pivots = jnp.sum(jnp.where(eye_mask(n), state[:, :n], 0.0), axis=1, keepdims=True)
    return state[:, n:] / jnp.sqrt(pivots)


def both_columns(core, own, other):
    first = core == 0
    return jnp.concatenate(
        [jnp.where(first, own, other), jnp.where(first, other, own)], axis=0
    )


def quotient(value, size):
    if size & (size - 1) == 0:
        return lax.shift_right_logical(value, jnp.int32(size.bit_length() - 1))
    return lax.div(value, jnp.int32(size))


def remainder(value, size):
    if size & (size - 1) == 0:
        return lax.bitwise_and(value, jnp.int32(size - 1))
    return lax.rem(value, jnp.int32(size))


def plan_body(dims, list_order, me, *refs):
    row_count, capacity, slots, blocks_here = dims
    lists, (emb, after, idx_out) = refs[:row_count], refs[row_count : row_count + 3]
    sends, (idx, left) = refs[row_count + 3 : -2], refs[-2:]
    row = me[0]
    for i in range(slots):
        for line in (0, 1, 4, 5):
            idx[line, i] = 0
        idx[3, i] = slots
    lists = dict(zip(list_order, [one.ready() for one in lists]))

    def each(step, start):
        if slots <= 8:
            for s in range(slots):
                start = step(s, start)
        else:
            lax.fori_loop(0, slots, step, start)

    for k in range(row_count):

        def step(s, counts, k=k):
            near = lists[k][0, s]
            far = lists[k][1, s]
            owner = quotient(far, blocks_here)
            if k > 0:
                hit = (owner == row) & (counts[0] < capacity)
                slot = jnp.where(hit, k * capacity + counts[0], slots)
                idx[4, slot] = far - row * blocks_here
                idx[5, slot] = near
                return (counts[0] + hit.astype(jnp.int32),)
            shift = remainder(owner - row + row_count, row_count)
            rank = counts[0]
            for d in range(1, row_count):
                rank = jnp.where(shift == d, counts[d], rank)
            slot = jnp.where(rank < capacity, shift * capacity + rank, slots)
            idx[0, slot] = near - row * blocks_here
            idx[1, slot] = far
            idx[3, slot] = s
            slot = jnp.where(shift == 0, slot, slots)
            idx[4, slot] = far - row * blocks_here
            idx[5, slot] = near
            return tuple(counts[d] + (shift == d).astype(jnp.int32) for d in range(row_count))

        each(step, (jnp.int32(0),) * (row_count if k == 0 else 1))
    leave = pltpu.make_async_copy(idx, idx_out, left)
    leave.start()
    for k in range(1, row_count):
        for j in range(capacity):
            sends[k - 1][j * BLOCK : (j + 1) * BLOCK, :] = emb[at_block(idx[4, k * capacity + j]), :]
    leave.wait()


def squares(block):
    return jnp.sum(jnp.square(block.astype(F32)), axis=1, keepdims=True)


def as_row(column):
    return jnp.sum(jnp.where(eye_mask(BLOCK), column, 0.0), axis=0, keepdims=True)


def partial_distance(left, right, left_sq, right_row):
    inner = lax.dot_general(left, right, NT, preferred_element_type=F32)
    return left_sq + right_row - 2.0 * inner


def self_distance_body(own_blocks, tile_count, me, emb, out):
    for i in range(own_blocks):
        block = emb[at_block(i * tile_count + me[1]), :]
        block_sq = squares(block)
        out[i * BLOCK : (i + 1) * BLOCK, :] = partial_distance(
            block, block, block_sq, as_row(block_sq)
        )


def squares_body(capacity, idx, emb, out, home):
    for b in range(out.shape[0] // BLOCK):
        part = slice(b * BLOCK, (b + 1) * BLOCK)
        out[part, :] = jnp.broadcast_to(squares(emb[part, :]), (BLOCK, BLOCK))
    idx = idx.ready()
    for j in range(capacity):
        left, right = at_block(idx[0, j]), at_block(idx[4, j])
        home[j * BLOCK : (j + 1) * BLOCK, :] = partial_distance(
            emb[left, :], emb[right, :], out[left, :], as_row(out[right, :])
        )


def pair_distance_body(order, capacity, idx, emb, own_squares, home, *refs):
    far, out = dict(zip(order, refs)), refs[-1]
    rows = {}
    for k in order:
        for j in range(capacity):
            rows[k, j] = as_row(squares(far[k][j * BLOCK : (j + 1) * BLOCK, :]))
    idx = idx.ready()
    out[: capacity * BLOCK, :] = home[...]
    for k in range(1, len(order) + 1):
        for j in range(capacity):
            slot = k * capacity + j
            left = emb[at_block(idx[0, slot]), :]
            left_sq = own_squares[at_block(idx[0, slot]), :]
            right = far[k][j * BLOCK : (j + 1) * BLOCK, :]
            part = slice(slot * BLOCK, (slot + 1) * BLOCK)
            out[part, :] = partial_distance(left, right, left_sq, rows[k, j])


def self_tile_body(own_blocks, mine, other, packed, sums):
    for i in range(own_blocks):
        part = slice(i * BLOCK, (i + 1) * BLOCK)
        tile = jnp.exp(-kernel_gamma * (mine[part, :] + other[part, :] - 2.0))
        tile = jnp.where(eye_mask(BLOCK), 0.0, tile)
        packed[i] = pack(tile)
        sums[i : i + 1, :] = jnp.sum(tile, axis=0, keepdims=True)


def pair_tile_body(dims, me, idx, live_count, mine, other, self_sums, codes, powers, parts, near_tiles, home_tiles, table, *sends):
    row_count, capacity, per_core, blocks_here, tile_count = dims
    row, tile_index, core = me[0], me[1], me[2]
    table[...] = jnp.zeros(table.shape, F32)
    for i in range(self_sums.shape[0]):
        table[pl.ds(row * blocks_here + i * tile_count + tile_index, 1), :] = self_sums[i : i + 1, :]

    def add(block, line):
        place = pl.ds(block, 1)
        table[place, :] = table[place, :] + line

    all_tiles = jnp.exp(-kernel_gamma * (mine[...] + other[...] - 2.0))
    idx = idx.ready()
    live_count = live_count.ready()[0]
    for k in range(row_count):
        tiles = []
        for j in range(capacity):
            slot = k * capacity + j
            tile = all_tiles[slot * BLOCK : (slot + 1) * BLOCK]
            tile = jnp.where(idx[3, slot] < live_count, tile, 0.0)
            turned = tile.T
            near_tiles[slot] = pack(turned)
            add(row * blocks_here + idx[0, slot], jnp.sum(turned, axis=0, keepdims=True))
            add(idx[1, slot], jnp.sum(tile, axis=0, keepdims=True))
            if k == 0:
                home_tiles[j] = pack(tile)
            tiles.append(tile)
        if k > 0:
            lines = ([], [])
            for inner in range(per_core):
                at = slice(inner * BLOCK, (inner + 1) * BLOCK)
                steps, power, part = encode(jnp.where(core == 0, tiles[inner], tiles[per_core + inner]))
                sends[k - 1][at, :] = steps
                lines[0].append(power)
                lines[1].append(part)
            pick_columns(idx, k, row_count, capacity, codes, powers, parts, sends[k - 1], per_core * BLOCK, lines)


def encode_blocks(values, codes, powers, parts):
    for b in range(powers.shape[0]):
        at = slice(b * BLOCK, (b + 1) * BLOCK)
        steps, power, part = encode(values[:, at])
        codes[:, at] = steps
        powers[b : b + 1, :] = power
        parts[b : b + 1, :] = part


def start_body(values, codes, powers, parts):
    encode_blocks(values, codes, powers, parts)


def split_body(row_count, per_core, *refs):
    others = row_count - 1
    messages, outs = refs[:others], refs[-others:]
    for message, out in zip(messages, outs):
        scales = scale_rows(message[message.shape[0] - CODE_ROWS :, :])
        for inner in range(per_core):
            steps = message[inner * BLOCK : (inner + 1) * BLOCK, :]
            out[inner] = pack(decode(steps, scales[inner : inner + 1, :]))


def pick_columns(idx, k, row_count, capacity, codes, powers, parts, send, base, lines):
    count = codes.shape[0]
    back = row_count - k
    blocks = [idx[0, k * capacity + j] for j in range(capacity)]
    blocks += [idx[4, back * capacity + j] for j in range(capacity)]
    for place, block in enumerate(blocks):
        send[base + place * count : base + (place + 1) * count, :] = codes[:, at_block(block)]
        lines[0].append(powers[pl.ds(block, 1), :])
        lines[1].append(parts[pl.ds(block, 1), :])
    send[base + len(blocks) * count :, :] = as_rows(*lines, CODE_ROWS)


def add_product(out, block, packed, values):
    place = at_block(block)
    out[:, place] = out[:, place] + product(packed, values)


def apply_own(dims, me, idx, inverse, own, near_tiles, home_tiles, self_tiles, out):
    row_count, capacity, per_core, blocks_here, tile_count = dims
    row, tile_index = me[0], me[1]
    out[...] = jnp.zeros(out.shape, F32)

    def scaled(block):
        return own[:, at_block(block)] * inverse[pl.ds(row * blocks_here + block, 1), :]

    for i in range(blocks_here // tile_count):
        block = i * tile_count + tile_index
        add_product(out, block, self_tiles[i], scaled(block))
    idx = idx.ready()
    for j in range(capacity):
        add_product(out, idx[0, j], near_tiles[j], scaled(idx[4, j]))
        add_product(out, idx[4, j], home_tiles[j], scaled(idx[0, j]))
    return idx


def apply_far(dims, me, idx, inverse, received, base, near_tiles, sent, shared, out):
    row_count, capacity, per_core, blocks_here, tile_count = dims
    core = me[2]
    count = out.shape[0]
    lines = [scale_rows(message[message.shape[0] - CODE_ROWS :, :]) for message in received]
    first_line = base // BLOCK

    def arrived(k, place, block):
        steps = received[k - 1][pl.ds(pl.multiple_of(base + place * count, CODE_ROWS), count), :]
        rows = lines[k - 1][first_line : first_line + 2 * capacity, :]
        return decode(steps, row_at(rows, place) * inverse[pl.ds(block, 1), :])

    for k in range(1, row_count):
        for j in range(capacity):
            slot = k * capacity + j
            values = arrived(row_count - k, capacity + j, idx[1, slot])
            add_product(out, idx[0, slot], near_tiles[slot], values)
            inner = j % per_core
            if j < per_core:
                place = core * per_core + inner
                packed = sent[k - 1][inner]
            else:
                place = (1 - core) * per_core + inner
                packed = shared[k - 1][inner]
            slot = k * capacity + place
            add_product(out, idx[4, slot], packed, arrived(k, place, idx[5, slot]))


def first_own_body(dims, me, idx, mine, other, own, near_tiles, home_tiles, self_tiles, out, degree, inverse):
    total = mine[...] + other[...]
    degree[...] = total
    inverse[...] = 1.0 / jnp.sqrt(total)
    apply_own(dims, me, idx, inverse, own, near_tiles, home_tiles, self_tiles, out)


def first_far_body(dims, coded, me, idx, inverse, started, near_tiles, *refs):
    row_count, per_core = dims[0], dims[2]
    others = row_count - 1
    sent, shared, messages = refs[:others], refs[others : 2 * others], refs[2 * others : 3 * others]
    out, total = refs[3 * others :]
    total[...] = started[...]
    apply_far(dims, me, idx.ready(), inverse, messages, per_core * BLOCK, near_tiles, sent, shared, total)
    put_sum(coded, total, out)


def second_apply_body(dims, me, idx, inverse, after, own, home_tiles, self_tiles, near_tiles, *refs):
    others = dims[0] - 1
    sent, shared, received = refs[:others], refs[others : 2 * others], refs[2 * others : 3 * others]
    out = refs[-1]
    idx = apply_own(dims, me, idx, inverse, own, near_tiles, home_tiles, self_tiles, out)
    apply_far(dims, me, idx, inverse, received, 0, near_tiles, sent, shared, out)


def send_sum_body(coded, total, after, out):
    put_sum(coded, total, out)


def put_sum(coded, total, out):
    if not coded:
        out[...] = total[...]
        return
    lines = ([], [])
    blocks_here = total.shape[1] // BLOCK
    for b in range(blocks_here):
        at = slice(b * BLOCK, (b + 1) * BLOCK)
        steps, power, part = encode(total[:, at])
        out[:, at] = steps
        lines[0].append(power)
        lines[1].append(part)
    out[:, blocks_here * BLOCK :] = as_rows(*lines, out.shape[0])


def take_sum(coded, me, blocks_here, inverse, mine, other, out):
    if coded:
        tail = blocks_here * BLOCK
        my_scales, other_scales = scale_rows(mine[:, tail:]), scale_rows(other[:, tail:])
    for b in range(blocks_here):
        at = slice(b * BLOCK, (b + 1) * BLOCK)
        row = inverse[pl.ds(me[0] * blocks_here + b, 1), :]
        if coded:
            line = slice(b, b + 1)
            value = decode(mine[:, at], my_scales[line]) + decode(other[:, at], other_scales[line])
        else:
            value = mine[:, at] + other[:, at]
        out[:, at] = value * row


def mapped_body(dims, coded, me, idx, inverse, mine, other, out, *refs):
    row_count, capacity, per_core, blocks_here, tile_count = dims
    sends, (codes, powers, parts) = refs[:-3], refs[-3:]
    take_sum(coded, me, blocks_here, inverse, mine, other, out)
    encode_blocks(out, codes, powers, parts)
    idx = idx.ready()
    for k in range(1, row_count):
        pick_columns(idx, k, row_count, capacity, codes, powers, parts, sends[k - 1], 0, ([], []))


def last_mapped_body(blocks_here, coded, me, inverse, mine, other, after, out):
    take_sum(coded, me, blocks_here, inverse, mine, other, out)


def folded(square):
    half = square.shape[0] // 2
    return jnp.concatenate([square[:half], square[half:]], axis=1)


def unfolded(terms):
    total = functools.reduce(lambda total, term: total + term[...], terms[1:], terms[0][...])
    width = total.shape[1] // 2
    return jnp.concatenate([total[:, :width], total[:, width:]], axis=0)


def gram_body(me, own, other, out):
    full = both_columns(me[2], own[...], other[...])
    out[...] = folded(gram(pack(full), full.shape[0]))


def factor_body(after, *refs):
    refs[-1][...] = lower_inverse(unfolded(refs[:-1]))


def second_gram_body(me, factor, own, other, mapped, out):
    full = both_columns(me[2], own[...], other[...])
    parts = thirds(times(factor[...], pack(full)))
    mapped[...] = parts[: mapped.shape[0]]
    out[...] = folded(gram(parts, full.shape[0]))


def final_body(me, mapped, *refs):
    terms, (out, value, sent) = refs[:-3], refs[-3:]
    factor = lower_inverse(unfolded(terms))
    own_cols = value.shape[0]
    part = jnp.where(me[2] == 0, factor[:own_cols], factor[own_cols:])
    copies = []
    chunk = value.shape[1] // sent.shape[0]
    for i in range(sent.shape[0]):
        at = slice(i * chunk, (i + 1) * chunk)
        value[:, at] = times(part, mapped[:, at])
        copies.append(pltpu.make_async_copy(value.at[:, at], out.at[:, at], sent.at[i]))
        copies[-1].start()
    for copy in copies:
        copy.wait()


def shift_by(value, axes, size, shift):
    return lax.ppermute(value, axes, [(i, (i + shift) % size) for i in range(size)])


def row_terms(value, row_count):
    return [value] + [shift_by(value, "rows", row_count, k) for k in range(1, row_count)]


def pair_step(value, name, flip):
    return lax.ppermute(value, name, [(i, i ^ flip) for i in range(lax.axis_size(name))])


def pair_sum(value, axes):
    terms = None
    steps = [(name, 1 << bit) for name in axes for bit in range((lax.axis_size(name) - 1).bit_length())]
    for name, flip in steps:
        if terms is not None:
            value = terms[0] + terms[1]
        terms = (value, pair_step(value, name, flip))
    return terms


def local(embeddings, start, pair_list, pair_count):
    row_count = lax.axis_size("rows")
    tile_count = lax.axis_size("tiles")
    core_count = lax.axis_size("cols")
    row_index = lax.axis_index("rows")
    tile_index = lax.axis_index("tiles")
    col_index = lax.axis_index("cols")
    rows_here, half_features = embeddings.shape
    blocks_here = rows_here // BLOCK
    slots = pair_list.shape[2]
    capacity = slots // row_count
    per_core = capacity // core_count
    own_blocks = blocks_here // tile_count
    own_cols = start.shape[1]
    block_count = row_count * blocks_here
    others = range(1, row_count)

    list_order = [0, *sorted(others, key=lambda k: k * (row_count - k))]
    lists = [shift_by(pair_list[0], "rows", row_count, k) if k else pair_list[0] for k in list_order]
    self_part = call(
        functools.partial(self_distance_body, own_blocks, tile_count),
        sds((own_blocks * BLOCK, BLOCK), F32),
        [ME, embeddings],
    )
    planned = call(
        functools.partial(plan_body, (row_count, capacity, slots, blocks_here), list_order),
        [sds((6, slots + 1), jnp.int32)] + [sds((capacity * BLOCK, half_features), BF16) for _ in others],
        [ME, *lists, embeddings, self_part],
        late=range(1, 1 + row_count),
        any_in=(row_count + 2,),
        any_out=(0,),
        scratch=[pltpu.SMEM((6, slots + 1), jnp.int32), pltpu.SemaphoreType.DMA],
    )
    idx, sends = planned[0], planned[1:]
    order = sorted(others, key=lambda k: abs(k - row_count // 2))
    far = [shift_by(sends[k - 1], "rows", row_count, -k) for k in order]

    self_other = shift_by(self_part, "cols", core_count, 1)
    self_tiles, self_sums = call(
        functools.partial(self_tile_body, own_blocks),
        [sds((own_blocks, 2 * BLOCK, BLOCK), BF16), sds((own_blocks, BLOCK), F32)],
        [self_part, self_other],
    )
    values = start.T
    code_shapes = [((own_cols, rows_here), jnp.int16), ((blocks_here, BLOCK), F32), ((blocks_here, BLOCK), F32)]
    start_codes = call(start_body, [sds(*shape) for shape in code_shapes], [values])
    code_scratch = [pltpu.VMEM(*shape) for shape in code_shapes]
    coded = tile_count == 2
    own_squares, home = call(
        functools.partial(squares_body, capacity),
        [sds((rows_here, BLOCK), F32), sds((capacity * BLOCK, BLOCK), F32)],
        [idx, embeddings],
        late=(0,),
    )
    pair_part = call(
        functools.partial(pair_distance_body, order, capacity),
        sds((slots * BLOCK, BLOCK), F32),
        [idx, embeddings, own_squares, home, *far],
        late=(0,),
    )
    pair_other = shift_by(pair_part, "cols", core_count, 1)

    dims = (row_count, capacity, per_core, blocks_here, tile_count)
    table = sds((block_count, BLOCK), F32)
    picked = 2 * capacity * own_cols
    tiles = call(
        functools.partial(pair_tile_body, dims),
        [sds((slots, 2 * BLOCK, BLOCK), BF16), sds((capacity, 2 * BLOCK, BLOCK), BF16), table]
        + [sds((per_core * BLOCK + picked + CODE_ROWS, BLOCK), jnp.int16) for _ in others],
        [ME, idx, pair_count, pair_part, pair_other, self_sums, *start_codes],
        late=(1, 2),
    )
    near_tiles, home_tiles, degrees, sends = tiles[0], tiles[1], tiles[2], tiles[3:]
    degrees = functools.reduce(jnp.add, row_terms(degrees, row_count))
    degree_terms = pair_sum(degrees, ("tiles",))
    messages = [shift_by(sends[k - 1], "rows", row_count, k) for k in others]
    sent = call(
        functools.partial(split_body, row_count, per_core),
        [sds((per_core, 2 * BLOCK, BLOCK), BF16) for _ in others],
        [*messages, degree_terms[1]],
        any_in=(row_count - 1,),
    )
    shared = [shift_by(tile, "cols", core_count, 1) for tile in sent]

    block_shape = sds((own_cols, rows_here), F32)
    sum_shape = sds((own_cols, rows_here + BLOCK), jnp.int16) if coded else block_shape
    square = sds((2 * own_cols, 2 * own_cols), F32)
    folded_square = sds((own_cols, 4 * own_cols), F32)

    started, degree, inverse = call(
        functools.partial(first_own_body, dims),
        [block_shape, table, table],
        [ME, idx, *degree_terms, values, near_tiles, home_tiles, self_tiles],
        late=(1,),
    )
    part = call(
        functools.partial(first_far_body, dims, coded),
        sum_shape,
        [ME, idx, inverse, started, near_tiles, *sent, *shared, *messages],
        late=(1,),
        scratch=[pltpu.VMEM((own_cols, rows_here), F32)],
    )
    mine, other = pair_sum(part, ("tiles",))
    first = call(
        functools.partial(mapped_body, dims, coded),
        [block_shape] + [sds((picked + CODE_ROWS, BLOCK), jnp.int16) for _ in others],
        [ME, idx, inverse, mine, other],
        late=(1,),
        scratch=code_scratch,
    )
    mapped, sends = first[0], first[1:]
    received = [shift_by(sends[k - 1], "rows", row_count, k) for k in others]

    mapped_other = shift_by(mapped, "cols", core_count, 1)
    first_gram = call(gram_body, folded_square, [ME, mapped, mapped_other])
    part = call(
        functools.partial(second_apply_body, dims),
        block_shape,
        [ME, idx, inverse, first_gram, mapped, home_tiles, self_tiles, near_tiles, *sent, *shared, *received],
        late=(1,),
        any_in=(3,),
    )
    steps = (row_count - 1).bit_length()
    for bit in range(steps - 1):
        first_gram = first_gram + pair_step(first_gram, "rows", 1 << bit)
    part = call(functools.partial(send_sum_body, coded), sum_shape, [part, first_gram])
    gram_terms = (first_gram, pair_step(first_gram, "rows", 1 << (steps - 1)))
    mine, other = pair_sum(part, ("tiles",))
    second = call(
        functools.partial(last_mapped_body, blocks_here, coded),
        block_shape,
        [ME, inverse, mine, other, gram_terms[1]],
        any_in=(4,),
    )
    second_other = shift_by(second, "cols", core_count, 1)
    factor = call(factor_body, square, [second, *gram_terms], any_in=(0,))
    full, second_gram = call(
        second_gram_body,
        [sds((4 * own_cols, rows_here), BF16), folded_square],
        [ME, factor, second, second_other],
    )
    vectors = call(
        final_body,
        block_shape,
        [ME, full, *row_terms(second_gram, row_count)],
        any_out=(0,),
        scratch=[pltpu.VMEM((own_cols, rows_here), F32), pltpu.SemaphoreType.DMA((4,))],
    )
    own_degree = lax.dynamic_slice_in_dim(degree, row_index * blocks_here, blocks_here, 0)
    return (vectors.T, own_degree.reshape(rows_here))


def solution(mesh):
    in_specs = (
        P(("groups", "rows"), "cols"),
        P(("groups", "rows"), "cols"),
        P(("groups", "rows", "tiles"), None, None),
        P(("groups", "rows", "tiles")),
    )
    out_specs = (P(("groups", "rows"), "cols"), P(("groups", "rows")))
    return jax.shard_map(local, mesh=mesh, in_specs=in_specs, out_specs=out_specs, check_vma=False)
```

```python
import functools

import jax
import jax.numpy as jnp
from jax import lax
from jax.experimental import pallas as pl
from jax.experimental.pallas import tpu as pltpu
from jax.sharding import PartitionSpec as P

BLOCK = 128
kernel_gamma = 14.0
CODE_TOP = 32767.0
PART_TOP = 16384.0
CODE_ROWS = 16

VMEM = pl.BlockSpec(memory_space=pltpu.VMEM)
ANY = pl.BlockSpec(memory_space=pl.ANY)
F32 = jnp.float32
BF16 = jnp.bfloat16
HIGHEST = lax.Precision.HIGHEST
NT = (((1,), (1,)), ((), ()))


ME = None


def with_position(body):
    def inner(*refs):
        return body([lax.axis_index(name) for name in ("rows", "tiles", "cols")], *refs)

    return inner


class Late:
    def __init__(self, source, table, arrived):
        self.table = table
        self.copy = pltpu.make_async_copy(source, table, arrived)
        self.copy.start()

    def ready(self):
        self.copy.wait()
        return self.table


def with_late(body, places, count):
    def inner(*refs):
        refs, tables, arrived = refs[:-1 - count], refs[-1 - count : -1], refs[-1]
        refs = list(refs)
        for i, place in enumerate(places):
            refs[place] = Late(refs[place], tables[i], arrived.at[i])
        body(*refs)

    return inner


def call(body, outs, args, late=(), any_in=(), scratch=(), any_out=()):
    if args[0] is ME:
        body, args = with_position(body), args[1:]
        late, any_in = [[i - 1 for i in places] for places in (late, any_in)]
    if late:
        scratch = [
            *scratch,
            *[pltpu.SMEM(args[i].shape, args[i].dtype) for i in late],
            pltpu.SemaphoreType.DMA((len(late),)),
        ]
        any_in = [*any_in, *late]
        body = with_late(body, late, len(late))
    single = not isinstance(outs, (list, tuple))
    shapes = [outs] if single else list(outs)
    result = pl.pallas_call(
        body,
        out_shape=shapes,
        in_specs=[ANY if i in any_in else VMEM for i in range(len(args))],
        out_specs=[ANY if i in any_out else VMEM for i in range(len(shapes))],
        scratch_shapes=list(scratch),
        compiler_params=pltpu.CompilerParams(vmem_limit_bytes=48 * 2**20),
    )(*args)
    return result[0] if single else result


def sds(shape, dtype):
    return jax.ShapeDtypeStruct(shape, dtype)


def at_block(index):
    return pl.ds(pl.multiple_of(index * BLOCK, BLOCK), BLOCK)


def eye_mask(size):
    return lax.broadcasted_iota(jnp.int32, (size, size), 0) == lax.broadcasted_iota(
        jnp.int32, (size, size), 1
    )


def halves(value):
    high = value.astype(BF16)
    low = (value - high.astype(F32)).astype(BF16)
    return high, low


def pack(tile):
    return jnp.concatenate(halves(tile), axis=0)


def scale_of(power, part):
    return jnp.exp2(power) * (part * (1.0 / PART_TOP))


def encode(values):
    most = jnp.maximum(jnp.max(jnp.abs(values), axis=0, keepdims=True), 1e-30)
    power = jnp.floor(jnp.log2(most)) + 1.0
    part = jnp.floor(most * jnp.exp2(-power) * PART_TOP) + 1.0
    steps = jnp.floor(values * (CODE_TOP / scale_of(power, part)) + 0.5)
    steps = jnp.minimum(jnp.maximum(steps, -CODE_TOP), CODE_TOP)
    return steps.astype(jnp.int32).astype(jnp.int16), power, part


def decode(steps, scale):
    return steps.astype(jnp.int32).astype(F32) * (scale * (1.0 / CODE_TOP))


def as_rows(powers, parts, count):
    fill = jnp.zeros((count // 2 - len(powers), BLOCK), F32)
    fill = [fill] if fill.shape[0] else []
    rows = jnp.concatenate([*powers, *fill, *parts, *fill], axis=0)
    return rows.astype(jnp.int32).astype(jnp.int16)


def scale_rows(rows):
    rows = rows.astype(jnp.int32).astype(F32)
    half = rows.shape[0] // 2
    return scale_of(rows[:half], rows[half:])


def row_at(rows, place):
    if isinstance(place, int):
        return rows[place : place + 1, :]
    line = rows[:1, :]
    for i in range(1, rows.shape[0]):
        line = jnp.where(place == i, rows[i : i + 1, :], line)
    return line


def product(packed, values):
    left = jnp.concatenate(halves(values), axis=0)
    both = jnp.dot(jnp.concatenate([left, left], axis=1), packed, preferred_element_type=F32)
    count = values.shape[0]
    return both[:count] + both[count:]


def thirds(value):
    high = value.astype(BF16)
    rest = value - high.astype(F32)
    middle = rest.astype(BF16)
    low = (rest - middle.astype(F32)).astype(BF16)
    return jnp.concatenate([high, middle, low], axis=0)


def gram(parts, n):
    cross = lax.dot_general(parts, parts, NT, preferred_element_type=F32)
    count = parts.shape[0] // n
    pairs = sorted(((i, j) for i in range(count) for j in range(count)), key=lambda p: -p[0] - p[1])
    total = None
    for i, j in pairs:
        piece = cross[i * n : (i + 1) * n, j * n : (j + 1) * n]
        total = piece if total is None else total + piece
    return total


def times(left, parts):
    m = left.shape[0]
    left = jnp.concatenate(halves(left), axis=0)
    both = jnp.dot(jnp.concatenate([left, left], axis=1), parts, preferred_element_type=F32)
    return both[m:] + both[:m]


def lower_inverse(matrix, step=8):
    n = matrix.shape[0]
    state = jnp.concatenate([matrix, eye_mask(n).astype(F32)], axis=1)
    done = []
    for j in range(0, n, step):
        top = j // 8 * 8
        if top > n - state.shape[0]:
            done.append(state[:8])
            state = state[8:]
        base = j - top
        rows = lax.broadcasted_iota(jnp.int32, state.shape, 0)
        columns = [jnp.broadcast_to(state[:, j + i : j + i + 1], state.shape) for i in range(step)]
        lines = [state[base + i : base + i + 1, :] for i in range(step)]
        pivot = [[columns[k][base + i : base + i + 1, :] for k in range(step)] for i in range(step)]
        for i in range(step):
            if i % 2 == 0:
                first, cross, second = pivot[i][i], pivot[i][i + 1], pivot[i + 1][i + 1]
                reciprocals = (1.0 / first, first / (first * second - cross * cross))
            reciprocal = reciprocals[i % 2]
            scaled = lines[i] * reciprocal
            ratio = [pivot[i][k] * reciprocal for k in range(step)]
            for k in range(i + 1, step):
                lines[k] = lines[k] - pivot[i][k] * scaled
                columns[k] = columns[k] - columns[i] * ratio[k]
                for m in range(k, step):
                    pivot[k][m] = pivot[k][m] - pivot[i][k] * ratio[m]
            state = state - jnp.where(rows > base + i, columns[i], 0.0) * scaled
    state = jnp.concatenate([*done, state], axis=0)
    pivots = jnp.sum(jnp.where(eye_mask(n), state[:, :n], 0.0), axis=1, keepdims=True)
    return state[:, n:] / jnp.sqrt(pivots)


def both_columns(core, own, other):
    first = core == 0
    return jnp.concatenate(
        [jnp.where(first, own, other), jnp.where(first, other, own)], axis=0
    )


def quotient(value, size):
    if size & (size - 1) == 0:
        return lax.shift_right_logical(value, jnp.int32(size.bit_length() - 1))
    return lax.div(value, jnp.int32(size))


def remainder(value, size):
    if size & (size - 1) == 0:
        return lax.bitwise_and(value, jnp.int32(size - 1))
    return lax.rem(value, jnp.int32(size))


def plan_body(dims, list_order, me, *refs):
    row_count, capacity, slots, blocks_here = dims
    lists, (emb, after, idx_out) = refs[:row_count], refs[row_count : row_count + 3]
    sends, (idx, left) = refs[row_count + 3 : -2], refs[-2:]
    row = me[0]
    for i in range(slots):
        for line in (0, 1, 4, 5):
            idx[line, i] = 0
        idx[3, i] = slots
    lists = dict(zip(list_order, [one.ready() for one in lists]))

    def each(step, start):
        if slots <= 8:
            for s in range(slots):
                start = step(s, start)
        else:
            lax.fori_loop(0, slots, step, start)

    for k in range(row_count):

        def step(s, counts, k=k):
            near = lists[k][0, s]
            far = lists[k][1, s]
            owner = quotient(far, blocks_here)
            if k > 0:
                hit = (owner == row) & (counts[0] < capacity)
                slot = jnp.where(hit, k * capacity + counts[0], slots)
                idx[4, slot] = far - row * blocks_here
                idx[5, slot] = near
                return (counts[0] + hit.astype(jnp.int32),)
            shift = remainder(owner - row + row_count, row_count)
            rank = counts[0]
            for d in range(1, row_count):
                rank = jnp.where(shift == d, counts[d], rank)
            slot = jnp.where(rank < capacity, shift * capacity + rank, slots)
            idx[0, slot] = near - row * blocks_here
            idx[1, slot] = far
            idx[3, slot] = s
            slot = jnp.where(shift == 0, slot, slots)
            idx[4, slot] = far - row * blocks_here
            idx[5, slot] = near
            return tuple(counts[d] + (shift == d).astype(jnp.int32) for d in range(row_count))

        each(step, (jnp.int32(0),) * (row_count if k == 0 else 1))
    leave = pltpu.make_async_copy(idx, idx_out, left)
    leave.start()
    for k in range(1, row_count):
        for j in range(capacity):
            sends[k - 1][j * BLOCK : (j + 1) * BLOCK, :] = emb[at_block(idx[4, k * capacity + j]), :]
    leave.wait()


def squares(block):
    return jnp.sum(jnp.square(block.astype(F32)), axis=1, keepdims=True)


def as_row(column):
    return jnp.sum(jnp.where(eye_mask(BLOCK), column, 0.0), axis=0, keepdims=True)


def partial_distance(left, right, left_sq, right_row):
    inner = lax.dot_general(left, right, NT, preferred_element_type=F32)
    return left_sq + right_row - 2.0 * inner


def self_distance_body(own_blocks, tile_count, me, emb, out):
    for i in range(own_blocks):
        block = emb[at_block(i * tile_count + me[1]), :]
        block_sq = squares(block)
        out[i * BLOCK : (i + 1) * BLOCK, :] = partial_distance(
            block, block, block_sq, as_row(block_sq)
        )


def squares_body(capacity, idx, emb, out, home):
    for b in range(out.shape[0] // BLOCK):
        part = slice(b * BLOCK, (b + 1) * BLOCK)
        out[part, :] = jnp.broadcast_to(squares(emb[part, :]), (BLOCK, BLOCK))
    idx = idx.ready()
    for j in range(capacity):
        left, right = at_block(idx[0, j]), at_block(idx[4, j])
        home[j * BLOCK : (j + 1) * BLOCK, :] = partial_distance(
            emb[left, :], emb[right, :], out[left, :], as_row(out[right, :])
        )


def pair_distance_body(order, capacity, idx, emb, own_squares, home, *refs):
    far, out = dict(zip(order, refs)), refs[-1]
    rows = {}
    for k in order:
        for j in range(capacity):
            rows[k, j] = as_row(squares(far[k][j * BLOCK : (j + 1) * BLOCK, :]))
    idx = idx.ready()
    out[: capacity * BLOCK, :] = home[...]
    for k in range(1, len(order) + 1):
        for j in range(capacity):
            slot = k * capacity + j
            left = emb[at_block(idx[0, slot]), :]
            left_sq = own_squares[at_block(idx[0, slot]), :]
            right = far[k][j * BLOCK : (j + 1) * BLOCK, :]
            part = slice(slot * BLOCK, (slot + 1) * BLOCK)
            out[part, :] = partial_distance(left, right, left_sq, rows[k, j])


def self_tile_body(own_blocks, mine, other, packed, sums):
    for i in range(own_blocks):
        part = slice(i * BLOCK, (i + 1) * BLOCK)
        tile = jnp.exp(-kernel_gamma * (mine[part, :] + other[part, :] - 2.0))
        tile = jnp.where(eye_mask(BLOCK), 0.0, tile)
        packed[i] = pack(tile)
        sums[i : i + 1, :] = jnp.sum(tile, axis=0, keepdims=True)


def pair_tile_body(dims, me, idx, live_count, mine, other, self_sums, codes, powers, parts, near_tiles, home_tiles, table, *sends):
    row_count, capacity, per_core, blocks_here, tile_count = dims
    row, tile_index, core = me[0], me[1], me[2]
    table[...] = jnp.zeros(table.shape, F32)
    for i in range(self_sums.shape[0]):
        table[pl.ds(row * blocks_here + i * tile_count + tile_index, 1), :] = self_sums[i : i + 1, :]

    def add(block, line):
        place = pl.ds(block, 1)
        table[place, :] = table[place, :] + line

    all_tiles = jnp.exp(-kernel_gamma * (mine[...] + other[...] - 2.0))
    idx = idx.ready()
    live_count = live_count.ready()[0]
    for k in range(row_count):
        tiles = []
        for j in range(capacity):
            slot = k * capacity + j
            tile = all_tiles[slot * BLOCK : (slot + 1) * BLOCK]
            tile = jnp.where(idx[3, slot] < live_count, tile, 0.0)
            turned = tile.T
            near_tiles[slot] = pack(turned)
            add(row * blocks_here + idx[0, slot], jnp.sum(turned, axis=0, keepdims=True))
            add(idx[1, slot], jnp.sum(tile, axis=0, keepdims=True))
            if k == 0:
                home_tiles[j] = pack(tile)
            tiles.append(tile)
        if k > 0:
            lines = ([], [])
            for inner in range(per_core):
                at = slice(inner * BLOCK, (inner + 1) * BLOCK)
                steps, power, part = encode(jnp.where(core == 0, tiles[inner], tiles[per_core + inner]))
                sends[k - 1][at, :] = steps
                lines[0].append(power)
                lines[1].append(part)
            pick_columns(idx, k, row_count, capacity, codes, powers, parts, sends[k - 1], per_core * BLOCK, lines)


def encode_blocks(values, codes, powers, parts):
    for b in range(powers.shape[0]):
        at = slice(b * BLOCK, (b + 1) * BLOCK)
        steps, power, part = encode(values[:, at])
        codes[:, at] = steps
        powers[b : b + 1, :] = power
        parts[b : b + 1, :] = part


def start_body(values, codes, powers, parts):
    encode_blocks(values, codes, powers, parts)


def split_body(row_count, per_core, *refs):
    others = row_count - 1
    messages, outs = refs[:others], refs[-others:]
    for message, out in zip(messages, outs):
        scales = scale_rows(message[message.shape[0] - CODE_ROWS :, :])
        for inner in range(per_core):
            steps = message[inner * BLOCK : (inner + 1) * BLOCK, :]
            out[inner] = pack(decode(steps, scales[inner : inner + 1, :]))


def pick_columns(idx, k, row_count, capacity, codes, powers, parts, send, base, lines):
    count = codes.shape[0]
    back = row_count - k
    blocks = [idx[0, k * capacity + j] for j in range(capacity)]
    blocks += [idx[4, back * capacity + j] for j in range(capacity)]
    for place, block in enumerate(blocks):
        send[base + place * count : base + (place + 1) * count, :] = codes[:, at_block(block)]
        lines[0].append(powers[pl.ds(block, 1), :])
        lines[1].append(parts[pl.ds(block, 1), :])
    send[base + len(blocks) * count :, :] = as_rows(*lines, CODE_ROWS)


def add_product(out, block, packed, values):
    place = at_block(block)
    out[:, place] = out[:, place] + product(packed, values)


def apply_own(dims, me, idx, inverse, own, near_tiles, home_tiles, self_tiles, out):
    row_count, capacity, per_core, blocks_here, tile_count = dims
    row, tile_index = me[0], me[1]
    out[...] = jnp.zeros(out.shape, F32)

    def scaled(block):
        return own[:, at_block(block)] * inverse[pl.ds(row * blocks_here + block, 1), :]

    for i in range(blocks_here // tile_count):
        block = i * tile_count + tile_index
        add_product(out, block, self_tiles[i], scaled(block))
    idx = idx.ready()
    for j in range(capacity):
        add_product(out, idx[0, j], near_tiles[j], scaled(idx[4, j]))
        add_product(out, idx[4, j], home_tiles[j], scaled(idx[0, j]))
    return idx


def apply_far(dims, me, idx, inverse, received, base, near_tiles, sent, shared, out):
    row_count, capacity, per_core, blocks_here, tile_count = dims
    core = me[2]
    count = out.shape[0]
    lines = [scale_rows(message[message.shape[0] - CODE_ROWS :, :]) for message in received]
    first_line = base // BLOCK

    def arrived(k, place, block):
        steps = received[k - 1][pl.ds(pl.multiple_of(base + place * count, CODE_ROWS), count), :]
        rows = lines[k - 1][first_line : first_line + 2 * capacity, :]
        return decode(steps, row_at(rows, place) * inverse[pl.ds(block, 1), :])

    for k in range(1, row_count):
        for j in range(capacity):
            slot = k * capacity + j
            values = arrived(row_count - k, capacity + j, idx[1, slot])
            add_product(out, idx[0, slot], near_tiles[slot], values)
            inner = j % per_core
            if j < per_core:
                place = core * per_core + inner
                packed = sent[k - 1][inner]
            else:
                place = (1 - core) * per_core + inner
                packed = shared[k - 1][inner]
            slot = k * capacity + place
            add_product(out, idx[4, slot], packed, arrived(k, place, idx[5, slot]))


def first_own_body(dims, me, idx, mine, other, own, near_tiles, home_tiles, self_tiles, out, degree, inverse):
    total = mine[...] + other[...]
    degree[...] = total
    inverse[...] = 1.0 / jnp.sqrt(total)
    apply_own(dims, me, idx, inverse, own, near_tiles, home_tiles, self_tiles, out)


def first_far_body(dims, coded, me, idx, inverse, started, near_tiles, *refs):
    row_count, per_core = dims[0], dims[2]
    others = row_count - 1
    sent, shared, messages = refs[:others], refs[others : 2 * others], refs[2 * others : 3 * others]
    out, total = refs[3 * others :]
    total[...] = started[...]
    apply_far(dims, me, idx.ready(), inverse, messages, per_core * BLOCK, near_tiles, sent, shared, total)
    put_sum(coded, total, out)


def second_apply_body(dims, me, idx, inverse, after, own, home_tiles, self_tiles, near_tiles, *refs):
    others = dims[0] - 1
    sent, shared, received = refs[:others], refs[others : 2 * others], refs[2 * others : 3 * others]
    out = refs[-1]
    idx = apply_own(dims, me, idx, inverse, own, near_tiles, home_tiles, self_tiles, out)
    apply_far(dims, me, idx, inverse, received, 0, near_tiles, sent, shared, out)


def send_sum_body(coded, total, after, out):
    put_sum(coded, total, out)


def put_sum(coded, total, out):
    if not coded:
        out[...] = total[...]
        return
    lines = ([], [])
    blocks_here = total.shape[1] // BLOCK
    for b in range(blocks_here):
        at = slice(b * BLOCK, (b + 1) * BLOCK)
        steps, power, part = encode(total[:, at])
        out[:, at] = steps
        lines[0].append(power)
        lines[1].append(part)
    out[:, blocks_here * BLOCK :] = as_rows(*lines, out.shape[0])


def take_sum(coded, me, blocks_here, inverse, mine, other, out):
    if coded:
        tail = blocks_here * BLOCK
        my_scales, other_scales = scale_rows(mine[:, tail:]), scale_rows(other[:, tail:])
    for b in range(blocks_here):
        at = slice(b * BLOCK, (b + 1) * BLOCK)
        row = inverse[pl.ds(me[0] * blocks_here + b, 1), :]
        if coded:
            line = slice(b, b + 1)
            value = decode(mine[:, at], my_scales[line]) + decode(other[:, at], other_scales[line])
        else:
            value = mine[:, at] + other[:, at]
        out[:, at] = value * row


def mapped_body(dims, coded, me, idx, inverse, mine, other, out, *refs):
    row_count, capacity, per_core, blocks_here, tile_count = dims
    sends, (codes, powers, parts) = refs[:-3], refs[-3:]
    take_sum(coded, me, blocks_here, inverse, mine, other, out)
    encode_blocks(out, codes, powers, parts)
    idx = idx.ready()
    for k in range(1, row_count):
        pick_columns(idx, k, row_count, capacity, codes, powers, parts, sends[k - 1], 0, ([], []))


def last_mapped_body(blocks_here, coded, me, inverse, mine, other, after, out):
    take_sum(coded, me, blocks_here, inverse, mine, other, out)


def folded(square):
    half = square.shape[0] // 2
    return jnp.concatenate([square[:half], square[half:]], axis=1)


def unfolded(terms):
    total = functools.reduce(lambda total, term: total + term[...], terms[1:], terms[0][...])
    width = total.shape[1] // 2
    return jnp.concatenate([total[:, :width], total[:, width:]], axis=0)


def gram_body(me, own, other, out):
    full = both_columns(me[2], own[...], other[...])
    out[...] = folded(gram(pack(full), full.shape[0]))


def factor_body(after, *refs):
    refs[-1][...] = lower_inverse(unfolded(refs[:-1]))


def second_gram_body(me, factor, own, other, mapped, out):
    full = both_columns(me[2], own[...], other[...])
    parts = thirds(times(factor[...], pack(full)))
    mapped[...] = parts[: mapped.shape[0]]
    out[...] = folded(gram(parts, full.shape[0]))


def final_body(me, mapped, *refs):
    terms, (out, value, sent) = refs[:-3], refs[-3:]
    factor = lower_inverse(unfolded(terms))
    own_cols = value.shape[0]
    part = jnp.where(me[2] == 0, factor[:own_cols], factor[own_cols:])
    copies = []
    chunk = value.shape[1] // sent.shape[0]
    for i in range(sent.shape[0]):
        at = slice(i * chunk, (i + 1) * chunk)
        value[:, at] = times(part, mapped[:, at])
        copies.append(pltpu.make_async_copy(value.at[:, at], out.at[:, at], sent.at[i]))
        copies[-1].start()
    for copy in copies:
        copy.wait()


def shift_by(value, axes, size, shift):
    return lax.ppermute(value, axes, [(i, (i + shift) % size) for i in range(size)])


def row_terms(value, row_count):
    return [value] + [shift_by(value, "rows", row_count, k) for k in range(1, row_count)]


def pair_step(value, name, flip):
    return lax.ppermute(value, name, [(i, i ^ flip) for i in range(lax.axis_size(name))])


def pair_sum(value, axes):
    terms = None
    steps = [(name, 1 << bit) for name in axes for bit in range((lax.axis_size(name) - 1).bit_length())]
    for name, flip in steps:
        if terms is not None:
            value = terms[0] + terms[1]
        terms = (value, pair_step(value, name, flip))
    return terms


def local(embeddings, start, pair_list, pair_count):
    row_count = lax.axis_size("rows")
    tile_count = lax.axis_size("tiles")
    core_count = lax.axis_size("cols")
    row_index = lax.axis_index("rows")
    tile_index = lax.axis_index("tiles")
    col_index = lax.axis_index("cols")
    rows_here, half_features = embeddings.shape
    blocks_here = rows_here // BLOCK
    slots = pair_list.shape[2]
    capacity = slots // row_count
    per_core = capacity // core_count
    own_blocks = blocks_here // tile_count
    own_cols = start.shape[1]
    block_count = row_count * blocks_here
    others = range(1, row_count)

    list_order = [0, *sorted(others, key=lambda k: k * (row_count - k))]
    lists = [shift_by(pair_list[0], "rows", row_count, k) if k else pair_list[0] for k in list_order]
    self_part = call(
        functools.partial(self_distance_body, own_blocks, tile_count),
        sds((own_blocks * BLOCK, BLOCK), F32),
        [ME, embeddings],
    )
    planned = call(
        functools.partial(plan_body, (row_count, capacity, slots, blocks_here), list_order),
        [sds((6, slots + 1), jnp.int32)] + [sds((capacity * BLOCK, half_features), BF16) for _ in others],
        [ME, *lists, embeddings, self_part],
        late=range(1, 1 + row_count),
        any_in=(row_count + 2,),
        any_out=(0,),
        scratch=[pltpu.SMEM((6, slots + 1), jnp.int32), pltpu.SemaphoreType.DMA],
    )
    idx, sends = planned[0], planned[1:]
    order = sorted(others, key=lambda k: abs(k - row_count // 2))
    far = [shift_by(sends[k - 1], "rows", row_count, -k) for k in order]

    self_other = shift_by(self_part, "cols", core_count, 1)
    self_tiles, self_sums = call(
        functools.partial(self_tile_body, own_blocks),
        [sds((own_blocks, 2 * BLOCK, BLOCK), BF16), sds((own_blocks, BLOCK), F32)],
        [self_part, self_other],
    )
    values = start.T
    code_shapes = [((own_cols, rows_here), jnp.int16), ((blocks_here, BLOCK), F32), ((blocks_here, BLOCK), F32)]
    start_codes = call(start_body, [sds(*shape) for shape in code_shapes], [values])
    code_scratch = [pltpu.VMEM(*shape) for shape in code_shapes]
    coded = tile_count == 2
    own_squares, home = call(
        functools.partial(squares_body, capacity),
        [sds((rows_here, BLOCK), F32), sds((capacity * BLOCK, BLOCK), F32)],
        [idx, embeddings],
        late=(0,),
    )
    pair_part = call(
        functools.partial(pair_distance_body, order, capacity),
        sds((slots * BLOCK, BLOCK), F32),
        [idx, embeddings, own_squares, home, *far],
        late=(0,),
    )
    pair_other = shift_by(pair_part, "cols", core_count, 1)

    dims = (row_count, capacity, per_core, blocks_here, tile_count)
    table = sds((block_count, BLOCK), F32)
    picked = 2 * capacity * own_cols
    tiles = call(
        functools.partial(pair_tile_body, dims),
        [sds((slots, 2 * BLOCK, BLOCK), BF16), sds((capacity, 2 * BLOCK, BLOCK), BF16), table]
        + [sds((per_core * BLOCK + picked + CODE_ROWS, BLOCK), jnp.int16) for _ in others],
        [ME, idx, pair_count, pair_part, pair_other, self_sums, *start_codes],
        late=(1, 2),
    )
    near_tiles, home_tiles, degrees, sends = tiles[0], tiles[1], tiles[2], tiles[3:]
    degrees = functools.reduce(jnp.add, row_terms(degrees, row_count))
    degree_terms = pair_sum(degrees, ("tiles",))
    messages = [shift_by(sends[k - 1], "rows", row_count, k) for k in others]
    sent = call(
        functools.partial(split_body, row_count, per_core),
        [sds((per_core, 2 * BLOCK, BLOCK), BF16) for _ in others],
        [*messages, degree_terms[1]],
        any_in=(row_count - 1,),
    )
    shared = [shift_by(tile, "cols", core_count, 1) for tile in sent]

    block_shape = sds((own_cols, rows_here), F32)
    sum_shape = sds((own_cols, rows_here + BLOCK), jnp.int16) if coded else block_shape
    square = sds((2 * own_cols, 2 * own_cols), F32)
    folded_square = sds((own_cols, 4 * own_cols), F32)

    started, degree, inverse = call(
        functools.partial(first_own_body, dims),
        [block_shape, table, table],
        [ME, idx, *degree_terms, values, near_tiles, home_tiles, self_tiles],
        late=(1,),
    )
    part = call(
        functools.partial(first_far_body, dims, coded),
        sum_shape,
        [ME, idx, inverse, started, near_tiles, *sent, *shared, *messages],
        late=(1,),
        scratch=[pltpu.VMEM((own_cols, rows_here), F32)],
    )
    mine, other = pair_sum(part, ("tiles",))
    first = call(
        functools.partial(mapped_body, dims, coded),
        [block_shape] + [sds((picked + CODE_ROWS, BLOCK), jnp.int16) for _ in others],
        [ME, idx, inverse, mine, other],
        late=(1,),
        scratch=code_scratch,
    )
    mapped, sends = first[0], first[1:]
    received = [shift_by(sends[k - 1], "rows", row_count, k) for k in others]

    mapped_other = shift_by(mapped, "cols", core_count, 1)
    first_gram = call(gram_body, folded_square, [ME, mapped, mapped_other])
    part = call(
        functools.partial(second_apply_body, dims),
        block_shape,
        [ME, idx, inverse, first_gram, mapped, home_tiles, self_tiles, near_tiles, *sent, *shared, *received],
        late=(1,),
        any_in=(3,),
    )
    steps = (row_count - 1).bit_length()
    for bit in range(steps - 1):
        first_gram = first_gram + pair_step(first_gram, "rows", 1 << bit)
    part = call(functools.partial(send_sum_body, coded), sum_shape, [part, first_gram])
    gram_terms = (first_gram, pair_step(first_gram, "rows", 1 << (steps - 1)))
    mine, other = pair_sum(part, ("tiles",))
    second = call(
        functools.partial(last_mapped_body, blocks_here, coded),
        block_shape,
        [ME, inverse, mine, other, gram_terms[1]],
        any_in=(4,),
    )
    second_other = shift_by(second, "cols", core_count, 1)
    factor = call(factor_body, square, [second, *gram_terms], any_in=(0,))
    full, second_gram = call(
        second_gram_body,
        [sds((4 * own_cols, rows_here), BF16), folded_square],
        [ME, factor, second, second_other],
    )
    vectors = call(
        final_body,
        block_shape,
        [ME, full, *row_terms(second_gram, row_count)],
        any_out=(0,),
        scratch=[pltpu.VMEM((own_cols, rows_here), F32), pltpu.SemaphoreType.DMA((4,))],
    )
    own_degree = lax.dynamic_slice_in_dim(degree, row_index * blocks_here, blocks_here, 0)
    return (vectors.T, own_degree.reshape(rows_here))


def solution(mesh):
    in_specs = (
        P(("groups", "rows"), "cols"),
        P(("groups", "rows"), "cols"),
        P(("groups", "rows", "tiles"), None, None),
        P(("groups", "rows", "tiles")),
    )
    out_specs = (P(("groups", "rows"), "cols"), P(("groups", "rows")))
    return jax.shard_map(local, mesh=mesh, in_specs=in_specs, out_specs=out_specs, check_vma=False)
```

```python
import functools

import jax
import jax.numpy as jnp
from jax import lax
from jax.experimental import pallas as pl
from jax.experimental.pallas import tpu as pltpu
from jax.sharding import PartitionSpec as P

BLOCK = 128
kernel_gamma = 14.0
CODE_TOP = 32767.0
PART_TOP = 16384.0
CODE_ROWS = 16

VMEM = pl.BlockSpec(memory_space=pltpu.VMEM)
ANY = pl.BlockSpec(memory_space=pl.ANY)
F32 = jnp.float32
BF16 = jnp.bfloat16
HIGHEST = lax.Precision.HIGHEST
NT = (((1,), (1,)), ((), ()))


ME = None


def with_position(body):
    def inner(*refs):
        return body([lax.axis_index(name) for name in ("rows", "tiles", "cols")], *refs)

    return inner


class Late:
    def __init__(self, source, table, arrived):
        self.table = table
        self.copy = pltpu.make_async_copy(source, table, arrived)
        self.copy.start()

    def ready(self):
        self.copy.wait()
        return self.table


def with_late(body, places, count):
    def inner(*refs):
        refs, tables, arrived = refs[:-1 - count], refs[-1 - count : -1], refs[-1]
        refs = list(refs)
        for i, place in enumerate(places):
            refs[place] = Late(refs[place], tables[i], arrived.at[i])
        body(*refs)

    return inner


def call(body, outs, args, late=(), any_in=(), scratch=(), any_out=()):
    if args[0] is ME:
        body, args = with_position(body), args[1:]
        late, any_in = [[i - 1 for i in places] for places in (late, any_in)]
    if late:
        scratch = [
            *scratch,
            *[pltpu.SMEM(args[i].shape, args[i].dtype) for i in late],
            pltpu.SemaphoreType.DMA((len(late),)),
        ]
        any_in = [*any_in, *late]
        body = with_late(body, late, len(late))
    single = not isinstance(outs, (list, tuple))
    shapes = [outs] if single else list(outs)
    result = pl.pallas_call(
        body,
        out_shape=shapes,
        in_specs=[ANY if i in any_in else VMEM for i in range(len(args))],
        out_specs=[ANY if i in any_out else VMEM for i in range(len(shapes))],
        scratch_shapes=list(scratch),
        compiler_params=pltpu.CompilerParams(vmem_limit_bytes=48 * 2**20),
    )(*args)
    return result[0] if single else result


def sds(shape, dtype):
    return jax.ShapeDtypeStruct(shape, dtype)


def at_block(index):
    return pl.ds(pl.multiple_of(index * BLOCK, BLOCK), BLOCK)


def eye_mask(size):
    return lax.broadcasted_iota(jnp.int32, (size, size), 0) == lax.broadcasted_iota(
        jnp.int32, (size, size), 1
    )


def halves(value):
    high = value.astype(BF16)
    low = (value - high.astype(F32)).astype(BF16)
    return high, low


def pack(tile):
    return jnp.concatenate(halves(tile), axis=0)


def scale_of(power, part):
    return jnp.exp2(power) * (part * (1.0 / PART_TOP))


def encode(values):
    most = jnp.maximum(jnp.max(jnp.abs(values), axis=0, keepdims=True), 1e-30)
    power = jnp.floor(jnp.log2(most)) + 1.0
    part = jnp.floor(most * jnp.exp2(-power) * PART_TOP) + 1.0
    steps = jnp.floor(values * (CODE_TOP / scale_of(power, part)) + 0.5)
    steps = jnp.minimum(jnp.maximum(steps, -CODE_TOP), CODE_TOP)
    return steps.astype(jnp.int32).astype(jnp.int16), power, part


def decode(steps, scale):
    return steps.astype(jnp.int32).astype(F32) * (scale * (1.0 / CODE_TOP))


def as_rows(powers, parts, count):
    fill = jnp.zeros((count // 2 - len(powers), BLOCK), F32)
    fill = [fill] if fill.shape[0] else []
    rows = jnp.concatenate([*powers, *fill, *parts, *fill], axis=0)
    return rows.astype(jnp.int32).astype(jnp.int16)


def scale_rows(rows):
    rows = rows.astype(jnp.int32).astype(F32)
    half = rows.shape[0] // 2
    return scale_of(rows[:half], rows[half:])


def row_at(rows, place):
    if isinstance(place, int):
        return rows[place : place + 1, :]
    line = rows[:1, :]
    for i in range(1, rows.shape[0]):
        line = jnp.where(place == i, rows[i : i + 1, :], line)
    return line


def product(packed, values):
    left = jnp.concatenate(halves(values), axis=0)
    both = jnp.dot(jnp.concatenate([left, left], axis=1), packed, preferred_element_type=F32)
    count = values.shape[0]
    return both[:count] + both[count:]


def thirds(value):
    high = value.astype(BF16)
    rest = value - high.astype(F32)
    middle = rest.astype(BF16)
    low = (rest - middle.astype(F32)).astype(BF16)
    return jnp.concatenate([high, middle, low], axis=0)


def gram(parts, n):
    cross = lax.dot_general(parts, parts, NT, preferred_element_type=F32)
    count = parts.shape[0] // n
    pairs = sorted(((i, j) for i in range(count) for j in range(count)), key=lambda p: -p[0] - p[1])
    total = None
    for i, j in pairs:
        piece = cross[i * n : (i + 1) * n, j * n : (j + 1) * n]
        total = piece if total is None else total + piece
    return total


def times(left, parts):
    m = left.shape[0]
    left = jnp.concatenate(halves(left), axis=0)
    both = jnp.dot(jnp.concatenate([left, left], axis=1), parts, preferred_element_type=F32)
    return both[m:] + both[:m]


def lower_inverse(matrix, step=8):
    n = matrix.shape[0]
    state = jnp.concatenate([matrix, eye_mask(n).astype(F32)], axis=1)
    done = []
    for j in range(0, n, step):
        top = j // 8 * 8
        if top > n - state.shape[0]:
            done.append(state[:8])
            state = state[8:]
        base = j - top
        rows = lax.broadcasted_iota(jnp.int32, state.shape, 0)
        columns = [jnp.broadcast_to(state[:, j + i : j + i + 1], state.shape) for i in range(step)]
        lines = [state[base + i : base + i + 1, :] for i in range(step)]
        pivot = [[columns[k][base + i : base + i + 1, :] for k in range(step)] for i in range(step)]
        for i in range(step):
            if i % 2 == 0:
                first, cross, second = pivot[i][i], pivot[i][i + 1], pivot[i + 1][i + 1]
                reciprocals = (1.0 / first, first / (first * second - cross * cross))
            reciprocal = reciprocals[i % 2]
            scaled = lines[i] * reciprocal
            ratio = [pivot[i][k] * reciprocal for k in range(step)]
            for k in range(i + 1, step):
                lines[k] = lines[k] - pivot[i][k] * scaled
                columns[k] = columns[k] - columns[i] * ratio[k]
                for m in range(k, step):
                    pivot[k][m] = pivot[k][m] - pivot[i][k] * ratio[m]
            state = state - jnp.where(rows > base + i, columns[i], 0.0) * scaled
    state = jnp.concatenate([*done, state], axis=0)
    pivots = jnp.sum(jnp.where(eye_mask(n), state[:, :n], 0.0), axis=1, keepdims=True)
    return state[:, n:] / jnp.sqrt(pivots)


def both_columns(core, own, other):
    first = core == 0
    return jnp.concatenate(
        [jnp.where(first, own, other), jnp.where(first, other, own)], axis=0
    )


def quotient(value, size):
    if size & (size - 1) == 0:
        return lax.shift_right_logical(value, jnp.int32(size.bit_length() - 1))
    return lax.div(value, jnp.int32(size))


def remainder(value, size):
    if size & (size - 1) == 0:
        return lax.bitwise_and(value, jnp.int32(size - 1))
    return lax.rem(value, jnp.int32(size))


def plan_body(dims, list_order, me, *refs):
    row_count, capacity, slots, blocks_here = dims
    lists, (emb, after, idx_out) = refs[:row_count], refs[row_count : row_count + 3]
    sends, (idx, left) = refs[row_count + 3 : -2], refs[-2:]
    row = me[0]
    for i in range(slots):
        for line in (0, 1, 4, 5):
            idx[line, i] = 0
        idx[3, i] = slots
    lists = dict(zip(list_order, [one.ready() for one in lists]))

    def each(step, start):
        if slots <= 8:
            for s in range(slots):
                start = step(s, start)
        else:
            lax.fori_loop(0, slots, step, start)

    for k in range(row_count):

        def step(s, counts, k=k):
            near = lists[k][0, s]
            far = lists[k][1, s]
            owner = quotient(far, blocks_here)
            if k > 0:
                hit = (owner == row) & (counts[0] < capacity)
                slot = jnp.where(hit, k * capacity + counts[0], slots)
                idx[4, slot] = far - row * blocks_here
                idx[5, slot] = near
                return (counts[0] + hit.astype(jnp.int32),)
            shift = remainder(owner - row + row_count, row_count)
            rank = counts[0]
            for d in range(1, row_count):
                rank = jnp.where(shift == d, counts[d], rank)
            slot = jnp.where(rank < capacity, shift * capacity + rank, slots)
            idx[0, slot] = near - row * blocks_here
            idx[1, slot] = far
            idx[3, slot] = s
            slot = jnp.where(shift == 0, slot, slots)
            idx[4, slot] = far - row * blocks_here
            idx[5, slot] = near
            return tuple(counts[d] + (shift == d).astype(jnp.int32) for d in range(row_count))

        each(step, (jnp.int32(0),) * (row_count if k == 0 else 1))
    leave = pltpu.make_async_copy(idx, idx_out, left)
    leave.start()
    for k in range(1, row_count):
        for j in range(capacity):
            sends[k - 1][j * BLOCK : (j + 1) * BLOCK, :] = emb[at_block(idx[4, k * capacity + j]), :]
    leave.wait()


def squares(block):
    return jnp.sum(jnp.square(block.astype(F32)), axis=1, keepdims=True)


def as_row(column):
    return jnp.sum(jnp.where(eye_mask(BLOCK), column, 0.0), axis=0, keepdims=True)


def partial_distance(left, right, left_sq, right_row):
    inner = lax.dot_general(left, right, NT, preferred_element_type=F32)
    return left_sq + right_row - 2.0 * inner


def self_distance_body(own_blocks, tile_count, me, emb, out):
    for i in range(own_blocks):
        block = emb[at_block(i * tile_count + me[1]), :]
        block_sq = squares(block)
        out[i * BLOCK : (i + 1) * BLOCK, :] = partial_distance(
            block, block, block_sq, as_row(block_sq)
        )


def squares_body(capacity, idx, emb, out, home):
    for b in range(out.shape[0] // BLOCK):
        part = slice(b * BLOCK, (b + 1) * BLOCK)
        out[part, :] = jnp.broadcast_to(squares(emb[part, :]), (BLOCK, BLOCK))
    idx = idx.ready()
    for j in range(capacity):
        left, right = at_block(idx[0, j]), at_block(idx[4, j])
        home[j * BLOCK : (j + 1) * BLOCK, :] = partial_distance(
            emb[left, :], emb[right, :], out[left, :], as_row(out[right, :])
        )


def pair_distance_body(order, capacity, idx, emb, own_squares, home, *refs):
    far, out = dict(zip(order, refs)), refs[-1]
    rows = {}
    for k in order:
        for j in range(capacity):
            rows[k, j] = as_row(squares(far[k][j * BLOCK : (j + 1) * BLOCK, :]))
    idx = idx.ready()
    out[: capacity * BLOCK, :] = home[...]
    for k in range(1, len(order) + 1):
        for j in range(capacity):
            slot = k * capacity + j
            left = emb[at_block(idx[0, slot]), :]
            left_sq = own_squares[at_block(idx[0, slot]), :]
            right = far[k][j * BLOCK : (j + 1) * BLOCK, :]
            part = slice(slot * BLOCK, (slot + 1) * BLOCK)
            out[part, :] = partial_distance(left, right, left_sq, rows[k, j])


def self_tile_body(own_blocks, mine, other, packed, sums):
    for i in range(own_blocks):
        part = slice(i * BLOCK, (i + 1) * BLOCK)
        tile = jnp.exp(-kernel_gamma * (mine[part, :] + other[part, :] - 2.0))
        tile = jnp.where(eye_mask(BLOCK), 0.0, tile)
        packed[i] = pack(tile)
        sums[i : i + 1, :] = jnp.sum(tile, axis=0, keepdims=True)


def pair_tile_body(dims, me, idx, live_count, mine, other, self_sums, codes, powers, parts, near_tiles, home_tiles, table, *sends):
    row_count, capacity, per_core, blocks_here, tile_count = dims
    row, tile_index, core = me[0], me[1], me[2]
    table[...] = jnp.zeros(table.shape, F32)
    for i in range(self_sums.shape[0]):
        table[pl.ds(row * blocks_here + i * tile_count + tile_index, 1), :] = self_sums[i : i + 1, :]

    def add(block, line):
        place = pl.ds(block, 1)
        table[place, :] = table[place, :] + line

    all_tiles = jnp.exp(-kernel_gamma * (mine[...] + other[...] - 2.0))
    idx = idx.ready()
    live_count = live_count.ready()[0]
    for k in range(row_count):
        tiles = []
        for j in range(capacity):
            slot = k * capacity + j
            tile = all_tiles[slot * BLOCK : (slot + 1) * BLOCK]
            tile = jnp.where(idx[3, slot] < live_count, tile, 0.0)
            turned = tile.T
            near_tiles[slot] = pack(turned)
            add(row * blocks_here + idx[0, slot], jnp.sum(turned, axis=0, keepdims=True))
            add(idx[1, slot], jnp.sum(tile, axis=0, keepdims=True))
            if k == 0:
                home_tiles[j] = pack(tile)
            tiles.append(tile)
        if k > 0:
            lines = ([], [])
            for inner in range(per_core):
                at = slice(inner * BLOCK, (inner + 1) * BLOCK)
                steps, power, part = encode(jnp.where(core == 0, tiles[inner], tiles[per_core + inner]))
                sends[k - 1][at, :] = steps
                lines[0].append(power)
                lines[1].append(part)
            pick_columns(idx, k, row_count, capacity, codes, powers, parts, sends[k - 1], per_core * BLOCK, lines)


def encode_blocks(values, codes, powers, parts):
    for b in range(powers.shape[0]):
        at = slice(b * BLOCK, (b + 1) * BLOCK)
        steps, power, part = encode(values[:, at])
        codes[:, at] = steps
        powers[b : b + 1, :] = power
        parts[b : b + 1, :] = part


def start_body(values, codes, powers, parts):
    encode_blocks(values, codes, powers, parts)


def split_body(row_count, per_core, *refs):
    others = row_count - 1
    messages, outs = refs[:others], refs[-others:]
    for message, out in zip(messages, outs):
        scales = scale_rows(message[message.shape[0] - CODE_ROWS :, :])
        for inner in range(per_core):
            steps = message[inner * BLOCK : (inner + 1) * BLOCK, :]
            out[inner] = pack(decode(steps, scales[inner : inner + 1, :]))


def pick_columns(idx, k, row_count, capacity, codes, powers, parts, send, base, lines):
    count = codes.shape[0]
    back = row_count - k
    blocks = [idx[0, k * capacity + j] for j in range(capacity)]
    blocks += [idx[4, back * capacity + j] for j in range(capacity)]
    for place, block in enumerate(blocks):
        send[base + place * count : base + (place + 1) * count, :] = codes[:, at_block(block)]
        lines[0].append(powers[pl.ds(block, 1), :])
        lines[1].append(parts[pl.ds(block, 1), :])
    send[base + len(blocks) * count :, :] = as_rows(*lines, CODE_ROWS)


def add_product(out, block, packed, values):
    place = at_block(block)
    out[:, place] = out[:, place] + product(packed, values)


def apply_own(dims, me, idx, inverse, own, near_tiles, home_tiles, self_tiles, out):
    row_count, capacity, per_core, blocks_here, tile_count = dims
    row, tile_index = me[0], me[1]
    out[...] = jnp.zeros(out.shape, F32)

    def scaled(block):
        return own[:, at_block(block)] * inverse[pl.ds(row * blocks_here + block, 1), :]

    for i in range(blocks_here // tile_count):
        block = i * tile_count + tile_index
        add_product(out, block, self_tiles[i], scaled(block))
    idx = idx.ready()
    for j in range(capacity):
        add_product(out, idx[0, j], near_tiles[j], scaled(idx[4, j]))
        add_product(out, idx[4, j], home_tiles[j], scaled(idx[0, j]))
    return idx


def apply_far(dims, me, idx, inverse, received, base, near_tiles, sent, shared, out):
    row_count, capacity, per_core, blocks_here, tile_count = dims
    core = me[2]
    count = out.shape[0]
    lines = [scale_rows(message[message.shape[0] - CODE_ROWS :, :]) for message in received]
    first_line = base // BLOCK

    def arrived(k, place, block):
        steps = received[k - 1][pl.ds(pl.multiple_of(base + place * count, CODE_ROWS), count), :]
        rows = lines[k - 1][first_line : first_line + 2 * capacity, :]
        return decode(steps, row_at(rows, place) * inverse[pl.ds(block, 1), :])

    for k in range(1, row_count):
        for j in range(capacity):
            slot = k * capacity + j
            values = arrived(row_count - k, capacity + j, idx[1, slot])
            add_product(out, idx[0, slot], near_tiles[slot], values)
            inner = j % per_core
            if j < per_core:
                place = core * per_core + inner
                packed = sent[k - 1][inner]
            else:
                place = (1 - core) * per_core + inner
                packed = shared[k - 1][inner]
            slot = k * capacity + place
            add_product(out, idx[4, slot], packed, arrived(k, place, idx[5, slot]))


def first_own_body(dims, me, idx, mine, other, own, near_tiles, home_tiles, self_tiles, out, degree, inverse):
    total = mine[...] + other[...]
    degree[...] = total
    inverse[...] = 1.0 / jnp.sqrt(total)
    apply_own(dims, me, idx, inverse, own, near_tiles, home_tiles, self_tiles, out)


def first_far_body(dims, coded, me, idx, inverse, started, near_tiles, *refs):
    row_count, per_core = dims[0], dims[2]
    others = row_count - 1
    sent, shared, messages = refs[:others], refs[others : 2 * others], refs[2 * others : 3 * others]
    out, total = refs[3 * others :]
    total[...] = started[...]
    apply_far(dims, me, idx.ready(), inverse, messages, per_core * BLOCK, near_tiles, sent, shared, total)
    put_sum(coded, total, out)


def second_apply_body(dims, me, idx, inverse, after, own, home_tiles, self_tiles, near_tiles, *refs):
    others = dims[0] - 1
    sent, shared, received = refs[:others], refs[others : 2 * others], refs[2 * others : 3 * others]
    out = refs[-1]
    idx = apply_own(dims, me, idx, inverse, own, near_tiles, home_tiles, self_tiles, out)
    apply_far(dims, me, idx, inverse, received, 0, near_tiles, sent, shared, out)


def send_sum_body(coded, total, after, out):
    put_sum(coded, total, out)


def put_sum(coded, total, out):
    if not coded:
        out[...] = total[...]
        return
    lines = ([], [])
    blocks_here = total.shape[1] // BLOCK
    for b in range(blocks_here):
        at = slice(b * BLOCK, (b + 1) * BLOCK)
        steps, power, part = encode(total[:, at])
        out[:, at] = steps
        lines[0].append(power)
        lines[1].append(part)
    out[:, blocks_here * BLOCK :] = as_rows(*lines, out.shape[0])


def take_sum(coded, me, blocks_here, inverse, mine, other, out):
    if coded:
        tail = blocks_here * BLOCK
        my_scales, other_scales = scale_rows(mine[:, tail:]), scale_rows(other[:, tail:])
    for b in range(blocks_here):
        at = slice(b * BLOCK, (b + 1) * BLOCK)
        row = inverse[pl.ds(me[0] * blocks_here + b, 1), :]
        if coded:
            line = slice(b, b + 1)
            value = decode(mine[:, at], my_scales[line]) + decode(other[:, at], other_scales[line])
        else:
            value = mine[:, at] + other[:, at]
        out[:, at] = value * row


def mapped_body(dims, coded, me, idx, inverse, mine, other, out, *refs):
    row_count, capacity, per_core, blocks_here, tile_count = dims
    sends, (codes, powers, parts) = refs[:-3], refs[-3:]
    take_sum(coded, me, blocks_here, inverse, mine, other, out)
    encode_blocks(out, codes, powers, parts)
    idx = idx.ready()
    for k in range(1, row_count):
        pick_columns(idx, k, row_count, capacity, codes, powers, parts, sends[k - 1], 0, ([], []))


def last_mapped_body(blocks_here, coded, me, inverse, mine, other, after, out):
    take_sum(coded, me, blocks_here, inverse, mine, other, out)


def folded(square):
    half = square.shape[0] // 2
    return jnp.concatenate([square[:half], square[half:]], axis=1)


def unfolded(terms):
    total = functools.reduce(lambda total, term: total + term[...], terms[1:], terms[0][...])
    width = total.shape[1] // 2
    return jnp.concatenate([total[:, :width], total[:, width:]], axis=0)


def gram_body(me, own, other, out):
    full = both_columns(me[2], own[...], other[...])
    out[...] = folded(gram(pack(full), full.shape[0]))


def factor_body(after, *refs):
    refs[-1][...] = lower_inverse(unfolded(refs[:-1]))


def second_gram_body(me, factor, own, other, mapped, out):
    full = both_columns(me[2], own[...], other[...])
    parts = thirds(times(factor[...], pack(full)))
    mapped[...] = parts[: mapped.shape[0]]
    out[...] = folded(gram(parts, full.shape[0]))


def final_body(me, mapped, *refs):
    terms, (out, value, sent) = refs[:-3], refs[-3:]
    factor = lower_inverse(unfolded(terms))
    own_cols = value.shape[0]
    part = jnp.where(me[2] == 0, factor[:own_cols], factor[own_cols:])
    copies = []
    chunk = value.shape[1] // sent.shape[0]
    for i in range(sent.shape[0]):
        at = slice(i * chunk, (i + 1) * chunk)
        value[:, at] = times(part, mapped[:, at])
        copies.append(pltpu.make_async_copy(value.at[:, at], out.at[:, at], sent.at[i]))
        copies[-1].start()
    for copy in copies:
        copy.wait()


def shift_by(value, axes, size, shift):
    return lax.ppermute(value, axes, [(i, (i + shift) % size) for i in range(size)])


def row_terms(value, row_count):
    return [value] + [shift_by(value, "rows", row_count, k) for k in range(1, row_count)]


def pair_step(value, name, flip):
    return lax.ppermute(value, name, [(i, i ^ flip) for i in range(lax.axis_size(name))])


def pair_sum(value, axes):
    terms = None
    steps = [(name, 1 << bit) for name in axes for bit in range((lax.axis_size(name) - 1).bit_length())]
    for name, flip in steps:
        if terms is not None:
            value = terms[0] + terms[1]
        terms = (value, pair_step(value, name, flip))
    return terms


def local(embeddings, start, pair_list, pair_count):
    row_count = lax.axis_size("rows")
    tile_count = lax.axis_size("tiles")
    core_count = lax.axis_size("cols")
    row_index = lax.axis_index("rows")
    tile_index = lax.axis_index("tiles")
    col_index = lax.axis_index("cols")
    rows_here, half_features = embeddings.shape
    blocks_here = rows_here // BLOCK
    slots = pair_list.shape[2]
    capacity = slots // row_count
    per_core = capacity // core_count
    own_blocks = blocks_here // tile_count
    own_cols = start.shape[1]
    block_count = row_count * blocks_here
    others = range(1, row_count)

    list_order = [0, *sorted(others, key=lambda k: k * (row_count - k))]
    lists = [shift_by(pair_list[0], "rows", row_count, k) if k else pair_list[0] for k in list_order]
    self_part = call(
        functools.partial(self_distance_body, own_blocks, tile_count),
        sds((own_blocks * BLOCK, BLOCK), F32),
        [ME, embeddings],
    )
    planned = call(
        functools.partial(plan_body, (row_count, capacity, slots, blocks_here), list_order),
        [sds((6, slots + 1), jnp.int32)] + [sds((capacity * BLOCK, half_features), BF16) for _ in others],
        [ME, *lists, embeddings, self_part],
        late=range(1, 1 + row_count),
        any_in=(row_count + 2,),
        any_out=(0,),
        scratch=[pltpu.SMEM((6, slots + 1), jnp.int32), pltpu.SemaphoreType.DMA],
    )
    idx, sends = planned[0], planned[1:]
    order = sorted(others, key=lambda k: abs(k - row_count // 2))
    far = [shift_by(sends[k - 1], "rows", row_count, -k) for k in order]

    self_other = shift_by(self_part, "cols", core_count, 1)
    self_tiles, self_sums = call(
        functools.partial(self_tile_body, own_blocks),
        [sds((own_blocks, 2 * BLOCK, BLOCK), BF16), sds((own_blocks, BLOCK), F32)],
        [self_part, self_other],
    )
    values = start.T
    code_shapes = [((own_cols, rows_here), jnp.int16), ((blocks_here, BLOCK), F32), ((blocks_here, BLOCK), F32)]
    start_codes = call(start_body, [sds(*shape) for shape in code_shapes], [values])
    code_scratch = [pltpu.VMEM(*shape) for shape in code_shapes]
    coded = tile_count == 2
    own_squares, home = call(
        functools.partial(squares_body, capacity),
        [sds((rows_here, BLOCK), F32), sds((capacity * BLOCK, BLOCK), F32)],
        [idx, embeddings],
        late=(0,),
    )
    pair_part = call(
        functools.partial(pair_distance_body, order, capacity),
        sds((slots * BLOCK, BLOCK), F32),
        [idx, embeddings, own_squares, home, *far],
        late=(0,),
    )
    pair_other = shift_by(pair_part, "cols", core_count, 1)

    dims = (row_count, capacity, per_core, blocks_here, tile_count)
    table = sds((block_count, BLOCK), F32)
    picked = 2 * capacity * own_cols
    tiles = call(
        functools.partial(pair_tile_body, dims),
        [sds((slots, 2 * BLOCK, BLOCK), BF16), sds((capacity, 2 * BLOCK, BLOCK), BF16), table]
        + [sds((per_core * BLOCK + picked + CODE_ROWS, BLOCK), jnp.int16) for _ in others],
        [ME, idx, pair_count, pair_part, pair_other, self_sums, *start_codes],
        late=(1, 2),
    )
    near_tiles, home_tiles, degrees, sends = tiles[0], tiles[1], tiles[2], tiles[3:]
    degrees = functools.reduce(
        jnp.add, [degrees] + [shift_by(degrees, "rows", row_count, k) for k in reversed(others)]
    )
    degree_terms = pair_sum(degrees, ("tiles",))
    messages = [shift_by(sends[k - 1], "rows", row_count, k) for k in others]
    sent = call(
        functools.partial(split_body, row_count, per_core),
        [sds((per_core, 2 * BLOCK, BLOCK), BF16) for _ in others],
        [*messages, degree_terms[1]],
        any_in=(row_count - 1,),
    )
    shared = [shift_by(tile, "cols", core_count, 1) for tile in sent]

    block_shape = sds((own_cols, rows_here), F32)
    sum_shape = sds((own_cols, rows_here + BLOCK), jnp.int16) if coded else block_shape
    square = sds((2 * own_cols, 2 * own_cols), F32)
    folded_square = sds((own_cols, 4 * own_cols), F32)

    started, degree, inverse = call(
        functools.partial(first_own_body, dims),
        [block_shape, table, table],
        [ME, idx, *degree_terms, values, near_tiles, home_tiles, self_tiles],
        late=(1,),
    )
    part = call(
        functools.partial(first_far_body, dims, coded),
        sum_shape,
        [ME, idx, inverse, started, near_tiles, *sent, *shared, *messages],
        late=(1,),
        scratch=[pltpu.VMEM((own_cols, rows_here), F32)],
    )
    mine, other = pair_sum(part, ("tiles",))
    first = call(
        functools.partial(mapped_body, dims, coded),
        [block_shape] + [sds((picked + CODE_ROWS, BLOCK), jnp.int16) for _ in others],
        [ME, idx, inverse, mine, other],
        late=(1,),
        scratch=code_scratch,
    )
    mapped, sends = first[0], first[1:]
    received = [shift_by(sends[k - 1], "rows", row_count, k) for k in others]

    mapped_other = shift_by(mapped, "cols", core_count, 1)
    first_gram = call(gram_body, folded_square, [ME, mapped, mapped_other])
    part = call(
        functools.partial(second_apply_body, dims),
        block_shape,
        [ME, idx, inverse, first_gram, mapped, home_tiles, self_tiles, near_tiles, *sent, *shared, *received],
        late=(1,),
        any_in=(3,),
    )
    steps = (row_count - 1).bit_length()
    for bit in range(steps - 1):
        first_gram = first_gram + pair_step(first_gram, "rows", 1 << bit)
    part = call(functools.partial(send_sum_body, coded), sum_shape, [part, first_gram])
    gram_terms = (first_gram, pair_step(first_gram, "rows", 1 << (steps - 1)))
    mine, other = pair_sum(part, ("tiles",))
    second = call(
        functools.partial(last_mapped_body, blocks_here, coded),
        block_shape,
        [ME, inverse, mine, other, gram_terms[1]],
        any_in=(4,),
    )
    second_other = shift_by(second, "cols", core_count, 1)
    factor = call(factor_body, square, [second, *gram_terms], any_in=(0,))
    full, second_gram = call(
        second_gram_body,
        [sds((4 * own_cols, rows_here), BF16), folded_square],
        [ME, factor, second, second_other],
    )
    vectors = call(
        final_body,
        block_shape,
        [ME, full, *row_terms(second_gram, row_count)],
        any_out=(0,),
        scratch=[pltpu.VMEM((own_cols, rows_here), F32), pltpu.SemaphoreType.DMA((4,))],
    )
    own_degree = lax.dynamic_slice_in_dim(degree, row_index * blocks_here, blocks_here, 0)
    return (vectors.T, own_degree.reshape(rows_here))


def solution(mesh):
    in_specs = (
        P(("groups", "rows"), "cols"),
        P(("groups", "rows"), "cols"),
        P(("groups", "rows", "tiles"), None, None),
        P(("groups", "rows", "tiles")),
    )
    out_specs = (P(("groups", "rows"), "cols"), P(("groups", "rows")))
    return jax.shard_map(local, mesh=mesh, in_specs=in_specs, out_specs=out_specs, check_vma=False)
```
